32 devices in a mesh: rows: 8 (over z, y), seq: 4 (over x, core).
Axes of the slice: x: 2, y: 2, z: 4, core: 2. Of those that a mesh axis runs over, the one named last changes fastest.
Arguments:
- hidden_in: bfloat16 [2, 16, 1024, 768], P(None, 'rows', 'seq'), may hold values from -6 to 6
- segments: int32 [2, 16, 1024], P(None, 'rows', 'seq'), may hold values from 0 to 1, as said below
- grad_mask: int32 [2, 16, 1024], P(None, 'rows', 'seq'), may hold values 0 or 1
- grad_out: bfloat16 [2, 16, 1024, 768], P(None, 'rows', 'seq'), may hold values from -6 to 6
- query_proj: bfloat16 [768, 768], replicated, may hold values from -0.21875 to 0.21875
- query_bias: bfloat16 [768], replicated, may hold values from -3 to 3
- key_proj: bfloat16 [768, 768], replicated, may hold values from -0.21875 to 0.21875
- value_proj: bfloat16 [768, 768], replicated, may hold values from -0.21875 to 0.21875
- value_bias: bfloat16 [768], replicated, may hold values from -3 to 3
- output_proj: bfloat16 [768, 768], replicated, may hold values from -0.875 to 0.875
- output_bias: bfloat16 [768], replicated, may hold values from -1.75 to 1.75
- first_gain: bfloat16 [768], replicated, may hold values from 0.25 to 1.75
- first_shift: bfloat16 [768], replicated, may hold values from -3 to 3
- expand_proj: bfloat16 [768, 3072], replicated, may hold values from -0.21875 to 0.21875
- expand_bias: bfloat16 [3072], replicated, may hold values from -3 to 3
- shrink_proj: bfloat16 [3072, 768], replicated, may hold values from -0.109375 to 0.109375
- shrink_bias: bfloat16 [768], replicated, may hold values from -1.75 to 1.75
- second_gain: bfloat16 [768], replicated, may hold values from 0.25 to 1.75
- second_shift: bfloat16 [768], replicated, may hold values from -3 to 3
Outputs:
- layer_out: bfloat16 [2, 16, 1024, 768], P(None, 'rows', 'seq')
- grad_in: bfloat16 [2, 16, 1024, 768], P(None, 'rows', 'seq')
- query_proj_grad: float32 [768, 768], replicated
- query_bias_grad: float32 [768], replicated
- key_proj_grad: float32 [768, 768], replicated
- value_proj_grad: float32 [768, 768], replicated
- value_bias_grad: float32 [768], replicated
- output_proj_grad: float32 [768, 768], replicated
- output_bias_grad: float32 [768], replicated
- first_gain_grad: float32 [768], replicated
- first_shift_grad: float32 [768], replicated
- expand_proj_grad: float32 [768, 3072], replicated
- expand_bias_grad: float32 [3072], replicated
- shrink_proj_grad: float32 [3072, 768], replicated
- shrink_bias_grad: float32 [768], replicated
- second_gain_grad: float32 [768], replicated
- second_shift_grad: float32 [768], replicated
The draws below stay inside these ranges and needn't reach their ends.
Inputs may be any that keep to these rules, and one draw needn't show every extreme that they name: `segments`: in every row the segment numbers are 0 up to a cut and 1 after it; both occur in every row.
All inputs are finite; a program needn't handle non-finite values. No bound on the sum of `grad_mask` on one device may be relied on, other than what follows from the above.
Results may differ from the reference program's by a relative error of at most 0.013.
Values may be sent and summed in bfloat16 or wider, within the bound.
No kernel may reach another device: no remote copies, remote signals or barrier semaphores. Data moves between devices by JAX's collectives and lax.ppermute only.
A program may use at most 320 MiB of HBM per device.

```python
import jax
import jax.numpy as jnp
from jax import lax

D = 768
H = 12
DH = 64
FF = 3072
ROW_LEN = 1024
MICRO = 2
MB_ROWS = 2
BATCH = 16


def draw_segments(key, part):
    key = jax.random.fold_in(key, 11)
    first_key, second_key, third_key = jax.random.split(key, 3)
    middle_cut = jax.random.randint(first_key, (MICRO, BATCH), ROW_LEN // 4, 3 * ROW_LEN // 4 + 1)
    late_cut = jax.random.randint(second_key, (MICRO, BATCH), ROW_LEN - ROW_LEN // 32, ROW_LEN)
    chosen = jax.random.randint(third_key, (MICRO, BATCH // MB_ROWS), 0, MB_ROWS)
    row_place = jnp.arange(BATCH, dtype=jnp.int32) % MB_ROWS
    special = jnp.repeat(chosen, MB_ROWS, axis=1) == row_place[None, :]
    boundary = jnp.where(special, late_cut, middle_cut)
    position = jnp.arange(ROW_LEN, dtype=jnp.int32)
    return (position[None, None, :] >= boundary[..., None]).astype(jnp.int32)


def set_ends(values, rng, least, largest):
    longest = values.shape.index(max(values.shape))
    spots = []
    for shift in (0, 1):
        where = [jax.random.randint(jax.random.fold_in(rng, axis), (), 0, length) for axis, length in enumerate(values.shape)]
        where[longest] = (where[longest] + shift) % values.shape[longest]
        spots.append(tuple(where))
    return values.at[spots[0]].set(least).at[spots[1]].set(largest)


def block_scale(key, extent, cuts, smallest, largest):
    level, own = 1.0, jax.random.fold_in(key, 6)
    for axis_at, parts in cuts:
        heights = jnp.exp(jax.random.uniform(jax.random.fold_in(own, axis_at), (parts,), jnp.float32, smallest / len(cuts), largest / len(cuts)))
        level = level * jnp.repeat(heights, extent[axis_at] // parts).reshape([-1 if axis == axis_at else 1 for axis in range(len(extent))])
    return level


def gaussian(key, extent, width, most, cuts=(), held_as=jnp.bfloat16):
    entries = jax.random.normal(key, extent, jnp.float32) * width
    if len(cuts) > 0:
        entries = block_scale(key, extent, cuts, -0.22, 0.18) * entries
    return jnp.clip(entries, min=-most, max=most).astype(held_as)


def setup_inputs(seed: int = 0) -> dict:
    seeds = jax.random.split(jax.random.key(seed), 20)
    hidden_in = gaussian(seeds[0], (MICRO, BATCH, ROW_LEN, D), 1.0, 6.0, ((1, 8), (2, 4)))
    segments = draw_segments(jax.random.fold_in(seeds[19], 71), 0)
    grad_mask = set_ends((jax.random.randint(seeds[2], (MICRO, BATCH, ROW_LEN), 0, 12) < 1).astype(jnp.int32), jax.random.fold_in(seeds[2], 1), 0, 1)
    grad_out = gaussian(seeds[3], (MICRO, BATCH, ROW_LEN, D), 1.0, 6.0, ((1, 8), (2, 4)))
    query_proj = gaussian(seeds[4], (D, D), D ** -0.5, 0.21875)
    query_bias = gaussian(seeds[5], (D,), 0.5, 3.0)
    key_proj = gaussian(seeds[6], (D, D), D ** -0.5, 0.21875)
    value_proj = gaussian(seeds[7], (D, D), D ** -0.5, 0.21875)
    value_bias = gaussian(seeds[8], (D,), 0.5, 3.0)
    output_proj = gaussian(seeds[9], (D, D), (D // 16) ** -0.5, 0.875)
    output_bias = gaussian(seeds[10], (D,), 0.3, 1.75)
    first_gain = jnp.clip(1.0 + 0.15 * jax.random.normal(seeds[11], (D,), jnp.float32), 0.25, 1.75).astype(jnp.bfloat16)
    first_shift = gaussian(seeds[12], (D,), 0.5, 3.0)
    expand_proj = gaussian(seeds[13], (D, FF), D ** -0.5, 0.21875)
    expand_bias = gaussian(seeds[14], (FF,), 0.5, 3.0)
    shrink_proj = gaussian(seeds[15], (FF, D), FF ** -0.5, 0.109375)
    shrink_bias = gaussian(seeds[16], (D,), 0.3, 1.75)
    second_gain = jnp.clip(1.0 + 0.15 * jax.random.normal(seeds[17], (D,), jnp.float32), 0.25, 1.75).astype(jnp.bfloat16)
    second_shift = gaussian(seeds[18], (D,), 0.5, 3.0)
    return {"hidden_in": hidden_in, "segments": segments, "grad_mask": grad_mask, "grad_out": grad_out, "query_proj": query_proj, "query_bias": query_bias, "key_proj": key_proj, "value_proj": value_proj, "value_bias": value_bias, "output_proj": output_proj, "output_bias": output_bias, "first_gain": first_gain, "first_shift": first_shift, "expand_proj": expand_proj, "expand_bias": expand_bias, "shrink_proj": shrink_proj, "shrink_bias": shrink_bias, "second_gain": second_gain, "second_shift": second_shift}


@jax.custom_vjp
def low(v):
    return lax.optimization_barrier(v.astype(jnp.bfloat16)).astype(jnp.float32)

@jax.custom_vjp
def low_back(v):
    return v

def low_keep(v):
    return (low(v), None)

def low_pass(kept, grad):
    return (grad,)

def back_keep(v):
    return (v, None)

def back_low(kept, grad):
    return (low(grad),)
low.defvjp(low_keep, low_pass)
low_back.defvjp(back_keep, back_low)

def both_round(values):
    return low(low_back(values))

def matmul_hi(first, second):
    return jnp.dot(first, second, precision=lax.Precision.HIGHEST)

def layer_norm(values, gain, shift):
    centred = values - lax.optimization_barrier(jnp.mean(values, -1, keepdims=True))
    spread = lax.optimization_barrier(jnp.mean(centred * centred, -1, keepdims=True))
    return gain * centred * lax.rsqrt(spread + 1e-06) + shift

def layer(params, inputs, seg_rows):
    query_proj, query_bias, key_proj, value_proj, value_bias, output_proj, output_bias, first_gain, first_shift, expand_proj, expand_bias, shrink_proj, shrink_bias, second_gain, second_shift = params
    count = inputs.shape[0]
    queries = both_round(matmul_hi(inputs, query_proj) + query_bias)
    keys = both_round(matmul_hi(inputs, key_proj))
    values = both_round(matmul_hi(inputs, value_proj) + value_bias)
    query_heads = queries.reshape(count, ROW_LEN, H, DH)
    key_heads = keys.reshape(count, ROW_LEN, H, DH)
    value_heads = values.reshape(count, ROW_LEN, H, DH)
    raw = jnp.einsum('bqhd,bkhd->bhqk', query_heads, key_heads, precision=lax.Precision.HIGHEST)
    same = seg_rows[:, None, :, None] == seg_rows[:, None, None, :]
    scores = jnp.where(same, low_back(raw * 0.125), -1e+30)
    peak = lax.optimization_barrier(jnp.max(scores, -1, keepdims=True))
    raised = jnp.exp(scores - peak)
    probs = raised / lax.optimization_barrier(jnp.sum(raised, -1, keepdims=True))
    mixed = jnp.einsum('bhqk,bkhd->bqhd', low(probs), value_heads, precision=lax.Precision.HIGHEST)
    mixed = both_round(mixed.reshape(count, ROW_LEN, D))
    first_sum = inputs + low_back(matmul_hi(mixed, output_proj) + output_bias)
    normed = layer_norm(first_sum, first_gain, first_shift)
    expanded = low_back(matmul_hi(low(normed), expand_proj) + expand_bias)
    activated = low(jax.nn.gelu(expanded, approximate=False))
    second_sum = normed + low_back(matmul_hi(activated, shrink_proj) + shrink_bias)
    return layer_norm(second_sum, second_gain, second_shift)

def reference(hidden_in, segments, grad_mask, grad_out, query_proj, query_bias, key_proj, value_proj, value_bias, output_proj, output_bias, first_gain, first_shift, expand_proj, expand_bias, shrink_proj, shrink_bias, second_gain, second_shift):
    params = tuple((weight.astype(jnp.float32) for weight in (query_proj, query_bias, key_proj, value_proj, value_bias, output_proj, output_bias, first_gain, first_shift, expand_proj, expand_bias, shrink_proj, shrink_bias, second_gain, second_shift)))
    xs_rows = hidden_in.reshape(-1, 2, ROW_LEN, D)
    seg_all = segments.reshape(-1, 2, ROW_LEN)
    mask_all = grad_mask.reshape(-1, 2, ROW_LEN)
    cot_all = grad_out.reshape(-1, 2, ROW_LEN, D)

    def step(totals, item):
        inputs, seg_rows, mask_rows, cot_rows = item

        def forward(weights, values):
            return layer(weights, values, seg_rows)
        result, backward = jax.vjp(forward, params, inputs.astype(jnp.float32))
        upstream = cot_rows.astype(jnp.float32) * mask_rows[..., None].astype(jnp.float32)
        weight_grads, input_grad = backward(upstream)
        totals = jax.tree.map(lambda first, second: first + second, totals, weight_grads)
        return (totals, (result.astype(jnp.bfloat16), input_grad.astype(jnp.bfloat16)))
    start = tuple((jnp.zeros_like(weight) for weight in params))
    grads, (outputs, input_grads) = lax.scan(step, start, (xs_rows, seg_all, mask_all, cot_all))
    return (outputs.reshape(hidden_in.shape), input_grads.reshape(hidden_in.shape), grads[0], grads[1], grads[2], grads[3], grads[4], grads[5], grads[6], grads[7], grads[8], grads[9], grads[10], grads[11], grads[12], grads[13], grads[14])
```

```python
import functools

import jax
import jax.numpy as jnp
from jax import lax
from jax.experimental import pallas as pl
from jax.experimental.pallas import tpu as pltpu
from jax.sharding import PartitionSpec as P

DH = 64
PAIR = 128
MASKED = 1e30
F32 = jnp.float32
BF16 = jnp.bfloat16
NT = (((1,), (1,)), ((), ()))
NN = (((1,), (0,)), ((), ()))


def left_dot(first, second):
    return lax.dot_general(first, second, (((0,), (0,)), ((), ())), preferred_element_type=F32)


def right_dot(first, second):
    return lax.dot_general(first, second, NT, preferred_element_type=F32)


def layer_norm(values, gain, shift):
    centred = values - jnp.mean(values, -1, keepdims=True)
    spread = jnp.mean(centred * centred, -1, keepdims=True)
    return gain * centred * lax.rsqrt(spread + 1e-06) + shift


def gelu_exact(values):
    return jax.nn.gelu(values, approximate=False)


def column_sum(values):
    return jnp.sum(values.astype(F32), 0)


def split_three(values):
    high = values.astype(BF16)
    rest = values - high.astype(F32)
    middle = rest.astype(BF16)
    low = (rest - middle.astype(F32)).astype(BF16)
    return high.astype(F32), middle.astype(F32), low.astype(F32)


def own_lanes(shape, head):
    lane = lax.broadcasted_iota(jnp.int32, shape, 1)
    own = lane < DH if head == 0 else lane >= DH
    return own, lane % DH


def key_features(lane, seg):
    return jnp.where(
        lane < 3,
        1.0,
        jnp.where(lane == 3, -MASKED * (1.0 - seg), jnp.where(lane == 4, -MASKED * seg, 0.0)),
    ).astype(BF16)


def forward_kernel(q_ref, k_ref, v_ref, seg_q_ref, seg_k_ref, mixed_ref, query_ref, *, block):
    queries = q_ref.shape[0]
    keys = k_ref.shape[0]
    for head in range(2):
        own_k, lane_k = own_lanes((keys, PAIR), head)
        key_side = jnp.where(own_k, k_ref[...], key_features(lane_k, seg_k_ref[...].astype(F32)))
        value_side = jnp.where(own_k, v_ref[...], jnp.ones((), BF16))
        own_q, lane_q = own_lanes((block, PAIR), head)
        for start in range(0, queries, block):
            here = slice(start, start + block)
            q = q_ref[here, :]
            seg = seg_q_ref[here, :].astype(F32)
            seg_side = jnp.where(lane_q == 3, seg, jnp.where(lane_q == 4, 1.0 - seg, 0.0))
            query_side = jnp.where(own_q, q, seg_side.astype(BF16))
            scores = lax.dot_general(query_side, key_side, NT, preferred_element_type=F32)
            peak = jnp.max(scores, -1, keepdims=True)
            raised = jnp.exp(scores - peak).astype(BF16)
            summed = lax.dot_general(raised, value_side, NN, preferred_element_type=F32)
            total = summed[:, DH : DH + 1] if head == 0 else summed[:, 0:1]
            mixed = (summed / total).astype(BF16)
            shift = jnp.broadcast_to(-(peak + jnp.log(total)), (block, PAIR))
            high, middle, low = split_three(shift)
            extra = jnp.where(
                lane_q == 0,
                high,
                jnp.where(lane_q == 1, middle, jnp.where(lane_q == 2, low, seg_side)),
            )
            query_ref[head, here, :] = jnp.where(own_q, q, extra.astype(BF16))
            if head == 0:
                mixed_ref[here, :] = mixed
            else:
                mixed_ref[here, :] = jnp.where(own_q, mixed, mixed_ref[here, :])


def attention_forward(q, k, v, seg_q, seg_k):
    queries, width = q.shape
    keys = k.shape[0]
    pairs = width // PAIR
    column = lambda i: (0, i)
    whole = lambda i: (0, 0)
    return pl.pallas_call(
        functools.partial(forward_kernel, block=min(512, queries)),
        grid=(pairs,),
        in_specs=[
            pl.BlockSpec((queries, PAIR), column),
            pl.BlockSpec((keys, PAIR), column),
            pl.BlockSpec((keys, PAIR), column),
            pl.BlockSpec((queries, PAIR), whole),
            pl.BlockSpec((keys, PAIR), whole),
        ],
        out_specs=[
            pl.BlockSpec((queries, PAIR), column),
            pl.BlockSpec((2, queries, PAIR), lambda i: (i, 0, 0)),
        ],
        out_shape=[
            jax.ShapeDtypeStruct((queries, width), BF16),
            jax.ShapeDtypeStruct((2 * pairs, queries, PAIR), BF16),
        ],
        compiler_params=pltpu.CompilerParams(vmem_limit_bytes=40 * 2**20),
        cost_estimate=pl.CostEstimate(
            flops=16 * queries * keys * width,
            bytes_accessed=10 * queries * width,
            transcendentals=2 * pairs * queries * keys,
        ),
        name="attention_forward",
    )(q, k, v, seg_q, seg_k)


def backward_kernel(
    query_ref, k_ref, v_ref, seg_k_ref, mixed_ref, d_mixed_ref, dq_ref, dk_ref, dv_ref, dqt, *, block
):
    queries = mixed_ref.shape[0]
    keys = k_ref.shape[0]
    d_mixed = d_mixed_ref[...]
    product = d_mixed.astype(F32) * mixed_ref[...].astype(F32)
    for head in range(2):
        own_q, lane_q = own_lanes((queries, PAIR), head)
        own_k, lane_k = own_lanes((block, PAIR), head)
        delta = -jnp.sum(jnp.where(own_q, product, 0.0), -1, keepdims=True)
        high, middle, low = split_three(jnp.broadcast_to(delta, (queries, PAIR)))
        extra = jnp.where(
            lane_q == 0, high, jnp.where(lane_q == 1, middle, jnp.where(lane_q == 2, low, 0.0))
        )
        d_side = jnp.where(own_q, d_mixed, extra.astype(BF16))
        query_side = query_ref[head]
        ones = jnp.where(lane_k < 3, 1.0, 0.0).astype(BF16)
        for start in range(0, keys, block):
            here = slice(start, start + block)
            k = k_ref[here, :]
            seg = seg_k_ref[here, :].astype(F32)
            key_side = jnp.where(own_k, k, key_features(lane_k, seg))
            value_side = jnp.where(own_k, v_ref[here, :], ones)
            shifted = lax.dot_general(key_side, query_side, NT, preferred_element_type=F32)
            probs = jnp.exp(shifted)
            d_probs = lax.dot_general(value_side, d_side, NT, preferred_element_type=F32)
            d_scores = (probs * d_probs).astype(BF16)
            dv = lax.dot_general(probs.astype(BF16), d_mixed, NN, preferred_element_type=F32)
            dk = lax.dot_general(d_scores, query_side, NN, preferred_element_type=F32)
            turned = k.T[head * DH : (head + 1) * DH, :]
            dq = lax.dot_general(turned, d_scores, NN, preferred_element_type=F32)
            mine = slice(head * DH, (head + 1) * DH)
            if start == 0:
                dqt[mine, :] = dq
            else:
                dqt[mine, :] += dq
            dv = dv.astype(dv_ref.dtype)
            dk = dk.astype(dk_ref.dtype)
            if head == 0:
                dk_ref[here, :] = dk
                dv_ref[here, :] = dv
            else:
                dk_ref[here, :] = jnp.where(own_k, dk, dk_ref[here, :])
                dv_ref[here, :] = jnp.where(own_k, dv, dv_ref[here, :])
    dq_ref[...] = (dqt[...] * 0.125).astype(BF16).T


def attention_backward(query_side, k, v, seg_k, mixed, d_mixed, kept):
    queries, width = mixed.shape
    keys = k.shape[0]
    pairs = width // PAIR
    column = lambda i: (0, i)
    return pl.pallas_call(
        functools.partial(backward_kernel, block=min(512, keys)),
        grid=(pairs,),
        in_specs=[
            pl.BlockSpec((2, queries, PAIR), lambda i: (i, 0, 0)),
            pl.BlockSpec((keys, PAIR), column),
            pl.BlockSpec((keys, PAIR), column),
            pl.BlockSpec((keys, PAIR), lambda i: (0, 0)),
            pl.BlockSpec((queries, PAIR), column),
            pl.BlockSpec((queries, PAIR), column),
        ],
        out_specs=[
            pl.BlockSpec((queries, PAIR), column),
            pl.BlockSpec((keys, PAIR), column),
            pl.BlockSpec((keys, PAIR), column),
        ],
        out_shape=[
            jax.ShapeDtypeStruct((queries, width), BF16),
            jax.ShapeDtypeStruct((keys, width), kept),
            jax.ShapeDtypeStruct((keys, width), kept),
        ],
        scratch_shapes=[pltpu.VMEM((PAIR, queries), F32)],
        compiler_params=pltpu.CompilerParams(vmem_limit_bytes=40 * 2**20),
        cost_estimate=pl.CostEstimate(
            flops=40 * queries * keys * width,
            bytes_accessed=14 * queries * width,
            transcendentals=2 * pairs * queries * keys,
        ),
        name="attention_backward",
    )(query_side, k, v, seg_k, mixed, d_mixed)


def swap(values, axis, size, bit):
    return lax.ppermute(values, axis, [(i, i ^ (1 << bit)) for i in range(size)])


def bit_of(axis, bit):
    return (lax.axis_index(axis) >> bit) & 1


def half_of(values, which):
    count = values.shape[0] // 2
    return lax.dynamic_slice_in_dim(values, which * count, count, 0)


def scatter_sum(values, stages):
    for axis, size, bit in stages:
        mine = bit_of(axis, bit)
        got = swap(half_of(values, 1 - mine), axis, size, bit)
        values = (half_of(values, mine).astype(F32) + got.astype(F32)).astype(BF16)
    return values


def gather_back(values, stages):
    for axis, size, bit in reversed(stages):
        mine = bit_of(axis, bit)
        got = swap(values, axis, size, bit)
        values = jnp.concatenate(
            [jnp.where(mine == 0, values, got), jnp.where(mine == 0, got, values)], 0
        )
    return values


def solution(mesh):
    seq_size = mesh.shape["seq"]
    rows_size = mesh.shape["rows"]
    seq_bits = seq_size.bit_length() - 1
    rows_bits = rows_size.bit_length() - 1
    x_stages = [("seq", seq_size, bit) for bit in range(1, seq_bits)]
    yz_stages = [("rows", rows_size, bit) for bit in range(rows_bits)]

    def all_sum(half, stages, axis):
        core = bit_of("seq", 0)
        got = swap(half(1 - core).astype(BF16), "seq", seq_size, 0)
        mine = (half(core) + got.astype(F32)).astype(BF16)
        mine = gather_back(scatter_sum(mine, stages), stages)
        got = swap(mine, "seq", seq_size, 0)
        return jnp.concatenate(
            [jnp.where(core == 0, mine, got), jnp.where(core == 0, got, mine)], axis
        ).astype(F32)

    def small_sum(values):
        for axis, size, bit in [("seq", seq_size, 0)] + x_stages + yz_stages:
            values = values + swap(values, axis, size, bit)
        return values

    def body(
        hidden_in,
        segments,
        grad_mask,
        grad_out,
        query_proj,
        query_bias,
        key_proj,
        value_proj,
        value_bias,
        output_proj,
        output_bias,
        first_gain,
        first_shift,
        expand_proj,
        expand_bias,
        shrink_proj,
        shrink_bias,
        second_gain,
        second_shift,
    ):
        micro, rows_here, piece, width = hidden_in.shape
        units = expand_proj.shape[1]
        held = micro * rows_here
        sharers = seq_size // held
        tokens = held * piece
        place = lax.axis_index("seq")
        source_at = place % held
        row_at = place // sharers

        def trade(to_rows, part):
            there = [(s, (s % held ^ part) * sharers + s // held) for s in range(seq_size)]
            return there if to_rows else [(b, a) for a, b in there]

        def to_rows(values):
            flat = values.reshape((held,) + values.shape[2:])
            parts = []
            for part in range(held):
                sent = lax.dynamic_index_in_dim(flat, source_at ^ part, 0, False)
                parts.append(lax.ppermute(sent, "seq", trade(True, part)))
            return jnp.concatenate(parts, 0)

        def to_pieces(values):
            back = jnp.zeros((held, piece) + values.shape[1:], values.dtype)
            for part in range(held):
                sent = values[part * piece : (part + 1) * piece]
                got = lax.ppermute(sent, "seq", trade(False, part))
                back = lax.dynamic_update_index_in_dim(back, got, source_at ^ part, 0)
            return back.reshape((micro, rows_here, piece) + values.shape[1:])

        same_row = [[r * sharers + g for g in range(sharers)] for r in range(held)]

        def all_keys(values):
            if sharers == 1:
                return values
            return lax.all_gather(values, "seq", axis=0, tiled=True, axis_index_groups=same_row)

        def own_keys(values):
            if sharers == 1:
                return values
            return lax.psum_scatter(
                values, "seq", scatter_dimension=0, tiled=True, axis_index_groups=same_row
            ).astype(BF16)

        query_add = query_bias.astype(F32)
        value_add = value_bias.astype(F32)
        output_add = output_bias.astype(F32)
        expand_add = expand_bias.astype(F32)
        shrink_add = shrink_bias.astype(F32)
        gain_one = first_gain.astype(F32)
        shift_one = first_shift.astype(F32)
        gain_two = second_gain.astype(F32)
        shift_two = second_shift.astype(F32)

        inputs = to_rows(hidden_in)
        seg = to_rows(segments)
        upstream = to_rows(grad_out * grad_mask[..., None].astype(BF16)).astype(F32)

        queries = ((jnp.dot(inputs, query_proj, preferred_element_type=F32) + query_add) * 0.125).astype(BF16)
        keys = all_keys(jnp.dot(inputs, key_proj, preferred_element_type=F32).astype(BF16))
        values = all_keys(
            (jnp.dot(inputs, value_proj, preferred_element_type=F32) + value_add).astype(BF16)
        )
        seg_q = jnp.broadcast_to(seg[:, None].astype(BF16), (tokens, PAIR))
        seg_k = all_keys(seg_q)
        mixed, query_side = attention_forward(queries, keys, values, seg_q, seg_k)
        first_sum = (
            inputs.astype(F32) + jnp.dot(mixed, output_proj, preferred_element_type=F32) + output_add
        )
        normed, first_back = jax.vjp(layer_norm, first_sum, gain_one, shift_one)
        normed_low = normed.astype(BF16)
        expanded = jnp.dot(normed_low, expand_proj, preferred_element_type=F32) + expand_add
        activated, gelu_back = jax.vjp(gelu_exact, expanded)
        active_low = activated.astype(BF16)
        second_sum = (
            normed + jnp.dot(active_low, shrink_proj, preferred_element_type=F32) + shrink_add
        )
        result, second_back = jax.vjp(layer_norm, second_sum, gain_two, shift_two)
        layer_out = to_pieces(result.astype(BF16))

        d_second, d_gain_two, d_shift_two = second_back(upstream)
        d_down = d_second.astype(BF16)

        def column_half(first, second):
            count = second.shape[1] // 2
            return lambda which: left_dot(
                first, lax.dynamic_slice_in_dim(second, which * count, count, 1)
            )

        def row_half(first, second):
            count = first.shape[1] // 2
            return lambda which: left_dot(
                lax.dynamic_slice_in_dim(first, which * count, count, 1), second
            )

        shrink_grad = all_sum(row_half(active_low, d_down), yz_stages + x_stages, 0)
        d_active = right_dot(d_down, shrink_proj)
        (d_expand,) = gelu_back(d_active)
        d_expand_low = d_expand.astype(BF16)
        expand_grad = all_sum(
            column_half(normed_low, d_expand_low), x_stages + yz_stages, 1
        )
        d_normed = d_second + right_dot(d_expand_low, expand_proj)
        d_first, d_gain_one, d_shift_one = first_back(d_normed)
        d_attn = d_first.astype(BF16)
        d_mixed = right_dot(d_attn, output_proj).astype(BF16)
        output_grad = all_sum(column_half(mixed, d_attn), yz_stages + x_stages, 1)
        d_query, d_keys, d_values = attention_backward(
            query_side, keys, values, seg_k, mixed, d_mixed, BF16 if sharers == 1 else F32
        )
        d_key = own_keys(d_keys)
        d_value = own_keys(d_values)
        d_input = (
            d_first
            + right_dot(d_query, query_proj)
            + right_dot(d_key, key_proj)
            + right_dot(d_value, value_proj)
        )
        grad_in = to_pieces(d_input.astype(BF16))

        def input_half(which):
            return jnp.concatenate(
                [column_half(inputs, d)(which) for d in (d_query, d_key, d_value)], 0
            )

        input_grad = all_sum(input_half, yz_stages + x_stages, 1)
        small = [
            column_sum(d_query),
            column_sum(d_value),
            column_sum(d_attn),
            d_gain_one,
            d_shift_one,
            column_sum(d_expand_low),
            column_sum(d_down),
            d_gain_two,
            d_shift_two,
        ]
        totals = small_sum(jnp.concatenate(small).reshape(-1, width)).reshape(-1)
        vectors = []
        at = 0
        for part in small:
            vectors.append(totals[at : at + part.shape[0]])
            at += part.shape[0]
        return (
            layer_out,
            grad_in,
            input_grad[:width],
            vectors[0],
            input_grad[width : 2 * width],
            input_grad[2 * width :],
            vectors[1],
            output_grad,
            vectors[2],
            vectors[3],
            vectors[4],
            expand_grad,
            vectors[5],
            shrink_grad,
            vectors[6],
            vectors[7],
            vectors[8],
        )

    split = P(None, "rows", "seq", None)
    whole = P()
    return jax.shard_map(
        body,
        mesh=mesh,
        in_specs=(split, P(None, "rows", "seq"), P(None, "rows", "seq"), split) + (whole,) * 15,
        out_specs=(split, split) + (whole,) * 15,
        check_vma=False,
    )
```

```python
import functools

import jax
import jax.numpy as jnp
from jax import lax
from jax.experimental import pallas as pl
from jax.experimental.pallas import tpu as pltpu
from jax.sharding import PartitionSpec as P

DH = 64
PAIR = 128
MASKED = 1e30
F32 = jnp.float32
BF16 = jnp.bfloat16
NT = (((1,), (1,)), ((), ()))
NN = (((1,), (0,)), ((), ()))


def left_dot(first, second):
    return lax.dot_general(first, second, (((0,), (0,)), ((), ())), preferred_element_type=F32)


def right_dot(first, second):
    return lax.dot_general(first, second, NT, preferred_element_type=F32)


def split_three(values):
    high = values.astype(BF16)
    rest = values - high.astype(F32)
    middle = rest.astype(BF16)
    low = (rest - middle.astype(F32)).astype(BF16)
    return high.astype(F32), middle.astype(F32), low.astype(F32)


def own_lanes(shape, head):
    lane = lax.broadcasted_iota(jnp.int32, shape, 1)
    own = lane < DH if head == 0 else lane >= DH
    return own, lane % DH


def key_features(lane, seg):
    return jnp.where(
        lane < 3,
        1.0,
        jnp.where(lane == 3, -MASKED * (1.0 - seg), jnp.where(lane == 4, -MASKED * seg, 0.0)),
    ).astype(BF16)


def forward_kernel(q_ref, k_ref, v_ref, seg_q_ref, seg_k_ref, mixed_ref, query_ref, *, block):
    queries = q_ref.shape[0]
    keys = k_ref.shape[0]
    for head in range(2):
        own_k, lane_k = own_lanes((keys, PAIR), head)
        key_side = jnp.where(own_k, k_ref[...], key_features(lane_k, seg_k_ref[...].astype(F32)))
        value_side = jnp.where(own_k, v_ref[...], jnp.ones((), BF16))
        own_q, lane_q = own_lanes((block, PAIR), head)
        for start in range(0, queries, block):
            here = slice(start, start + block)
            q = q_ref[here, :]
            seg = seg_q_ref[here, :].astype(F32)
            seg_side = jnp.where(lane_q == 3, seg, jnp.where(lane_q == 4, 1.0 - seg, 0.0))
            query_side = jnp.where(own_q, q, seg_side.astype(BF16))
            scores = lax.dot_general(query_side, key_side, NT, preferred_element_type=F32)
            peak = jnp.max(scores, -1, keepdims=True)
            raised = jnp.exp(scores - peak).astype(BF16)
            summed = lax.dot_general(raised, value_side, NN, preferred_element_type=F32)
            total = summed[:, DH : DH + 1] if head == 0 else summed[:, 0:1]
            mixed = (summed / total).astype(BF16)
            shift = jnp.broadcast_to(-(peak + jnp.log(total)), (block, PAIR))
            high, middle, low = split_three(shift)
            extra = jnp.where(
                lane_q == 0,
                high,
                jnp.where(lane_q == 1, middle, jnp.where(lane_q == 2, low, seg_side)),
            )
            query_ref[head, here, :] = jnp.where(own_q, q, extra.astype(BF16))
            if head == 0:
                mixed_ref[here, :] = mixed
            else:
                mixed_ref[here, :] = jnp.where(own_q, mixed, mixed_ref[here, :])


def attention_forward(q, k, v, seg_q, seg_k):
    queries, width = q.shape
    keys = k.shape[0]
    pairs = width // PAIR
    column = lambda i: (0, i)
    whole = lambda i: (0, 0)
    return pl.pallas_call(
        functools.partial(forward_kernel, block=min(512, queries)),
        grid=(pairs,),
        in_specs=[
            pl.BlockSpec((queries, PAIR), column),
            pl.BlockSpec((keys, PAIR), column),
            pl.BlockSpec((keys, PAIR), column),
            pl.BlockSpec((queries, PAIR), whole),
            pl.BlockSpec((keys, PAIR), whole),
        ],
        out_specs=[
            pl.BlockSpec((queries, PAIR), column),
            pl.BlockSpec((2, queries, PAIR), lambda i: (i, 0, 0)),
        ],
        out_shape=[
            jax.ShapeDtypeStruct((queries, width), BF16),
            jax.ShapeDtypeStruct((2 * pairs, queries, PAIR), BF16),
        ],
        compiler_params=pltpu.CompilerParams(vmem_limit_bytes=40 * 2**20),
        cost_estimate=pl.CostEstimate(
            flops=16 * queries * keys * width,
            bytes_accessed=10 * queries * width,
            transcendentals=2 * pairs * queries * keys,
        ),
        name="attention_forward",
    )(q, k, v, seg_q, seg_k)


def backward_kernel(
    query_ref, k_ref, v_ref, seg_k_ref, mixed_ref, d_mixed_ref, *refs, block
):
    dq_ref, dk_ref, dv_ref, dqt = refs[-4:]
    queries = mixed_ref.shape[0]
    keys = k_ref.shape[0]
    d_mixed = d_mixed_ref[...]
    product = d_mixed.astype(F32) * mixed_ref[...].astype(F32)
    for head in range(2):
        own_q, lane_q = own_lanes((queries, PAIR), head)
        own_k, lane_k = own_lanes((block, PAIR), head)
        delta = -jnp.sum(jnp.where(own_q, product, 0.0), -1, keepdims=True)
        high, middle, low = split_three(jnp.broadcast_to(delta, (queries, PAIR)))
        extra = jnp.where(
            lane_q == 0, high, jnp.where(lane_q == 1, middle, jnp.where(lane_q == 2, low, 0.0))
        )
        d_side = jnp.where(own_q, d_mixed, extra.astype(BF16))
        query_side = query_ref[head]
        ones = jnp.where(lane_k < 3, 1.0, 0.0).astype(BF16)
        for start in range(0, keys, block):
            here = slice(start, start + block)
            k = k_ref[here, :]
            seg = seg_k_ref[here, :].astype(F32)
            key_side = jnp.where(own_k, k, key_features(lane_k, seg))
            value_side = jnp.where(own_k, v_ref[here, :], ones)
            shifted = lax.dot_general(key_side, query_side, NT, preferred_element_type=F32)
            probs = jnp.exp(shifted)
            d_probs = lax.dot_general(value_side, d_side, NT, preferred_element_type=F32)
            d_scores = (probs * d_probs).astype(BF16)
            dv = lax.dot_general(probs.astype(BF16), d_mixed, NN, preferred_element_type=F32)
            dk = lax.dot_general(d_scores, query_side, NN, preferred_element_type=F32)
            turned = k.T[head * DH : (head + 1) * DH, :]
            dq = lax.dot_general(turned, d_scores, NN, preferred_element_type=F32)
            mine = slice(head * DH, (head + 1) * DH)
            if start == 0:
                dqt[mine, :] = dq
            else:
                dqt[mine, :] += dq
            dv = dv.astype(dv_ref.dtype)
            dk = dk.astype(dk_ref.dtype)
            if head == 0:
                dk_ref[here, :] = dk
                dv_ref[here, :] = dv
            else:
                dk_ref[here, :] = jnp.where(own_k, dk, dk_ref[here, :])
                dv_ref[here, :] = jnp.where(own_k, dv, dv_ref[here, :])
    dq_ref[...] = (dqt[...] * 0.125).astype(BF16).T


def attention_backward(query_side, k, v, seg_k, mixed, d_mixed, kept, first, count, before):
    queries, width = mixed.shape
    keys = k.shape[0]
    column = lambda i: (0, i + first)
    held = [] if before is None else list(before)
    return pl.pallas_call(
        functools.partial(backward_kernel, block=min(512, keys)),
        grid=(count,),
        in_specs=[
            pl.BlockSpec((2, queries, PAIR), lambda i: (i + first, 0, 0)),
            pl.BlockSpec((keys, PAIR), column),
            pl.BlockSpec((keys, PAIR), column),
            pl.BlockSpec((keys, PAIR), lambda i: (0, 0)),
            pl.BlockSpec((queries, PAIR), column),
            pl.BlockSpec((queries, PAIR), column),
        ]
        + [pl.BlockSpec(memory_space=pl.ANY)] * len(held),
        out_specs=[
            pl.BlockSpec((queries, PAIR), column),
            pl.BlockSpec((keys, PAIR), column),
            pl.BlockSpec((keys, PAIR), column),
        ],
        input_output_aliases={6 + i: i for i in range(len(held))},
        out_shape=[
            jax.ShapeDtypeStruct((queries, width), BF16),
            jax.ShapeDtypeStruct((keys, width), kept),
            jax.ShapeDtypeStruct((keys, width), kept),
        ],
        scratch_shapes=[pltpu.VMEM((PAIR, queries), F32)],
        compiler_params=pltpu.CompilerParams(vmem_limit_bytes=40 * 2**20),
        cost_estimate=pl.CostEstimate(
            flops=40 * queries * keys * PAIR * count,
            bytes_accessed=14 * queries * PAIR * count,
            transcendentals=2 * count * queries * keys,
        ),
        name="attention_backward",
    )(query_side, k, v, seg_k, mixed, d_mixed, *held)


def dot(first, second, dims=NN):
    return lax.dot_general(first, second, dims, preferred_element_type=F32)


def gelu_pair(values):
    below = 0.5 + 0.5 * lax.erf(values * 0.7071067811865476)
    density = jnp.exp(-0.5 * values * values) * 0.3989422804014327
    return values * below, below + values * density


def normalise(values):
    centred = values - jnp.mean(values, -1, keepdims=True)
    scale = lax.rsqrt(jnp.mean(centred * centred, -1, keepdims=True) + 1e-06)
    return centred * scale, scale


def norm_back(upstream, hat, scale, gain):
    d_hat = upstream * gain
    return scale * (
        d_hat
        - jnp.mean(d_hat, -1, keepdims=True)
        - hat * jnp.mean(d_hat * hat, -1, keepdims=True)
    )


def stack_rows(rows):
    filler = jnp.zeros((8 - len(rows), rows[0].shape[1]), F32)
    return jnp.concatenate(rows + [filler], 0)


def feed_forward_kernel(
    inputs_ref,
    mixed_ref,
    output_proj_ref,
    output_bias_ref,
    gain_one_ref,
    shift_one_ref,
    expand_ref,
    expand_bias_ref,
    shrink_ref,
    shrink_bias_ref,
    gain_two_ref,
    shift_two_ref,
    *refs,
    steps,
    held,
):
    upstream_refs = refs[:held]
    hat_ref, scale_ref, normed_ref, active_t_ref, slope_ref = refs[held : held + 5]
    d_second_ref, d_down_ref, sums_ref = refs[held + 5 : held + 8]
    out_refs = refs[held + 8 : -1]
    total = refs[-1]
    block = total.shape[0] // held
    step = pl.program_id(0)
    tokens = total.shape[0]
    pieces = [slice(start, start + block) for start in range(0, tokens, block)]

    @pl.when(step == 0)
    def _():
        for here in pieces:
            first_sum = (
                inputs_ref[here, :].astype(F32)
                + dot(mixed_ref[here, :], output_proj_ref[...])
                + output_bias_ref[...].astype(F32)
            )
            hat, scale = normalise(first_sum)
            hat_ref[here, :] = hat
            scale_ref[here, :] = jnp.broadcast_to(scale, (block, PAIR))
            normed = gain_one_ref[...].astype(F32) * hat + shift_one_ref[...].astype(F32)
            normed_ref[here, :] = normed.astype(BF16)
            total[here, :] = normed + shrink_bias_ref[...].astype(F32)

    for here in pieces:
        expanded = dot(normed_ref[here, :], expand_ref[...]) + expand_bias_ref[...].astype(F32)
        active, slope = gelu_pair(expanded)
        active = active.astype(BF16)
        slope_ref[here, :] = slope.astype(BF16)
        active_t_ref[:, here] = active.T
        total[here, :] += dot(active, shrink_ref[...])

    @pl.when(step == steps - 1)
    def _():
        gain = gain_two_ref[...].astype(F32)
        d_gain = jnp.zeros((1, total.shape[1]), F32)
        d_shift = d_gain
        d_bias = d_gain
        for here, upstream_ref, out_ref in zip(pieces, upstream_refs, out_refs):
            hat, scale = normalise(total[here, :])
            out_ref[...] = (gain * hat + shift_two_ref[...].astype(F32)).astype(BF16)
            upstream = upstream_ref[...].astype(F32)
            d_gain += jnp.sum(upstream * hat, 0, keepdims=True)
            d_shift += jnp.sum(upstream, 0, keepdims=True)
            d_second = norm_back(upstream, hat, scale, gain)
            d_second_ref[here, :] = d_second
            d_down = d_second.astype(BF16)
            d_down_ref[here, :] = d_down
            d_bias += jnp.sum(d_down.astype(F32), 0, keepdims=True)
        sums_ref[...] = stack_rows([d_gain, d_shift, d_bias])


def fixed(*shape):
    return pl.BlockSpec(shape, lambda i: (0,) * len(shape), pipeline_mode=pl.Buffered(1))


def shapes(*pairs):
    return [jax.ShapeDtypeStruct(shape, dtype) for shape, dtype in pairs]


def feed_forward(inputs, mixed, upstream, weights, block=512):
    tokens, width = inputs.shape
    units = weights[4].shape[1]
    steps = units // block
    held = len(upstream)
    piece = tokens // held
    row = fixed(1, width)
    return pl.pallas_call(
        functools.partial(feed_forward_kernel, steps=steps, held=held),
        grid=(steps,),
        in_specs=[fixed(tokens, width)] * 2
        + [fixed(width, width), row, row, row]
        + [
            pl.BlockSpec((width, block), lambda i: (0, i)),
            pl.BlockSpec((1, block), lambda i: (0, i)),
            pl.BlockSpec((block, width), lambda i: (i, 0)),
            row,
            row,
            row,
        ]
        + [fixed(piece, width)] * held,
        out_specs=[
            fixed(tokens, width),
            fixed(tokens, PAIR),
            fixed(tokens, width),
            pl.BlockSpec((block, tokens), lambda i: (i, 0)),
            pl.BlockSpec((tokens, block), lambda i: (0, i)),
            fixed(tokens, width),
            fixed(tokens, width),
            fixed(8, width),
        ]
        + [fixed(piece, width)] * held,
        out_shape=shapes(
            ((tokens, width), F32),
            ((tokens, PAIR), F32),
            ((tokens, width), BF16),
            ((units, tokens), BF16),
            ((tokens, units), BF16),
            ((tokens, width), F32),
            ((tokens, width), BF16),
            ((8, width), F32),
            *[((piece, width), BF16)] * held,
        ),
        scratch_shapes=[pltpu.VMEM((tokens, width), F32)],
        compiler_params=pltpu.CompilerParams(vmem_limit_bytes=36 * 2**20),
        cost_estimate=pl.CostEstimate(
            flops=6 * tokens * width * units, bytes_accessed=50 * 2**20, transcendentals=0
        ),
        name="feed_forward",
    )(inputs, mixed, *weights, *upstream)


def feed_back_kernel(
    which_ref,
    d_down_ref,
    before_ref,
    slope_ref,
    active_t_ref,
    shrink_ref,
    expand_ref,
    normed_ref,
    *refs,
    steps,
    block,
    last,
):
    if last:
        hat_ref, scale_ref, gain_ref, output_proj_ref = refs[:4]
        grads_ref, bias_ref, d_first_ref, d_attn_ref, d_mixed_ref, sums_ref, turned, total = refs[4:]
    else:
        grads_ref, bias_ref, total, turned = refs
    step = pl.program_id(0)
    tokens = total.shape[0]
    pieces = [slice(start, start + block) for start in range(0, tokens, block)]

    @pl.when(step == 0)
    def _():
        total[...] = before_ref[...]

    bias = jnp.zeros((1, slope_ref.shape[1]), F32)
    for here in pieces:
        d_active = dot(d_down_ref[here, :], shrink_ref[...], NT)
        d_expand = (d_active * slope_ref[here, :].astype(F32)).astype(BF16)
        turned[:, here] = d_expand.T
        bias += jnp.sum(d_expand.astype(F32), 0, keepdims=True)
        total[here, :] += dot(d_expand, expand_ref[...], NT)
    bias_ref[...] = bias
    grads_ref[0] = dot(active_t_ref[...], d_down_ref[...]).astype(BF16)
    grads_ref[1] = dot(turned[...], normed_ref[...]).astype(BF16)

    if last:

        @pl.when(step == steps - 1)
        def _():
            gain = gain_ref[...].astype(F32)
            d_gain = jnp.zeros((1, total.shape[1]), F32)
            d_shift = d_gain
            d_bias = d_gain
            for here in pieces:
                d_normed = total[here, :]
                hat = hat_ref[here, :]
                d_gain += jnp.sum(d_normed * hat, 0, keepdims=True)
                d_shift += jnp.sum(d_normed, 0, keepdims=True)
                d_first = norm_back(d_normed, hat, scale_ref[here, :][:, 0:1], gain)
                d_first_ref[here, :] = d_first
                d_attn = d_first.astype(BF16)
                d_attn_ref[here, :] = d_attn
                d_bias += jnp.sum(d_attn.astype(F32), 0, keepdims=True)
                d_mixed_ref[here, :] = dot(d_attn, output_proj_ref[...], NT).astype(BF16)
            sums_ref[...] = stack_rows([d_gain, d_shift, d_bias])


def feed_back(which, d_down, before, slope, active_t, shrink, expand, normed, norm, block=512):
    tokens, width = d_down.shape
    half = slope.shape[1] // 2
    steps = half // block
    last = norm is not None
    at = lambda i, which: which[0] * steps + i
    whole = lambda *shape: pl.BlockSpec(
        shape, lambda i, which: (0,) * len(shape), pipeline_mode=pl.Buffered(1)
    )
    in_specs = [
        whole(tokens, width),
        whole(tokens, width),
        pl.BlockSpec((tokens, block), lambda i, which: (0, at(i, which))),
        pl.BlockSpec((block, tokens), lambda i, which: (at(i, which), 0)),
        pl.BlockSpec((block, width), lambda i, which: (at(i, which), 0)),
        pl.BlockSpec((width, block), lambda i, which: (0, at(i, which))),
        whole(tokens, width),
    ]
    out_specs = [
        pl.BlockSpec((2, block, width), lambda i, which: (0, i, 0)),
        pl.BlockSpec((1, block), lambda i, which: (0, i)),
    ]
    out_shape = shapes(((2, half, width), BF16), ((1, half), F32))
    scratch = [pltpu.VMEM((block, tokens), BF16)]
    if last:
        in_specs += [whole(tokens, width), whole(tokens, PAIR), whole(1, width), whole(width, width)]
        out_specs += [whole(tokens, width)] * 3 + [whole(8, width)]
        out_shape += shapes(
            ((tokens, width), F32), ((tokens, width), BF16), ((tokens, width), BF16), ((8, width), F32)
        )
        scratch.append(pltpu.VMEM((tokens, width), F32))
    else:
        out_specs.append(whole(tokens, width))
        out_shape += shapes(((tokens, width), F32))
    return pl.pallas_call(
        functools.partial(feed_back_kernel, steps=steps, block=min(512, tokens), last=last),
        grid_spec=pltpu.PrefetchScalarGridSpec(
            num_scalar_prefetch=1,
            grid=(steps,),
            in_specs=in_specs,
            out_specs=out_specs,
            scratch_shapes=scratch,
        ),
        out_shape=out_shape,
        compiler_params=pltpu.CompilerParams(vmem_limit_bytes=36 * 2**20),
        cost_estimate=pl.CostEstimate(
            flops=8 * tokens * width * half, bytes_accessed=30 * 2**20, transcendentals=0
        ),
        name="feed_back_last" if last else "feed_back",
    )(which, d_down, before, slope, active_t, shrink, expand, normed, *(norm or ()))


def weight_kernel(which_ref, inputs_ref, mixed_ref, dq_ref, dk_ref, dv_ref, d_attn_ref, out_ref):
    count = inputs_ref.shape[1] // 2
    columns = pl.ds(pl.multiple_of(which_ref[0] * count, PAIR), count)
    inputs_t = inputs_ref[:, columns].T
    out_ref[0 * count : 1 * count, :] = dot(inputs_t, dq_ref[...]).astype(BF16)
    out_ref[1 * count : 2 * count, :] = dot(inputs_t, dk_ref[...]).astype(BF16)
    out_ref[2 * count : 3 * count, :] = dot(inputs_t, dv_ref[...]).astype(BF16)
    out_ref[3 * count : 4 * count, :] = dot(mixed_ref[:, columns].T, d_attn_ref[...]).astype(BF16)
    if out_ref.shape[0] > 4 * count:
        out_ref[4 * count :, :] = jnp.zeros((out_ref.shape[0] - 4 * count, out_ref.shape[1]), BF16)


def weight_halves(which, inputs, mixed, dq, dk, dv, d_attn, unit):
    tokens, width = inputs.shape
    rows = -(-2 * width // unit) * unit
    return pl.pallas_call(
        weight_kernel,
        grid_spec=pltpu.PrefetchScalarGridSpec(
            num_scalar_prefetch=1,
            grid=(1,),
            in_specs=[pl.BlockSpec((tokens, width), lambda i, which: (0, 0))] * 6,
            out_specs=pl.BlockSpec((rows, width), lambda i, which: (0, 0)),
        ),
        out_shape=jax.ShapeDtypeStruct((rows, width), BF16),
        compiler_params=pltpu.CompilerParams(vmem_limit_bytes=40 * 2**20),
        cost_estimate=pl.CostEstimate(
            flops=4 * tokens * width * width, bytes_accessed=12 * 2**20, transcendentals=0
        ),
        name="weight_halves",
    )(which, inputs, mixed, dq, dk, dv, d_attn)


def feed_out_kernel(core_ref, own_ref, got_ref, shrink_ref, expand_ref, *, steps):
    own = core_ref[0] == pl.program_id(0)
    step = pl.program_id(1)

    for mine, ref in ((True, own_ref), (False, got_ref)):

        @pl.when((own == mine) & (step < steps))
        def _(ref=ref):
            shrink_ref[...] = ref[...].astype(F32)

        @pl.when((own == mine) & (step >= steps))
        def _(ref=ref):
            expand_ref[...] = ref[...].T.astype(F32)


def feed_out(core, own, got, block=512):
    width = own.shape[1]
    half = own.shape[0] // 2
    steps = half // block

    def source(mine):
        def index(h, i, core):
            return (jnp.where((core[0] == h) == mine, i, 0), 0)

        return pl.BlockSpec((block, width), index)

    shrink_at = lambda h, i, core: (h * steps + jnp.minimum(i, steps - 1), 0)
    expand_at = lambda h, i, core: (0, h * steps + jnp.maximum(i - steps, 0))
    return pl.pallas_call(
        functools.partial(feed_out_kernel, steps=steps),
        grid_spec=pltpu.PrefetchScalarGridSpec(
            num_scalar_prefetch=1,
            grid=(2, 2 * steps),
            in_specs=[source(True), source(False)],
            out_specs=[
                pl.BlockSpec((block, width), shrink_at),
                pl.BlockSpec((width, block), expand_at),
            ],
        ),
        out_shape=shapes(((2 * half, width), F32), ((width, 2 * half), F32)),
        compiler_params=pltpu.CompilerParams(vmem_limit_bytes=24 * 2**20),
        cost_estimate=pl.CostEstimate(
            flops=half * width, bytes_accessed=24 * half * width, transcendentals=0
        ),
        name="feed_out",
    )(core, own, got)


def attn_out_kernel(core_ref, own_ref, got_ref, *out_refs):
    own = core_ref[0] == pl.program_id(1)
    for index, out_ref in enumerate(out_refs):
        for mine, ref in ((True, own_ref), (False, got_ref)):

            @pl.when((own == mine) & (pl.program_id(0) == index))
            def _(ref=ref, out_ref=out_ref):
                out_ref[...] = ref[...].astype(F32)


def attn_out(core, own, got, width):
    half = width // 2

    def source(mine):
        return pl.BlockSpec((half, width), lambda m, h, core: (m, 0))

    def target(index):
        at = lambda m, h, core: (jnp.where(m < index, 0, jnp.where(m == index, h, 1)), 0)
        return pl.BlockSpec((half, width), at)

    return pl.pallas_call(
        attn_out_kernel,
        grid_spec=pltpu.PrefetchScalarGridSpec(
            num_scalar_prefetch=1,
            grid=(4, 2),
            in_specs=[source(True), source(False)],
            out_specs=[target(index) for index in range(4)],
        ),
        out_shape=shapes(*[((width, width), F32)] * 4),
        compiler_params=pltpu.CompilerParams(vmem_limit_bytes=24 * 2**20),
        name="attn_out",
    )(core, own, got)


def rows_of(ref, which, count, base=0):
    return ref[pl.ds(pl.multiple_of(base + which * count, 16), count), :]


def sum_of(terms):
    return functools.reduce(lambda a, b: a + b, [t.astype(F32) for t in terms]).astype(BF16)


def scatter_kernel(bits_ref, *refs, groups):
    ins, outs = refs[: 2 * groups], refs[2 * groups :]
    for group in range(groups):
        terms = ins[2 * group : 2 * group + 2]
        sent_ref, kept_ref = outs[2 * group : 2 * group + 2]
        count = kept_ref.shape[0]
        here = bits_ref[group]
        sent_ref[...] = sum_of([rows_of(term, 1 - here, count) for term in terms])
        kept_ref[...] = sum_of([rows_of(term, here, count) for term in terms])


def local_call(kernel, bits, values, out_shape, name):
    vmem = pl.BlockSpec(memory_space=pltpu.VMEM)
    return pl.pallas_call(
        kernel,
        in_specs=[pl.BlockSpec(memory_space=pltpu.SMEM)] + [vmem] * len(values),
        out_specs=[vmem] * len(out_shape),
        out_shape=out_shape,
        compiler_params=pltpu.CompilerParams(vmem_limit_bytes=24 * 2**20),
        name=name,
    )(bits, *values)


def scatter_local(bits, pairs):
    groups = len(pairs)
    counts = [kept.shape[0] // 2 for kept, _ in pairs]
    width = pairs[0][0].shape[1]
    outs = local_call(
        functools.partial(scatter_kernel, groups=groups),
        bits,
        [value for pair in pairs for value in pair],
        shapes(*[((count, width), BF16) for count in counts for _ in range(2)]),
        "scatter_local",
    )
    return [outs[2 * i : 2 * i + 2] for i in range(groups)]


def scatter_first(bits, own, got, counts, blocks=2):
    width = own.shape[1]
    outs = []
    base = 0
    for group, count in enumerate(counts):
        block = count // 2 // blocks
        first = base // block

        def source(i, bits, group=group, first=first):
            kept = i // blocks
            return (first + jnp.where(kept == 1, bits[group], 1 - bits[group]) * blocks + i % blocks, 0)

        outs.append(
            pl.pallas_call(
                first_split_kernel,
                grid_spec=pltpu.PrefetchScalarGridSpec(
                    num_scalar_prefetch=1,
                    grid=(2 * blocks,),
                    in_specs=[pl.BlockSpec((block, width), source)] * 2,
                    out_specs=[
                        pl.BlockSpec((block, width), lambda i, bits: (jnp.minimum(i, blocks - 1), 0)),
                        pl.BlockSpec((block, width), lambda i, bits: (jnp.maximum(i - blocks, 0), 0)),
                    ],
                ),
                out_shape=shapes(*[((count // 2, width), BF16)] * 2),
                compiler_params=pltpu.CompilerParams(vmem_limit_bytes=16 * 2**20),
                name="scatter_first",
            )(bits, own, got)
        )
        base += count
    return outs


def first_split_kernel(bits_ref, own_ref, got_ref, sent_ref, kept_ref):
    del bits_ref
    sending = pl.program_id(0) < pl.num_programs(0) // 2
    value = sum_of([own_ref[...], got_ref[...]])

    @pl.when(sending)
    def _():
        sent_ref[...] = value

    @pl.when(jnp.logical_not(sending))
    def _():
        kept_ref[...] = value


def split_two(values):
    high = values.astype(BF16)
    return high, (values - high.astype(F32)).astype(BF16)


SMALL = 32


def put_small(ref, at, values):
    high, low = split_two(values)
    ref[at : at + SMALL // 2, :] = high
    ref[at + SMALL // 2 : at + SMALL, :] = low


def get_small(ref, at):
    half = SMALL // 2
    return ref[at : at + half, :].astype(F32) + ref[at + half : at + SMALL, :].astype(F32)


def settle_kernel(bits_ref, *refs, groups, small):
    del bits_ref
    ins, outs = refs[: 2 * groups], refs[2 * groups + small :]
    for group in range(groups):
        count = ins[2 * group].shape[0]
        outs[group][0:count, :] = sum_of([ins[2 * group][...], ins[2 * group + 1][...]])
        if small and group == 0:
            put_small(outs[group], count, refs[2 * groups][...])


def settle_local(bits, pairs, small):
    width = pairs[0][0].shape[1]
    counts = [kept.shape[0] for kept, _ in pairs]
    if small is not None:
        counts[0] += SMALL
    return local_call(
        functools.partial(settle_kernel, groups=len(pairs), small=int(small is not None)),
        bits,
        [value for pair in pairs for value in pair] + ([] if small is None else [small]),
        shapes(*[((count, width), BF16) for count in counts]),
        "settle_local",
    )


def join_kernel(bits_ref, *refs, groups, small, merged):
    ins, outs = refs[: 2 * groups], refs[2 * groups :]
    base = 0
    for group in range(groups):
        own_ref, got_ref = ins[2 * group : 2 * group + 2]
        extra = SMALL if small and group == 0 else 0
        count = own_ref.shape[0] - extra
        out_ref = outs[0 if merged else group]
        here = bits_ref[group]
        for half, ref in ((here, own_ref), (1 - here, got_ref)):
            out_ref[pl.ds(pl.multiple_of(base + half * count, 16), count), :] = ref[0:count, :]
        if extra:
            at = out_ref.shape[0] - SMALL if merged else base + 2 * count
            put_small(out_ref, at, get_small(own_ref, count) + get_small(got_ref, count))
        if merged:
            base += 2 * count


def join_local(bits, pairs, small, merged):
    width = pairs[0][0].shape[1]
    counts = [2 * own.shape[0] for own, _ in pairs]
    if small:
        counts[0] -= SMALL
    if merged:
        counts = [sum(counts)]
    return local_call(
        functools.partial(join_kernel, groups=len(pairs), small=small, merged=merged),
        bits,
        [value for pair in pairs for value in pair],
        shapes(*[((count, width), BF16) for count in counts]),
        "join_local",
    )


def tie(*values):
    return lax.optimization_barrier(values)


def pick(which, parts):
    if len(parts) == 1:
        return parts[0]
    half = len(parts) // 2
    return jnp.where(which < half, pick(which, parts[:half]), pick(which - half, parts[half:]))


def column_sum(values):
    return jnp.sum(values.astype(F32), 0)


class Stage:
    def __init__(self, sizes, bits):
        self.bits = bits
        rows, seq = sizes
        self.pairs = []
        for index in range(rows * seq):
            axis, bit = bits[index & 1]
            self.pairs.append((index, index ^ ((1 << bit) * (seq if axis == "rows" else 1))))

    def here(self):
        first, second = [(lax.axis_index(axis) >> bit) & 1 for axis, bit in self.bits]
        if self.bits[0] == self.bits[1]:
            return first
        return jnp.where(lax.axis_index("seq") & 1 == 0, first, second)

    def swap(self, values):
        return lax.ppermute(values, ("rows", "seq"), self.pairs)


def total_over_chips(own, got, core_stage, orders, small=None):
    depth = len(orders[0][1])
    groups = range(len(orders))

    def bits_at(step):
        return jnp.stack([stages[step].here() for _, stages in orders]).astype(jnp.int32)

    def pairs_of(flat):
        return [flat[i : i + 2] for i in range(0, len(flat), 2)]

    def send(step, values, keep):
        flat = []
        for group in groups:
            flat += [keep[group], orders[group][1][step].swap(values[group])]
        return flat

    parts = scatter_first(bits_at(0), own, got, [count for count, _ in orders])
    for step in range(1, depth + 1):
        flat = yield send(step - 1, [p[0] for p in parts], [p[1] for p in parts])
        if step < depth:
            parts = scatter_local(bits_at(step), pairs_of(flat))
    values = settle_local(bits_at(0), pairs_of(flat), small)
    for step in reversed(range(depth)):
        flat = yield send(step, values, values)
        values = join_local(bits_at(step), pairs_of(flat), small is not None, step == 0)
    both = yield [values[0], core_stage.swap(values[0])]
    return both


def arriving(values):
    values = yield values
    return values


class Flow:
    def __init__(self, steps):
        self.steps = steps
        self.pending = next(steps)
        self.result = None


def advance(flows, *values):
    flows = [flow for flow in flows if flow.result is None]
    count = len(values)
    tied = tie(*values, *[value for flow in flows for value in flow.pending])
    at = count
    for flow in flows:
        arrived = list(tied[at : at + len(flow.pending)])
        at += len(flow.pending)
        try:
            flow.pending = flow.steps.send(arrived)
        except StopIteration as end:
            flow.pending = []
            flow.result = end.value
    return tied[:count]


def solution(mesh):
    seq_size = mesh.shape["seq"]
    rows_size = mesh.shape["rows"]
    seq_bits = seq_size.bit_length() - 1
    rows_bits = rows_size.bit_length() - 1
    off_chip = [("seq", bit) for bit in range(1, seq_bits)]
    off_chip += [("rows", bit) for bit in range(rows_bits)]
    first, *middle, ahead, final = off_chip
    sizes = (rows_size, seq_size)
    core_stage = Stage(sizes, [("seq", 0)] * 2)
    straight = [first] + middle + [ahead, final]
    turned = middle + [ahead, first, final]
    spun = [ahead, first] + middle + [final]
    wide = [Stage(sizes, bits) for bits in zip(straight, turned)]
    slim = [Stage(sizes, bits) for bits in zip(spun, spun)]

    def body(
        hidden_in,
        segments,
        grad_mask,
        grad_out,
        query_proj,
        query_bias,
        key_proj,
        value_proj,
        value_bias,
        output_proj,
        output_bias,
        first_gain,
        first_shift,
        expand_proj,
        expand_bias,
        shrink_proj,
        shrink_bias,
        second_gain,
        second_shift,
    ):
        micro, rows_here, piece, width = hidden_in.shape
        held = micro * rows_here
        sharers = seq_size // held
        tokens = held * piece
        source_at = lax.axis_index("seq") % held
        core = core_stage.here()
        core_at = core.reshape(1).astype(jnp.int32)

        def trade(to_rows, part):
            there = [(s, (s % held ^ part) * sharers + s // held) for s in range(seq_size)]
            return there if to_rows else [(b, a) for a, b in there]

        def to_rows(values):
            return [
                lax.ppermute(
                    lax.dynamic_index_in_dim(values, source_at ^ part, 0, False),
                    "seq",
                    trade(True, part),
                )
                for part in range(held)
            ]

        def send_pieces(values):
            return [
                lax.ppermute(values[part], "seq", trade(False, part))
                for part in range(held)
            ]

        def place_pieces(parts):
            placed = [pick(source_at ^ slot, parts) for slot in range(held)]
            return jnp.stack(placed).reshape((micro, rows_here) + parts[0].shape)

        same_row = [[r * sharers + g for g in range(sharers)] for r in range(held)]

        def all_keys(values):
            if sharers == 1:
                return values
            return lax.all_gather(values, "seq", axis=0, tiled=True, axis_index_groups=same_row)

        def own_keys(values):
            if sharers == 1:
                return values
            return lax.psum_scatter(
                values, "seq", scatter_dimension=0, tiled=True, axis_index_groups=same_row
            ).astype(BF16)

        marks = segments.reshape(held, piece, 1).astype(BF16)
        marks = to_rows(jnp.broadcast_to(marks, (held, piece, PAIR)))
        inputs = jnp.concatenate(to_rows(hidden_in.reshape(held, piece, width)), 0)
        seg_q = jnp.concatenate(marks, 0)
        masked = (grad_out * grad_mask[..., None].astype(BF16)).reshape(held, piece, width)
        masked, inputs, seg_q = tie(masked, inputs, seg_q)
        upstream = to_rows(masked)

        queries = (
            (dot(inputs, query_proj) + query_bias.astype(F32)) * 0.125
        ).astype(BF16)
        keys = all_keys(dot(inputs, key_proj).astype(BF16))
        values = all_keys((dot(inputs, value_proj) + value_bias.astype(F32)).astype(BF16))
        seg_k = all_keys(seg_q)
        mixed, query_side = attention_forward(queries, keys, values, seg_q, seg_k)
        row = lambda vector: vector.reshape(1, -1)
        hat, scale, normed, active_t, slope, d_second, d_down, second_sums, *result = feed_forward(
            inputs,
            mixed,
            upstream,
            (
                output_proj,
                row(output_bias),
                row(first_gain),
                row(first_shift),
                expand_proj,
                row(expand_bias),
                shrink_proj,
                row(shrink_bias),
                row(second_gain),
                row(second_shift),
            ),
        )
        layer_flow = Flow(arriving(send_pieces(result)))

        def chips(own, got, orders, small=None):
            return Flow(total_over_chips(own, got, core_stage, orders, small))

        back = functools.partial(
            feed_back,
            slope=slope,
            active_t=active_t,
            shrink=shrink_proj,
            expand=expand_proj,
            normed=normed,
        )
        other, other_bias, d_normed = back(1 - core_at, d_down, d_second, norm=None)
        half = other.shape[1]
        got = core_stage.swap(other.reshape(2 * half, width))
        own, own_bias, d_first, d_attn, d_mixed, first_sums = back(
            core_at, d_down, d_normed, norm=(hat, scale, row(first_gain), output_proj)
        )
        own, got, d_mixed = advance([layer_flow], own.reshape(2 * half, width), got, d_mixed)
        unit = 16 << len(off_chip)

        def thirds(count):
            less = count // unit // 3 * unit
            return [(count - less, wide)] + ([(less, slim)] if less else [])

        feed_flow = chips(own, got, thirds(2 * half))

        pairs = width // PAIR
        kept = BF16 if sharers == 1 else F32
        grads = None
        for first, last in ((0, pairs // 2), (pairs // 2, pairs - 1), (pairs - 1, pairs)):
            grads = attention_backward(
                query_side, keys, values, seg_k, mixed, d_mixed, kept, first, last - first, grads
            )
            *grads, d_mixed = advance([feed_flow], *grads, d_mixed)

        d_query, d_keys, d_values = grads
        d_key = own_keys(d_keys)
        d_value = own_keys(d_values)
        four = (inputs, mixed, d_query, d_key, d_value, d_attn, unit)
        other = weight_halves(1 - core_at, *four)
        got = core_stage.swap(other)
        own = weight_halves(core_at, *four)
        rows = [
            column_sum(d_query).reshape(1, width),
            column_sum(d_value).reshape(1, width),
            first_sums[2:3],
            first_sums[0:2],
            pick(core, [own_bias, other_bias]).reshape(-1, width),
            pick(core, [other_bias, own_bias]).reshape(-1, width),
            second_sums[2:3],
            second_sums[0:2],
        ]
        filled = sum(r.shape[0] for r in rows)
        small = jnp.concatenate(rows + [jnp.zeros((SMALL // 2 - filled, width), F32)], 0)
        own, got, small, d_query, d_key, d_value = tie(own, got, small, d_query, d_key, d_value)
        attn_flow = chips(own, got, thirds(own.shape[0]), small)
        d_input = (
            d_first
            + right_dot(d_query, query_proj)
            + right_dot(d_key, key_proj)
            + right_dot(d_value, value_proj)
        ).astype(BF16)
        (d_input,) = advance([feed_flow], d_input)
        piece_flow = Flow(
            arriving(send_pieces([d_input[i * piece : (i + 1) * piece] for i in range(held)]))
        )

        advance([attn_flow])
        advance([feed_flow, attn_flow])
        advance([feed_flow, attn_flow, piece_flow])
        advance([attn_flow])
        advance([feed_flow, attn_flow])
        while feed_flow.result is None:
            advance([feed_flow, attn_flow])
        shrink_grad, expand_grad = feed_out(core_at, *feed_flow.result)
        grad_in = place_pieces(piece_flow.result)
        layer_out = place_pieces(layer_flow.result)
        shrink_grad, expand_grad, grad_in, layer_out = advance(
            [attn_flow], shrink_grad, expand_grad, grad_in, layer_out
        )
        while attn_flow.result is None:
            advance([attn_flow])
        own, got = attn_flow.result
        attn_grads = attn_out(core_at, own, got, width)
        tail = [value[-SMALL:].astype(F32) for value in (own, got)]
        tail = [value[: SMALL // 2] + value[SMALL // 2 :] for value in tail]
        totals = tail[0] + tail[1]
        ff_rows = 2 * half // width
        vectors = [totals[i] for i in range(5)]
        vectors.append(totals[5 : 5 + ff_rows].reshape(-1))
        vectors += [totals[i] for i in range(5 + ff_rows, 8 + ff_rows)]
        return (
            layer_out,
            grad_in,
            attn_grads[0],
            vectors[0],
            attn_grads[1],
            attn_grads[2],
            vectors[1],
            attn_grads[3],
            vectors[2],
            vectors[3],
            vectors[4],
            expand_grad,
            vectors[5],
            shrink_grad,
            vectors[6],
            vectors[7],
            vectors[8],
        )

    split = P(None, "rows", "seq", None)
    whole = P()
    return jax.shard_map(
        body,
        mesh=mesh,
        in_specs=(split, P(None, "rows", "seq"), P(None, "rows", "seq"), split) + (whole,) * 15,
        out_specs=(split, split) + (whole,) * 15,
        check_vma=False,
    )
```

```python
import functools

import jax
import jax.numpy as jnp
from jax import lax
from jax.experimental import pallas as pl
from jax.experimental.pallas import tpu as pltpu
from jax.sharding import PartitionSpec as P

DH = 64
PAIR = 128
MASKED = 1e30
F32 = jnp.float32
BF16 = jnp.bfloat16
NT = (((1,), (1,)), ((), ()))
NN = (((1,), (0,)), ((), ()))
BRIEF = pl.CostEstimate(flops=1, bytes_accessed=1, transcendentals=0)


def left_dot(first, second):
    return lax.dot_general(first, second, (((0,), (0,)), ((), ())), preferred_element_type=F32)


def right_dot(first, second):
    return lax.dot_general(first, second, NT, preferred_element_type=F32)


def split_three(values):
    high = values.astype(BF16)
    rest = values - high.astype(F32)
    middle = rest.astype(BF16)
    low = (rest - middle.astype(F32)).astype(BF16)
    return high.astype(F32), middle.astype(F32), low.astype(F32)


def own_lanes(shape, head):
    lane = lax.broadcasted_iota(jnp.int32, shape, 1)
    own = lane < DH if head == 0 else lane >= DH
    return own, lane % DH


def key_features(lane, seg):
    return jnp.where(
        lane < 3,
        1.0,
        jnp.where(lane == 3, -MASKED * (1.0 - seg), jnp.where(lane == 4, -MASKED * seg, 0.0)),
    ).astype(BF16)


def forward_kernel(q_ref, k_ref, v_ref, seg_q_ref, seg_k_ref, mixed_ref, query_ref, *, block):
    queries = q_ref.shape[0]
    keys = k_ref.shape[0]
    for head in range(2):
        own_k, lane_k = own_lanes((keys, PAIR), head)
        key_side = jnp.where(own_k, k_ref[...], key_features(lane_k, seg_k_ref[...].astype(F32)))
        value_side = jnp.where(own_k, v_ref[...], jnp.ones((), BF16))
        own_q, lane_q = own_lanes((block, PAIR), head)
        for start in range(0, queries, block):
            here = slice(start, start + block)
            q = q_ref[here, :]
            seg = seg_q_ref[here, :].astype(F32)
            seg_side = jnp.where(lane_q == 3, seg, jnp.where(lane_q == 4, 1.0 - seg, 0.0))
            query_side = jnp.where(own_q, q, seg_side.astype(BF16))
            scores = lax.dot_general(query_side, key_side, NT, preferred_element_type=F32)
            peak = jnp.max(scores, -1, keepdims=True)
            raised = jnp.exp(scores - peak).astype(BF16)
            summed = lax.dot_general(raised, value_side, NN, preferred_element_type=F32)
            total = summed[:, DH : DH + 1] if head == 0 else summed[:, 0:1]
            mixed = (summed / total).astype(BF16)
            shift = jnp.broadcast_to(-(peak + jnp.log(total)), (block, PAIR))
            high, middle, low = split_three(shift)
            extra = jnp.where(
                lane_q == 0,
                high,
                jnp.where(lane_q == 1, middle, jnp.where(lane_q == 2, low, seg_side)),
            )
            query_ref[head, here, :] = jnp.where(own_q, q, extra.astype(BF16))
            if head == 0:
                mixed_ref[here, :] = mixed
            else:
                mixed_ref[here, :] = jnp.where(own_q, mixed, mixed_ref[here, :])


def attention_forward(q, k, v, seg_q, seg_k):
    queries, width = q.shape
    keys = k.shape[0]
    pairs = width // PAIR
    column = lambda i: (0, i)
    whole = lambda i: (0, 0)
    return pl.pallas_call(
        functools.partial(forward_kernel, block=min(512, queries)),
        grid=(pairs,),
        in_specs=[
            pl.BlockSpec((queries, PAIR), column),
            pl.BlockSpec((keys, PAIR), column),
            pl.BlockSpec((keys, PAIR), column),
            pl.BlockSpec((queries, PAIR), whole),
            pl.BlockSpec((keys, PAIR), whole),
        ],
        out_specs=[
            pl.BlockSpec((queries, PAIR), column),
            pl.BlockSpec((2, queries, PAIR), lambda i: (i, 0, 0)),
        ],
        out_shape=[
            pltpu.HBM((queries, width), BF16),
            pltpu.HBM((2 * pairs, queries, PAIR), BF16),
        ],
        compiler_params=pltpu.CompilerParams(vmem_limit_bytes=24 * 2**20),
        cost_estimate=BRIEF,
        name="attention_forward",
    )(q, k, v, seg_q, seg_k)


def backward_kernel(
    query_ref, k_ref, v_ref, seg_k_ref, mixed_ref, d_mixed_ref, *refs, block
):
    dq_ref, dk_ref, dv_ref, dqt = refs[-4:]
    queries = mixed_ref.shape[0]
    keys = k_ref.shape[0]
    d_mixed = d_mixed_ref[...]
    product = d_mixed.astype(F32) * mixed_ref[...].astype(F32)
    for head in range(2):
        own_q, lane_q = own_lanes((queries, PAIR), head)
        own_k, lane_k = own_lanes((block, PAIR), head)
        delta = -jnp.sum(jnp.where(own_q, product, 0.0), -1, keepdims=True)
        high, middle, low = split_three(jnp.broadcast_to(delta, (queries, PAIR)))
        extra = jnp.where(
            lane_q == 0, high, jnp.where(lane_q == 1, middle, jnp.where(lane_q == 2, low, 0.0))
        )
        d_side = jnp.where(own_q, d_mixed, extra.astype(BF16))
        query_side = query_ref[head]
        ones = jnp.where(lane_k < 3, 1.0, 0.0).astype(BF16)
        for start in range(0, keys, block):
            here = slice(start, start + block)
            k = k_ref[here, :]
            seg = seg_k_ref[here, :].astype(F32)
            key_side = jnp.where(own_k, k, key_features(lane_k, seg))
            value_side = jnp.where(own_k, v_ref[here, :], ones)
            shifted = lax.dot_general(key_side, query_side, NT, preferred_element_type=F32)
            probs = jnp.exp(shifted)
            d_probs = lax.dot_general(value_side, d_side, NT, preferred_element_type=F32)
            d_scores = (probs * d_probs).astype(BF16)
            dv = lax.dot_general(probs.astype(BF16), d_mixed, NN, preferred_element_type=F32)
            dk = lax.dot_general(d_scores, query_side, NN, preferred_element_type=F32)
            turned = k.T[head * DH : (head + 1) * DH, :]
            dq = lax.dot_general(turned, d_scores, NN, preferred_element_type=F32)
            mine = slice(head * DH, (head + 1) * DH)
            if start == 0:
                dqt[mine, :] = dq
            else:
                dqt[mine, :] += dq
            dv = dv.astype(dv_ref.dtype)
            dk = dk.astype(dk_ref.dtype)
            if head == 0:
                dk_ref[here, :] = dk
                dv_ref[here, :] = dv
            else:
                dk_ref[here, :] = jnp.where(own_k, dk, dk_ref[here, :])
                dv_ref[here, :] = jnp.where(own_k, dv, dv_ref[here, :])
    dq_ref[...] = (dqt[...] * 0.125).astype(BF16).T


def attention_backward(query_side, k, v, seg_k, mixed, d_mixed, kept, first, count, before):
    queries, width = mixed.shape
    keys = k.shape[0]
    column = lambda i: (0, i + first)
    held = [] if before is None else list(before)
    return pl.pallas_call(
        functools.partial(backward_kernel, block=min(512, keys)),
        grid=(count,),
        in_specs=[
            pl.BlockSpec((2, queries, PAIR), lambda i: (i + first, 0, 0)),
            pl.BlockSpec((keys, PAIR), column),
            pl.BlockSpec((keys, PAIR), column),
            pl.BlockSpec((keys, PAIR), lambda i: (0, 0)),
            pl.BlockSpec((queries, PAIR), column),
            pl.BlockSpec((queries, PAIR), column),
        ]
        + [pl.BlockSpec(memory_space=pl.ANY)] * len(held),
        out_specs=[
            pl.BlockSpec((queries, PAIR), column),
            pl.BlockSpec((keys, PAIR), column),
            pl.BlockSpec((keys, PAIR), column),
        ],
        input_output_aliases={6 + i: i for i in range(len(held))},
        out_shape=[
            pltpu.HBM((queries, width), BF16),
            pltpu.HBM((keys, width), kept),
            pltpu.HBM((keys, width), kept),
        ],
        scratch_shapes=[pltpu.VMEM((PAIR, queries), F32)],
        compiler_params=pltpu.CompilerParams(vmem_limit_bytes=24 * 2**20),
        cost_estimate=BRIEF,
        name="attention_backward",
    )(in_hbm(query_side), k, v, seg_k, in_hbm(mixed), in_hbm(d_mixed), *map(in_hbm, held))


def dot(first, second, dims=NN):
    return lax.dot_general(first, second, dims, preferred_element_type=F32)


def gelu_pair(values):
    below = 0.5 + 0.5 * lax.erf(values * 0.7071067811865476)
    density = jnp.exp(-0.5 * values * values) * 0.3989422804014327
    return values * below, below + values * density


def normalise(values):
    centred = values - jnp.mean(values, -1, keepdims=True)
    scale = lax.rsqrt(jnp.mean(centred * centred, -1, keepdims=True) + 1e-06)
    return centred * scale, scale


def norm_back(upstream, hat, scale, gain):
    d_hat = upstream * gain
    return scale * (
        d_hat
        - jnp.mean(d_hat, -1, keepdims=True)
        - hat * jnp.mean(d_hat * hat, -1, keepdims=True)
    )


def stack_rows(rows):
    filler = jnp.zeros((8 - len(rows), rows[0].shape[1]), F32)
    return jnp.concatenate(rows + [filler], 0)


def feed_forward_kernel(
    inputs_ref,
    mixed_ref,
    output_proj_ref,
    output_bias_ref,
    gain_one_ref,
    shift_one_ref,
    expand_ref,
    expand_bias_ref,
    shrink_ref,
    shrink_bias_ref,
    gain_two_ref,
    shift_two_ref,
    *refs,
    steps,
    held,
):
    upstream_refs = refs[:held]
    hat_out, scale_ref, normed_out, active_t_ref, slope_ref = refs[held : held + 5]
    d_down_ref, sums_ref = refs[held + 5 : held + 7]
    out_refs = refs[held + 7 : 2 * held + 7]
    total, hat_ref, normed_ref, sems = refs[2 * held + 7 :]
    block = total.shape[0] // held
    early = [
        pltpu.make_async_copy(hat_ref, hat_out, sems.at[0]),
        pltpu.make_async_copy(normed_ref, normed_out, sems.at[1]),
    ]
    step = pl.program_id(0)
    tokens = total.shape[0]
    pieces = [slice(start, start + block) for start in range(0, tokens, block)]

    @pl.when(step == 0)
    def _():
        for here in pieces:
            first_sum = (
                inputs_ref[here, :].astype(F32)
                + dot(mixed_ref[here, :], output_proj_ref[...])
                + output_bias_ref[...].astype(F32)
            )
            hat, scale = normalise(first_sum)
            hat_ref[here, :] = hat.astype(BF16)
            scale_ref[here, :] = jnp.broadcast_to(scale, (block, PAIR))
            normed = gain_one_ref[...].astype(F32) * hat + shift_one_ref[...].astype(F32)
            normed_ref[here, :] = normed.astype(BF16)
            total[here, :] = normed + shrink_bias_ref[...].astype(F32)
        for copy in early:
            copy.start()

    for here in pieces:
        expanded = dot(normed_ref[here, :], expand_ref[...]) + expand_bias_ref[...].astype(F32)
        active, slope = gelu_pair(expanded)
        active = active.astype(BF16)
        slope_ref[here, :] = slope.astype(BF16)
        active_t_ref[:, here] = active.T
        total[here, :] += dot(active, shrink_ref[...])

    @pl.when(step == steps - 1)
    def _():
        gain = gain_two_ref[...].astype(F32)
        d_gain = jnp.zeros((1, total.shape[1]), F32)
        d_shift = d_gain
        d_bias = d_gain
        for here, upstream_ref, out_ref in zip(pieces, upstream_refs, out_refs):
            hat, scale = normalise(total[here, :])
            out_ref[...] = (gain * hat + shift_two_ref[...].astype(F32)).astype(BF16)
            upstream = upstream_ref[...].astype(F32)
            d_gain += jnp.sum(upstream * hat, 0, keepdims=True)
            d_shift += jnp.sum(upstream, 0, keepdims=True)
            d_down = norm_back(upstream, hat, scale, gain).astype(BF16)
            d_down_ref[here, :] = d_down
            d_bias += jnp.sum(d_down.astype(F32), 0, keepdims=True)
        sums_ref[...] = stack_rows([d_gain, d_shift, d_bias])
        for copy in early:
            copy.wait()


def in_hbm(values):
    return pltpu.with_memory_space_constraint(values, pltpu.HBM)


def hbm_shapes(*pairs):
    return [pltpu.HBM(shape, dtype) for shape, dtype in pairs]


def fixed(*shape):
    return pl.BlockSpec(shape, lambda i: (0,) * len(shape), pipeline_mode=pl.Buffered(1))


def shapes(*pairs):
    return [jax.ShapeDtypeStruct(shape, dtype) for shape, dtype in pairs]


def feed_forward(inputs, mixed, upstream, weights, block=512):
    tokens, width = inputs.shape
    units = weights[4].shape[1]
    steps = units // block
    held = len(upstream)
    piece = tokens // held
    row = fixed(1, width)
    return pl.pallas_call(
        functools.partial(feed_forward_kernel, steps=steps, held=held),
        grid=(steps,),
        in_specs=[fixed(tokens, width)] * 2
        + [fixed(width, width), row, row, row]
        + [
            pl.BlockSpec((width, block), lambda i: (0, i)),
            pl.BlockSpec((1, block), lambda i: (0, i)),
            pl.BlockSpec((block, width), lambda i: (i, 0)),
            row,
            row,
            row,
        ]
        + [fixed(piece, width)] * held,
        out_specs=[
            pl.BlockSpec(memory_space=pl.ANY),
            fixed(tokens, PAIR),
            pl.BlockSpec(memory_space=pl.ANY),
            pl.BlockSpec((block, tokens), lambda i: (i, 0)),
            pl.BlockSpec((tokens, block), lambda i: (0, i)),
            fixed(tokens, width),
            fixed(8, width),
        ]
        + [fixed(piece, width)] * held,
        out_shape=hbm_shapes(
            ((tokens, width), BF16),
            ((tokens, PAIR), F32),
            ((tokens, width), BF16),
            ((units, tokens), BF16),
            ((tokens, units), BF16),
            ((tokens, width), BF16),
            ((8, width), F32),
        )
        + shapes(*[((piece, width), BF16)] * held),
        scratch_shapes=[
            pltpu.VMEM((tokens, width), F32),
            pltpu.VMEM((tokens, width), BF16),
            pltpu.VMEM((tokens, width), BF16),
            pltpu.SemaphoreType.DMA((2,)),
        ],
        compiler_params=pltpu.CompilerParams(vmem_limit_bytes=36 * 2**20),
        cost_estimate=BRIEF,
        name="feed_forward",
    )(inputs, in_hbm(mixed), *map(in_hbm, weights), *upstream)


def feed_back_kernel(
    which_ref,
    d_down_ref,
    slope_ref,
    active_t_ref,
    shrink_ref,
    expand_ref,
    normed_ref,
    *refs,
    steps,
    block,
    last,
):
    step = pl.program_id(0)
    if last:
        gain_ref, *late_refs = refs[:5]
        grads_ref, bias_ref, d_attn_ref, d_mixed_ref, sums_ref = refs[5:10]
        turned, total, hat_ref, scale_ref, output_proj_ref, sems = refs[10:]
        late = [
            pltpu.make_async_copy(source, target, sems.at[index])
            for index, (source, target) in enumerate(
                zip(late_refs, (d_attn_ref, hat_ref, scale_ref, output_proj_ref))
            )
        ]

        @pl.when(step == 0)
        def _():
            for copy in late:
                copy.start()

    else:
        grads_ref, bias_ref, total_ref, turned, total = refs
    tokens = total.shape[0]
    pieces = [slice(start, start + block) for start in range(0, tokens, block)]

    @pl.when(step == 0)
    def _():
        total[...] = jnp.zeros_like(total)
        bias_ref[...] = jnp.zeros_like(bias_ref)

    bias = jnp.zeros((1, slope_ref.shape[1]), F32)
    for here in pieces:
        d_active = dot(d_down_ref[here, :], shrink_ref[...], NT)
        d_expand = (d_active * slope_ref[here, :].astype(F32)).astype(BF16)
        turned[:, here] = d_expand.T
        bias += jnp.sum(d_expand.astype(F32), 0, keepdims=True)
        total[here, :] += dot(d_expand, expand_ref[...], NT)
    row = lax.broadcasted_iota(jnp.int32, bias_ref.shape, 0)
    bias_ref[...] = jnp.where(row == step, bias, bias_ref[...])
    grads_ref[0] = dot(active_t_ref[...], d_down_ref[...]).astype(BF16)
    grads_ref[1] = dot(turned[...], normed_ref[...]).astype(BF16)

    if not last:

        @pl.when(step == steps - 1)
        def _():
            total_ref[...] = total[...].astype(BF16)

    else:

        @pl.when(step == steps - 1)
        def _():
            for copy in late:
                copy.wait()
            gain = gain_ref[...].astype(F32)
            d_gain = jnp.zeros((1, total.shape[1]), F32)
            d_shift = d_gain
            d_bias = d_gain
            for here in pieces:
                d_normed = total[here, :] + (
                    d_down_ref[here, :].astype(F32) + d_attn_ref[here, :].astype(F32)
                )
                hat = hat_ref[here, :].astype(F32)
                d_gain += jnp.sum(d_normed * hat, 0, keepdims=True)
                d_shift += jnp.sum(d_normed, 0, keepdims=True)
                d_attn = norm_back(d_normed, hat, scale_ref[here, :][:, 0:1], gain).astype(BF16)
                d_attn_ref[here, :] = d_attn
                d_bias += jnp.sum(d_attn.astype(F32), 0, keepdims=True)
                d_mixed_ref[here, :] = dot(d_attn, output_proj_ref[...], NT).astype(BF16)
            sums_ref[...] = stack_rows([d_gain, d_shift, d_bias])


def feed_back(which, d_down, slope, active_t, shrink, expand, normed, norm, block=512):
    tokens, width = d_down.shape
    half = slope.shape[1] // 2
    steps = half // block
    last = norm is not None
    at = lambda i, which: which[0] * steps + i
    whole = lambda *shape: pl.BlockSpec(
        shape, lambda i, which: (0,) * len(shape), pipeline_mode=pl.Buffered(1)
    )
    in_specs = [
        whole(tokens, width),
        pl.BlockSpec((tokens, block), lambda i, which: (0, at(i, which))),
        pl.BlockSpec((block, tokens), lambda i, which: (at(i, which), 0)),
        pl.BlockSpec((block, width), lambda i, which: (at(i, which), 0)),
        pl.BlockSpec((width, block), lambda i, which: (0, at(i, which))),
        whole(tokens, width),
    ]
    out_specs = [
        pl.BlockSpec((2, block, width), lambda i, which: (0, i, 0)),
        whole(8, block),
    ]
    out_shape = hbm_shapes(((2, half, width), BF16), ((8, block), F32))
    scratch = [pltpu.VMEM((block, tokens), BF16), pltpu.VMEM((tokens, width), F32)]
    extra = ()
    if last:
        gain, *late = norm
        extra = (gain, *map(in_hbm, late))
        in_specs += [whole(1, width)] + [pl.BlockSpec(memory_space=pl.ANY)] * len(late)
        out_specs += [whole(tokens, width)] * 2 + [whole(8, width)]
        out_shape += hbm_shapes(
            ((tokens, width), BF16), ((tokens, width), BF16), ((8, width), F32)
        )
        scratch += [
            pltpu.VMEM((tokens, width), BF16),
            pltpu.VMEM((tokens, PAIR), F32),
            pltpu.VMEM((width, width), BF16),
            pltpu.SemaphoreType.DMA((4,)),
        ]
    else:
        out_specs.append(whole(tokens, width))
        out_shape += hbm_shapes(((tokens, width), BF16))
    return pl.pallas_call(
        functools.partial(feed_back_kernel, steps=steps, block=min(512, tokens), last=last),
        grid_spec=pltpu.PrefetchScalarGridSpec(
            num_scalar_prefetch=1,
            grid=(steps,),
            in_specs=in_specs,
            out_specs=out_specs,
            scratch_shapes=scratch,
        ),
        out_shape=out_shape,
        compiler_params=pltpu.CompilerParams(vmem_limit_bytes=44 * 2**20),
        cost_estimate=BRIEF,
        name="feed_back_last" if last else "feed_back",
    )(which, *map(in_hbm, (d_down, slope, active_t, shrink, expand, normed)), *extra)


def weight_kernel(which_ref, *refs, steps):
    sources = refs[:6]
    if steps:
        sums_refs, (out_ref, small_ref), rest = refs[6:10], refs[10:12], refs[12:]
    else:
        (out_ref,), rest = refs[6:7], refs[7:]
    targets, sems = rest[:6], rest[6]
    inputs_ref, dq_ref, dk_ref, dv_ref, mixed_ref, d_attn_ref = targets
    copies = [
        pltpu.make_async_copy(source, target, sems.at[index])
        for index, (source, target) in enumerate(zip(sources, targets))
    ]
    for copy in copies:
        copy.start()
    count = inputs_ref.shape[1] // 2
    columns = pl.ds(pl.multiple_of(which_ref[0] * count, PAIR), count)
    if out_ref.shape[0] > 4 * count:
        out_ref[4 * count :, :] = jnp.zeros((out_ref.shape[0] - 4 * count, out_ref.shape[1]), BF16)
    copies[0].wait()
    turned = inputs_ref[:, columns].T
    for at, right_ref in enumerate((dq_ref, dk_ref, dv_ref, d_attn_ref)):
        copies[at + 1].wait()
        if at == 3:
            copies[5].wait()
            turned = mixed_ref[:, columns].T
        out_ref[at * count : (at + 1) * count, :] = dot(turned, right_ref[...]).astype(BF16)
    if steps:
        first_sums_ref, second_sums_ref, own_bias_ref, other_bias_ref = sums_refs
        small_ref[...] = jnp.zeros_like(small_ref)
        small_ref[0:1, :] = jnp.sum(dq_ref[...].astype(F32), 0, keepdims=True)
        small_ref[1:2, :] = jnp.sum(dv_ref[...].astype(F32), 0, keepdims=True)
        small_ref[2:5, :] = first_sums_ref[0:3, :]
        small_ref[5:8, :] = second_sums_ref[0:3, :]
        block = own_bias_ref.shape[1]
        own, other = own_bias_ref[0:steps, :], other_bias_ref[0:steps, :]
        lower = which_ref[0] == 0
        small_ref[8 : 8 + steps, 0:block] = jnp.where(lower, own, other)
        small_ref[8 + steps : 8 + 2 * steps, 0:block] = jnp.where(lower, other, own)


def weight_half(which, values, unit, sums=(), steps=0):
    tokens, width = values[0].shape
    rows = -(-2 * width // unit) * unit
    vmem = pl.BlockSpec(memory_space=pltpu.VMEM)
    anywhere = pl.BlockSpec(memory_space=pl.ANY)
    out_shape = shapes(((rows, width), BF16))
    if steps:
        out_shape += shapes(((SMALL // 2, width), F32))
    return pl.pallas_call(
        functools.partial(weight_kernel, steps=steps),
        in_specs=[pl.BlockSpec(memory_space=pltpu.SMEM)] + [anywhere] * 6 + [vmem] * len(sums),
        out_specs=[vmem] * len(out_shape),
        out_shape=out_shape,
        scratch_shapes=[pltpu.VMEM((tokens, width), BF16)] * 6 + [pltpu.SemaphoreType.DMA((6,))],
        compiler_params=pltpu.CompilerParams(vmem_limit_bytes=28 * 2**20),
        cost_estimate=BRIEF,
        name="weight_half",
    )(which, *map(in_hbm, values), *sums)


def input_grad_kernel(*refs, held):
    sources, outs = refs[:7], refs[7 : 7 + held]
    (d_attn, *factors), sems = refs[7 + held : 14 + held], refs[-1]
    copies = [
        pltpu.make_async_copy(source, target, sems.at[index])
        for index, (source, target) in enumerate(zip(sources, (d_attn, *factors)))
    ]
    for copy in copies:
        copy.start()
    piece = outs[0].shape[0]
    total = None
    for index in range(3):
        for copy in copies[2 * index + 1 : 2 * index + 3]:
            copy.wait()
    copies[0].wait()
    for number, out_ref in enumerate(outs):
        here = slice(number * piece, (number + 1) * piece)
        total = d_attn[here, :].astype(F32)
        for index in range(3):
            total += dot(factors[2 * index][here, :], factors[2 * index + 1][...], NT)
        out_ref[...] = total.astype(BF16)


def input_grad(d_attn, factors, held):
    tokens, width = d_attn.shape
    anywhere = pl.BlockSpec(memory_space=pl.ANY)
    values = [d_attn] + [value for pair in factors for value in pair]
    return pl.pallas_call(
        functools.partial(input_grad_kernel, held=held),
        in_specs=[anywhere] * 7,
        out_specs=[pl.BlockSpec(memory_space=pltpu.VMEM)] * held,
        out_shape=shapes(*[((tokens // held, width), BF16)] * held),
        scratch_shapes=[pltpu.VMEM(value.shape, BF16) for value in values]
        + [pltpu.SemaphoreType.DMA((7,))],
        compiler_params=pltpu.CompilerParams(vmem_limit_bytes=24 * 2**20),
        cost_estimate=BRIEF,
        name="input_grad",
    )(*map(in_hbm, values))


def feed_out_kernel(which_ref, half_ref, *refs, steps):
    del which_ref
    shrink_ref, expand_ref = refs[-2:]

    @pl.when(pl.program_id(0) < steps)
    def _():
        shrink_ref[...] = half_ref[...].astype(F32)

    @pl.when(pl.program_id(0) >= steps)
    def _():
        expand_ref[...] = half_ref[...].T.astype(F32)


def feed_out(which, values, before=(), block=512):
    width = values.shape[1]
    half = values.shape[0] // 2
    steps = half // block
    return pl.pallas_call(
        functools.partial(feed_out_kernel, steps=steps),
        grid_spec=pltpu.PrefetchScalarGridSpec(
            num_scalar_prefetch=1,
            grid=(2 * steps,),
            in_specs=[pl.BlockSpec((block, width), lambda i, which: (i, 0))]
            + [pl.BlockSpec(memory_space=pl.ANY)] * len(before),
            out_specs=[
                pl.BlockSpec(
                    (block, width),
                    lambda i, which: (which[0] * steps + jnp.minimum(i, steps - 1), 0),
                ),
                pl.BlockSpec(
                    (width, block),
                    lambda i, which: (0, which[0] * steps + jnp.maximum(i - steps, 0)),
                ),
            ],
        ),
        out_shape=shapes(((2 * half, width), F32), ((width, 2 * half), F32)),
        input_output_aliases={2 + i: i for i in range(len(before))},
        compiler_params=pltpu.CompilerParams(vmem_limit_bytes=16 * 2**20),
        cost_estimate=BRIEF,
        name="feed_out",
    )(which, values, *before)


def attn_out_kernel(which_ref, half_ref, *refs):
    del which_ref
    for index, out_ref in enumerate(refs[-4:]):

        @pl.when(pl.program_id(0) == index)
        def _(out_ref=out_ref):
            out_ref[...] = half_ref[...].astype(F32)


def attn_out(which, values, before=()):
    width = values.shape[1]
    half = width // 2
    return pl.pallas_call(
        attn_out_kernel,
        grid_spec=pltpu.PrefetchScalarGridSpec(
            num_scalar_prefetch=1,
            grid=(4,),
            in_specs=[pl.BlockSpec((half, width), lambda i, which: (i, 0))]
            + [pl.BlockSpec(memory_space=pl.ANY)] * len(before),
            out_specs=[pl.BlockSpec((half, width), lambda i, which: (which[0], 0))] * 4,
        ),
        out_shape=shapes(*[((width, width), F32)] * 4),
        input_output_aliases={2 + i: i for i in range(len(before))},
        compiler_params=pltpu.CompilerParams(vmem_limit_bytes=24 * 2**20),
        cost_estimate=BRIEF,
        name="attn_out",
    )(which, values, *before)


def place_kernel(at_ref, *refs):
    del at_ref
    out_ref = refs[-1]
    for index, ref in enumerate(refs[:-1]):

        @pl.when(pl.program_id(0) == index)
        def _(ref=ref):
            out_ref[0] = ref[...]


def place(at, parts):
    piece, width = parts[0].shape
    held = len(parts)
    return pl.pallas_call(
        place_kernel,
        grid_spec=pltpu.PrefetchScalarGridSpec(
            num_scalar_prefetch=1,
            grid=(held,),
            in_specs=[pl.BlockSpec((piece, width), lambda i, at: (0, 0))] * held,
            out_specs=pl.BlockSpec((1, piece, width), lambda i, at: (at[0] ^ i, 0, 0)),
        ),
        out_shape=jax.ShapeDtypeStruct((held, piece, width), BF16),
        compiler_params=pltpu.CompilerParams(vmem_limit_bytes=16 * 2**20),
        cost_estimate=BRIEF,
        name="place",
    )(at, *parts)


def rows_of(ref, which, count, base=0):
    return ref[pl.ds(pl.multiple_of(base + which * count, 16), count), :]


def sum_of(terms):
    return functools.reduce(lambda a, b: a + b, [t.astype(F32) for t in terms]).astype(BF16)


def scatter_kernel(bits_ref, *refs, groups):
    outs = refs[-2 * groups :]
    ins = refs[: -2 * groups]
    together = len(ins) == 2
    base = 0
    for group in range(groups):
        terms = ins if together else ins[2 * group : 2 * group + 2]
        sent_ref, kept_ref = outs[2 * group : 2 * group + 2]
        count = kept_ref.shape[0]
        here = bits_ref[group]
        sent_ref[...] = sum_of([rows_of(term, 1 - here, count, base) for term in terms])
        kept_ref[...] = sum_of([rows_of(term, here, count, base) for term in terms])
        if together:
            base += 2 * count


def local_call(kernel, bits, values, out_shape, name):
    vmem = pl.BlockSpec(memory_space=pltpu.VMEM)
    return pl.pallas_call(
        kernel,
        in_specs=[pl.BlockSpec(memory_space=pltpu.SMEM)] + [vmem] * len(values),
        out_specs=[vmem] * len(out_shape),
        out_shape=out_shape,
        compiler_params=pltpu.CompilerParams(vmem_limit_bytes=24 * 2**20),
        cost_estimate=BRIEF,
        name=name,
    )(bits, *values)


def scatter_local(bits, pairs, counts=None):
    if counts is None:
        counts = [kept.shape[0] for kept, _ in pairs]
    groups = len(counts)
    counts = [count // 2 for count in counts]
    width = pairs[0][0].shape[1]
    outs = local_call(
        functools.partial(scatter_kernel, groups=groups),
        bits,
        [value for pair in pairs for value in pair],
        shapes(*[((count, width), BF16) for count in counts for _ in range(2)]),
        "scatter_local",
    )
    return [outs[2 * i : 2 * i + 2] for i in range(groups)]


def scatter_first_kernel(bits_ref, own_at, got_at, *refs, counts):
    outs, (own, got, sems) = refs[:-3], refs[-3:]
    spans = []
    base = 0
    for group, count in enumerate(counts):
        for kept in range(2):
            half = bits_ref[group] if kept else 1 - bits_ref[group]
            start = pl.multiple_of(base + half * (count // 2), 16)
            spans.append((start, count // 2, outs[2 * group + kept]))
        base += count
    spans = spans[0::2] + spans[1::2]
    copies = []
    for index, (start, count, _) in enumerate(spans):
        rows = pl.ds(start, count)
        for which, (source, target) in enumerate(((own_at, own), (got_at, got))):
            copies.append(
                pltpu.make_async_copy(source.at[rows], target.at[rows], sems.at[2 * index + which])
            )
            copies[-1].start()
    for index, (start, count, out_ref) in enumerate(spans):
        for copy in copies[2 * index : 2 * index + 2]:
            copy.wait()
        rows = pl.ds(start, count)
        out_ref[...] = sum_of([own[rows, :], got[rows, :]])


def scatter_first(bits, own, got, counts):
    rows, width = own.shape
    anywhere = pl.BlockSpec(memory_space=pl.ANY)
    vmem = pl.BlockSpec(memory_space=pltpu.VMEM)
    outs = pl.pallas_call(
        functools.partial(scatter_first_kernel, counts=counts),
        in_specs=[pl.BlockSpec(memory_space=pltpu.SMEM), anywhere, anywhere],
        out_specs=[vmem] * (2 * len(counts)),
        out_shape=shapes(*[((count // 2, width), BF16) for count in counts for _ in range(2)]),
        scratch_shapes=[pltpu.VMEM((rows, width), BF16)] * 2
        + [pltpu.SemaphoreType.DMA((4 * len(counts),))],
        compiler_params=pltpu.CompilerParams(vmem_limit_bytes=24 * 2**20),
        cost_estimate=BRIEF,
        name="scatter_first",
    )(bits, in_hbm(own), in_hbm(got))
    return [outs[2 * group : 2 * group + 2] for group in range(len(counts))]


def split_two(values):
    high = values.astype(BF16)
    return high, (values - high.astype(F32)).astype(BF16)


SMALL = 32


def put_small(ref, at, values):
    high, low = split_two(values)
    ref[at : at + SMALL // 2, :] = high
    ref[at + SMALL // 2 : at + SMALL, :] = low


def get_small(ref, at):
    half = SMALL // 2
    return ref[at : at + half, :].astype(F32) + ref[at + half : at + SMALL, :].astype(F32)


def settle_kernel(bits_ref, *refs, groups, small):
    del bits_ref
    ins, outs = refs[: 2 * groups], refs[2 * groups + small :]
    for group in range(groups):
        count = ins[2 * group].shape[0]
        outs[group][0:count, :] = sum_of([ins[2 * group][...], ins[2 * group + 1][...]])
        if small and group == 0:
            put_small(outs[group], count, refs[2 * groups][...])


def settle_local(bits, pairs, small):
    width = pairs[0][0].shape[1]
    counts = [kept.shape[0] for kept, _ in pairs]
    if small is not None:
        counts[0] += SMALL
    return local_call(
        functools.partial(settle_kernel, groups=len(pairs), small=int(small is not None)),
        bits,
        [value for pair in pairs for value in pair] + ([] if small is None else [small]),
        shapes(*[((count, width), BF16) for count in counts]),
        "settle_local",
    )


def join_kernel(bits_ref, *refs, groups, small, merged):
    ins, outs = refs[: 2 * groups], refs[2 * groups :]
    base = 0
    for group in range(groups):
        own_ref, got_ref = ins[2 * group : 2 * group + 2]
        extra = SMALL if small and group == 0 else 0
        count = own_ref.shape[0] - extra
        out_ref = outs[0 if merged else group]
        here = bits_ref[group]
        for half, ref in ((here, own_ref), (1 - here, got_ref)):
            out_ref[pl.ds(pl.multiple_of(base + half * count, 16), count), :] = ref[0:count, :]
        if extra:
            at = out_ref.shape[0] - SMALL if merged else base + 2 * count
            put_small(out_ref, at, get_small(own_ref, count) + get_small(got_ref, count))
        if merged:
            base += 2 * count


def join_local(bits, pairs, small, merged):
    width = pairs[0][0].shape[1]
    counts = [2 * own.shape[0] for own, _ in pairs]
    if small:
        counts[0] -= SMALL
    if merged:
        counts = [sum(counts)]
    return local_call(
        functools.partial(join_kernel, groups=len(pairs), small=small, merged=merged),
        bits,
        [value for pair in pairs for value in pair],
        shapes(*[((count, width), BF16) for count in counts]),
        "join_local",
    )


def tie(*values):
    return lax.optimization_barrier(values)


def pick(which, parts):
    if len(parts) == 1:
        return parts[0]
    half = len(parts) // 2
    return jnp.where(which < half, pick(which, parts[:half]), pick(which - half, parts[half:]))


def column_sum(values):
    return jnp.sum(values.astype(F32), 0)


class Stage:
    def __init__(self, sizes, bits):
        self.bits = bits
        rows, seq = sizes
        self.pairs = []
        for index in range(rows * seq):
            axis, bit = bits[index & 1]
            self.pairs.append((index, index ^ ((1 << bit) * (seq if axis == "rows" else 1))))

    def here(self):
        first, second = [(lax.axis_index(axis) >> bit) & 1 for axis, bit in self.bits]
        if self.bits[0] == self.bits[1]:
            return first
        return jnp.where(lax.axis_index("seq") & 1 == 0, first, second)

    def swap(self, values):
        return lax.ppermute(values, ("rows", "seq"), self.pairs)


def total_over_chips(own, got, core_stage, orders, small=None, near=False):
    depth = len(orders[0][1])
    groups = range(len(orders))

    def bits_at(step):
        return jnp.stack([stages[step].here() for _, stages in orders]).astype(jnp.int32)

    def pairs_of(flat):
        return [flat[i : i + 2] for i in range(0, len(flat), 2)]

    def send(step, values, keep):
        flat = []
        for group in groups:
            flat += [keep[group], orders[group][1][step].swap(values[group])]
        return flat

    counts = [count for count, _ in orders]
    if near:
        parts = scatter_local(bits_at(0), [[own, got]], counts)
    else:
        parts = scatter_first(bits_at(0), own, got, counts)
    for step in range(1, depth + 1):
        flat = yield send(step - 1, [p[0] for p in parts], [p[1] for p in parts])
        if step < depth:
            parts = scatter_local(bits_at(step), pairs_of(flat))
    values = settle_local(bits_at(0), pairs_of(flat), small)
    for step in reversed(range(depth)):
        flat = yield send(step, values, values)
        values = join_local(bits_at(step), pairs_of(flat), small is not None, step == 0)
    both = yield [values[0], core_stage.swap(values[0])]
    return both


def arriving(values):
    values = yield values
    return values[1::2]


class Flow:
    def __init__(self, steps, left):
        self.steps = steps
        self.left = left
        self.pending = next(steps)
        self.result = None


class Timetable:
    def __init__(self):
        self.flows = []

    def open(self, steps, left=1):
        self.flows.append(Flow(steps, left))
        return self.flows[-1]

    def advance(self, moving, *values):
        flows = [flow for flow in self.flows if flow.result is None]
        held = [flow.pending if flow in moving else flow.pending[0::2] for flow in flows]
        tied = list(tie(*values, *[value for part in held for value in part]))
        values, tied = tied[: len(values)], tied[len(values) :]
        for flow, part in zip(flows, held):
            back, tied = tied[: len(part)], tied[len(part) :]
            if flow not in moving:
                flow.pending[0::2] = back
                continue
            flow.left -= 1
            try:
                flow.pending = flow.steps.send(back)
            except StopIteration as end:
                flow.result = end.value
        return self.settle(*values) if moving and values else values

    def settle(self, *values):
        return self.advance([], *values)


def solution(mesh):
    seq_size = mesh.shape["seq"]
    rows_size = mesh.shape["rows"]
    seq_bits = seq_size.bit_length() - 1
    rows_bits = rows_size.bit_length() - 1
    off_chip = [("seq", bit) for bit in range(1, seq_bits)]
    off_chip += [("rows", bit) for bit in range(rows_bits)]
    first, *middle, ahead, final = off_chip
    sizes = (rows_size, seq_size)
    core_stage = Stage(sizes, [("seq", 0)] * 2)
    straight = [first] + middle + [ahead, final]
    turned = middle + [ahead, first, final]
    spun = [ahead, first] + middle + [final]
    wide = [Stage(sizes, bits) for bits in zip(straight, turned)]
    slim = [Stage(sizes, bits) for bits in zip(spun, spun)]

    def body(
        hidden_in,
        segments,
        grad_mask,
        grad_out,
        query_proj,
        query_bias,
        key_proj,
        value_proj,
        value_bias,
        output_proj,
        output_bias,
        first_gain,
        first_shift,
        expand_proj,
        expand_bias,
        shrink_proj,
        shrink_bias,
        second_gain,
        second_shift,
    ):
        micro, rows_here, piece, width = hidden_in.shape
        held = micro * rows_here
        sharers = seq_size // held
        tokens = held * piece
        source_at = lax.axis_index("seq") % held
        core = core_stage.here()
        core_at = core.reshape(1).astype(jnp.int32)

        def trade(to_rows, part):
            there = [(s, (s % held ^ part) * sharers + s // held) for s in range(seq_size)]
            return there if to_rows else [(b, a) for a, b in there]

        def to_rows(values):
            return [
                lax.ppermute(
                    lax.dynamic_index_in_dim(values, source_at ^ part, 0, False),
                    "seq",
                    trade(True, part),
                )
                for part in range(held)
            ]

        def send_pieces(values):
            return [
                value
                for part in range(held)
                for value in (values[part], lax.ppermute(values[part], "seq", trade(False, part)))
            ]

        def place_pieces(parts):
            at = source_at.reshape(1).astype(jnp.int32)
            return place(at, parts).reshape((micro, rows_here) + parts[0].shape)

        same_row = [[r * sharers + g for g in range(sharers)] for r in range(held)]

        def all_keys(values):
            if sharers == 1:
                return values
            return lax.all_gather(values, "seq", axis=0, tiled=True, axis_index_groups=same_row)

        def own_keys(values):
            if sharers == 1:
                return values
            return lax.psum_scatter(
                values, "seq", scatter_dimension=0, tiled=True, axis_index_groups=same_row
            ).astype(BF16)

        flat = hidden_in.reshape(held, piece, width)
        far = [lax.dynamic_index_in_dim(flat, source_at ^ part, 0, False) for part in (3, 2)]
        *far, flat, marks = tie(*far, flat, segments)
        near = [lax.dynamic_index_in_dim(flat, source_at ^ part, 0, False) for part in (1, 0)]
        marks = marks.reshape(held, piece, 1).astype(BF16)
        marks = jnp.broadcast_to(marks, (held, piece, PAIR))
        inputs = [
            lax.ppermute(value, "seq", trade(True, part))
            for part, value in zip((3, 2, 1, 0), far + near)
        ]
        inputs = jnp.concatenate(inputs[::-1], 0)
        seg_q = jnp.concatenate(to_rows(marks), 0)
        masked = (grad_out * grad_mask[..., None].astype(BF16)).reshape(held, piece, width)
        masked, inputs, seg_q = tie(masked, inputs, seg_q)
        upstream = to_rows(masked)

        queries = (
            (dot(inputs, query_proj) + query_bias.astype(F32)) * 0.125
        ).astype(BF16)
        keys = all_keys(dot(inputs, key_proj).astype(BF16))
        values = all_keys((dot(inputs, value_proj) + value_bias.astype(F32)).astype(BF16))
        seg_k = all_keys(seg_q)
        mixed, query_side = attention_forward(queries, keys, values, seg_q, seg_k)
        row = lambda vector: vector.reshape(1, -1)
        hat, scale, normed, active_t, slope, d_down, second_sums, *result = feed_forward(
            inputs,
            mixed,
            upstream,
            (
                output_proj,
                row(output_bias),
                row(first_gain),
                row(first_shift),
                expand_proj,
                row(expand_bias),
                shrink_proj,
                row(shrink_bias),
                row(second_gain),
                row(second_shift),
            ),
        )
        table = Timetable()
        advance = table.advance
        layer_flow = table.open(arriving(send_pieces(result)))

        def chips(own, got, orders, small=None):
            near = small is not None
            steps = total_over_chips(own, got, core_stage, orders, small, near)
            return table.open(steps, 2 * len(wide) + 1)

        back = functools.partial(
            feed_back,
            slope=slope,
            active_t=active_t,
            shrink=shrink_proj,
            expand=expand_proj,
            normed=normed,
        )
        other, other_bias, d_normed = back(1 - core_at, d_down, norm=None)
        half = other.shape[1]
        got = core_stage.swap(other.reshape(2 * half, width))
        own, own_bias, d_attn, d_mixed, first_sums = back(
            core_at, d_down, norm=(row(first_gain), d_normed, hat, scale, output_proj)
        )
        own, got, d_mixed = advance([layer_flow], own.reshape(2 * half, width), got, d_mixed)
        unit = 16 << len(off_chip)

        def thirds(count):
            less = count // unit // 3 * unit
            return [(count - less, wide)] + ([(less, slim)] if less else [])

        feed_flow = chips(own, got, thirds(2 * half))

        pairs = width // PAIR
        kept = BF16 if sharers == 1 else F32
        grads = None
        for first, last in ((0, pairs // 2), (pairs // 2, pairs - 1), (pairs - 1, pairs)):
            grads = attention_backward(
                query_side, keys, values, seg_k, mixed, d_mixed, kept, first, last - first, grads
            )
            *grads, d_mixed = advance([feed_flow], *grads, d_mixed)

        d_query, d_keys, d_values = grads
        d_key = own_keys(d_keys)
        d_value = own_keys(d_values)
        steps = half // other_bias.shape[1]
        values = (inputs, d_query, d_key, d_value, mixed, d_attn)
        (other,) = weight_half(1 - core_at, values, unit)
        other, *values = advance([], other, *values)
        got = core_stage.swap(other)
        own, small = weight_half(
            core_at, values, unit, (first_sums, second_sums, own_bias, other_bias), steps
        )
        own, got, small = advance([feed_flow], own, got, small)
        attn_flow = chips(own, got, thirds(own.shape[0]), small)
        d_query, d_key, d_value = advance([], d_query, d_key, d_value)
        d_input = input_grad(
            d_attn, ((d_query, query_proj), (d_key, key_proj), (d_value, value_proj)), held
        )
        d_input = advance([feed_flow], *d_input)
        piece_flow = table.open(arriving(send_pieces(d_input)))

        layer_out = place_pieces(layer_flow.result)
        (layer_out,) = advance([attn_flow], layer_out)
        advance([feed_flow])
        advance([attn_flow])
        advance([attn_flow])
        advance([feed_flow, piece_flow])
        grad_in = place_pieces(piece_flow.result)
        (grad_in,) = advance([attn_flow], grad_in)
        advance([attn_flow])
        while feed_flow.left > 1:
            advance([feed_flow])
        feed_grads = feed_out(core_at, feed_flow.pending[0])
        feed_grads = advance([attn_flow], *feed_grads)
        advance([feed_flow])
        feed_grads = feed_out(1 - core_at, feed_flow.result[1], feed_grads)
        feed_grads = advance([], *feed_grads)
        while attn_flow.left > 1:
            advance([attn_flow])
        attn_grads = attn_out(core_at, attn_flow.pending[0])
        attn_grads = advance([attn_flow], *attn_grads)
        own, got = attn_flow.result
        attn_grads = attn_out(1 - core_at, got, attn_grads)
        totals = [value[-SMALL:].astype(F32) for value in (own, got)]
        totals = [value[: SMALL // 2] + value[SMALL // 2 :] for value in totals]
        totals = totals[0] + totals[1]
        shrink_grad, expand_grad = feed_grads
        expand_bias_grad = totals[8 : 8 + 2 * steps, : other_bias.shape[1]].reshape(-1)
        return (
            layer_out,
            grad_in,
            attn_grads[0],
            totals[0],
            attn_grads[1],
            attn_grads[2],
            totals[1],
            attn_grads[3],
            totals[4],
            totals[2],
            totals[3],
            expand_grad,
            expand_bias_grad,
            shrink_grad,
            totals[7],
            totals[5],
            totals[6],
        )

    split = P(None, "rows", "seq", None)
    whole = P()
    return jax.shard_map(
        body,
        mesh=mesh,
        in_specs=(split, P(None, "rows", "seq"), P(None, "rows", "seq"), split) + (whole,) * 15,
        out_specs=(split, split) + (whole,) * 15,
        check_vma=False,
    )
```

```python
import functools

import jax
import jax.numpy as jnp
from jax import lax
from jax.experimental import pallas as pl
from jax.experimental.pallas import tpu as pltpu
from jax.sharding import PartitionSpec as P

DH = 64
PAIR = 128
MASKED = 1e30
F32 = jnp.float32
BF16 = jnp.bfloat16
NT = (((1,), (1,)), ((), ()))
NN = (((1,), (0,)), ((), ()))
BRIEF = pl.CostEstimate(flops=1, bytes_accessed=1, transcendentals=0)


def left_dot(first, second):
    return lax.dot_general(first, second, (((0,), (0,)), ((), ())), preferred_element_type=F32)


def right_dot(first, second):
    return lax.dot_general(first, second, NT, preferred_element_type=F32)


def split_three(values):
    high = values.astype(BF16)
    rest = values - high.astype(F32)
    middle = rest.astype(BF16)
    low = (rest - middle.astype(F32)).astype(BF16)
    return high.astype(F32), middle.astype(F32), low.astype(F32)


def own_lanes(shape, head):
    lane = lax.broadcasted_iota(jnp.int32, shape, 1)
    own = lane < DH if head == 0 else lane >= DH
    return own, lane % DH


def key_features(lane, seg):
    return jnp.where(
        lane < 3,
        1.0,
        jnp.where(lane == 3, -MASKED * (1.0 - seg), jnp.where(lane == 4, -MASKED * seg, 0.0)),
    ).astype(BF16)


def forward_kernel(q_ref, k_ref, v_ref, seg_q_ref, seg_k_ref, mixed_ref, query_ref, *, block):
    queries = q_ref.shape[0]
    keys = k_ref.shape[0]
    for head in range(2):
        own_k, lane_k = own_lanes((keys, PAIR), head)
        key_side = jnp.where(own_k, k_ref[...], key_features(lane_k, seg_k_ref[...].astype(F32)))
        value_side = jnp.where(own_k, v_ref[...], jnp.ones((), BF16))
        own_q, lane_q = own_lanes((block, PAIR), head)
        for start in range(0, queries, block):
            here = slice(start, start + block)
            q = q_ref[here, :]
            seg = seg_q_ref[here, :].astype(F32)
            seg_side = jnp.where(lane_q == 3, seg, jnp.where(lane_q == 4, 1.0 - seg, 0.0))
            query_side = jnp.where(own_q, q, seg_side.astype(BF16))
            scores = lax.dot_general(query_side, key_side, NT, preferred_element_type=F32)
            peak = jnp.max(scores, -1, keepdims=True)
            raised = jnp.exp(scores - peak).astype(BF16)
            summed = lax.dot_general(raised, value_side, NN, preferred_element_type=F32)
            total = summed[:, DH : DH + 1] if head == 0 else summed[:, 0:1]
            mixed = (summed / total).astype(BF16)
            shift = jnp.broadcast_to(-(peak + jnp.log(total)), (block, PAIR))
            high, middle, low = split_three(shift)
            extra = jnp.where(
                lane_q == 0,
                high,
                jnp.where(lane_q == 1, middle, jnp.where(lane_q == 2, low, seg_side)),
            )
            query_ref[head, here, :] = jnp.where(own_q, q, extra.astype(BF16))
            if head == 0:
                mixed_ref[here, :] = mixed
            else:
                mixed_ref[here, :] = jnp.where(own_q, mixed, mixed_ref[here, :])


def attention_forward(q, k, v, seg_q, seg_k):
    queries, width = q.shape
    keys = k.shape[0]
    pairs = width // PAIR
    column = lambda i: (0, i)
    whole = lambda i: (0, 0)
    return pl.pallas_call(
        functools.partial(forward_kernel, block=min(512, queries)),
        grid=(pairs,),
        in_specs=[
            pl.BlockSpec((queries, PAIR), column),
            pl.BlockSpec((keys, PAIR), column),
            pl.BlockSpec((keys, PAIR), column),
            pl.BlockSpec((queries, PAIR), whole),
            pl.BlockSpec((keys, PAIR), whole),
        ],
        out_specs=[
            pl.BlockSpec((queries, PAIR), column),
            pl.BlockSpec((2, queries, PAIR), lambda i: (i, 0, 0)),
        ],
        out_shape=[
            pltpu.HBM((queries, width), BF16),
            pltpu.HBM((2 * pairs, queries, PAIR), BF16),
        ],
        compiler_params=pltpu.CompilerParams(vmem_limit_bytes=24 * 2**20),
        cost_estimate=BRIEF,
        name="attention_forward",
    )(q, k, v, seg_q, seg_k)


def backward_kernel(
    query_ref, k_ref, v_ref, seg_k_ref, mixed_ref, d_mixed_ref, *refs, block
):
    dq_ref, dk_ref, dv_ref, dqt = refs[-4:]
    queries = mixed_ref.shape[0]
    keys = k_ref.shape[0]
    d_mixed = d_mixed_ref[...]
    product = d_mixed.astype(F32) * mixed_ref[...].astype(F32)
    for head in range(2):
        own_q, lane_q = own_lanes((queries, PAIR), head)
        own_k, lane_k = own_lanes((block, PAIR), head)
        delta = -jnp.sum(jnp.where(own_q, product, 0.0), -1, keepdims=True)
        high, middle, low = split_three(jnp.broadcast_to(delta, (queries, PAIR)))
        extra = jnp.where(
            lane_q == 0, high, jnp.where(lane_q == 1, middle, jnp.where(lane_q == 2, low, 0.0))
        )
        d_side = jnp.where(own_q, d_mixed, extra.astype(BF16))
        query_side = query_ref[head]
        ones = jnp.where(lane_k < 3, 1.0, 0.0).astype(BF16)
        for start in range(0, keys, block):
            here = slice(start, start + block)
            k = k_ref[here, :]
            seg = seg_k_ref[here, :].astype(F32)
            key_side = jnp.where(own_k, k, key_features(lane_k, seg))
            value_side = jnp.where(own_k, v_ref[here, :], ones)
            shifted = lax.dot_general(key_side, query_side, NT, preferred_element_type=F32)
            probs = jnp.exp(shifted)
            d_probs = lax.dot_general(value_side, d_side, NT, preferred_element_type=F32)
            d_scores = (probs * d_probs).astype(BF16)
            dv = lax.dot_general(probs.astype(BF16), d_mixed, NN, preferred_element_type=F32)
            dk = lax.dot_general(d_scores, query_side, NN, preferred_element_type=F32)
            turned = k.T[head * DH : (head + 1) * DH, :]
            dq = lax.dot_general(turned, d_scores, NN, preferred_element_type=F32)
            mine = slice(head * DH, (head + 1) * DH)
            if start == 0:
                dqt[mine, :] = dq
            else:
                dqt[mine, :] += dq
            dv = dv.astype(dv_ref.dtype)
            dk = dk.astype(dk_ref.dtype)
            if head == 0:
                dk_ref[here, :] = dk
                dv_ref[here, :] = dv
            else:
                dk_ref[here, :] = jnp.where(own_k, dk, dk_ref[here, :])
                dv_ref[here, :] = jnp.where(own_k, dv, dv_ref[here, :])
    dq_ref[...] = (dqt[...] * 0.125).astype(BF16).T


def attention_backward(query_side, k, v, seg_k, mixed, d_mixed, kept, first, count, before):
    queries, width = mixed.shape
    keys = k.shape[0]
    column = lambda i: (0, i + first)
    held = [] if before is None else list(before)
    return pl.pallas_call(
        functools.partial(backward_kernel, block=min(512, keys)),
        grid=(count,),
        in_specs=[
            pl.BlockSpec((2, queries, PAIR), lambda i: (i + first, 0, 0)),
            pl.BlockSpec((keys, PAIR), column),
            pl.BlockSpec((keys, PAIR), column),
            pl.BlockSpec((keys, PAIR), lambda i: (0, 0)),
            pl.BlockSpec((queries, PAIR), column),
            pl.BlockSpec((queries, PAIR), column),
        ]
        + [pl.BlockSpec(memory_space=pl.ANY)] * len(held),
        out_specs=[
            pl.BlockSpec((queries, PAIR), column),
            pl.BlockSpec((keys, PAIR), column),
            pl.BlockSpec((keys, PAIR), column),
        ],
        input_output_aliases={6 + i: i for i in range(len(held))},
        out_shape=[
            pltpu.HBM((queries, width), BF16),
            pltpu.HBM((keys, width), kept),
            pltpu.HBM((keys, width), kept),
        ],
        scratch_shapes=[pltpu.VMEM((PAIR, queries), F32)],
        compiler_params=pltpu.CompilerParams(vmem_limit_bytes=24 * 2**20),
        cost_estimate=BRIEF,
        name="attention_backward",
    )(in_hbm(query_side), k, v, seg_k, in_hbm(mixed), in_hbm(d_mixed), *map(in_hbm, held))


def dot(first, second, dims=NN):
    return lax.dot_general(first, second, dims, preferred_element_type=F32)


def gelu_pair(values):
    below = 0.5 + 0.5 * lax.erf(values * 0.7071067811865476)
    density = jnp.exp(-0.5 * values * values) * 0.3989422804014327
    return values * below, below + values * density


def normalise(values):
    centred = values - jnp.mean(values, -1, keepdims=True)
    scale = lax.rsqrt(jnp.mean(centred * centred, -1, keepdims=True) + 1e-06)
    return centred * scale, scale


def norm_back(upstream, hat, scale, gain):
    d_hat = upstream * gain
    return scale * (
        d_hat
        - jnp.mean(d_hat, -1, keepdims=True)
        - hat * jnp.mean(d_hat * hat, -1, keepdims=True)
    )


def stack_rows(rows):
    filler = jnp.zeros((8 - len(rows), rows[0].shape[1]), F32)
    return jnp.concatenate(rows + [filler], 0)


def feed_forward_kernel(
    inputs_ref,
    mixed_ref,
    output_proj_ref,
    output_bias_ref,
    gain_one_ref,
    shift_one_ref,
    expand_ref,
    expand_bias_ref,
    shrink_ref,
    shrink_bias_ref,
    gain_two_ref,
    shift_two_ref,
    *refs,
    steps,
    held,
):
    upstream_refs = refs[:held]
    hat_out, scale_ref, normed_out, active_t_ref, slope_ref = refs[held : held + 5]
    d_down_ref, sums_ref = refs[held + 5 : held + 7]
    out_refs = refs[held + 7 : 2 * held + 7]
    total, hat_ref, normed_ref, sems = refs[2 * held + 7 :]
    block = total.shape[0] // held
    early = [
        pltpu.make_async_copy(hat_ref, hat_out, sems.at[0]),
        pltpu.make_async_copy(normed_ref, normed_out, sems.at[1]),
    ]
    step = pl.program_id(0)
    tokens = total.shape[0]
    pieces = [slice(start, start + block) for start in range(0, tokens, block)]

    @pl.when(step == 0)
    def _():
        for here in pieces:
            first_sum = (
                inputs_ref[here, :].astype(F32)
                + dot(mixed_ref[here, :], output_proj_ref[...])
                + output_bias_ref[...].astype(F32)
            )
            hat, scale = normalise(first_sum)
            hat_ref[here, :] = hat.astype(BF16)
            scale_ref[here, :] = jnp.broadcast_to(scale, (block, PAIR))
            normed = gain_one_ref[...].astype(F32) * hat + shift_one_ref[...].astype(F32)
            normed_ref[here, :] = normed.astype(BF16)
            total[here, :] = normed + shrink_bias_ref[...].astype(F32)
        for copy in early:
            copy.start()

    for here in pieces:
        expanded = dot(normed_ref[here, :], expand_ref[...]) + expand_bias_ref[...].astype(F32)
        active, slope = gelu_pair(expanded)
        active = active.astype(BF16)
        slope_ref[here, :] = slope.astype(BF16)
        active_t_ref[:, here] = active.T
        total[here, :] += dot(active, shrink_ref[...])

    @pl.when(step == steps - 1)
    def _():
        gain = gain_two_ref[...].astype(F32)
        d_gain = jnp.zeros((1, total.shape[1]), F32)
        d_shift = d_gain
        d_bias = d_gain
        for here, upstream_ref, out_ref in zip(pieces, upstream_refs, out_refs):
            hat, scale = normalise(total[here, :])
            out_ref[...] = (gain * hat + shift_two_ref[...].astype(F32)).astype(BF16)
            upstream = upstream_ref[...].astype(F32)
            d_gain += jnp.sum(upstream * hat, 0, keepdims=True)
            d_shift += jnp.sum(upstream, 0, keepdims=True)
            d_down = norm_back(upstream, hat, scale, gain).astype(BF16)
            d_down_ref[here, :] = d_down
            d_bias += jnp.sum(d_down.astype(F32), 0, keepdims=True)
        sums_ref[...] = stack_rows([d_gain, d_shift, d_bias])
        for copy in early:
            copy.wait()


def in_hbm(values):
    return pltpu.with_memory_space_constraint(values, pltpu.HBM)


def hbm_shapes(*pairs):
    return [pltpu.HBM(shape, dtype) for shape, dtype in pairs]


def fixed(*shape):
    return pl.BlockSpec(shape, lambda i: (0,) * len(shape), pipeline_mode=pl.Buffered(1))


def shapes(*pairs):
    return [jax.ShapeDtypeStruct(shape, dtype) for shape, dtype in pairs]


def feed_forward(inputs, mixed, upstream, weights, block=768):
    tokens, width = inputs.shape
    units = weights[4].shape[1]
    steps = units // block
    held = len(upstream)
    piece = tokens // held
    row = fixed(1, width)
    return pl.pallas_call(
        functools.partial(feed_forward_kernel, steps=steps, held=held),
        grid=(steps,),
        in_specs=[fixed(tokens, width)] * 2
        + [fixed(width, width), row, row, row]
        + [
            pl.BlockSpec((width, block), lambda i: (0, i)),
            pl.BlockSpec((1, block), lambda i: (0, i)),
            pl.BlockSpec((block, width), lambda i: (i, 0)),
            row,
            row,
            row,
        ]
        + [fixed(piece, width)] * held,
        out_specs=[
            pl.BlockSpec(memory_space=pl.ANY),
            fixed(tokens, PAIR),
            pl.BlockSpec(memory_space=pl.ANY),
            pl.BlockSpec((block, tokens), lambda i: (i, 0)),
            pl.BlockSpec((tokens, block), lambda i: (0, i)),
            fixed(tokens, width),
            fixed(8, width),
        ]
        + [fixed(piece, width)] * held,
        out_shape=hbm_shapes(
            ((tokens, width), BF16),
            ((tokens, PAIR), F32),
            ((tokens, width), BF16),
            ((units, tokens), BF16),
            ((tokens, units), BF16),
            ((tokens, width), BF16),
            ((8, width), F32),
        )
        + shapes(*[((piece, width), BF16)] * held),
        scratch_shapes=[
            pltpu.VMEM((tokens, width), F32),
            pltpu.VMEM((tokens, width), BF16),
            pltpu.VMEM((tokens, width), BF16),
            pltpu.SemaphoreType.DMA((2,)),
        ],
        compiler_params=pltpu.CompilerParams(vmem_limit_bytes=36 * 2**20),
        cost_estimate=BRIEF,
        name="feed_forward",
    )(inputs, in_hbm(mixed), *map(in_hbm, weights), *upstream)


def feed_back_kernel(
    which_ref,
    d_down_ref,
    slope_ref,
    active_t_ref,
    shrink_ref,
    expand_ref,
    normed_ref,
    *refs,
    steps,
    block,
    last,
):
    step = pl.program_id(0)
    if last:
        gain_ref, *late_refs = refs[:5]
        grads_ref, bias_ref, d_attn_ref, d_mixed_ref, sums_ref = refs[5:10]
        turned, total, hat_ref, scale_ref, output_proj_ref, sems = refs[10:]
        late = [
            pltpu.make_async_copy(source, target, sems.at[index])
            for index, (source, target) in enumerate(
                zip(late_refs, (d_attn_ref, hat_ref, scale_ref, output_proj_ref))
            )
        ]

        @pl.when(step == 0)
        def _():
            for copy in late:
                copy.start()

    else:
        grads_ref, bias_ref, total_ref, turned, total = refs
    tokens = total.shape[0]
    pieces = [slice(start, start + block) for start in range(0, tokens, block)]

    @pl.when(step == 0)
    def _():
        total[...] = jnp.zeros_like(total)
        bias_ref[...] = jnp.zeros_like(bias_ref)

    bias = jnp.zeros((1, slope_ref.shape[1]), F32)
    for here in pieces:
        d_active = dot(d_down_ref[here, :], shrink_ref[...], NT)
        d_expand = (d_active * slope_ref[here, :].astype(F32)).astype(BF16)
        turned[:, here] = d_expand.T
        bias += jnp.sum(d_expand.astype(F32), 0, keepdims=True)
        total[here, :] += dot(d_expand, expand_ref[...], NT)
    row = lax.broadcasted_iota(jnp.int32, bias_ref.shape, 0)
    bias_ref[...] = jnp.where(row == step, bias, bias_ref[...])
    grads_ref[0] = dot(active_t_ref[...], d_down_ref[...]).astype(BF16)
    grads_ref[1] = dot(turned[...], normed_ref[...]).astype(BF16)

    if not last:

        @pl.when(step == steps - 1)
        def _():
            total_ref[...] = total[...].astype(BF16)

    else:

        @pl.when(step == steps - 1)
        def _():
            for copy in late:
                copy.wait()
            gain = gain_ref[...].astype(F32)
            d_gain = jnp.zeros((1, total.shape[1]), F32)
            d_shift = d_gain
            d_bias = d_gain
            for here in pieces:
                d_normed = total[here, :] + (
                    d_down_ref[here, :].astype(F32) + d_attn_ref[here, :].astype(F32)
                )
                hat = hat_ref[here, :].astype(F32)
                d_gain += jnp.sum(d_normed * hat, 0, keepdims=True)
                d_shift += jnp.sum(d_normed, 0, keepdims=True)
                d_attn = norm_back(d_normed, hat, scale_ref[here, :][:, 0:1], gain).astype(BF16)
                d_attn_ref[here, :] = d_attn
                d_bias += jnp.sum(d_attn.astype(F32), 0, keepdims=True)
                d_mixed_ref[here, :] = dot(d_attn, output_proj_ref[...], NT).astype(BF16)
            sums_ref[...] = stack_rows([d_gain, d_shift, d_bias])


def feed_back(which, d_down, slope, active_t, shrink, expand, normed, norm, block=512):
    tokens, width = d_down.shape
    half = slope.shape[1] // 2
    steps = half // block
    last = norm is not None
    at = lambda i, which: which[0] * steps + i
    whole = lambda *shape: pl.BlockSpec(
        shape, lambda i, which: (0,) * len(shape), pipeline_mode=pl.Buffered(1)
    )
    in_specs = [
        whole(tokens, width),
        pl.BlockSpec((tokens, block), lambda i, which: (0, at(i, which))),
        pl.BlockSpec((block, tokens), lambda i, which: (at(i, which), 0)),
        pl.BlockSpec((block, width), lambda i, which: (at(i, which), 0)),
        pl.BlockSpec((width, block), lambda i, which: (0, at(i, which))),
        whole(tokens, width),
    ]
    out_specs = [
        pl.BlockSpec((2, block, width), lambda i, which: (0, i, 0)),
        whole(8, block),
    ]
    out_shape = hbm_shapes(((2, half, width), BF16), ((8, block), F32))
    scratch = [pltpu.VMEM((block, tokens), BF16), pltpu.VMEM((tokens, width), F32)]
    extra = ()
    if last:
        gain, *late = norm
        extra = (gain, *map(in_hbm, late))
        in_specs += [whole(1, width)] + [pl.BlockSpec(memory_space=pl.ANY)] * len(late)
        out_specs += [whole(tokens, width)] * 2 + [whole(8, width)]
        out_shape += hbm_shapes(
            ((tokens, width), BF16), ((tokens, width), BF16), ((8, width), F32)
        )
        scratch += [
            pltpu.VMEM((tokens, width), BF16),
            pltpu.VMEM((tokens, PAIR), F32),
            pltpu.VMEM((width, width), BF16),
            pltpu.SemaphoreType.DMA((4,)),
        ]
    else:
        out_specs.append(whole(tokens, width))
        out_shape += hbm_shapes(((tokens, width), BF16))
    return pl.pallas_call(
        functools.partial(feed_back_kernel, steps=steps, block=min(512, tokens), last=last),
        grid_spec=pltpu.PrefetchScalarGridSpec(
            num_scalar_prefetch=1,
            grid=(steps,),
            in_specs=in_specs,
            out_specs=out_specs,
            scratch_shapes=scratch,
        ),
        out_shape=out_shape,
        compiler_params=pltpu.CompilerParams(vmem_limit_bytes=44 * 2**20),
        cost_estimate=BRIEF,
        name="feed_back_last" if last else "feed_back",
    )(which, *map(in_hbm, (d_down, slope, active_t, shrink, expand, normed)), *extra)


def weight_kernel(
    core_ref,
    first_sums_ref,
    second_sums_ref,
    own_bias_ref,
    other_bias_ref,
    *refs,
    steps,
):
    sources, (other_ref, own_ref, small_ref) = refs[:6], refs[6:9]
    targets, (inputs_t, mixed_t, sems) = refs[9:15], refs[15:]
    inputs_ref, dq_ref, dk_ref, dv_ref, mixed_ref, d_attn_ref = targets
    copies = [
        pltpu.make_async_copy(source, target, sems.at[index])
        for index, (source, target) in enumerate(zip(sources, targets))
    ]
    for copy in copies:
        copy.start()
    count = inputs_ref.shape[1] // 2
    core = core_ref[0]
    for ref in (other_ref, own_ref):
        if ref.shape[0] > 4 * count:
            ref[4 * count :, :] = jnp.zeros((ref.shape[0] - 4 * count, ref.shape[1]), BF16)
    copies[0].wait()
    inputs_t[...] = inputs_ref[...].T
    for at, right_ref in enumerate((dq_ref, dk_ref, dv_ref, d_attn_ref)):
        copies[at + 1].wait()
        left_ref = inputs_t
        if at == 3:
            copies[5].wait()
            mixed_t[...] = mixed_ref[...].T
            left_ref = mixed_t
        for half, out_ref in ((1 - core, other_ref), (core, own_ref)):
            rows = pl.ds(pl.multiple_of(half * count, PAIR), count)
            out_ref[at * count : (at + 1) * count, :] = dot(left_ref[rows, :], right_ref[...]).astype(
                BF16
            )
    small_ref[...] = jnp.zeros_like(small_ref)
    small_ref[0:1, :] = jnp.sum(dq_ref[...].astype(F32), 0, keepdims=True)
    small_ref[1:2, :] = jnp.sum(dv_ref[...].astype(F32), 0, keepdims=True)
    small_ref[2:5, :] = first_sums_ref[0:3, :]
    small_ref[5:8, :] = second_sums_ref[0:3, :]
    block = own_bias_ref.shape[1]
    own, other = own_bias_ref[0:steps, :], other_bias_ref[0:steps, :]
    small_ref[8 : 8 + steps, 0:block] = jnp.where(core == 0, own, other)
    small_ref[8 + steps : 8 + 2 * steps, 0:block] = jnp.where(core == 0, other, own)


def weight_halves(core, values, unit, sums, steps):
    tokens, width = values[0].shape
    rows = -(-2 * width // unit) * unit
    vmem = pl.BlockSpec(memory_space=pltpu.VMEM)
    anywhere = pl.BlockSpec(memory_space=pl.ANY)
    return pl.pallas_call(
        functools.partial(weight_kernel, steps=steps),
        in_specs=[pl.BlockSpec(memory_space=pltpu.SMEM)] + [vmem] * 4 + [anywhere] * 6,
        out_specs=[vmem] * 3,
        out_shape=shapes(
            ((rows, width), BF16), ((rows, width), BF16), ((SMALL // 2, width), F32)
        ),
        scratch_shapes=[pltpu.VMEM((tokens, width), BF16)] * 6
        + [pltpu.VMEM((width, tokens), BF16)] * 2
        + [pltpu.SemaphoreType.DMA((6,))],
        compiler_params=pltpu.CompilerParams(vmem_limit_bytes=32 * 2**20),
        cost_estimate=BRIEF,
        name="weight_halves",
    )(core, *sums, *map(in_hbm, values))


def input_grad_kernel(*refs, held):
    sources, outs = refs[:7], refs[7 : 7 + held]
    (d_attn, *factors), sems = refs[7 + held : 14 + held], refs[-1]
    copies = [
        pltpu.make_async_copy(source, target, sems.at[index])
        for index, (source, target) in enumerate(zip(sources, (d_attn, *factors)))
    ]
    for copy in copies:
        copy.start()
    piece = outs[0].shape[0]
    total = None
    for index in range(3):
        for copy in copies[2 * index + 1 : 2 * index + 3]:
            copy.wait()
    copies[0].wait()
    for number, out_ref in enumerate(outs):
        here = slice(number * piece, (number + 1) * piece)
        total = d_attn[here, :].astype(F32)
        for index in range(3):
            total += dot(factors[2 * index][here, :], factors[2 * index + 1][...], NT)
        out_ref[...] = total.astype(BF16)


def input_grad(d_attn, factors, held):
    tokens, width = d_attn.shape
    anywhere = pl.BlockSpec(memory_space=pl.ANY)
    values = [d_attn] + [value for pair in factors for value in pair]
    return pl.pallas_call(
        functools.partial(input_grad_kernel, held=held),
        in_specs=[anywhere] * 7,
        out_specs=[pl.BlockSpec(memory_space=pltpu.VMEM)] * held,
        out_shape=shapes(*[((tokens // held, width), BF16)] * held),
        scratch_shapes=[pltpu.VMEM(value.shape, BF16) for value in values]
        + [pltpu.SemaphoreType.DMA((7,))],
        compiler_params=pltpu.CompilerParams(vmem_limit_bytes=24 * 2**20),
        cost_estimate=BRIEF,
        name="input_grad",
    )(*map(in_hbm, values))


def feed_out_kernel(which_ref, half_ref, *refs, steps):
    del which_ref
    shrink_ref, expand_ref = refs[-2:]

    @pl.when(pl.program_id(0) < steps)
    def _():
        shrink_ref[...] = half_ref[...].astype(F32)

    @pl.when(pl.program_id(0) >= steps)
    def _():
        expand_ref[...] = half_ref[...].T.astype(F32)


def feed_out(which, values, before=(), block=512):
    width = values.shape[1]
    half = values.shape[0] // 2
    steps = half // block
    return pl.pallas_call(
        functools.partial(feed_out_kernel, steps=steps),
        grid_spec=pltpu.PrefetchScalarGridSpec(
            num_scalar_prefetch=1,
            grid=(2 * steps,),
            in_specs=[pl.BlockSpec((block, width), lambda i, which: (i, 0))]
            + [pl.BlockSpec(memory_space=pl.ANY)] * len(before),
            out_specs=[
                pl.BlockSpec(
                    (block, width),
                    lambda i, which: (which[0] * steps + jnp.minimum(i, steps - 1), 0),
                ),
                pl.BlockSpec(
                    (width, block),
                    lambda i, which: (0, which[0] * steps + jnp.maximum(i - steps, 0)),
                ),
            ],
        ),
        out_shape=shapes(((2 * half, width), F32), ((width, 2 * half), F32)),
        input_output_aliases={2 + i: i for i in range(len(before))},
        compiler_params=pltpu.CompilerParams(vmem_limit_bytes=16 * 2**20),
        cost_estimate=BRIEF,
        name="feed_out",
    )(which, values, *before)


def attn_out_kernel(which_ref, half_ref, *refs):
    del which_ref
    for index, out_ref in enumerate(refs[-4:]):

        @pl.when(pl.program_id(0) == index)
        def _(out_ref=out_ref):
            out_ref[...] = half_ref[...].astype(F32)


def attn_out(which, values, before=()):
    width = values.shape[1]
    half = width // 2
    return pl.pallas_call(
        attn_out_kernel,
        grid_spec=pltpu.PrefetchScalarGridSpec(
            num_scalar_prefetch=1,
            grid=(4,),
            in_specs=[pl.BlockSpec((half, width), lambda i, which: (i, 0))]
            + [pl.BlockSpec(memory_space=pl.ANY)] * len(before),
            out_specs=[pl.BlockSpec((half, width), lambda i, which: (which[0], 0))] * 4,
        ),
        out_shape=shapes(*[((width, width), F32)] * 4),
        input_output_aliases={2 + i: i for i in range(len(before))},
        compiler_params=pltpu.CompilerParams(vmem_limit_bytes=24 * 2**20),
        cost_estimate=BRIEF,
        name="attn_out",
    )(which, values, *before)


def place_kernel(at_ref, *refs):
    del at_ref
    out_ref = refs[-1]
    for index, ref in enumerate(refs[:-1]):

        @pl.when(pl.program_id(0) == index)
        def _(ref=ref):
            out_ref[0] = ref[...]


def place(at, parts):
    piece, width = parts[0].shape
    held = len(parts)
    return pl.pallas_call(
        place_kernel,
        grid_spec=pltpu.PrefetchScalarGridSpec(
            num_scalar_prefetch=1,
            grid=(held,),
            in_specs=[pl.BlockSpec((piece, width), lambda i, at: (0, 0))] * held,
            out_specs=pl.BlockSpec((1, piece, width), lambda i, at: (at[0] ^ i, 0, 0)),
        ),
        out_shape=jax.ShapeDtypeStruct((held, piece, width), BF16),
        compiler_params=pltpu.CompilerParams(vmem_limit_bytes=16 * 2**20),
        cost_estimate=BRIEF,
        name="place",
    )(at, *parts)


def rows_of(ref, which, count, base=0):
    return ref[pl.ds(pl.multiple_of(base + which * count, 16), count), :]


def sum_of(terms):
    return functools.reduce(lambda a, b: a + b, [t.astype(F32) for t in terms]).astype(BF16)


def scatter_kernel(bits_ref, *refs, groups):
    outs = refs[-2 * groups :]
    ins = refs[: -2 * groups]
    together = len(ins) == 2
    base = 0
    for group in range(groups):
        terms = ins if together else ins[2 * group : 2 * group + 2]
        sent_ref, kept_ref = outs[2 * group : 2 * group + 2]
        count = kept_ref.shape[0]
        here = bits_ref[group]
        sent_ref[...] = sum_of([rows_of(term, 1 - here, count, base) for term in terms])
        kept_ref[...] = sum_of([rows_of(term, here, count, base) for term in terms])
        if together:
            base += 2 * count


def local_call(kernel, bits, values, out_shape, name):
    vmem = pl.BlockSpec(memory_space=pltpu.VMEM)
    return pl.pallas_call(
        kernel,
        in_specs=[pl.BlockSpec(memory_space=pltpu.SMEM)] + [vmem] * len(values),
        out_specs=[vmem] * len(out_shape),
        out_shape=out_shape,
        compiler_params=pltpu.CompilerParams(vmem_limit_bytes=24 * 2**20),
        cost_estimate=BRIEF,
        name=name,
    )(bits, *values)


def scatter_local(bits, pairs, counts=None):
    if counts is None:
        counts = [kept.shape[0] for kept, _ in pairs]
    groups = len(counts)
    counts = [count // 2 for count in counts]
    width = pairs[0][0].shape[1]
    outs = local_call(
        functools.partial(scatter_kernel, groups=groups),
        bits,
        [value for pair in pairs for value in pair],
        shapes(*[((count, width), BF16) for count in counts for _ in range(2)]),
        "scatter_local",
    )
    return [outs[2 * i : 2 * i + 2] for i in range(groups)]


def scatter_first_kernel(bits_ref, own_at, got_at, *refs, counts):
    outs, (own, got, sems) = refs[:-3], refs[-3:]
    spans = []
    base = 0
    for group, count in enumerate(counts):
        for kept in range(2):
            half = bits_ref[group] if kept else 1 - bits_ref[group]
            start = pl.multiple_of(base + half * (count // 2), 16)
            spans.append((start, count // 2, outs[2 * group + kept]))
        base += count
    spans = spans[0::2] + spans[1::2]
    copies = []
    for index, (start, count, _) in enumerate(spans):
        rows = pl.ds(start, count)
        for which, (source, target) in enumerate(((own_at, own), (got_at, got))):
            copies.append(
                pltpu.make_async_copy(source.at[rows], target.at[rows], sems.at[2 * index + which])
            )
            copies[-1].start()
    for index, (start, count, out_ref) in enumerate(spans):
        for copy in copies[2 * index : 2 * index + 2]:
            copy.wait()
        rows = pl.ds(start, count)
        out_ref[...] = sum_of([own[rows, :], got[rows, :]])


def scatter_first(bits, own, got, counts):
    rows, width = own.shape
    anywhere = pl.BlockSpec(memory_space=pl.ANY)
    vmem = pl.BlockSpec(memory_space=pltpu.VMEM)
    outs = pl.pallas_call(
        functools.partial(scatter_first_kernel, counts=counts),
        in_specs=[pl.BlockSpec(memory_space=pltpu.SMEM), anywhere, anywhere],
        out_specs=[vmem] * (2 * len(counts)),
        out_shape=shapes(*[((count // 2, width), BF16) for count in counts for _ in range(2)]),
        scratch_shapes=[pltpu.VMEM((rows, width), BF16)] * 2
        + [pltpu.SemaphoreType.DMA((4 * len(counts),))],
        compiler_params=pltpu.CompilerParams(vmem_limit_bytes=24 * 2**20),
        cost_estimate=BRIEF,
        name="scatter_first",
    )(bits, in_hbm(own), in_hbm(got))
    return [outs[2 * group : 2 * group + 2] for group in range(len(counts))]


def split_two(values):
    high = values.astype(BF16)
    return high, (values - high.astype(F32)).astype(BF16)


SMALL = 32


def put_small(ref, at, values):
    high, low = split_two(values)
    ref[at : at + SMALL // 2, :] = high
    ref[at + SMALL // 2 : at + SMALL, :] = low


def get_small(ref, at):
    half = SMALL // 2
    return ref[at : at + half, :].astype(F32) + ref[at + half : at + SMALL, :].astype(F32)


def settle_kernel(bits_ref, *refs, groups, small):
    del bits_ref
    ins, outs = refs[: 2 * groups], refs[2 * groups + small :]
    for group in range(groups):
        count = ins[2 * group].shape[0]
        outs[group][0:count, :] = sum_of([ins[2 * group][...], ins[2 * group + 1][...]])
        if small and group == 0:
            put_small(outs[group], count, refs[2 * groups][...])


def settle_local(bits, pairs, small):
    width = pairs[0][0].shape[1]
    counts = [kept.shape[0] for kept, _ in pairs]
    if small is not None:
        counts[0] += SMALL
    return local_call(
        functools.partial(settle_kernel, groups=len(pairs), small=int(small is not None)),
        bits,
        [value for pair in pairs for value in pair] + ([] if small is None else [small]),
        shapes(*[((count, width), BF16) for count in counts]),
        "settle_local",
    )


def add_kernel(bits_ref, *refs, groups, small):
    del bits_ref
    ins, outs = refs[: 2 * groups], refs[2 * groups :]
    for group in range(groups):
        own_ref, got_ref = ins[2 * group : 2 * group + 2]
        extra = SMALL if small and group == 0 else 0
        count = own_ref.shape[0] - extra
        outs[group][0:count, :] = sum_of([own_ref[0:count, :], got_ref[0:count, :]])
        if extra:
            put_small(outs[group], count, get_small(own_ref, count) + get_small(got_ref, count))


def add_local(bits, pairs, small):
    return local_call(
        functools.partial(add_kernel, groups=len(pairs), small=small),
        bits,
        [value for pair in pairs for value in pair],
        shapes(*[(own.shape, BF16) for own, _ in pairs]),
        "add_local",
    )


def join_kernel(bits_ref, *refs, groups, small, merged, pieces):
    ins, outs = refs[: 2 * pieces * groups], list(refs[2 * pieces * groups :])
    parts = len(outs) // groups
    base = 0
    for group in range(groups):
        owns = ins[2 * pieces * group : 2 * pieces * group + 2 * pieces : 2]
        gots = ins[2 * pieces * group + 1 : 2 * pieces * group + 2 * pieces : 2]
        extra = SMALL if small and group == 0 else 0
        count = owns[0].shape[0] - extra
        here = bits_ref[group]
        if parts > 1:
            for half, out_ref in enumerate(outs[2 * group : 2 * group + 2]):

                @pl.when(here == half)
                def _(out_ref=out_ref):
                    out_ref[...] = owns[0][...]

                @pl.when(here != half)
                def _(out_ref=out_ref):
                    out_ref[...] = gots[0][...]

            continue
        out_ref = outs[0 if merged else group]
        whole = count * pieces
        for half, refs_of in ((here, owns), (1 - here, gots)):
            for index, ref in enumerate(refs_of):
                start = pl.multiple_of(base + half * whole + index * count, 16)
                out_ref[pl.ds(start, count), :] = ref[0:count, :]
        if extra:
            at = out_ref.shape[0] - SMALL if merged else base + 2 * whole
            put_small(out_ref, at, get_small(owns[0], count) + get_small(gots[0], count))
        if merged:
            base += 2 * whole


def join_local(bits, arrived, small, merged, parts=1):
    width = arrived[0][0].shape[1]
    pieces = len(arrived[0]) // 2
    counts = [2 * pieces * group[0].shape[0] for group in arrived]
    if small:
        counts[0] -= SMALL
    if merged:
        counts = [sum(counts)]
    counts = [count // parts for count in counts for _ in range(parts)]
    return local_call(
        functools.partial(
            join_kernel, groups=len(arrived), small=small, merged=merged, pieces=pieces
        ),
        bits,
        [value for group in arrived for value in group],
        shapes(*[((count, width), BF16) for count in counts]),
        "join_local",
    )


def tie(*values):
    return lax.optimization_barrier(values)


def pick(which, parts):
    if len(parts) == 1:
        return parts[0]
    half = len(parts) // 2
    return jnp.where(which < half, pick(which, parts[:half]), pick(which - half, parts[half:]))


def column_sum(values):
    return jnp.sum(values.astype(F32), 0)


class Stage:
    def __init__(self, sizes, bits):
        self.bits = bits
        rows, seq = sizes
        self.pairs = []
        for index in range(rows * seq):
            axis, bit = bits[index & 1]
            self.pairs.append((index, index ^ ((1 << bit) * (seq if axis == "rows" else 1))))

    def here(self):
        first, second = [(lax.axis_index(axis) >> bit) & 1 for axis, bit in self.bits]
        if self.bits[0] == self.bits[1]:
            return first
        return jnp.where(lax.axis_index("seq") & 1 == 0, first, second)

    def swap(self, values):
        return lax.ppermute(values, ("rows", "seq"), self.pairs)


def total_over_chips(own, got, core_stage, orders, small=None, near=False):
    depth = len(orders[0][1])
    groups = range(len(orders))

    def bits_at(step):
        return jnp.stack([stages[step].here() for _, stages in orders]).astype(jnp.int32)

    def pairs_of(flat):
        return [flat[i : i + 2] for i in range(0, len(flat), 2)]

    def send(step, values, keep):
        flat = []
        for group in groups:
            flat += [keep[group], orders[group][1][step].swap(values[group])]
        return flat

    counts = [count for count, _ in orders]
    if near:
        parts = scatter_local(bits_at(0), [[own, got]], counts)
    else:
        parts = scatter_first(bits_at(0), own, got, counts)
    last = depth - 1 if near else depth
    for step in range(1, last + 1):
        flat = yield send(step - 1, [p[0] for p in parts], [p[1] for p in parts])
        if step < last:
            parts = scatter_local(bits_at(step), pairs_of(flat))
    values = settle_local(bits_at(0), pairs_of(flat), small)
    if near:
        flat = yield send(last, values, values)
        values = add_local(bits_at(0), pairs_of(flat), small is not None)
    carried = small is not None
    for step in reversed(range(last)):
        flat = yield send(step, values, values)
        parts = 2 if step == 1 and not carried else 1
        values = join_local(bits_at(step), pairs_of(flat), carried, step == 0, parts)
        if parts > 1:
            lower = yield send(0, values[0::2], values[0::2])
            upper = yield send(0, values[1::2], values[1::2])
            arrived = [list(low) + list(high) for low, high in zip(pairs_of(lower), pairs_of(upper))]
            values = join_local(bits_at(0), arrived, carried, True)
            break
    both = yield [values[0], core_stage.swap(values[0])]
    return both


def arriving(values):
    values = yield values
    return values[1::2]


class Flow:
    def __init__(self, steps, left):
        self.steps = steps
        self.left = left
        self.pending = next(steps)
        self.result = None


class Timetable:
    def __init__(self):
        self.flows = []

    def open(self, steps, left=1):
        self.flows.append(Flow(steps, left))
        return self.flows[-1]

    def advance(self, moving, *values):
        flows = [flow for flow in self.flows if flow.result is None]
        held = [flow.pending if flow in moving else flow.pending[0::2] for flow in flows]
        tied = list(tie(*values, *[value for part in held for value in part]))
        values, tied = tied[: len(values)], tied[len(values) :]
        for flow, part in zip(flows, held):
            back, tied = tied[: len(part)], tied[len(part) :]
            if flow not in moving:
                flow.pending[0::2] = back
                continue
            flow.left -= 1
            try:
                flow.pending = flow.steps.send(back)
            except StopIteration as end:
                flow.result = end.value
        return self.settle(*values) if moving and values else values

    def settle(self, *values):
        return self.advance([], *values)


def solution(mesh):
    seq_size = mesh.shape["seq"]
    rows_size = mesh.shape["rows"]
    seq_bits = seq_size.bit_length() - 1
    rows_bits = rows_size.bit_length() - 1
    off_chip = [("seq", bit) for bit in range(1, seq_bits)]
    off_chip += [("rows", bit) for bit in range(rows_bits)]
    first, *middle, ahead, final = off_chip
    sizes = (rows_size, seq_size)
    core_stage = Stage(sizes, [("seq", 0)] * 2)
    straight = [first] + middle + [ahead, final]
    turned = middle + [ahead, first, final]
    spun = [ahead, first] + middle + [final]
    wide = [Stage(sizes, bits) for bits in zip(straight, turned)]
    slim = [Stage(sizes, bits) for bits in zip(spun, spun)]

    def body(
        hidden_in,
        segments,
        grad_mask,
        grad_out,
        query_proj,
        query_bias,
        key_proj,
        value_proj,
        value_bias,
        output_proj,
        output_bias,
        first_gain,
        first_shift,
        expand_proj,
        expand_bias,
        shrink_proj,
        shrink_bias,
        second_gain,
        second_shift,
    ):
        micro, rows_here, piece, width = hidden_in.shape
        held = micro * rows_here
        sharers = seq_size // held
        tokens = held * piece
        source_at = lax.axis_index("seq") % held
        core = core_stage.here()
        core_at = core.reshape(1).astype(jnp.int32)

        def trade(to_rows, part):
            there = [(s, (s % held ^ part) * sharers + s // held) for s in range(seq_size)]
            return there if to_rows else [(b, a) for a, b in there]

        def to_rows(values):
            return [
                lax.ppermute(
                    lax.dynamic_index_in_dim(values, source_at ^ part, 0, False),
                    "seq",
                    trade(True, part),
                )
                for part in range(held)
            ]

        def send_pieces(values):
            return [
                value
                for part in range(held)
                for value in (values[part], lax.ppermute(values[part], "seq", trade(False, part)))
            ]

        def place_pieces(parts):
            at = source_at.reshape(1).astype(jnp.int32)
            return place(at, parts).reshape((micro, rows_here) + parts[0].shape)

        same_row = [[r * sharers + g for g in range(sharers)] for r in range(held)]

        def all_keys(values):
            if sharers == 1:
                return values
            return lax.all_gather(values, "seq", axis=0, tiled=True, axis_index_groups=same_row)

        def own_keys(values):
            if sharers == 1:
                return values
            return lax.psum_scatter(
                values, "seq", scatter_dimension=0, tiled=True, axis_index_groups=same_row
            ).astype(BF16)

        flat = hidden_in.reshape(held, piece, width)
        far = [lax.dynamic_index_in_dim(flat, source_at ^ part, 0, False) for part in (3, 2)]
        *far, flat, marks = tie(*far, flat, segments)
        near = [lax.dynamic_index_in_dim(flat, source_at ^ part, 0, False) for part in (1, 0)]
        marks = marks.reshape(held, piece, 1).astype(BF16)
        marks = jnp.broadcast_to(marks, (held, piece, PAIR))
        inputs = [
            lax.ppermute(value, "seq", trade(True, part))
            for part, value in zip((3, 2, 1, 0), far + near)
        ]
        inputs = jnp.concatenate(inputs[::-1], 0)
        seg_q = jnp.concatenate(to_rows(marks), 0)
        masked = (grad_out * grad_mask[..., None].astype(BF16)).reshape(held, piece, width)
        masked, inputs, seg_q = tie(masked, inputs, seg_q)
        upstream = to_rows(masked)

        queries = (
            (dot(inputs, query_proj) + query_bias.astype(F32)) * 0.125
        ).astype(BF16)
        keys = all_keys(dot(inputs, key_proj).astype(BF16))
        values = all_keys((dot(inputs, value_proj) + value_bias.astype(F32)).astype(BF16))
        seg_k = all_keys(seg_q)
        mixed, query_side = attention_forward(queries, keys, values, seg_q, seg_k)
        row = lambda vector: vector.reshape(1, -1)
        hat, scale, normed, active_t, slope, d_down, second_sums, *result = feed_forward(
            inputs,
            mixed,
            upstream,
            (
                output_proj,
                row(output_bias),
                row(first_gain),
                row(first_shift),
                expand_proj,
                row(expand_bias),
                shrink_proj,
                row(shrink_bias),
                row(second_gain),
                row(second_shift),
            ),
        )
        table = Timetable()
        advance = table.advance
        layer_flow = table.open(arriving(send_pieces(result)))

        def chips(own, got, orders, small=None):
            near = small is not None
            steps = total_over_chips(own, got, core_stage, orders, small, near)
            return table.open(steps, 2 * len(wide) + (0 if near else 2))

        back = functools.partial(
            feed_back,
            slope=slope,
            active_t=active_t,
            shrink=shrink_proj,
            expand=expand_proj,
            normed=normed,
        )
        other, other_bias, d_normed = back(1 - core_at, d_down, norm=None)
        half = other.shape[1]
        got = core_stage.swap(other.reshape(2 * half, width))
        own, own_bias, d_attn, d_mixed, first_sums = back(
            core_at, d_down, norm=(row(first_gain), d_normed, hat, scale, output_proj)
        )
        own, got, d_mixed = advance([layer_flow], own.reshape(2 * half, width), got, d_mixed)
        unit = 16 << len(off_chip)

        def thirds(count):
            less = count // unit // 3 * unit
            return [(count - less, wide)] + ([(less, slim)] if less else [])

        feed_flow = chips(own, got, thirds(2 * half))

        pairs = width // PAIR
        kept = BF16 if sharers == 1 else F32
        grads = None
        for first, last in ((0, pairs),):
            grads = attention_backward(
                query_side, keys, values, seg_k, mixed, d_mixed, kept, first, last - first, grads
            )
            *grads, d_mixed = advance([feed_flow], *grads, d_mixed)

        d_query, d_keys, d_values = grads
        d_key = own_keys(d_keys)
        d_value = own_keys(d_values)
        steps = half // other_bias.shape[1]
        other, own, small = weight_halves(
            core_at,
            (inputs, d_query, d_key, d_value, mixed, d_attn),
            unit,
            (first_sums, second_sums, own_bias, other_bias),
            steps,
        )
        other, own, small, d_query, d_key, d_value = advance(
            [feed_flow], other, own, small, d_query, d_key, d_value
        )
        got = core_stage.swap(other)
        d_input = input_grad(
            d_attn, ((d_query, query_proj), (d_key, key_proj), (d_value, value_proj)), held
        )
        own, got, small, *d_input = advance([feed_flow], own, got, small, *d_input)
        attn_flow = chips(own, got, [(own.shape[0], wide)], small)
        piece_flow = table.open(arriving(send_pieces(d_input)))

        both = [feed_flow, attn_flow]
        layer_out = place_pieces(list(map(in_hbm, layer_flow.result)))
        (layer_out,) = advance(both, layer_out)
        advance(both + [piece_flow])
        grad_in = place_pieces(piece_flow.result)
        (grad_in,) = advance(both, grad_in)
        while feed_flow.left > 1:
            advance(both)
        feed_grads = feed_out(core_at, feed_flow.pending[0])
        feed_grads = advance(both, *feed_grads)
        feed_grads = feed_out(1 - core_at, feed_flow.result[1], feed_grads)
        while attn_flow.left > 1:
            feed_grads = advance([attn_flow], *feed_grads)
        attn_grads = attn_out(core_at, attn_flow.pending[0])
        attn_grads = advance([attn_flow], *attn_grads)
        own, got = attn_flow.result
        attn_grads = attn_out(1 - core_at, got, attn_grads)
        totals = [value[-SMALL:].astype(F32) for value in (own, got)]
        totals = [value[: SMALL // 2] + value[SMALL // 2 :] for value in totals]
        totals = totals[0] + totals[1]
        shrink_grad, expand_grad = feed_grads
        expand_bias_grad = totals[8 : 8 + 2 * steps, : other_bias.shape[1]].reshape(-1)
        return (
            layer_out,
            grad_in,
            attn_grads[0],
            totals[0],
            attn_grads[1],
            attn_grads[2],
            totals[1],
            attn_grads[3],
            totals[4],
            totals[2],
            totals[3],
            expand_grad,
            expand_bias_grad,
            shrink_grad,
            totals[7],
            totals[5],
            totals[6],
        )

    split = P(None, "rows", "seq", None)
    whole = P()
    return jax.shard_map(
        body,
        mesh=mesh,
        in_specs=(split, P(None, "rows", "seq"), P(None, "rows", "seq"), split) + (whole,) * 15,
        out_specs=(split, split) + (whole,) * 15,
        check_vma=False,
    )
```

```python
import functools

import jax
import jax.numpy as jnp
from jax import lax
from jax.experimental import pallas as pl
from jax.experimental.pallas import tpu as pltpu
from jax.sharding import PartitionSpec as P

DH = 64
PAIR = 128
MASKED = 1e30
F32 = jnp.float32
BF16 = jnp.bfloat16
NT = (((1,), (1,)), ((), ()))
NN = (((1,), (0,)), ((), ()))
BRIEF = pl.CostEstimate(flops=1, bytes_accessed=1, transcendentals=0)


def left_dot(first, second):
    return lax.dot_general(first, second, (((0,), (0,)), ((), ())), preferred_element_type=F32)


def right_dot(first, second):
    return lax.dot_general(first, second, NT, preferred_element_type=F32)


def split_three(values):
    high = values.astype(BF16)
    rest = values - high.astype(F32)
    middle = rest.astype(BF16)
    low = (rest - middle.astype(F32)).astype(BF16)
    return high.astype(F32), middle.astype(F32), low.astype(F32)


def own_lanes(shape, head):
    lane = lax.broadcasted_iota(jnp.int32, shape, 1)
    own = lane < DH if head == 0 else lane >= DH
    return own, lane % DH


def key_features(lane, seg):
    return jnp.where(
        lane < 3,
        1.0,
        jnp.where(lane == 3, -MASKED * (1.0 - seg), jnp.where(lane == 4, -MASKED * seg, 0.0)),
    ).astype(BF16)


def forward_kernel(q_ref, k_ref, v_ref, seg_q_ref, seg_k_ref, mixed_ref, query_ref, *, block):
    queries = q_ref.shape[0]
    keys = k_ref.shape[0]
    for head in range(2):
        own_k, lane_k = own_lanes((keys, PAIR), head)
        key_side = jnp.where(own_k, k_ref[...], key_features(lane_k, seg_k_ref[...].astype(F32)))
        value_side = jnp.where(own_k, v_ref[...], jnp.ones((), BF16))
        own_q, lane_q = own_lanes((block, PAIR), head)
        for start in range(0, queries, block):
            here = slice(start, start + block)
            q = q_ref[here, :]
            seg = seg_q_ref[here, :].astype(F32)
            seg_side = jnp.where(lane_q == 3, seg, jnp.where(lane_q == 4, 1.0 - seg, 0.0))
            query_side = jnp.where(own_q, q, seg_side.astype(BF16))
            scores = lax.dot_general(query_side, key_side, NT, preferred_element_type=F32)
            peak = jnp.max(scores, -1, keepdims=True)
            raised = jnp.exp(scores - peak).astype(BF16)
            summed = lax.dot_general(raised, value_side, NN, preferred_element_type=F32)
            total = summed[:, DH : DH + 1] if head == 0 else summed[:, 0:1]
            mixed = (summed / total).astype(BF16)
            shift = jnp.broadcast_to(-(peak + jnp.log(total)), (block, PAIR))
            high, middle, low = split_three(shift)
            extra = jnp.where(
                lane_q == 0,
                high,
                jnp.where(lane_q == 1, middle, jnp.where(lane_q == 2, low, seg_side)),
            )
            query_ref[head, here, :] = jnp.where(own_q, q, extra.astype(BF16))
            if head == 0:
                mixed_ref[here, :] = mixed
            else:
                mixed_ref[here, :] = jnp.where(own_q, mixed, mixed_ref[here, :])


def attention_forward(q, k, v, seg_q, seg_k):
    queries, width = q.shape
    keys = k.shape[0]
    pairs = width // PAIR
    column = lambda i: (0, i)
    whole = lambda i: (0, 0)
    return pl.pallas_call(
        functools.partial(forward_kernel, block=min(512, queries)),
        grid=(pairs,),
        in_specs=[
            pl.BlockSpec((queries, PAIR), column),
            pl.BlockSpec((keys, PAIR), column),
            pl.BlockSpec((keys, PAIR), column),
            pl.BlockSpec((queries, PAIR), whole),
            pl.BlockSpec((keys, PAIR), whole),
        ],
        out_specs=[
            pl.BlockSpec((queries, PAIR), column),
            pl.BlockSpec((2, queries, PAIR), lambda i: (i, 0, 0)),
        ],
        out_shape=[
            pltpu.HBM((queries, width), BF16),
            pltpu.HBM((2 * pairs, queries, PAIR), BF16),
        ],
        compiler_params=pltpu.CompilerParams(vmem_limit_bytes=24 * 2**20),
        cost_estimate=BRIEF,
        name="attention_forward",
    )(q, k, v, seg_q, seg_k)


def backward_kernel(
    query_ref, k_ref, v_ref, seg_k_ref, mixed_ref, d_mixed_ref, *refs, block
):
    dq_ref, dk_ref, dv_ref, dqt = refs[-4:]
    queries = mixed_ref.shape[0]
    keys = k_ref.shape[0]
    d_mixed = d_mixed_ref[...]
    product = d_mixed.astype(F32) * mixed_ref[...].astype(F32)
    for head in range(2):
        own_q, lane_q = own_lanes((queries, PAIR), head)
        own_k, lane_k = own_lanes((block, PAIR), head)
        delta = -jnp.sum(jnp.where(own_q, product, 0.0), -1, keepdims=True)
        high, middle, low = split_three(jnp.broadcast_to(delta, (queries, PAIR)))
        extra = jnp.where(
            lane_q == 0, high, jnp.where(lane_q == 1, middle, jnp.where(lane_q == 2, low, 0.0))
        )
        d_side = jnp.where(own_q, d_mixed, extra.astype(BF16))
        query_side = query_ref[head]
        ones = jnp.where(lane_k < 3, 1.0, 0.0).astype(BF16)
        for start in range(0, keys, block):
            here = slice(start, start + block)
            k = k_ref[here, :]
            seg = seg_k_ref[here, :].astype(F32)
            key_side = jnp.where(own_k, k, key_features(lane_k, seg))
            value_side = jnp.where(own_k, v_ref[here, :], ones)
            shifted = lax.dot_general(key_side, query_side, NT, preferred_element_type=F32)
            probs = jnp.exp(shifted)
            d_probs = lax.dot_general(value_side, d_side, NT, preferred_element_type=F32)
            d_scores = (probs * d_probs).astype(BF16)
            dv = lax.dot_general(probs.astype(BF16), d_mixed, NN, preferred_element_type=F32)
            dk = lax.dot_general(d_scores, query_side, NN, preferred_element_type=F32)
            turned = k.T[head * DH : (head + 1) * DH, :]
            dq = lax.dot_general(turned, d_scores, NN, preferred_element_type=F32)
            mine = slice(head * DH, (head + 1) * DH)
            if start == 0:
                dqt[mine, :] = dq
            else:
                dqt[mine, :] += dq
            dv = dv.astype(dv_ref.dtype)
            dk = dk.astype(dk_ref.dtype)
            if head == 0:
                dk_ref[here, :] = dk
                dv_ref[here, :] = dv
            else:
                dk_ref[here, :] = jnp.where(own_k, dk, dk_ref[here, :])
                dv_ref[here, :] = jnp.where(own_k, dv, dv_ref[here, :])
    dq_ref[...] = (dqt[...] * 0.125).astype(BF16).T


def attention_backward(query_side, k, v, seg_k, mixed, d_mixed, kept, first, count, before):
    queries, width = mixed.shape
    keys = k.shape[0]
    column = lambda i: (0, i + first)
    held = [] if before is None else list(before)
    return pl.pallas_call(
        functools.partial(backward_kernel, block=min(512, keys)),
        grid=(count,),
        in_specs=[
            pl.BlockSpec((2, queries, PAIR), lambda i: (i + first, 0, 0)),
            pl.BlockSpec((keys, PAIR), column),
            pl.BlockSpec((keys, PAIR), column),
            pl.BlockSpec((keys, PAIR), lambda i: (0, 0)),
            pl.BlockSpec((queries, PAIR), column),
            pl.BlockSpec((queries, PAIR), column),
        ]
        + [pl.BlockSpec(memory_space=pl.ANY)] * len(held),
        out_specs=[
            pl.BlockSpec((queries, PAIR), column),
            pl.BlockSpec((keys, PAIR), column),
            pl.BlockSpec((keys, PAIR), column),
        ],
        input_output_aliases={6 + i: i for i in range(len(held))},
        out_shape=[
            pltpu.HBM((queries, width), BF16),
            pltpu.HBM((keys, width), kept),
            pltpu.HBM((keys, width), kept),
        ],
        scratch_shapes=[pltpu.VMEM((PAIR, queries), F32)],
        compiler_params=pltpu.CompilerParams(vmem_limit_bytes=24 * 2**20),
        cost_estimate=BRIEF,
        name="attention_backward",
    )(in_hbm(query_side), k, v, seg_k, in_hbm(mixed), in_hbm(d_mixed), *map(in_hbm, held))


def dot(first, second, dims=NN):
    return lax.dot_general(first, second, dims, preferred_element_type=F32)


def gelu_pair(values):
    below = 0.5 + 0.5 * lax.erf(values * 0.7071067811865476)
    density = jnp.exp(-0.5 * values * values) * 0.3989422804014327
    return values * below, below + values * density


def normalise(values):
    centred = values - jnp.mean(values, -1, keepdims=True)
    scale = lax.rsqrt(jnp.mean(centred * centred, -1, keepdims=True) + 1e-06)
    return centred * scale, scale


def norm_back(upstream, hat, scale, gain):
    d_hat = upstream * gain
    return scale * (
        d_hat
        - jnp.mean(d_hat, -1, keepdims=True)
        - hat * jnp.mean(d_hat * hat, -1, keepdims=True)
    )


def stack_rows(rows):
    filler = jnp.zeros((8 - len(rows), rows[0].shape[1]), F32)
    return jnp.concatenate(rows + [filler], 0)


def feed_forward_kernel(
    inputs_ref,
    mixed_ref,
    output_proj_ref,
    output_bias_ref,
    gain_one_ref,
    shift_one_ref,
    expand_ref,
    expand_bias_ref,
    shrink_ref,
    shrink_bias_ref,
    gain_two_ref,
    shift_two_ref,
    *refs,
    steps,
    held,
):
    upstream_refs = refs[:held]
    hat_out, scale_ref, normed_out, active_t_ref, slope_ref = refs[held : held + 5]
    d_down_ref, sums_ref = refs[held + 5 : held + 7]
    out_refs = refs[held + 7 : 2 * held + 7]
    total, hat_ref, normed_ref, sems = refs[2 * held + 7 :]
    block = total.shape[0] // held
    early = [
        pltpu.make_async_copy(hat_ref, hat_out, sems.at[0]),
        pltpu.make_async_copy(normed_ref, normed_out, sems.at[1]),
    ]
    step = pl.program_id(0)
    tokens = total.shape[0]
    pieces = [slice(start, start + block) for start in range(0, tokens, block)]

    @pl.when(step == 0)
    def _():
        for here in pieces:
            first_sum = (
                inputs_ref[here, :].astype(F32)
                + dot(mixed_ref[here, :], output_proj_ref[...])
                + output_bias_ref[...].astype(F32)
            )
            hat, scale = normalise(first_sum)
            hat_ref[here, :] = hat.astype(BF16)
            scale_ref[here, :] = jnp.broadcast_to(scale, (block, PAIR))
            normed = gain_one_ref[...].astype(F32) * hat + shift_one_ref[...].astype(F32)
            normed_ref[here, :] = normed.astype(BF16)
            total[here, :] = normed + shrink_bias_ref[...].astype(F32)
        for copy in early:
            copy.start()

    for here in pieces:
        expanded = dot(normed_ref[here, :], expand_ref[...]) + expand_bias_ref[...].astype(F32)
        active, slope = gelu_pair(expanded)
        active = active.astype(BF16)
        slope_ref[here, :] = slope.astype(BF16)
        active_t_ref[:, here] = active.T
        total[here, :] += dot(active, shrink_ref[...])

    @pl.when(step == steps - 1)
    def _():
        gain = gain_two_ref[...].astype(F32)
        d_gain = jnp.zeros((1, total.shape[1]), F32)
        d_shift = d_gain
        d_bias = d_gain
        for here, upstream_ref, out_ref in zip(pieces, upstream_refs, out_refs):
            hat, scale = normalise(total[here, :])
            out_ref[...] = (gain * hat + shift_two_ref[...].astype(F32)).astype(BF16)
            upstream = upstream_ref[...].astype(F32)
            d_gain += jnp.sum(upstream * hat, 0, keepdims=True)
            d_shift += jnp.sum(upstream, 0, keepdims=True)
            d_down = norm_back(upstream, hat, scale, gain).astype(BF16)
            d_down_ref[here, :] = d_down
            d_bias += jnp.sum(d_down.astype(F32), 0, keepdims=True)
        sums_ref[...] = stack_rows([d_gain, d_shift, d_bias])
        for copy in early:
            copy.wait()


def in_hbm(values):
    return pltpu.with_memory_space_constraint(values, pltpu.HBM)


def hbm_shapes(*pairs):
    return [pltpu.HBM(shape, dtype) for shape, dtype in pairs]


def fixed(*shape):
    return pl.BlockSpec(shape, lambda i: (0,) * len(shape), pipeline_mode=pl.Buffered(1))


def shapes(*pairs):
    return [jax.ShapeDtypeStruct(shape, dtype) for shape, dtype in pairs]


def feed_forward(inputs, mixed, upstream, weights, block=768):
    tokens, width = inputs.shape
    units = weights[4].shape[1]
    steps = units // block
    held = len(upstream)
    piece = tokens // held
    row = fixed(1, width)
    return pl.pallas_call(
        functools.partial(feed_forward_kernel, steps=steps, held=held),
        grid=(steps,),
        in_specs=[fixed(tokens, width)] * 2
        + [fixed(width, width), row, row, row]
        + [
            pl.BlockSpec((width, block), lambda i: (0, i)),
            pl.BlockSpec((1, block), lambda i: (0, i)),
            pl.BlockSpec((block, width), lambda i: (i, 0)),
            row,
            row,
            row,
        ]
        + [fixed(piece, width)] * held,
        out_specs=[
            pl.BlockSpec(memory_space=pl.ANY),
            fixed(tokens, PAIR),
            pl.BlockSpec(memory_space=pl.ANY),
            pl.BlockSpec((block, tokens), lambda i: (i, 0)),
            pl.BlockSpec((tokens, block), lambda i: (0, i)),
            fixed(tokens, width),
            fixed(8, width),
        ]
        + [fixed(piece, width)] * held,
        out_shape=hbm_shapes(
            ((tokens, width), BF16),
            ((tokens, PAIR), F32),
            ((tokens, width), BF16),
            ((units, tokens), BF16),
            ((tokens, units), BF16),
            ((tokens, width), BF16),
            ((8, width), F32),
        )
        + shapes(*[((piece, width), BF16)] * held),
        scratch_shapes=[
            pltpu.VMEM((tokens, width), F32),
            pltpu.VMEM((tokens, width), BF16),
            pltpu.VMEM((tokens, width), BF16),
            pltpu.SemaphoreType.DMA((2,)),
        ],
        compiler_params=pltpu.CompilerParams(vmem_limit_bytes=36 * 2**20),
        cost_estimate=BRIEF,
        name="feed_forward",
    )(inputs, in_hbm(mixed), *map(in_hbm, weights), *upstream)


def feed_back_kernel(
    which_ref,
    d_down_ref,
    slope_ref,
    active_t_ref,
    shrink_ref,
    expand_ref,
    normed_ref,
    *refs,
    steps,
    block,
    last,
):
    step = pl.program_id(0)
    if last:
        gain_ref, *late_refs = refs[:5]
        grads_ref, bias_ref, d_attn_ref, d_mixed_ref, sums_ref = refs[5:10]
        turned, total, hat_ref, scale_ref, output_proj_ref, sems = refs[10:]
        late = [
            pltpu.make_async_copy(source, target, sems.at[index])
            for index, (source, target) in enumerate(
                zip(late_refs, (d_attn_ref, hat_ref, scale_ref, output_proj_ref))
            )
        ]

        @pl.when(step == 0)
        def _():
            for copy in late:
                copy.start()

    else:
        grads_ref, bias_ref, total_ref, turned, total = refs
    tokens = total.shape[0]
    pieces = [slice(start, start + block) for start in range(0, tokens, block)]

    @pl.when(step == 0)
    def _():
        total[...] = jnp.zeros_like(total)
        bias_ref[...] = jnp.zeros_like(bias_ref)

    bias = jnp.zeros((1, slope_ref.shape[1]), F32)
    for here in pieces:
        d_active = dot(d_down_ref[here, :], shrink_ref[...], NT)
        d_expand = (d_active * slope_ref[here, :].astype(F32)).astype(BF16)
        turned[:, here] = d_expand.T
        bias += jnp.sum(d_expand.astype(F32), 0, keepdims=True)
        total[here, :] += dot(d_expand, expand_ref[...], NT)
    row = lax.broadcasted_iota(jnp.int32, bias_ref.shape, 0)
    bias_ref[...] = jnp.where(row == step, bias, bias_ref[...])
    grads_ref[0] = dot(active_t_ref[...], d_down_ref[...]).astype(BF16)
    grads_ref[1] = dot(turned[...], normed_ref[...]).astype(BF16)

    if not last:

        @pl.when(step == steps - 1)
        def _():
            total_ref[...] = total[...].astype(BF16)

    else:

        @pl.when(step == steps - 1)
        def _():
            for copy in late:
                copy.wait()
            gain = gain_ref[...].astype(F32)
            d_gain = jnp.zeros((1, total.shape[1]), F32)
            d_shift = d_gain
            d_bias = d_gain
            for here in pieces:
                d_normed = total[here, :] + (
                    d_down_ref[here, :].astype(F32) + d_attn_ref[here, :].astype(F32)
                )
                hat = hat_ref[here, :].astype(F32)
                d_gain += jnp.sum(d_normed * hat, 0, keepdims=True)
                d_shift += jnp.sum(d_normed, 0, keepdims=True)
                d_attn = norm_back(d_normed, hat, scale_ref[here, :][:, 0:1], gain).astype(BF16)
                d_attn_ref[here, :] = d_attn
                d_bias += jnp.sum(d_attn.astype(F32), 0, keepdims=True)
                d_mixed_ref[here, :] = dot(d_attn, output_proj_ref[...], NT).astype(BF16)
            sums_ref[...] = stack_rows([d_gain, d_shift, d_bias])


def feed_back(which, d_down, slope, active_t, shrink, expand, normed, norm, block=512):
    tokens, width = d_down.shape
    half = slope.shape[1] // 2
    steps = half // block
    last = norm is not None
    at = lambda i, which: which[0] * steps + i
    whole = lambda *shape: pl.BlockSpec(
        shape, lambda i, which: (0,) * len(shape), pipeline_mode=pl.Buffered(1)
    )
    in_specs = [
        whole(tokens, width),
        pl.BlockSpec((tokens, block), lambda i, which: (0, at(i, which))),
        pl.BlockSpec((block, tokens), lambda i, which: (at(i, which), 0)),
        pl.BlockSpec((block, width), lambda i, which: (at(i, which), 0)),
        pl.BlockSpec((width, block), lambda i, which: (0, at(i, which))),
        whole(tokens, width),
    ]
    out_specs = [
        pl.BlockSpec((2, block, width), lambda i, which: (0, i, 0)),
        whole(8, block),
    ]
    out_shape = hbm_shapes(((2, half, width), BF16), ((8, block), F32))
    scratch = [pltpu.VMEM((block, tokens), BF16), pltpu.VMEM((tokens, width), F32)]
    extra = ()
    if last:
        gain, *late = norm
        extra = (gain, *map(in_hbm, late))
        in_specs += [whole(1, width)] + [pl.BlockSpec(memory_space=pl.ANY)] * len(late)
        out_specs += [whole(tokens, width)] * 2 + [whole(8, width)]
        out_shape += hbm_shapes(
            ((tokens, width), BF16), ((tokens, width), BF16), ((8, width), F32)
        )
        scratch += [
            pltpu.VMEM((tokens, width), BF16),
            pltpu.VMEM((tokens, PAIR), F32),
            pltpu.VMEM((width, width), BF16),
            pltpu.SemaphoreType.DMA((4,)),
        ]
    else:
        out_specs.append(whole(tokens, width))
        out_shape += hbm_shapes(((tokens, width), BF16))
    return pl.pallas_call(
        functools.partial(feed_back_kernel, steps=steps, block=min(512, tokens), last=last),
        grid_spec=pltpu.PrefetchScalarGridSpec(
            num_scalar_prefetch=1,
            grid=(steps,),
            in_specs=in_specs,
            out_specs=out_specs,
            scratch_shapes=scratch,
        ),
        out_shape=out_shape,
        compiler_params=pltpu.CompilerParams(vmem_limit_bytes=44 * 2**20),
        cost_estimate=BRIEF,
        name="feed_back_last" if last else "feed_back",
    )(which, *map(in_hbm, (d_down, slope, active_t, shrink, expand, normed)), *extra)


def pack_kernel(at_ref, flat_ref, marks_ref, *refs, order):
    outs, sems = refs[:-1], refs[-1]
    piece = flat_ref.shape[1]
    for part, out_ref in zip(order, outs):
        marks = marks_ref[pl.ds(at_ref[0] ^ part, 1), :].astype(F32)
        out_ref[piece:, :] = jnp.zeros((MARK_ROWS, out_ref.shape[1]), BF16)
        out_ref[piece:, 0:piece] = jnp.broadcast_to(marks, (MARK_ROWS, piece)).astype(BF16)
    copies = [
        pltpu.make_async_copy(
            flat_ref.at[at_ref[0] ^ part], out_ref.at[pl.ds(0, piece)], sems.at[index]
        )
        for index, (part, out_ref) in enumerate(zip(order, outs))
    ]
    for copy in copies:
        copy.start()
    for copy in copies:
        copy.wait()


MARK_ROWS = 16


def pack(at, flat, marks, order):
    held, piece, width = flat.shape
    vmem = pl.BlockSpec(memory_space=pltpu.VMEM)
    return pl.pallas_call(
        functools.partial(pack_kernel, order=order),
        in_specs=[
            pl.BlockSpec(memory_space=pltpu.SMEM),
            pl.BlockSpec(memory_space=pl.ANY),
            vmem,
        ],
        out_specs=[vmem] * held,
        out_shape=shapes(*[((piece + MARK_ROWS, width), BF16)] * held),
        scratch_shapes=[pltpu.SemaphoreType.DMA((held,))],
        compiler_params=pltpu.CompilerParams(vmem_limit_bytes=16 * 2**20),
        cost_estimate=BRIEF,
        name="pack",
    )(at, in_hbm(flat), marks)


def unpack_kernel(*refs):
    parts, (rows_ref, marks_ref) = refs[:-2], refs[-2:]
    piece = rows_ref.shape[0] // len(parts)
    for index, ref in enumerate(parts):
        here = slice(index * piece, (index + 1) * piece)
        rows_ref[here, :] = ref[0:piece, :]
        marks = ref[piece:, 0:piece].astype(F32)[0:1, :]
        marks_ref[here, :] = jnp.broadcast_to(marks, (PAIR, piece)).T.astype(BF16)


def unpack(parts):
    width = parts[0].shape[1]
    tokens = len(parts) * (parts[0].shape[0] - MARK_ROWS)
    return pl.pallas_call(
        unpack_kernel,
        grid=(1,),
        in_specs=[fixed(*part.shape) for part in parts],
        out_specs=[fixed(tokens, width), fixed(tokens, PAIR)],
        out_shape=hbm_shapes(((tokens, width), BF16), ((tokens, PAIR), BF16)),
        compiler_params=pltpu.CompilerParams(vmem_limit_bytes=16 * 2**20),
        cost_estimate=BRIEF,
        name="unpack",
    )(*parts)


def weight_kernel(
    core_ref,
    first_sums_ref,
    second_sums_ref,
    own_bias_ref,
    other_bias_ref,
    *refs,
    steps,
):
    sources, (other_ref, own_ref, small_ref) = refs[:6], refs[6:9]
    targets, (inputs_t, mixed_t, sems) = refs[9:15], refs[15:]
    inputs_ref, dq_ref, dk_ref, dv_ref, mixed_ref, d_attn_ref = targets
    copies = [
        pltpu.make_async_copy(source, target, sems.at[index])
        for index, (source, target) in enumerate(zip(sources, targets))
    ]
    for copy in copies:
        copy.start()
    count = inputs_ref.shape[1] // 2
    core = core_ref[0]
    for ref in (other_ref, own_ref):
        if ref.shape[0] > 4 * count:
            ref[4 * count :, :] = jnp.zeros((ref.shape[0] - 4 * count, ref.shape[1]), BF16)
    copies[0].wait()
    inputs_t[...] = inputs_ref[...].T
    for at, right_ref in enumerate((dq_ref, dk_ref, dv_ref, d_attn_ref)):
        copies[at + 1].wait()
        left_ref = inputs_t
        if at == 3:
            copies[5].wait()
            mixed_t[...] = mixed_ref[...].T
            left_ref = mixed_t
        for half, out_ref in ((1 - core, other_ref), (core, own_ref)):
            rows = pl.ds(pl.multiple_of(half * count, PAIR), count)
            out_ref[at * count : (at + 1) * count, :] = dot(left_ref[rows, :], right_ref[...]).astype(
                BF16
            )
    small_ref[...] = jnp.zeros_like(small_ref)
    small_ref[0:1, :] = jnp.sum(dq_ref[...].astype(F32), 0, keepdims=True)
    small_ref[1:2, :] = jnp.sum(dv_ref[...].astype(F32), 0, keepdims=True)
    small_ref[2:5, :] = first_sums_ref[0:3, :]
    small_ref[5:8, :] = second_sums_ref[0:3, :]
    block = own_bias_ref.shape[1]
    own, other = own_bias_ref[0:steps, :], other_bias_ref[0:steps, :]
    small_ref[8 : 8 + steps, 0:block] = jnp.where(core == 0, own, other)
    small_ref[8 + steps : 8 + 2 * steps, 0:block] = jnp.where(core == 0, other, own)


def weight_halves(core, values, unit, sums, steps):
    tokens, width = values[0].shape
    rows = -(-2 * width // unit) * unit
    vmem = pl.BlockSpec(memory_space=pltpu.VMEM)
    anywhere = pl.BlockSpec(memory_space=pl.ANY)
    return pl.pallas_call(
        functools.partial(weight_kernel, steps=steps),
        in_specs=[pl.BlockSpec(memory_space=pltpu.SMEM)] + [vmem] * 4 + [anywhere] * 6,
        out_specs=[vmem] * 3,
        out_shape=shapes(
            ((rows, width), BF16), ((rows, width), BF16), ((SMALL, width), F32)
        ),
        scratch_shapes=[pltpu.VMEM((tokens, width), BF16)] * 6
        + [pltpu.VMEM((width, tokens), BF16)] * 2
        + [pltpu.SemaphoreType.DMA((6,))],
        compiler_params=pltpu.CompilerParams(vmem_limit_bytes=32 * 2**20),
        cost_estimate=BRIEF,
        name="weight_halves",
    )(core, *sums, *map(in_hbm, values))


def input_grad_kernel(*refs, held):
    sources, outs = refs[:7], refs[7 : 7 + held]
    (d_attn, *factors), sems = refs[7 + held : 14 + held], refs[-1]
    copies = [
        pltpu.make_async_copy(source, target, sems.at[index])
        for index, (source, target) in enumerate(zip(sources, (d_attn, *factors)))
    ]
    for copy in copies:
        copy.start()
    piece = outs[0].shape[0]
    total = None
    for index in range(3):
        for copy in copies[2 * index + 1 : 2 * index + 3]:
            copy.wait()
    copies[0].wait()
    for number, out_ref in enumerate(outs):
        here = slice(number * piece, (number + 1) * piece)
        total = d_attn[here, :].astype(F32)
        for index in range(3):
            total += dot(factors[2 * index][here, :], factors[2 * index + 1][...], NT)
        out_ref[...] = total.astype(BF16)


def input_grad(d_attn, factors, held):
    tokens, width = d_attn.shape
    anywhere = pl.BlockSpec(memory_space=pl.ANY)
    values = [d_attn] + [value for pair in factors for value in pair]
    return pl.pallas_call(
        functools.partial(input_grad_kernel, held=held),
        in_specs=[anywhere] * 7,
        out_specs=[pl.BlockSpec(memory_space=pltpu.VMEM)] * held,
        out_shape=shapes(*[((tokens // held, width), BF16)] * held),
        scratch_shapes=[pltpu.VMEM(value.shape, BF16) for value in values]
        + [pltpu.SemaphoreType.DMA((7,))],
        compiler_params=pltpu.CompilerParams(vmem_limit_bytes=24 * 2**20),
        cost_estimate=BRIEF,
        name="input_grad",
    )(*map(in_hbm, values))


def feed_out_kernel(which_ref, half_ref, *refs, steps):
    del which_ref
    shrink_ref, expand_ref = refs[-2:]

    @pl.when(pl.program_id(0) < steps)
    def _():
        shrink_ref[...] = half_ref[...].astype(F32)

    @pl.when(pl.program_id(0) >= steps)
    def _():
        expand_ref[...] = half_ref[...].T.astype(F32)


def feed_out(which, values, before=(), block=512):
    width = values.shape[1]
    half = values.shape[0] // 2
    steps = half // block
    return pl.pallas_call(
        functools.partial(feed_out_kernel, steps=steps),
        grid_spec=pltpu.PrefetchScalarGridSpec(
            num_scalar_prefetch=1,
            grid=(2 * steps,),
            in_specs=[pl.BlockSpec((block, width), lambda i, which: (i, 0))]
            + [pl.BlockSpec(memory_space=pl.ANY)] * len(before),
            out_specs=[
                pl.BlockSpec(
                    (block, width),
                    lambda i, which: (which[0] * steps + jnp.minimum(i, steps - 1), 0),
                ),
                pl.BlockSpec(
                    (width, block),
                    lambda i, which: (0, which[0] * steps + jnp.maximum(i - steps, 0)),
                ),
            ],
        ),
        out_shape=shapes(((2 * half, width), F32), ((width, 2 * half), F32)),
        input_output_aliases={2 + i: i for i in range(len(before))},
        compiler_params=pltpu.CompilerParams(vmem_limit_bytes=16 * 2**20),
        cost_estimate=BRIEF,
        name="feed_out",
    )(which, values, *before)


def attn_out_kernel(which_ref, half_ref, *refs):
    del which_ref
    for index, out_ref in enumerate(refs[-4:]):

        @pl.when(pl.program_id(0) == index)
        def _(out_ref=out_ref):
            out_ref[...] = half_ref[...].astype(F32)


def attn_out(which, values, before=()):
    width = values.shape[1]
    half = width // 2
    return pl.pallas_call(
        attn_out_kernel,
        grid_spec=pltpu.PrefetchScalarGridSpec(
            num_scalar_prefetch=1,
            grid=(4,),
            in_specs=[pl.BlockSpec((half, width), lambda i, which: (i, 0))]
            + [pl.BlockSpec(memory_space=pl.ANY)] * len(before),
            out_specs=[pl.BlockSpec((half, width), lambda i, which: (which[0], 0))] * 4,
        ),
        out_shape=shapes(*[((width, width), F32)] * 4),
        input_output_aliases={2 + i: i for i in range(len(before))},
        compiler_params=pltpu.CompilerParams(vmem_limit_bytes=24 * 2**20),
        cost_estimate=BRIEF,
        name="attn_out",
    )(which, values, *before)


def place_kernel(at_ref, *refs):
    del at_ref
    out_ref = refs[-1]
    for index, ref in enumerate(refs[:-1]):

        @pl.when(pl.program_id(0) == index)
        def _(ref=ref):
            out_ref[0] = ref[...]


def place(at, parts):
    piece, width = parts[0].shape
    held = len(parts)
    return pl.pallas_call(
        place_kernel,
        grid_spec=pltpu.PrefetchScalarGridSpec(
            num_scalar_prefetch=1,
            grid=(held,),
            in_specs=[pl.BlockSpec((piece, width), lambda i, at: (0, 0))] * held,
            out_specs=pl.BlockSpec((1, piece, width), lambda i, at: (at[0] ^ i, 0, 0)),
        ),
        out_shape=jax.ShapeDtypeStruct((held, piece, width), BF16),
        compiler_params=pltpu.CompilerParams(vmem_limit_bytes=16 * 2**20),
        cost_estimate=BRIEF,
        name="place",
    )(at, *parts)


def rows_of(ref, which, count, base=0):
    return ref[pl.ds(pl.multiple_of(base + which * count, 16), count), :]


def sum_of(terms):
    return functools.reduce(lambda a, b: a + b, [t.astype(F32) for t in terms]).astype(BF16)


def scatter_kernel(bits_ref, *refs, groups):
    outs = refs[-2 * groups :]
    ins = refs[: -2 * groups]
    together = len(ins) == 2
    base = 0
    for group in range(groups):
        terms = ins if together else ins[2 * group : 2 * group + 2]
        sent_ref, kept_ref = outs[2 * group : 2 * group + 2]
        count = kept_ref.shape[0]
        here = bits_ref[group]
        sent_ref[...] = sum_of([rows_of(term, 1 - here, count, base) for term in terms])
        kept_ref[...] = sum_of([rows_of(term, here, count, base) for term in terms])
        if together:
            base += 2 * count


def local_call(kernel, bits, values, out_shape, name):
    vmem = pl.BlockSpec(memory_space=pltpu.VMEM)
    return pl.pallas_call(
        kernel,
        in_specs=[pl.BlockSpec(memory_space=pltpu.SMEM)] + [vmem] * len(values),
        out_specs=[vmem] * len(out_shape),
        out_shape=out_shape,
        compiler_params=pltpu.CompilerParams(vmem_limit_bytes=24 * 2**20),
        cost_estimate=BRIEF,
        name=name,
    )(bits, *values)


def scatter_local(bits, pairs, counts=None):
    if counts is None:
        counts = [kept.shape[0] for kept, _ in pairs]
    groups = len(counts)
    counts = [count // 2 for count in counts]
    width = pairs[0][0].shape[1]
    outs = local_call(
        functools.partial(scatter_kernel, groups=groups),
        bits,
        [value for pair in pairs for value in pair],
        shapes(*[((count, width), BF16) for count in counts for _ in range(2)]),
        "scatter_local",
    )
    return [outs[2 * i : 2 * i + 2] for i in range(groups)]


def scatter_first_kernel(bits_ref, own_at, got_at, *refs, counts):
    outs, (own, got, sems) = refs[:-3], refs[-3:]
    spans = []
    base = 0
    for group, count in enumerate(counts):
        for kept in range(2):
            half = bits_ref[group] if kept else 1 - bits_ref[group]
            start = pl.multiple_of(base + half * (count // 2), 16)
            spans.append((start, count // 2, outs[2 * group + kept]))
        base += count
    spans = spans[0::2] + spans[1::2]
    copies = []
    for index, (start, count, _) in enumerate(spans):
        rows = pl.ds(start, count)
        for which, (source, target) in enumerate(((own_at, own), (got_at, got))):
            copies.append(
                pltpu.make_async_copy(source.at[rows], target.at[rows], sems.at[2 * index + which])
            )
            copies[-1].start()
    for index, (start, count, out_ref) in enumerate(spans):
        for copy in copies[2 * index : 2 * index + 2]:
            copy.wait()
        rows = pl.ds(start, count)
        out_ref[...] = sum_of([own[rows, :], got[rows, :]])


def scatter_first(bits, own, got, counts):
    rows, width = own.shape
    anywhere = pl.BlockSpec(memory_space=pl.ANY)
    vmem = pl.BlockSpec(memory_space=pltpu.VMEM)
    outs = pl.pallas_call(
        functools.partial(scatter_first_kernel, counts=counts),
        in_specs=[pl.BlockSpec(memory_space=pltpu.SMEM), anywhere, anywhere],
        out_specs=[vmem] * (2 * len(counts)),
        out_shape=shapes(*[((count // 2, width), BF16) for count in counts for _ in range(2)]),
        scratch_shapes=[pltpu.VMEM((rows, width), BF16)] * 2
        + [pltpu.SemaphoreType.DMA((4 * len(counts),))],
        compiler_params=pltpu.CompilerParams(vmem_limit_bytes=24 * 2**20),
        cost_estimate=BRIEF,
        name="scatter_first",
    )(bits, in_hbm(own), in_hbm(got))
    return [outs[2 * group : 2 * group + 2] for group in range(len(counts))]


SMALL = 16


def put_small(ref, at, values):
    ref[at : at + SMALL, :] = values.astype(BF16)


def get_small(ref, at):
    return ref[at : at + SMALL, :].astype(F32)


def settle_kernel(bits_ref, *refs, groups, small):
    del bits_ref
    ins, outs = refs[: 2 * groups], refs[2 * groups + small :]
    for group in range(groups):
        count = ins[2 * group].shape[0]
        outs[group][0:count, :] = sum_of([ins[2 * group][...], ins[2 * group + 1][...]])
        if small and group == 0:
            put_small(outs[group], count, refs[2 * groups][...])


def settle_local(bits, pairs, small):
    width = pairs[0][0].shape[1]
    counts = [kept.shape[0] for kept, _ in pairs]
    if small is not None:
        counts[0] += SMALL
    return local_call(
        functools.partial(settle_kernel, groups=len(pairs), small=int(small is not None)),
        bits,
        [value for pair in pairs for value in pair] + ([] if small is None else [small]),
        shapes(*[((count, width), BF16) for count in counts]),
        "settle_local",
    )


def add_kernel(bits_ref, *refs, groups, small):
    del bits_ref
    ins, outs = refs[: 2 * groups], refs[2 * groups :]
    for group in range(groups):
        own_ref, got_ref = ins[2 * group : 2 * group + 2]
        extra = SMALL if small and group == 0 else 0
        count = own_ref.shape[0] - extra
        outs[group][0:count, :] = sum_of([own_ref[0:count, :], got_ref[0:count, :]])
        if extra:
            put_small(outs[group], count, get_small(own_ref, count) + get_small(got_ref, count))


def add_local(bits, pairs, small):
    return local_call(
        functools.partial(add_kernel, groups=len(pairs), small=small),
        bits,
        [value for pair in pairs for value in pair],
        shapes(*[(own.shape, BF16) for own, _ in pairs]),
        "add_local",
    )


def join_kernel(bits_ref, *refs, groups, small, merged, pieces):
    ins, outs = refs[: 2 * pieces * groups], list(refs[2 * pieces * groups :])
    parts = len(outs) // groups
    base = 0
    for group in range(groups):
        owns = ins[2 * pieces * group : 2 * pieces * group + 2 * pieces : 2]
        gots = ins[2 * pieces * group + 1 : 2 * pieces * group + 2 * pieces : 2]
        extra = SMALL if small and group == 0 else 0
        count = owns[0].shape[0] - extra
        here = bits_ref[group]
        if parts > 1:
            for half, out_ref in enumerate(outs[2 * group : 2 * group + 2]):

                @pl.when(here == half)
                def _(out_ref=out_ref):
                    out_ref[...] = owns[0][...]

                @pl.when(here != half)
                def _(out_ref=out_ref):
                    out_ref[...] = gots[0][...]

            continue
        out_ref = outs[0 if merged else group]
        whole = count * pieces
        for half, refs_of in ((here, owns), (1 - here, gots)):
            for index, ref in enumerate(refs_of):
                start = pl.multiple_of(base + half * whole + index * count, 16)
                out_ref[pl.ds(start, count), :] = ref[0:count, :]
        if extra:
            at = out_ref.shape[0] - SMALL if merged else base + 2 * whole
            put_small(out_ref, at, get_small(owns[0], count) + get_small(gots[0], count))
        if merged:
            base += 2 * whole


def join_local(bits, arrived, small, merged, parts=1):
    width = arrived[0][0].shape[1]
    pieces = len(arrived[0]) // 2
    counts = [2 * pieces * group[0].shape[0] for group in arrived]
    if small:
        counts[0] -= SMALL
    if merged:
        counts = [sum(counts)]
    counts = [count // parts for count in counts for _ in range(parts)]
    return local_call(
        functools.partial(
            join_kernel, groups=len(arrived), small=small, merged=merged, pieces=pieces
        ),
        bits,
        [value for group in arrived for value in group],
        shapes(*[((count, width), BF16) for count in counts]),
        "join_local",
    )


def tie(*values):
    return lax.optimization_barrier(values)


def pick(which, parts):
    if len(parts) == 1:
        return parts[0]
    half = len(parts) // 2
    return jnp.where(which < half, pick(which, parts[:half]), pick(which - half, parts[half:]))


def column_sum(values):
    return jnp.sum(values.astype(F32), 0)


class Stage:
    def __init__(self, sizes, bits):
        self.bits = bits
        rows, seq = sizes
        self.pairs = []
        for index in range(rows * seq):
            axis, bit = bits[index & 1]
            self.pairs.append((index, index ^ ((1 << bit) * (seq if axis == "rows" else 1))))

    def here(self):
        first, second = [(lax.axis_index(axis) >> bit) & 1 for axis, bit in self.bits]
        if self.bits[0] == self.bits[1]:
            return first
        return jnp.where(lax.axis_index("seq") & 1 == 0, first, second)

    def swap(self, values):
        return lax.ppermute(values, ("rows", "seq"), self.pairs)


def total_over_chips(own, got, core_stage, orders, small=None, near=False):
    depth = len(orders[0][1])
    groups = range(len(orders))

    def bits_at(step):
        return jnp.stack([stages[step].here() for _, stages in orders]).astype(jnp.int32)

    def pairs_of(flat):
        return [flat[i : i + 2] for i in range(0, len(flat), 2)]

    def send(step, values, keep):
        flat = []
        for group in groups:
            flat += [keep[group], orders[group][1][step].swap(values[group])]
        return flat

    counts = [count for count, _ in orders]
    if near:
        parts = scatter_local(bits_at(0), [[own, got]], counts)
    else:
        parts = scatter_first(bits_at(0), own, got, counts)
    last = depth - 1 if near else depth
    for step in range(1, last + 1):
        flat = yield send(step - 1, [p[0] for p in parts], [p[1] for p in parts])
        if step < last:
            parts = scatter_local(bits_at(step), pairs_of(flat))
    values = settle_local(bits_at(0), pairs_of(flat), small)
    if near:
        flat = yield send(last, values, values)
        values = add_local(bits_at(0), pairs_of(flat), small is not None)
    carried = small is not None
    for step in reversed(range(last)):
        flat = yield send(step, values, values)
        parts = 2 if step == 1 and not carried else 1
        values = join_local(bits_at(step), pairs_of(flat), carried, step == 0, parts)
        if parts > 1:
            lower = yield send(0, values[0::2], values[0::2])
            upper = yield send(0, values[1::2], values[1::2])
            arrived = [list(low) + list(high) for low, high in zip(pairs_of(lower), pairs_of(upper))]
            values = join_local(bits_at(0), arrived, carried, True)
            break
    both = yield [values[0], core_stage.swap(values[0])]
    return both


def arriving(values):
    values = yield values
    return values[1::2]


class Flow:
    def __init__(self, steps, left):
        self.steps = steps
        self.left = left
        self.pending = next(steps)
        self.result = None


class Timetable:
    def __init__(self):
        self.flows = []

    def open(self, steps, left=1):
        self.flows.append(Flow(steps, left))
        return self.flows[-1]

    def advance(self, moving, *values):
        flows = [flow for flow in self.flows if flow.result is None]
        held = [flow.pending if flow in moving else flow.pending[0::2] for flow in flows]
        tied = list(tie(*values, *[value for part in held for value in part]))
        values, tied = tied[: len(values)], tied[len(values) :]
        for flow, part in zip(flows, held):
            back, tied = tied[: len(part)], tied[len(part) :]
            if flow not in moving:
                flow.pending[0::2] = back
                continue
            flow.left -= 1
            try:
                flow.pending = flow.steps.send(back)
            except StopIteration as end:
                flow.result = end.value
        return self.settle(*values) if moving and values else values

    def settle(self, *values):
        return self.advance([], *values)


def solution(mesh):
    seq_size = mesh.shape["seq"]
    rows_size = mesh.shape["rows"]
    seq_bits = seq_size.bit_length() - 1
    rows_bits = rows_size.bit_length() - 1
    off_chip = [("seq", bit) for bit in range(1, seq_bits)]
    off_chip += [("rows", bit) for bit in range(rows_bits)]
    first, *middle, ahead, final = off_chip
    sizes = (rows_size, seq_size)
    core_stage = Stage(sizes, [("seq", 0)] * 2)
    straight = [first] + middle + [ahead, final]
    turned = middle + [ahead, first, final]
    spun = [ahead, first] + middle + [final]
    wide = [Stage(sizes, bits) for bits in zip(straight, turned)]
    slim = [Stage(sizes, bits) for bits in zip(spun, spun)]

    def body(
        hidden_in,
        segments,
        grad_mask,
        grad_out,
        query_proj,
        query_bias,
        key_proj,
        value_proj,
        value_bias,
        output_proj,
        output_bias,
        first_gain,
        first_shift,
        expand_proj,
        expand_bias,
        shrink_proj,
        shrink_bias,
        second_gain,
        second_shift,
    ):
        micro, rows_here, piece, width = hidden_in.shape
        held = micro * rows_here
        sharers = seq_size // held
        tokens = held * piece
        source_at = lax.axis_index("seq") % held
        core = core_stage.here()
        core_at = core.reshape(1).astype(jnp.int32)

        def trade(to_rows, part):
            there = [(s, (s % held ^ part) * sharers + s // held) for s in range(seq_size)]
            return there if to_rows else [(b, a) for a, b in there]

        def to_rows(values):
            return [
                lax.ppermute(
                    lax.dynamic_index_in_dim(values, source_at ^ part, 0, False),
                    "seq",
                    trade(True, part),
                )
                for part in range(held)
            ]

        def send_pieces(values):
            return [
                value
                for part in range(held)
                for value in (values[part], lax.ppermute(values[part], "seq", trade(False, part)))
            ]

        def place_pieces(parts):
            at = source_at.reshape(1).astype(jnp.int32)
            return place(at, parts).reshape((micro, rows_here) + parts[0].shape)

        same_row = [[r * sharers + g for g in range(sharers)] for r in range(held)]

        def all_keys(values):
            if sharers == 1:
                return values
            return lax.all_gather(values, "seq", axis=0, tiled=True, axis_index_groups=same_row)

        def own_keys(values):
            if sharers == 1:
                return values
            return lax.psum_scatter(
                values, "seq", scatter_dimension=0, tiled=True, axis_index_groups=same_row
            ).astype(BF16)

        order = tuple(reversed(range(held)))
        packed = pack(
            source_at.reshape(1).astype(jnp.int32),
            hidden_in.reshape(held, piece, width),
            segments.reshape(held, piece),
            order,
        )
        arrived = [
            lax.ppermute(value, "seq", trade(True, part)) for part, value in zip(order, packed)
        ]
        inputs, seg_q = unpack(arrived[::-1])
        masked = (grad_out * grad_mask[..., None].astype(BF16)).reshape(held, piece, width)
        masked, inputs, seg_q = tie(masked, inputs, seg_q)
        upstream = to_rows(masked)

        queries = (
            (dot(inputs, query_proj) + query_bias.astype(F32)) * 0.125
        ).astype(BF16)
        keys = all_keys(dot(inputs, key_proj).astype(BF16))
        values = all_keys((dot(inputs, value_proj) + value_bias.astype(F32)).astype(BF16))
        seg_k = all_keys(seg_q)
        mixed, query_side = attention_forward(queries, keys, values, seg_q, seg_k)
        row = lambda vector: vector.reshape(1, -1)
        hat, scale, normed, active_t, slope, d_down, second_sums, *result = feed_forward(
            inputs,
            mixed,
            upstream,
            (
                output_proj,
                row(output_bias),
                row(first_gain),
                row(first_shift),
                expand_proj,
                row(expand_bias),
                shrink_proj,
                row(shrink_bias),
                row(second_gain),
                row(second_shift),
            ),
        )
        table = Timetable()
        advance = table.advance
        layer_flow = table.open(arriving(send_pieces(result)))

        def chips(own, got, orders, small=None):
            near = small is not None
            steps = total_over_chips(own, got, core_stage, orders, small, near)
            return table.open(steps, 2 * len(wide) + (0 if near else 2))

        back = functools.partial(
            feed_back,
            slope=slope,
            active_t=active_t,
            shrink=shrink_proj,
            expand=expand_proj,
            normed=normed,
        )
        other, other_bias, d_normed = back(1 - core_at, d_down, norm=None)
        half = other.shape[1]
        got = core_stage.swap(other.reshape(2 * half, width))
        own, own_bias, d_attn, d_mixed, first_sums = back(
            core_at, d_down, norm=(row(first_gain), d_normed, hat, scale, output_proj)
        )
        own, got, d_mixed = advance([layer_flow], own.reshape(2 * half, width), got, d_mixed)
        unit = 16 << len(off_chip)

        def thirds(count):
            less = count // unit // 3 * unit
            return [(count - less, wide)] + ([(less, slim)] if less else [])

        feed_flow = chips(own, got, thirds(2 * half))

        pairs = width // PAIR
        kept = BF16 if sharers == 1 else F32
        grads = None
        for first, last in ((0, pairs),):
            grads = attention_backward(
                query_side, keys, values, seg_k, mixed, d_mixed, kept, first, last - first, grads
            )
            *grads, d_mixed = advance([feed_flow], *grads, d_mixed)

        d_query, d_keys, d_values = grads
        d_key = own_keys(d_keys)
        d_value = own_keys(d_values)
        steps = half // other_bias.shape[1]
        other, own, small = weight_halves(
            core_at,
            (inputs, d_query, d_key, d_value, mixed, d_attn),
            unit,
            (first_sums, second_sums, own_bias, other_bias),
            steps,
        )
        other, own, small, d_query, d_key, d_value = advance(
            [feed_flow], other, own, small, d_query, d_key, d_value
        )
        got = core_stage.swap(other)
        d_input = input_grad(
            d_attn, ((d_query, query_proj), (d_key, key_proj), (d_value, value_proj)), held
        )
        own, got, small, *d_input = advance([feed_flow], own, got, small, *d_input)
        attn_flow = chips(own, got, [(own.shape[0], wide)], small)
        piece_flow = table.open(arriving(send_pieces(d_input)))

        both = [feed_flow, attn_flow]
        layer_out = place_pieces(list(map(in_hbm, layer_flow.result)))
        (layer_out,) = advance(both, layer_out)
        advance(both + [piece_flow])
        grad_in = place_pieces(piece_flow.result)
        (grad_in,) = advance(both, grad_in)
        while feed_flow.left > 1:
            advance(both)
        feed_grads = feed_out(core_at, feed_flow.pending[0])
        feed_grads = advance(both, *feed_grads)
        feed_grads = feed_out(1 - core_at, feed_flow.result[1], feed_grads)
        while attn_flow.left > 1:
            feed_grads = advance([attn_flow], *feed_grads)
        attn_grads = attn_out(core_at, attn_flow.pending[0])
        attn_grads = advance([attn_flow], *attn_grads)
        own, got = attn_flow.result
        attn_grads = attn_out(1 - core_at, got, attn_grads)
        totals = own[-SMALL:].astype(F32) + got[-SMALL:].astype(F32)
        shrink_grad, expand_grad = feed_grads
        expand_bias_grad = totals[8 : 8 + 2 * steps, : other_bias.shape[1]].reshape(-1)
        return (
            layer_out,
            grad_in,
            attn_grads[0],
            totals[0],
            attn_grads[1],
            attn_grads[2],
            totals[1],
            attn_grads[3],
            totals[4],
            totals[2],
            totals[3],
            expand_grad,
            expand_bias_grad,
            shrink_grad,
            totals[7],
            totals[5],
            totals[6],
        )

    split = P(None, "rows", "seq", None)
    whole = P()
    return jax.shard_map(
        body,
        mesh=mesh,
        in_specs=(split, P(None, "rows", "seq"), P(None, "rows", "seq"), split) + (whole,) * 15,
        out_specs=(split, split) + (whole,) * 15,
        check_vma=False,
    )
```

```python
import functools

import jax
import jax.numpy as jnp
from jax import lax
from jax.experimental import pallas as pl
from jax.experimental.pallas import tpu as pltpu
from jax.sharding import PartitionSpec as P

DH = 64
PAIR = 128
MASKED = 1e30
F32 = jnp.float32
BF16 = jnp.bfloat16
NT = (((1,), (1,)), ((), ()))
NN = (((1,), (0,)), ((), ()))
BRIEF = pl.CostEstimate(flops=1, bytes_accessed=1, transcendentals=0)


def left_dot(first, second):
    return lax.dot_general(first, second, (((0,), (0,)), ((), ())), preferred_element_type=F32)


def right_dot(first, second):
    return lax.dot_general(first, second, NT, preferred_element_type=F32)


def split_three(values):
    high = values.astype(BF16)
    rest = values - high.astype(F32)
    middle = rest.astype(BF16)
    low = (rest - middle.astype(F32)).astype(BF16)
    return high.astype(F32), middle.astype(F32), low.astype(F32)


def own_lanes(shape, head):
    lane = lax.broadcasted_iota(jnp.int32, shape, 1)
    own = lane < DH if head == 0 else lane >= DH
    return own, lane % DH


def key_features(lane, seg):
    return jnp.where(
        lane < 3,
        1.0,
        jnp.where(lane == 3, -MASKED * (1.0 - seg), jnp.where(lane == 4, -MASKED * seg, 0.0)),
    ).astype(BF16)


def forward_kernel(q_ref, k_ref, v_ref, seg_q_ref, seg_k_ref, mixed_ref, query_ref, *, block):
    queries = q_ref.shape[0]
    keys = k_ref.shape[0]
    for head in range(2):
        own_k, lane_k = own_lanes((keys, PAIR), head)
        key_side = jnp.where(own_k, k_ref[...], key_features(lane_k, seg_k_ref[...].astype(F32)))
        value_side = jnp.where(own_k, v_ref[...], jnp.ones((), BF16))
        own_q, lane_q = own_lanes((block, PAIR), head)
        for start in range(0, queries, block):
            here = slice(start, start + block)
            q = q_ref[here, :]
            seg = seg_q_ref[here, :].astype(F32)
            seg_side = jnp.where(lane_q == 3, seg, jnp.where(lane_q == 4, 1.0 - seg, 0.0))
            query_side = jnp.where(own_q, q, seg_side.astype(BF16))
            scores = lax.dot_general(query_side, key_side, NT, preferred_element_type=F32)
            peak = jnp.max(scores, -1, keepdims=True)
            raised = jnp.exp(scores - peak).astype(BF16)
            summed = lax.dot_general(raised, value_side, NN, preferred_element_type=F32)
            total = summed[:, DH : DH + 1] if head == 0 else summed[:, 0:1]
            mixed = (summed / total).astype(BF16)
            shift = jnp.broadcast_to(-(peak + jnp.log(total)), (block, PAIR))
            high, middle, low = split_three(shift)
            extra = jnp.where(
                lane_q == 0,
                high,
                jnp.where(lane_q == 1, middle, jnp.where(lane_q == 2, low, seg_side)),
            )
            query_ref[head, here, :] = jnp.where(own_q, q, extra.astype(BF16))
            if head == 0:
                mixed_ref[here, :] = mixed
            else:
                mixed_ref[here, :] = jnp.where(own_q, mixed, mixed_ref[here, :])


def attention_forward(q, k, v, seg_q, seg_k):
    queries, width = q.shape
    keys = k.shape[0]
    pairs = width // PAIR
    column = lambda i: (0, i)
    whole = lambda i: (0, 0)
    return pl.pallas_call(
        functools.partial(forward_kernel, block=min(512, queries)),
        grid=(pairs,),
        in_specs=[
            pl.BlockSpec((queries, PAIR), column),
            pl.BlockSpec((keys, PAIR), column),
            pl.BlockSpec((keys, PAIR), column),
            pl.BlockSpec((queries, PAIR), whole),
            pl.BlockSpec((keys, PAIR), whole),
        ],
        out_specs=[
            pl.BlockSpec((queries, PAIR), column),
            pl.BlockSpec((2, queries, PAIR), lambda i: (i, 0, 0)),
        ],
        out_shape=[
            pltpu.HBM((queries, width), BF16),
            pltpu.HBM((2 * pairs, queries, PAIR), BF16),
        ],
        compiler_params=pltpu.CompilerParams(vmem_limit_bytes=24 * 2**20),
        cost_estimate=BRIEF,
        name="attention_forward",
    )(q, k, v, seg_q, seg_k)


def backward_kernel(
    query_ref, k_ref, v_ref, seg_k_ref, mixed_ref, d_mixed_ref, *refs, block
):
    dq_ref, dk_ref, dv_ref, dqt = refs[-4:]
    queries = mixed_ref.shape[0]
    keys = k_ref.shape[0]
    d_mixed = d_mixed_ref[...]
    product = d_mixed.astype(F32) * mixed_ref[...].astype(F32)
    for head in range(2):
        own_q, lane_q = own_lanes((queries, PAIR), head)
        own_k, lane_k = own_lanes((block, PAIR), head)
        delta = -jnp.sum(jnp.where(own_q, product, 0.0), -1, keepdims=True)
        high, middle, low = split_three(jnp.broadcast_to(delta, (queries, PAIR)))
        extra = jnp.where(
            lane_q == 0, high, jnp.where(lane_q == 1, middle, jnp.where(lane_q == 2, low, 0.0))
        )
        d_side = jnp.where(own_q, d_mixed, extra.astype(BF16))
        query_side = query_ref[head]
        ones = jnp.where(lane_k < 3, 1.0, 0.0).astype(BF16)
        for start in range(0, keys, block):
            here = slice(start, start + block)
            k = k_ref[here, :]
            seg = seg_k_ref[here, :].astype(F32)
            key_side = jnp.where(own_k, k, key_features(lane_k, seg))
            value_side = jnp.where(own_k, v_ref[here, :], ones)
            shifted = lax.dot_general(key_side, query_side, NT, preferred_element_type=F32)
            probs = jnp.exp(shifted)
            d_probs = lax.dot_general(value_side, d_side, NT, preferred_element_type=F32)
            d_scores = (probs * d_probs).astype(BF16)
            dv = lax.dot_general(probs.astype(BF16), d_mixed, NN, preferred_element_type=F32)
            dk = lax.dot_general(d_scores, query_side, NN, preferred_element_type=F32)
            turned = k.T[head * DH : (head + 1) * DH, :]
            dq = lax.dot_general(turned, d_scores, NN, preferred_element_type=F32)
            mine = slice(head * DH, (head + 1) * DH)
            if start == 0:
                dqt[mine, :] = dq
            else:
                dqt[mine, :] += dq
            dv = dv.astype(dv_ref.dtype)
            dk = dk.astype(dk_ref.dtype)
            if head == 0:
                dk_ref[here, :] = dk
                dv_ref[here, :] = dv
            else:
                dk_ref[here, :] = jnp.where(own_k, dk, dk_ref[here, :])
                dv_ref[here, :] = jnp.where(own_k, dv, dv_ref[here, :])
    dq_ref[...] = (dqt[...] * 0.125).astype(BF16).T


def attention_backward(query_side, k, v, seg_k, mixed, d_mixed, kept, first, count, before):
    queries, width = mixed.shape
    keys = k.shape[0]
    column = lambda i: (0, i + first)
    held = [] if before is None else list(before)
    return pl.pallas_call(
        functools.partial(backward_kernel, block=min(512, keys)),
        grid=(count,),
        in_specs=[
            pl.BlockSpec((2, queries, PAIR), lambda i: (i + first, 0, 0)),
            pl.BlockSpec((keys, PAIR), column),
            pl.BlockSpec((keys, PAIR), column),
            pl.BlockSpec((keys, PAIR), lambda i: (0, 0)),
            pl.BlockSpec((queries, PAIR), column),
            pl.BlockSpec((queries, PAIR), column),
        ]
        + [pl.BlockSpec(memory_space=pl.ANY)] * len(held),
        out_specs=[
            pl.BlockSpec((queries, PAIR), column),
            pl.BlockSpec((keys, PAIR), column),
            pl.BlockSpec((keys, PAIR), column),
        ],
        input_output_aliases={6 + i: i for i in range(len(held))},
        out_shape=[
            pltpu.HBM((queries, width), BF16),
            pltpu.HBM((keys, width), kept),
            pltpu.HBM((keys, width), kept),
        ],
        scratch_shapes=[pltpu.VMEM((PAIR, queries), F32)],
        compiler_params=pltpu.CompilerParams(vmem_limit_bytes=24 * 2**20),
        cost_estimate=BRIEF,
        name="attention_backward",
    )(in_hbm(query_side), k, v, seg_k, in_hbm(mixed), in_hbm(d_mixed), *map(in_hbm, held))


def dot(first, second, dims=NN):
    return lax.dot_general(first, second, dims, preferred_element_type=F32)


def gelu_pair(values):
    below = 0.5 + 0.5 * lax.erf(values * 0.7071067811865476)
    density = jnp.exp(-0.5 * values * values) * 0.3989422804014327
    return values * below, below + values * density


def normalise(values):
    centred = values - jnp.mean(values, -1, keepdims=True)
    scale = lax.rsqrt(jnp.mean(centred * centred, -1, keepdims=True) + 1e-06)
    return centred * scale, scale


def norm_back(upstream, hat, scale, gain):
    d_hat = upstream * gain
    return scale * (
        d_hat
        - jnp.mean(d_hat, -1, keepdims=True)
        - hat * jnp.mean(d_hat * hat, -1, keepdims=True)
    )


def stack_rows(rows):
    filler = jnp.zeros((8 - len(rows), rows[0].shape[1]), F32)
    return jnp.concatenate(rows + [filler], 0)


def feed_forward_kernel(
    inputs_ref,
    mixed_ref,
    output_proj_ref,
    output_bias_ref,
    gain_one_ref,
    shift_one_ref,
    expand_ref,
    expand_bias_ref,
    shrink_ref,
    shrink_bias_ref,
    gain_two_ref,
    shift_two_ref,
    *refs,
    steps,
    held,
):
    upstream_refs = refs[:held]
    hat_out, scale_ref, normed_out, active_t_ref, slope_ref = refs[held : held + 5]
    d_down_ref, sums_ref = refs[held + 5 : held + 7]
    out_refs = refs[held + 7 : 2 * held + 7]
    total, hat_ref, normed_ref, sems = refs[2 * held + 7 :]
    block = total.shape[0] // held
    early = [
        pltpu.make_async_copy(hat_ref, hat_out, sems.at[0]),
        pltpu.make_async_copy(normed_ref, normed_out, sems.at[1]),
    ]
    step = pl.program_id(0)
    tokens = total.shape[0]
    pieces = [slice(start, start + block) for start in range(0, tokens, block)]

    @pl.when(step == 0)
    def _():
        for here in pieces:
            first_sum = (
                inputs_ref[here, :].astype(F32)
                + dot(mixed_ref[here, :], output_proj_ref[...])
                + output_bias_ref[...].astype(F32)
            )
            hat, scale = normalise(first_sum)
            hat_ref[here, :] = hat.astype(BF16)
            scale_ref[here, :] = jnp.broadcast_to(scale, (block, PAIR))
            normed = gain_one_ref[...].astype(F32) * hat + shift_one_ref[...].astype(F32)
            normed_ref[here, :] = normed.astype(BF16)
            total[here, :] = normed + shrink_bias_ref[...].astype(F32)
        for copy in early:
            copy.start()

    for here in pieces:
        expanded = dot(normed_ref[here, :], expand_ref[...]) + expand_bias_ref[...].astype(F32)
        active, slope = gelu_pair(expanded)
        active = active.astype(BF16)
        slope_ref[here, :] = slope.astype(BF16)
        active_t_ref[:, here] = active.T
        total[here, :] += dot(active, shrink_ref[...])

    @pl.when(step == steps - 1)
    def _():
        gain = gain_two_ref[...].astype(F32)
        d_gain = jnp.zeros((1, total.shape[1]), F32)
        d_shift = d_gain
        d_bias = d_gain
        for here, upstream_ref, out_ref in zip(pieces, upstream_refs, out_refs):
            hat, scale = normalise(total[here, :])
            out_ref[...] = (gain * hat + shift_two_ref[...].astype(F32)).astype(BF16)
            upstream = upstream_ref[...].astype(F32)
            d_gain += jnp.sum(upstream * hat, 0, keepdims=True)
            d_shift += jnp.sum(upstream, 0, keepdims=True)
            d_down = norm_back(upstream, hat, scale, gain).astype(BF16)
            d_down_ref[here, :] = d_down
            d_bias += jnp.sum(d_down.astype(F32), 0, keepdims=True)
        sums_ref[...] = stack_rows([d_gain, d_shift, d_bias])
        for copy in early:
            copy.wait()


def in_hbm(values):
    return pltpu.with_memory_space_constraint(values, pltpu.HBM)


def hbm_shapes(*pairs):
    return [pltpu.HBM(shape, dtype) for shape, dtype in pairs]


def fixed(*shape):
    return pl.BlockSpec(shape, lambda i: (0,) * len(shape), pipeline_mode=pl.Buffered(1))


def shapes(*pairs):
    return [jax.ShapeDtypeStruct(shape, dtype) for shape, dtype in pairs]


def feed_forward(inputs, mixed, upstream, weights, block=768):
    tokens, width = inputs.shape
    units = weights[4].shape[1]
    steps = units // block
    held = len(upstream)
    piece = tokens // held
    row = fixed(1, width)
    return pl.pallas_call(
        functools.partial(feed_forward_kernel, steps=steps, held=held),
        grid=(steps,),
        in_specs=[fixed(tokens, width)] * 2
        + [fixed(width, width), row, row, row]
        + [
            pl.BlockSpec((width, block), lambda i: (0, i)),
            pl.BlockSpec((1, block), lambda i: (0, i)),
            pl.BlockSpec((block, width), lambda i: (i, 0)),
            row,
            row,
            row,
        ]
        + [fixed(piece, width)] * held,
        out_specs=[
            pl.BlockSpec(memory_space=pl.ANY),
            fixed(tokens, PAIR),
            pl.BlockSpec(memory_space=pl.ANY),
            pl.BlockSpec((block, tokens), lambda i: (i, 0)),
            pl.BlockSpec((tokens, block), lambda i: (0, i)),
            fixed(tokens, width),
            fixed(8, width),
        ]
        + [fixed(piece, width)] * held,
        out_shape=hbm_shapes(
            ((tokens, width), BF16),
            ((tokens, PAIR), F32),
            ((tokens, width), BF16),
            ((units, tokens), BF16),
            ((tokens, units), BF16),
            ((tokens, width), BF16),
            ((8, width), F32),
        )
        + shapes(*[((piece, width), BF16)] * held),
        scratch_shapes=[
            pltpu.VMEM((tokens, width), F32),
            pltpu.VMEM((tokens, width), BF16),
            pltpu.VMEM((tokens, width), BF16),
            pltpu.SemaphoreType.DMA((2,)),
        ],
        compiler_params=pltpu.CompilerParams(vmem_limit_bytes=36 * 2**20),
        cost_estimate=BRIEF,
        name="feed_forward",
    )(inputs, in_hbm(mixed), *map(in_hbm, weights), *upstream)


def feed_back_kernel(
    which_ref,
    d_down_ref,
    slope_ref,
    active_t_ref,
    shrink_ref,
    expand_ref,
    normed_ref,
    *refs,
    steps,
    block,
    last,
):
    step = pl.program_id(0)
    if last:
        gain_ref, *late_refs = refs[:5]
        grads_ref, bias_ref, d_attn_ref, d_mixed_ref, sums_ref = refs[5:10]
        turned, total, hat_ref, scale_ref, output_proj_ref, sems = refs[10:]
        late = [
            pltpu.make_async_copy(source, target, sems.at[index])
            for index, (source, target) in enumerate(
                zip(late_refs, (d_attn_ref, hat_ref, scale_ref, output_proj_ref))
            )
        ]

        @pl.when(step == 0)
        def _():
            for copy in late:
                copy.start()

    else:
        grads_ref, bias_ref, total_ref, turned, total = refs
    tokens = total.shape[0]
    pieces = [slice(start, start + block) for start in range(0, tokens, block)]

    @pl.when(step == 0)
    def _():
        total[...] = jnp.zeros_like(total)
        bias_ref[...] = jnp.zeros_like(bias_ref)

    bias = jnp.zeros((1, slope_ref.shape[1]), F32)
    for here in pieces:
        d_active = dot(d_down_ref[here, :], shrink_ref[...], NT)
        d_expand = (d_active * slope_ref[here, :].astype(F32)).astype(BF16)
        turned[:, here] = d_expand.T
        bias += jnp.sum(d_expand.astype(F32), 0, keepdims=True)
        total[here, :] += dot(d_expand, expand_ref[...], NT)
    row = lax.broadcasted_iota(jnp.int32, bias_ref.shape, 0)
    bias_ref[...] = jnp.where(row == step, bias, bias_ref[...])
    grads_ref[0] = dot(active_t_ref[...], d_down_ref[...]).astype(BF16)
    grads_ref[1] = dot(turned[...], normed_ref[...]).astype(BF16)

    if not last:

        @pl.when(step == steps - 1)
        def _():
            total_ref[...] = total[...].astype(BF16)

    else:

        @pl.when(step == steps - 1)
        def _():
            for copy in late:
                copy.wait()
            gain = gain_ref[...].astype(F32)
            d_gain = jnp.zeros((1, total.shape[1]), F32)
            d_shift = d_gain
            d_bias = d_gain
            for here in pieces:
                d_normed = total[here, :] + (
                    d_down_ref[here, :].astype(F32) + d_attn_ref[here, :].astype(F32)
                )
                hat = hat_ref[here, :].astype(F32)
                d_gain += jnp.sum(d_normed * hat, 0, keepdims=True)
                d_shift += jnp.sum(d_normed, 0, keepdims=True)
                d_attn = norm_back(d_normed, hat, scale_ref[here, :][:, 0:1], gain).astype(BF16)
                d_attn_ref[here, :] = d_attn
                d_bias += jnp.sum(d_attn.astype(F32), 0, keepdims=True)
                d_mixed_ref[here, :] = dot(d_attn, output_proj_ref[...], NT).astype(BF16)
            sums_ref[...] = stack_rows([d_gain, d_shift, d_bias])


def feed_back(which, d_down, slope, active_t, shrink, expand, normed, norm, block=512):
    tokens, width = d_down.shape
    half = slope.shape[1] // 2
    steps = half // block
    last = norm is not None
    at = lambda i, which: which[0] * steps + i
    whole = lambda *shape: pl.BlockSpec(
        shape, lambda i, which: (0,) * len(shape), pipeline_mode=pl.Buffered(1)
    )
    in_specs = [
        whole(tokens, width),
        pl.BlockSpec((tokens, block), lambda i, which: (0, at(i, which))),
        pl.BlockSpec((block, tokens), lambda i, which: (at(i, which), 0)),
        pl.BlockSpec((block, width), lambda i, which: (at(i, which), 0)),
        pl.BlockSpec((width, block), lambda i, which: (0, at(i, which))),
        whole(tokens, width),
    ]
    out_specs = [
        pl.BlockSpec((2, block, width), lambda i, which: (0, i, 0)),
        whole(8, block),
    ]
    out_shape = hbm_shapes(((2, half, width), BF16), ((8, block), F32))
    scratch = [pltpu.VMEM((block, tokens), BF16), pltpu.VMEM((tokens, width), F32)]
    extra = ()
    if last:
        gain, *late = norm
        extra = (gain, *map(in_hbm, late))
        in_specs += [whole(1, width)] + [pl.BlockSpec(memory_space=pl.ANY)] * len(late)
        out_specs += [whole(tokens, width)] * 2 + [whole(8, width)]
        out_shape += hbm_shapes(
            ((tokens, width), BF16), ((tokens, width), BF16), ((8, width), F32)
        )
        scratch += [
            pltpu.VMEM((tokens, width), BF16),
            pltpu.VMEM((tokens, PAIR), F32),
            pltpu.VMEM((width, width), BF16),
            pltpu.SemaphoreType.DMA((4,)),
        ]
    else:
        out_specs.append(whole(tokens, width))
        out_shape += hbm_shapes(((tokens, width), BF16))
    return pl.pallas_call(
        functools.partial(feed_back_kernel, steps=steps, block=min(512, tokens), last=last),
        grid_spec=pltpu.PrefetchScalarGridSpec(
            num_scalar_prefetch=1,
            grid=(steps,),
            in_specs=in_specs,
            out_specs=out_specs,
            scratch_shapes=scratch,
        ),
        out_shape=out_shape,
        compiler_params=pltpu.CompilerParams(vmem_limit_bytes=44 * 2**20),
        cost_estimate=BRIEF,
        name="feed_back_last" if last else "feed_back",
    )(which, *map(in_hbm, (d_down, slope, active_t, shrink, expand, normed)), *extra)


def pack_kernel(at_ref, flat_ref, marks_ref, *refs, order):
    outs, sems = refs[:-1], refs[-1]
    piece = flat_ref.shape[1]
    for part, out_ref in zip(order, outs):
        marks = marks_ref[pl.ds(at_ref[0] ^ part, 1), :].astype(F32)
        out_ref[piece:, :] = jnp.zeros((MARK_ROWS, out_ref.shape[1]), BF16)
        out_ref[piece:, 0:piece] = jnp.broadcast_to(marks, (MARK_ROWS, piece)).astype(BF16)
    copies = [
        pltpu.make_async_copy(
            flat_ref.at[at_ref[0] ^ part], out_ref.at[pl.ds(0, piece)], sems.at[index]
        )
        for index, (part, out_ref) in enumerate(zip(order, outs))
    ]
    for copy in copies:
        copy.start()
    for copy in copies:
        copy.wait()


MARK_ROWS = 16


def pack(at, flat, marks, order):
    held, piece, width = flat.shape
    vmem = pl.BlockSpec(memory_space=pltpu.VMEM)
    return pl.pallas_call(
        functools.partial(pack_kernel, order=order),
        in_specs=[
            pl.BlockSpec(memory_space=pltpu.SMEM),
            pl.BlockSpec(memory_space=pl.ANY),
            vmem,
        ],
        out_specs=[vmem] * held,
        out_shape=shapes(*[((piece + MARK_ROWS, width), BF16)] * held),
        scratch_shapes=[pltpu.SemaphoreType.DMA((held,))],
        compiler_params=pltpu.CompilerParams(vmem_limit_bytes=16 * 2**20),
        cost_estimate=BRIEF,
        name="pack",
    )(at, in_hbm(flat), marks)


def unpack_kernel(*refs):
    parts, (rows_ref, marks_ref) = refs[:-2], refs[-2:]
    piece = rows_ref.shape[0] // len(parts)
    for index, ref in enumerate(parts):
        here = slice(index * piece, (index + 1) * piece)
        rows_ref[here, :] = ref[0:piece, :]
        marks = ref[piece:, 0:piece].astype(F32)[0:1, :]
        marks_ref[here, :] = jnp.broadcast_to(marks, (PAIR, piece)).T.astype(BF16)


def unpack(parts):
    width = parts[0].shape[1]
    tokens = len(parts) * (parts[0].shape[0] - MARK_ROWS)
    return pl.pallas_call(
        unpack_kernel,
        grid=(1,),
        in_specs=[fixed(*part.shape) for part in parts],
        out_specs=[fixed(tokens, width), fixed(tokens, PAIR)],
        out_shape=hbm_shapes(((tokens, width), BF16), ((tokens, PAIR), BF16)),
        compiler_params=pltpu.CompilerParams(vmem_limit_bytes=16 * 2**20),
        cost_estimate=BRIEF,
        name="unpack",
    )(*parts)


def weight_kernel(
    core_ref,
    first_sums_ref,
    second_sums_ref,
    own_bias_ref,
    other_bias_ref,
    *refs,
    steps,
):
    sources, (other_ref, own_ref, small_ref) = refs[:6], refs[6:9]
    targets, (inputs_t, mixed_t, sems) = refs[9:15], refs[15:]
    inputs_ref, dq_ref, dk_ref, dv_ref, mixed_ref, d_attn_ref = targets
    copies = [
        pltpu.make_async_copy(source, target, sems.at[index])
        for index, (source, target) in enumerate(zip(sources, targets))
    ]
    for copy in copies:
        copy.start()
    count = inputs_ref.shape[1] // 2
    core = core_ref[0]
    for ref in (other_ref, own_ref):
        if ref.shape[0] > 4 * count:
            ref[4 * count :, :] = jnp.zeros((ref.shape[0] - 4 * count, ref.shape[1]), BF16)
    copies[0].wait()
    inputs_t[...] = inputs_ref[...].T
    for at, right_ref in enumerate((dq_ref, dk_ref, dv_ref, d_attn_ref)):
        copies[at + 1].wait()
        left_ref = inputs_t
        if at == 3:
            copies[5].wait()
            mixed_t[...] = mixed_ref[...].T
            left_ref = mixed_t
        for half, out_ref in ((1 - core, other_ref), (core, own_ref)):
            rows = pl.ds(pl.multiple_of(half * count, PAIR), count)
            out_ref[at * count : (at + 1) * count, :] = dot(left_ref[rows, :], right_ref[...]).astype(
                BF16
            )
    small_ref[...] = jnp.zeros_like(small_ref)
    small_ref[0:1, :] = jnp.sum(dq_ref[...].astype(F32), 0, keepdims=True)
    small_ref[1:2, :] = jnp.sum(dv_ref[...].astype(F32), 0, keepdims=True)
    small_ref[2:5, :] = first_sums_ref[0:3, :]
    small_ref[5:8, :] = second_sums_ref[0:3, :]
    block = own_bias_ref.shape[1]
    own, other = own_bias_ref[0:steps, :], other_bias_ref[0:steps, :]
    small_ref[8 : 8 + steps, 0:block] = jnp.where(core == 0, own, other)
    small_ref[8 + steps : 8 + 2 * steps, 0:block] = jnp.where(core == 0, other, own)


def weight_halves(core, values, unit, sums, steps):
    tokens, width = values[0].shape
    rows = -(-2 * width // unit) * unit
    vmem = pl.BlockSpec(memory_space=pltpu.VMEM)
    anywhere = pl.BlockSpec(memory_space=pl.ANY)
    return pl.pallas_call(
        functools.partial(weight_kernel, steps=steps),
        in_specs=[pl.BlockSpec(memory_space=pltpu.SMEM)] + [vmem] * 4 + [anywhere] * 6,
        out_specs=[vmem] * 3,
        out_shape=shapes(
            ((rows, width), BF16), ((rows, width), BF16), ((SMALL, width), F32)
        ),
        scratch_shapes=[pltpu.VMEM((tokens, width), BF16)] * 6
        + [pltpu.VMEM((width, tokens), BF16)] * 2
        + [pltpu.SemaphoreType.DMA((6,))],
        compiler_params=pltpu.CompilerParams(vmem_limit_bytes=32 * 2**20),
        cost_estimate=BRIEF,
        name="weight_halves",
    )(core, *sums, *map(in_hbm, values))


def input_grad_kernel(*refs, held):
    sources, outs = refs[:7], refs[7 : 7 + held]
    (d_attn, *factors), total, sems = refs[7 + held : 14 + held], refs[-2], refs[-1]
    copies = [
        pltpu.make_async_copy(source, target, sems.at[index])
        for index, (source, target) in enumerate(zip(sources, (d_attn, *factors)))
    ]
    for copy in copies:
        copy.start()
    piece = outs[0].shape[0]
    copies[0].wait()
    for index in range(3):
        for copy in copies[2 * index + 1 : 2 * index + 3]:
            copy.wait()
        left, right = factors[2 * index : 2 * index + 2]
        for number, out_ref in enumerate(outs):
            here = slice(number * piece, (number + 1) * piece)
            before = d_attn[here, :].astype(F32) if index == 0 else total[here, :]
            value = before + dot(left[here, :], right[...], NT)
            if index < 2:
                total[here, :] = value
            else:
                out_ref[...] = value.astype(BF16)


def input_grad(d_attn, factors, held):
    tokens, width = d_attn.shape
    anywhere = pl.BlockSpec(memory_space=pl.ANY)
    values = [d_attn] + [value for pair in factors for value in pair]
    return pl.pallas_call(
        functools.partial(input_grad_kernel, held=held),
        in_specs=[anywhere] * 7,
        out_specs=[pl.BlockSpec(memory_space=pltpu.VMEM)] * held,
        out_shape=shapes(*[((tokens // held, width), BF16)] * held),
        scratch_shapes=[pltpu.VMEM(value.shape, BF16) for value in values]
        + [pltpu.VMEM((tokens, width), F32), pltpu.SemaphoreType.DMA((7,))],
        compiler_params=pltpu.CompilerParams(vmem_limit_bytes=24 * 2**20),
        cost_estimate=BRIEF,
        name="input_grad",
    )(*map(in_hbm, values))


def feed_out_kernel(which_ref, half_ref, *refs, steps):
    del which_ref
    shrink_ref, expand_ref = refs[-2:]

    @pl.when(pl.program_id(0) < steps)
    def _():
        shrink_ref[...] = half_ref[...].astype(F32)

    @pl.when(pl.program_id(0) >= steps)
    def _():
        expand_ref[...] = half_ref[...].T.astype(F32)


def feed_out(which, values, before=(), block=512):
    width = values.shape[1]
    half = values.shape[0] // 2
    steps = half // block
    return pl.pallas_call(
        functools.partial(feed_out_kernel, steps=steps),
        grid_spec=pltpu.PrefetchScalarGridSpec(
            num_scalar_prefetch=1,
            grid=(2 * steps,),
            in_specs=[pl.BlockSpec((block, width), lambda i, which: (i, 0))]
            + [pl.BlockSpec(memory_space=pl.ANY)] * len(before),
            out_specs=[
                pl.BlockSpec(
                    (block, width),
                    lambda i, which: (which[0] * steps + jnp.minimum(i, steps - 1), 0),
                ),
                pl.BlockSpec(
                    (width, block),
                    lambda i, which: (0, which[0] * steps + jnp.maximum(i - steps, 0)),
                ),
            ],
        ),
        out_shape=shapes(((2 * half, width), F32), ((width, 2 * half), F32)),
        input_output_aliases={2 + i: i for i in range(len(before))},
        compiler_params=pltpu.CompilerParams(vmem_limit_bytes=16 * 2**20),
        cost_estimate=BRIEF,
        name="feed_out",
    )(which, values, *before)


def attn_out_kernel(which_ref, half_ref, *refs):
    del which_ref
    for index, out_ref in enumerate(refs[-4:]):

        @pl.when(pl.program_id(0) == index)
        def _(out_ref=out_ref):
            out_ref[...] = half_ref[...].astype(F32)


def attn_out(which, values, before=()):
    width = values.shape[1]
    half = width // 2
    return pl.pallas_call(
        attn_out_kernel,
        grid_spec=pltpu.PrefetchScalarGridSpec(
            num_scalar_prefetch=1,
            grid=(4,),
            in_specs=[pl.BlockSpec((half, width), lambda i, which: (i, 0))]
            + [pl.BlockSpec(memory_space=pl.ANY)] * len(before),
            out_specs=[pl.BlockSpec((half, width), lambda i, which: (which[0], 0))] * 4,
        ),
        out_shape=shapes(*[((width, width), F32)] * 4),
        input_output_aliases={2 + i: i for i in range(len(before))},
        compiler_params=pltpu.CompilerParams(vmem_limit_bytes=24 * 2**20),
        cost_estimate=BRIEF,
        name="attn_out",
    )(which, values, *before)


def place_kernel(at_ref, *refs):
    del at_ref
    out_ref = refs[-1]
    for index, ref in enumerate(refs[:-1]):

        @pl.when(pl.program_id(0) == index)
        def _(ref=ref):
            out_ref[0] = ref[...]


def place(at, parts):
    piece, width = parts[0].shape
    held = len(parts)
    return pl.pallas_call(
        place_kernel,
        grid_spec=pltpu.PrefetchScalarGridSpec(
            num_scalar_prefetch=1,
            grid=(held,),
            in_specs=[pl.BlockSpec((piece, width), lambda i, at: (0, 0))] * held,
            out_specs=pl.BlockSpec((1, piece, width), lambda i, at: (at[0] ^ i, 0, 0)),
        ),
        out_shape=jax.ShapeDtypeStruct((held, piece, width), BF16),
        compiler_params=pltpu.CompilerParams(vmem_limit_bytes=16 * 2**20),
        cost_estimate=BRIEF,
        name="place",
    )(at, *parts)


def rows_of(ref, which, count, base=0):
    return ref[pl.ds(pl.multiple_of(base + which * count, 16), count), :]


def sum_of(terms):
    return functools.reduce(lambda a, b: a + b, [t.astype(F32) for t in terms]).astype(BF16)


def scatter_kernel(bits_ref, *refs, groups):
    outs = refs[-2 * groups :]
    ins = refs[: -2 * groups]
    together = len(ins) == 2
    base = 0
    for group in range(groups):
        terms = ins if together else ins[2 * group : 2 * group + 2]
        sent_ref, kept_ref = outs[2 * group : 2 * group + 2]
        count = kept_ref.shape[0]
        here = bits_ref[group]
        sent_ref[...] = sum_of([rows_of(term, 1 - here, count, base) for term in terms])
        kept_ref[...] = sum_of([rows_of(term, here, count, base) for term in terms])
        if together:
            base += 2 * count


def local_call(kernel, bits, values, out_shape, name):
    vmem = pl.BlockSpec(memory_space=pltpu.VMEM)
    return pl.pallas_call(
        kernel,
        in_specs=[pl.BlockSpec(memory_space=pltpu.SMEM)] + [vmem] * len(values),
        out_specs=[vmem] * len(out_shape),
        out_shape=out_shape,
        compiler_params=pltpu.CompilerParams(vmem_limit_bytes=24 * 2**20),
        cost_estimate=BRIEF,
        name=name,
    )(bits, *values)


def scatter_local(bits, pairs, counts=None):
    if counts is None:
        counts = [kept.shape[0] for kept, _ in pairs]
    groups = len(counts)
    counts = [count // 2 for count in counts]
    width = pairs[0][0].shape[1]
    outs = local_call(
        functools.partial(scatter_kernel, groups=groups),
        bits,
        [value for pair in pairs for value in pair],
        shapes(*[((count, width), BF16) for count in counts for _ in range(2)]),
        "scatter_local",
    )
    return [outs[2 * i : 2 * i + 2] for i in range(groups)]


def scatter_first_kernel(bits_ref, own_at, got_at, *refs, counts):
    outs, (own, got, sems) = refs[:-3], refs[-3:]
    spans = []
    base = 0
    for group, count in enumerate(counts):
        for kept in range(2):
            half = bits_ref[group] if kept else 1 - bits_ref[group]
            start = pl.multiple_of(base + half * (count // 2), 16)
            spans.append((start, count // 2, outs[2 * group + kept]))
        base += count
    spans = spans[0::2] + spans[1::2]
    copies = []
    for index, (start, count, _) in enumerate(spans):
        rows = pl.ds(start, count)
        for which, (source, target) in enumerate(((own_at, own), (got_at, got))):
            copies.append(
                pltpu.make_async_copy(source.at[rows], target.at[rows], sems.at[2 * index + which])
            )
            copies[-1].start()
    for index, (start, count, out_ref) in enumerate(spans):
        for copy in copies[2 * index : 2 * index + 2]:
            copy.wait()
        rows = pl.ds(start, count)
        out_ref[...] = sum_of([own[rows, :], got[rows, :]])


def scatter_first(bits, own, got, counts):
    rows, width = own.shape
    anywhere = pl.BlockSpec(memory_space=pl.ANY)
    vmem = pl.BlockSpec(memory_space=pltpu.VMEM)
    outs = pl.pallas_call(
        functools.partial(scatter_first_kernel, counts=counts),
        in_specs=[pl.BlockSpec(memory_space=pltpu.SMEM), anywhere, anywhere],
        out_specs=[vmem] * (2 * len(counts)),
        out_shape=shapes(*[((count // 2, width), BF16) for count in counts for _ in range(2)]),
        scratch_shapes=[pltpu.VMEM((rows, width), BF16)] * 2
        + [pltpu.SemaphoreType.DMA((4 * len(counts),))],
        compiler_params=pltpu.CompilerParams(vmem_limit_bytes=24 * 2**20),
        cost_estimate=BRIEF,
        name="scatter_first",
    )(bits, in_hbm(own), in_hbm(got))
    return [outs[2 * group : 2 * group + 2] for group in range(len(counts))]


SMALL = 16


def put_small(ref, at, values):
    ref[at : at + SMALL, :] = values.astype(BF16)


def get_small(ref, at):
    return ref[at : at + SMALL, :].astype(F32)


def settle_kernel(bits_ref, *refs, groups, small):
    del bits_ref
    ins, outs = refs[: 2 * groups], refs[2 * groups + small :]
    for group in range(groups):
        count = ins[2 * group].shape[0]
        outs[group][0:count, :] = sum_of([ins[2 * group][...], ins[2 * group + 1][...]])
        if small and group == 0:
            put_small(outs[group], count, refs[2 * groups][...])


def settle_local(bits, pairs, small):
    width = pairs[0][0].shape[1]
    counts = [kept.shape[0] for kept, _ in pairs]
    if small is not None:
        counts[0] += SMALL
    return local_call(
        functools.partial(settle_kernel, groups=len(pairs), small=int(small is not None)),
        bits,
        [value for pair in pairs for value in pair] + ([] if small is None else [small]),
        shapes(*[((count, width), BF16) for count in counts]),
        "settle_local",
    )


def add_kernel(bits_ref, *refs, groups, small):
    del bits_ref
    ins, outs = refs[: 2 * groups], refs[2 * groups :]
    for group in range(groups):
        own_ref, got_ref = ins[2 * group : 2 * group + 2]
        extra = SMALL if small and group == 0 else 0
        count = own_ref.shape[0] - extra
        outs[group][0:count, :] = sum_of([own_ref[0:count, :], got_ref[0:count, :]])
        if extra:
            put_small(outs[group], count, get_small(own_ref, count) + get_small(got_ref, count))


def add_local(bits, pairs, small):
    return local_call(
        functools.partial(add_kernel, groups=len(pairs), small=small),
        bits,
        [value for pair in pairs for value in pair],
        shapes(*[(own.shape, BF16) for own, _ in pairs]),
        "add_local",
    )


def join_kernel(bits_ref, *refs, groups, small, merged, pieces):
    ins, outs = refs[: 2 * pieces * groups], list(refs[2 * pieces * groups :])
    parts = len(outs) // groups
    base = 0
    for group in range(groups):
        owns = ins[2 * pieces * group : 2 * pieces * group + 2 * pieces : 2]
        gots = ins[2 * pieces * group + 1 : 2 * pieces * group + 2 * pieces : 2]
        extra = SMALL if small and group == 0 else 0
        count = owns[0].shape[0] - extra
        here = bits_ref[group]
        if parts > 1:
            for half, out_ref in enumerate(outs[2 * group : 2 * group + 2]):

                @pl.when(here == half)
                def _(out_ref=out_ref):
                    out_ref[...] = owns[0][...]

                @pl.when(here != half)
                def _(out_ref=out_ref):
                    out_ref[...] = gots[0][...]

            continue
        out_ref = outs[0 if merged else group]
        whole = count * pieces
        for half, refs_of in ((here, owns), (1 - here, gots)):
            for index, ref in enumerate(refs_of):
                start = pl.multiple_of(base + half * whole + index * count, 16)
                out_ref[pl.ds(start, count), :] = ref[0:count, :]
        if extra:
            at = out_ref.shape[0] - SMALL if merged else base + 2 * whole
            put_small(out_ref, at, get_small(owns[0], count) + get_small(gots[0], count))
        if merged:
            base += 2 * whole


def join_local(bits, arrived, small, merged, parts=1):
    width = arrived[0][0].shape[1]
    pieces = len(arrived[0]) // 2
    counts = [2 * pieces * group[0].shape[0] for group in arrived]
    if small:
        counts[0] -= SMALL
    if merged:
        counts = [sum(counts)]
    counts = [count // parts for count in counts for _ in range(parts)]
    return local_call(
        functools.partial(
            join_kernel, groups=len(arrived), small=small, merged=merged, pieces=pieces
        ),
        bits,
        [value for group in arrived for value in group],
        shapes(*[((count, width), BF16) for count in counts]),
        "join_local",
    )


def tie(*values):
    return lax.optimization_barrier(values)


def pick(which, parts):
    if len(parts) == 1:
        return parts[0]
    half = len(parts) // 2
    return jnp.where(which < half, pick(which, parts[:half]), pick(which - half, parts[half:]))


def column_sum(values):
    return jnp.sum(values.astype(F32), 0)


class Stage:
    def __init__(self, sizes, bits):
        self.bits = bits
        rows, seq = sizes
        self.pairs = []
        for index in range(rows * seq):
            axis, bit = bits[index & 1]
            self.pairs.append((index, index ^ ((1 << bit) * (seq if axis == "rows" else 1))))

    def here(self):
        first, second = [(lax.axis_index(axis) >> bit) & 1 for axis, bit in self.bits]
        if self.bits[0] == self.bits[1]:
            return first
        return jnp.where(lax.axis_index("seq") & 1 == 0, first, second)

    def swap(self, values):
        return lax.ppermute(values, ("rows", "seq"), self.pairs)


def total_over_chips(own, got, core_stage, orders, small=None, near=False):
    depth = len(orders[0][1])
    groups = range(len(orders))

    def bits_at(step):
        return jnp.stack([stages[step].here() for _, stages in orders]).astype(jnp.int32)

    def pairs_of(flat):
        return [flat[i : i + 2] for i in range(0, len(flat), 2)]

    def send(step, values, keep):
        flat = []
        for group in groups:
            flat += [keep[group], orders[group][1][step].swap(values[group])]
        return flat

    counts = [count for count, _ in orders]
    if near:
        parts = scatter_local(bits_at(0), [[own, got]], counts)
    else:
        parts = scatter_first(bits_at(0), own, got, counts)
    last = depth - 1 if near else depth
    for step in range(1, last + 1):
        flat = yield send(step - 1, [p[0] for p in parts], [p[1] for p in parts])
        if step < last:
            parts = scatter_local(bits_at(step), pairs_of(flat))
    values = settle_local(bits_at(0), pairs_of(flat), small)
    if near:
        flat = yield send(last, values, values)
        values = add_local(bits_at(0), pairs_of(flat), small is not None)
    carried = small is not None
    for step in reversed(range(last)):
        flat = yield send(step, values, values)
        parts = 2 if step == 1 and not carried else 1
        values = join_local(bits_at(step), pairs_of(flat), carried, step == 0, parts)
        if parts > 1:
            lower = yield send(0, values[0::2], values[0::2])
            upper = yield send(0, values[1::2], values[1::2])
            arrived = [list(low) + list(high) for low, high in zip(pairs_of(lower), pairs_of(upper))]
            values = join_local(bits_at(0), arrived, carried, True)
            break
    both = yield [values[0], core_stage.swap(values[0])]
    return both


def arriving(values):
    values = yield values
    return values[1::2]


class Flow:
    def __init__(self, steps, left):
        self.steps = steps
        self.left = left
        self.pending = next(steps)
        self.result = None


class Timetable:
    def __init__(self):
        self.flows = []

    def open(self, steps, left=1):
        self.flows.append(Flow(steps, left))
        return self.flows[-1]

    def advance(self, moving, *values):
        flows = [flow for flow in self.flows if flow.result is None]
        held = [flow.pending if flow in moving else flow.pending[0::2] for flow in flows]
        tied = list(tie(*values, *[value for part in held for value in part]))
        values, tied = tied[: len(values)], tied[len(values) :]
        for flow, part in zip(flows, held):
            back, tied = tied[: len(part)], tied[len(part) :]
            if flow not in moving:
                flow.pending[0::2] = back
                continue
            flow.left -= 1
            try:
                flow.pending = flow.steps.send(back)
            except StopIteration as end:
                flow.result = end.value
        return self.settle(*values) if moving and values else values

    def settle(self, *values):
        return self.advance([], *values)


def solution(mesh):
    seq_size = mesh.shape["seq"]
    rows_size = mesh.shape["rows"]
    seq_bits = seq_size.bit_length() - 1
    rows_bits = rows_size.bit_length() - 1
    off_chip = [("seq", bit) for bit in range(1, seq_bits)]
    off_chip += [("rows", bit) for bit in range(rows_bits)]
    first, *middle, ahead, final = off_chip
    sizes = (rows_size, seq_size)
    core_stage = Stage(sizes, [("seq", 0)] * 2)
    straight = [first] + middle + [ahead, final]
    turned = middle + [ahead, first, final]
    spun = [ahead, first] + middle + [final]
    wide = [Stage(sizes, bits) for bits in zip(straight, turned)]
    slim = [Stage(sizes, bits) for bits in zip(spun, spun)]

    def body(
        hidden_in,
        segments,
        grad_mask,
        grad_out,
        query_proj,
        query_bias,
        key_proj,
        value_proj,
        value_bias,
        output_proj,
        output_bias,
        first_gain,
        first_shift,
        expand_proj,
        expand_bias,
        shrink_proj,
        shrink_bias,
        second_gain,
        second_shift,
    ):
        micro, rows_here, piece, width = hidden_in.shape
        held = micro * rows_here
        sharers = seq_size // held
        tokens = held * piece
        source_at = lax.axis_index("seq") % held
        core = core_stage.here()
        core_at = core.reshape(1).astype(jnp.int32)

        def trade(to_rows, part):
            there = [(s, (s % held ^ part) * sharers + s // held) for s in range(seq_size)]
            return there if to_rows else [(b, a) for a, b in there]

        def to_rows(values):
            return [
                lax.ppermute(
                    lax.dynamic_index_in_dim(values, source_at ^ part, 0, False),
                    "seq",
                    trade(True, part),
                )
                for part in range(held)
            ]

        def send_pieces(values):
            return [
                value
                for part in range(held)
                for value in (values[part], lax.ppermute(values[part], "seq", trade(False, part)))
            ]

        def place_pieces(parts):
            at = source_at.reshape(1).astype(jnp.int32)
            return place(at, parts).reshape((micro, rows_here) + parts[0].shape)

        same_row = [[r * sharers + g for g in range(sharers)] for r in range(held)]

        def all_keys(values):
            if sharers == 1:
                return values
            return lax.all_gather(values, "seq", axis=0, tiled=True, axis_index_groups=same_row)

        def own_keys(values):
            if sharers == 1:
                return values
            return lax.psum_scatter(
                values, "seq", scatter_dimension=0, tiled=True, axis_index_groups=same_row
            ).astype(BF16)

        order = tuple(reversed(range(held)))
        packed = pack(
            source_at.reshape(1).astype(jnp.int32),
            hidden_in.reshape(held, piece, width),
            segments.reshape(held, piece),
            order,
        )
        arrived = [
            lax.ppermute(value, "seq", trade(True, part)) for part, value in zip(order, packed)
        ]
        inputs, seg_q = unpack(arrived[::-1])
        masked = (grad_out * grad_mask[..., None].astype(BF16)).reshape(held, piece, width)
        masked, inputs, seg_q = tie(masked, inputs, seg_q)
        upstream = to_rows(masked)

        queries = (
            (dot(inputs, query_proj) + query_bias.astype(F32)) * 0.125
        ).astype(BF16)
        keys = all_keys(dot(inputs, key_proj).astype(BF16))
        values = all_keys((dot(inputs, value_proj) + value_bias.astype(F32)).astype(BF16))
        seg_k = all_keys(seg_q)
        mixed, query_side = attention_forward(queries, keys, values, seg_q, seg_k)
        row = lambda vector: vector.reshape(1, -1)
        hat, scale, normed, active_t, slope, d_down, second_sums, *result = feed_forward(
            inputs,
            mixed,
            upstream,
            (
                output_proj,
                row(output_bias),
                row(first_gain),
                row(first_shift),
                expand_proj,
                row(expand_bias),
                shrink_proj,
                row(shrink_bias),
                row(second_gain),
                row(second_shift),
            ),
        )
        table = Timetable()
        advance = table.advance
        layer_flow = table.open(arriving(send_pieces(result)))

        def chips(own, got, orders, small=None):
            near = small is not None
            steps = total_over_chips(own, got, core_stage, orders, small, near)
            return table.open(steps, 2 * len(wide) + (0 if near else 2))

        back = functools.partial(
            feed_back,
            slope=slope,
            active_t=active_t,
            shrink=shrink_proj,
            expand=expand_proj,
            normed=normed,
        )
        other, other_bias, d_normed = back(1 - core_at, d_down, norm=None)
        half = other.shape[1]
        got = core_stage.swap(other.reshape(2 * half, width))
        own, own_bias, d_attn, d_mixed, first_sums = back(
            core_at, d_down, norm=(row(first_gain), d_normed, hat, scale, output_proj)
        )
        own, got, d_mixed = advance([layer_flow], own.reshape(2 * half, width), got, d_mixed)
        unit = 16 << len(off_chip)

        def thirds(count):
            less = count // unit // 3 * unit
            return [(count - less, wide)] + ([(less, slim)] if less else [])

        feed_flow = chips(own, got, thirds(2 * half))

        pairs = width // PAIR
        kept = BF16 if sharers == 1 else F32
        grads = None
        for first, last in ((0, pairs),):
            grads = attention_backward(
                query_side, keys, values, seg_k, mixed, d_mixed, kept, first, last - first, grads
            )
            *grads, d_mixed = advance([feed_flow], *grads, d_mixed)

        d_query, d_keys, d_values = grads
        d_key = own_keys(d_keys)
        d_value = own_keys(d_values)
        steps = half // other_bias.shape[1]
        other, own, small = weight_halves(
            core_at,
            (inputs, d_query, d_key, d_value, mixed, d_attn),
            unit,
            (first_sums, second_sums, own_bias, other_bias),
            steps,
        )
        other, own, small, d_query, d_key, d_value = advance(
            [feed_flow], other, own, small, d_query, d_key, d_value
        )
        got = core_stage.swap(other)
        d_input = input_grad(
            d_attn, ((d_query, query_proj), (d_key, key_proj), (d_value, value_proj)), held
        )
        own, got, small, *d_input = advance([feed_flow], own, got, small, *d_input)
        attn_flow = chips(own, got, [(own.shape[0], wide)], small)
        piece_flow = table.open(arriving(send_pieces(d_input)))

        both = [feed_flow, attn_flow]
        layer_out = place_pieces(list(map(in_hbm, layer_flow.result)))
        (layer_out,) = advance(both, layer_out)
        advance(both + [piece_flow])
        grad_in = place_pieces(piece_flow.result)
        (grad_in,) = advance(both, grad_in)
        while feed_flow.left > 1:
            advance(both)
        feed_grads = feed_out(core_at, feed_flow.pending[0])
        feed_grads = advance(both, *feed_grads)
        feed_grads = feed_out(1 - core_at, feed_flow.result[1], feed_grads)
        while attn_flow.left > 1:
            feed_grads = advance([attn_flow], *feed_grads)
        attn_grads = attn_out(core_at, attn_flow.pending[0])
        attn_grads = advance([attn_flow], *attn_grads)
        own, got = attn_flow.result
        attn_grads = attn_out(1 - core_at, got, attn_grads)
        totals = own[-SMALL:].astype(F32) + got[-SMALL:].astype(F32)
        shrink_grad, expand_grad = feed_grads
        expand_bias_grad = totals[8 : 8 + 2 * steps, : other_bias.shape[1]].reshape(-1)
        return (
            layer_out,
            grad_in,
            attn_grads[0],
            totals[0],
            attn_grads[1],
            attn_grads[2],
            totals[1],
            attn_grads[3],
            totals[4],
            totals[2],
            totals[3],
            expand_grad,
            expand_bias_grad,
            shrink_grad,
            totals[7],
            totals[5],
            totals[6],
        )

    split = P(None, "rows", "seq", None)
    whole = P()
    return jax.shard_map(
        body,
        mesh=mesh,
        in_specs=(split, P(None, "rows", "seq"), P(None, "rows", "seq"), split) + (whole,) * 15,
        out_specs=(split, split) + (whole,) * 15,
        check_vma=False,
    )
```

```python
import functools

import jax
import jax.numpy as jnp
from jax import lax
from jax.experimental import pallas as pl
from jax.experimental.pallas import tpu as pltpu
from jax.sharding import PartitionSpec as P

DH = 64
PAIR = 128
MASKED = 1e30
F32 = jnp.float32
BF16 = jnp.bfloat16
NT = (((1,), (1,)), ((), ()))
NN = (((1,), (0,)), ((), ()))
BRIEF = pl.CostEstimate(flops=1, bytes_accessed=1, transcendentals=0)


def left_dot(first, second):
    return lax.dot_general(first, second, (((0,), (0,)), ((), ())), preferred_element_type=F32)


def right_dot(first, second):
    return lax.dot_general(first, second, NT, preferred_element_type=F32)


def split_three(values):
    high = values.astype(BF16)
    rest = values - high.astype(F32)
    middle = rest.astype(BF16)
    low = (rest - middle.astype(F32)).astype(BF16)
    return high.astype(F32), middle.astype(F32), low.astype(F32)


def own_lanes(shape, head):
    lane = lax.broadcasted_iota(jnp.int32, shape, 1)
    own = lane < DH if head == 0 else lane >= DH
    return own, lane % DH


def key_features(lane, seg):
    return jnp.where(
        lane < 3,
        1.0,
        jnp.where(lane == 3, -MASKED * (1.0 - seg), jnp.where(lane == 4, -MASKED * seg, 0.0)),
    ).astype(BF16)


def forward_kernel(q_ref, k_ref, v_ref, seg_q_ref, seg_k_ref, mixed_ref, query_ref, *, block):
    queries = q_ref.shape[0]
    keys = k_ref.shape[0]
    for head in range(2):
        own_k, lane_k = own_lanes((keys, PAIR), head)
        key_side = jnp.where(own_k, k_ref[...], key_features(lane_k, seg_k_ref[...].astype(F32)))
        value_side = jnp.where(own_k, v_ref[...], jnp.ones((), BF16))
        own_q, lane_q = own_lanes((block, PAIR), head)
        for start in range(0, queries, block):
            here = slice(start, start + block)
            q = q_ref[here, :]
            seg = seg_q_ref[here, :].astype(F32)
            seg_side = jnp.where(lane_q == 3, seg, jnp.where(lane_q == 4, 1.0 - seg, 0.0))
            query_side = jnp.where(own_q, q, seg_side.astype(BF16))
            scores = lax.dot_general(query_side, key_side, NT, preferred_element_type=F32)
            peak = jnp.max(scores, -1, keepdims=True)
            raised = jnp.exp(scores - peak).astype(BF16)
            summed = lax.dot_general(raised, value_side, NN, preferred_element_type=F32)
            total = summed[:, DH : DH + 1] if head == 0 else summed[:, 0:1]
            mixed = (summed / total).astype(BF16)
            shift = jnp.broadcast_to(-(peak + jnp.log(total)), (block, PAIR))
            high, middle, low = split_three(shift)
            extra = jnp.where(
                lane_q == 0,
                high,
                jnp.where(lane_q == 1, middle, jnp.where(lane_q == 2, low, seg_side)),
            )
            query_ref[head, here, :] = jnp.where(own_q, q, extra.astype(BF16))
            if head == 0:
                mixed_ref[here, :] = mixed
            else:
                mixed_ref[here, :] = jnp.where(own_q, mixed, mixed_ref[here, :])


def attention_forward(q, k, v, seg_q, seg_k):
    queries, width = q.shape
    keys = k.shape[0]
    pairs = width // PAIR
    column = lambda i: (0, i)
    whole = lambda i: (0, 0)
    return pl.pallas_call(
        functools.partial(forward_kernel, block=min(512, queries)),
        grid=(pairs,),
        in_specs=[
            pl.BlockSpec((queries, PAIR), column),
            pl.BlockSpec((keys, PAIR), column),
            pl.BlockSpec((keys, PAIR), column),
            pl.BlockSpec((queries, PAIR), whole),
            pl.BlockSpec((keys, PAIR), whole),
        ],
        out_specs=[
            pl.BlockSpec((queries, PAIR), column),
            pl.BlockSpec((2, queries, PAIR), lambda i: (i, 0, 0)),
        ],
        out_shape=[
            pltpu.HBM((queries, width), BF16),
            pltpu.HBM((2 * pairs, queries, PAIR), BF16),
        ],
        compiler_params=pltpu.CompilerParams(vmem_limit_bytes=24 * 2**20),
        cost_estimate=BRIEF,
        name="attention_forward",
    )(q, k, v, seg_q, seg_k)


def backward_kernel(
    query_ref, k_ref, v_ref, seg_k_ref, mixed_ref, d_mixed_ref, *refs, block
):
    dq_ref, dk_ref, dv_ref, dqt = refs[-4:]
    queries = mixed_ref.shape[0]
    keys = k_ref.shape[0]
    d_mixed = d_mixed_ref[...]
    product = d_mixed.astype(F32) * mixed_ref[...].astype(F32)
    for head in range(2):
        own_q, lane_q = own_lanes((queries, PAIR), head)
        own_k, lane_k = own_lanes((block, PAIR), head)
        delta = -jnp.sum(jnp.where(own_q, product, 0.0), -1, keepdims=True)
        high, middle, low = split_three(jnp.broadcast_to(delta, (queries, PAIR)))
        extra = jnp.where(
            lane_q == 0, high, jnp.where(lane_q == 1, middle, jnp.where(lane_q == 2, low, 0.0))
        )
        d_side = jnp.where(own_q, d_mixed, extra.astype(BF16))
        query_side = query_ref[head]
        ones = jnp.where(lane_k < 3, 1.0, 0.0).astype(BF16)
        for start in range(0, keys, block):
            here = slice(start, start + block)
            k = k_ref[here, :]
            seg = seg_k_ref[here, :].astype(F32)
            key_side = jnp.where(own_k, k, key_features(lane_k, seg))
            value_side = jnp.where(own_k, v_ref[here, :], ones)
            shifted = lax.dot_general(key_side, query_side, NT, preferred_element_type=F32)
            probs = jnp.exp(shifted)
            d_probs = lax.dot_general(value_side, d_side, NT, preferred_element_type=F32)
            d_scores = (probs * d_probs).astype(BF16)
            dv = lax.dot_general(probs.astype(BF16), d_mixed, NN, preferred_element_type=F32)
            dk = lax.dot_general(d_scores, query_side, NN, preferred_element_type=F32)
            turned = k.T[head * DH : (head + 1) * DH, :]
            dq = lax.dot_general(turned, d_scores, NN, preferred_element_type=F32)
            mine = slice(head * DH, (head + 1) * DH)
            if start == 0:
                dqt[mine, :] = dq
            else:
                dqt[mine, :] += dq
            dv = dv.astype(dv_ref.dtype)
            dk = dk.astype(dk_ref.dtype)
            if head == 0:
                dk_ref[here, :] = dk
                dv_ref[here, :] = dv
            else:
                dk_ref[here, :] = jnp.where(own_k, dk, dk_ref[here, :])
                dv_ref[here, :] = jnp.where(own_k, dv, dv_ref[here, :])
    dq_ref[...] = (dqt[...] * 0.125).astype(BF16).T


def attention_backward(query_side, k, v, seg_k, mixed, d_mixed, kept, first, count, before):
    queries, width = mixed.shape
    keys = k.shape[0]
    column = lambda i: (0, i + first)
    held = [] if before is None else list(before)
    return pl.pallas_call(
        functools.partial(backward_kernel, block=min(512, keys)),
        grid=(count,),
        in_specs=[
            pl.BlockSpec((2, queries, PAIR), lambda i: (i + first, 0, 0)),
            pl.BlockSpec((keys, PAIR), column),
            pl.BlockSpec((keys, PAIR), column),
            pl.BlockSpec((keys, PAIR), lambda i: (0, 0)),
            pl.BlockSpec((queries, PAIR), column),
            pl.BlockSpec((queries, PAIR), column),
        ]
        + [pl.BlockSpec(memory_space=pl.ANY)] * len(held),
        out_specs=[
            pl.BlockSpec((queries, PAIR), column),
            pl.BlockSpec((keys, PAIR), column),
            pl.BlockSpec((keys, PAIR), column),
        ],
        input_output_aliases={6 + i: i for i in range(len(held))},
        out_shape=[
            pltpu.HBM((queries, width), BF16),
            pltpu.HBM((keys, width), kept),
            pltpu.HBM((keys, width), kept),
        ],
        scratch_shapes=[pltpu.VMEM((PAIR, queries), F32)],
        compiler_params=pltpu.CompilerParams(vmem_limit_bytes=24 * 2**20),
        cost_estimate=BRIEF,
        name="attention_backward",
    )(in_hbm(query_side), k, v, seg_k, in_hbm(mixed), in_hbm(d_mixed), *map(in_hbm, held))


def dot(first, second, dims=NN):
    return lax.dot_general(first, second, dims, preferred_element_type=F32)


def gelu_pair(values):
    below = 0.5 + 0.5 * lax.erf(values * 0.7071067811865476)
    density = jnp.exp(-0.5 * values * values) * 0.3989422804014327
    return values * below, below + values * density


def normalise(values):
    centred = values - jnp.mean(values, -1, keepdims=True)
    scale = lax.rsqrt(jnp.mean(centred * centred, -1, keepdims=True) + 1e-06)
    return centred * scale, scale


def norm_back(upstream, hat, scale, gain):
    d_hat = upstream * gain
    return scale * (
        d_hat
        - jnp.mean(d_hat, -1, keepdims=True)
        - hat * jnp.mean(d_hat * hat, -1, keepdims=True)
    )


def stack_rows(rows):
    filler = jnp.zeros((8 - len(rows), rows[0].shape[1]), F32)
    return jnp.concatenate(rows + [filler], 0)


def feed_forward_kernel(
    inputs_ref,
    mixed_ref,
    output_proj_ref,
    output_bias_ref,
    gain_one_ref,
    shift_one_ref,
    expand_ref,
    expand_bias_ref,
    shrink_ref,
    shrink_bias_ref,
    gain_two_ref,
    shift_two_ref,
    *refs,
    steps,
    held,
):
    upstream_refs = refs[:held]
    hat_out, scale_ref, normed_out, active_t_ref, slope_ref = refs[held : held + 5]
    d_down_ref, sums_ref = refs[held + 5 : held + 7]
    out_refs = refs[held + 7 : 2 * held + 7]
    total, hat_ref, normed_ref, sems = refs[2 * held + 7 :]
    block = total.shape[0] // held
    early = [
        pltpu.make_async_copy(hat_ref, hat_out, sems.at[0]),
        pltpu.make_async_copy(normed_ref, normed_out, sems.at[1]),
    ]
    step = pl.program_id(0)
    tokens = total.shape[0]
    pieces = [slice(start, start + block) for start in range(0, tokens, block)]

    @pl.when(step == 0)
    def _():
        for here in pieces:
            first_sum = (
                inputs_ref[here, :].astype(F32)
                + dot(mixed_ref[here, :], output_proj_ref[...])
                + output_bias_ref[...].astype(F32)
            )
            hat, scale = normalise(first_sum)
            hat_ref[here, :] = hat.astype(BF16)
            scale_ref[here, :] = jnp.broadcast_to(scale, (block, PAIR))
            normed = gain_one_ref[...].astype(F32) * hat + shift_one_ref[...].astype(F32)
            normed_ref[here, :] = normed.astype(BF16)
            total[here, :] = normed + shrink_bias_ref[...].astype(F32)
        for copy in early:
            copy.start()

    for here in pieces:
        expanded = dot(normed_ref[here, :], expand_ref[...]) + expand_bias_ref[...].astype(F32)
        active, slope = gelu_pair(expanded)
        active = active.astype(BF16)
        slope_ref[here, :] = slope.astype(BF16)
        active_t_ref[:, here] = active.T
        total[here, :] += dot(active, shrink_ref[...])

    @pl.when(step == steps - 1)
    def _():
        gain = gain_two_ref[...].astype(F32)
        d_gain = jnp.zeros((1, total.shape[1]), F32)
        d_shift = d_gain
        d_bias = d_gain
        for here, upstream_ref, out_ref in zip(pieces, upstream_refs, out_refs):
            hat, scale = normalise(total[here, :])
            out_ref[...] = (gain * hat + shift_two_ref[...].astype(F32)).astype(BF16)
            upstream = upstream_ref[...].astype(F32)
            d_gain += jnp.sum(upstream * hat, 0, keepdims=True)
            d_shift += jnp.sum(upstream, 0, keepdims=True)
            d_down = norm_back(upstream, hat, scale, gain).astype(BF16)
            d_down_ref[here, :] = d_down
            d_bias += jnp.sum(d_down.astype(F32), 0, keepdims=True)
        sums_ref[...] = stack_rows([d_gain, d_shift, d_bias])
        for copy in early:
            copy.wait()


def in_hbm(values):
    return pltpu.with_memory_space_constraint(values, pltpu.HBM)


def hbm_shapes(*pairs):
    return [pltpu.HBM(shape, dtype) for shape, dtype in pairs]


def fixed(*shape):
    return pl.BlockSpec(shape, lambda i: (0,) * len(shape), pipeline_mode=pl.Buffered(1))


def shapes(*pairs):
    return [jax.ShapeDtypeStruct(shape, dtype) for shape, dtype in pairs]


def feed_forward(inputs, mixed, upstream, weights, block=768):
    tokens, width = inputs.shape
    units = weights[4].shape[1]
    steps = units // block
    held = len(upstream)
    piece = tokens // held
    row = fixed(1, width)
    return pl.pallas_call(
        functools.partial(feed_forward_kernel, steps=steps, held=held),
        grid=(steps,),
        in_specs=[fixed(tokens, width)] * 2
        + [fixed(width, width), row, row, row]
        + [
            pl.BlockSpec((width, block), lambda i: (0, i)),
            pl.BlockSpec((1, block), lambda i: (0, i)),
            pl.BlockSpec((block, width), lambda i: (i, 0)),
            row,
            row,
            row,
        ]
        + [fixed(piece, width)] * held,
        out_specs=[
            pl.BlockSpec(memory_space=pl.ANY),
            fixed(tokens, PAIR),
            pl.BlockSpec(memory_space=pl.ANY),
            pl.BlockSpec((block, tokens), lambda i: (i, 0)),
            pl.BlockSpec((tokens, block), lambda i: (0, i)),
            fixed(tokens, width),
            fixed(8, width),
        ]
        + [fixed(piece, width)] * held,
        out_shape=hbm_shapes(
            ((tokens, width), BF16),
            ((tokens, PAIR), F32),
            ((tokens, width), BF16),
            ((units, tokens), BF16),
            ((tokens, units), BF16),
            ((tokens, width), BF16),
            ((8, width), F32),
        )
        + shapes(*[((piece, width), BF16)] * held),
        scratch_shapes=[
            pltpu.VMEM((tokens, width), F32),
            pltpu.VMEM((tokens, width), BF16),
            pltpu.VMEM((tokens, width), BF16),
            pltpu.SemaphoreType.DMA((2,)),
        ],
        compiler_params=pltpu.CompilerParams(vmem_limit_bytes=36 * 2**20),
        cost_estimate=BRIEF,
        name="feed_forward",
    )(inputs, in_hbm(mixed), *map(in_hbm, weights), *upstream)


def feed_back_kernel(
    which_ref,
    d_down_ref,
    slope_ref,
    active_t_ref,
    shrink_ref,
    expand_ref,
    normed_ref,
    *refs,
    steps,
    block,
    last,
):
    step = pl.program_id(0)
    if last:
        gain_ref, *late_refs = refs[:5]
        grads_ref, bias_ref, d_attn_ref, d_mixed_ref, sums_ref = refs[5:10]
        turned, total, hat_ref, scale_ref, output_proj_ref, sems = refs[10:]
        late = [
            pltpu.make_async_copy(source, target, sems.at[index])
            for index, (source, target) in enumerate(
                zip(late_refs, (d_attn_ref, hat_ref, scale_ref, output_proj_ref))
            )
        ]

        @pl.when(step == 0)
        def _():
            for copy in late:
                copy.start()

    else:
        grads_ref, bias_ref, total_ref, turned, total = refs
    tokens = total.shape[0]
    pieces = [slice(start, start + block) for start in range(0, tokens, block)]

    @pl.when(step == 0)
    def _():
        total[...] = jnp.zeros_like(total)
        bias_ref[...] = jnp.zeros_like(bias_ref)

    bias = jnp.zeros((1, slope_ref.shape[1]), F32)
    for here in pieces:
        d_active = dot(d_down_ref[here, :], shrink_ref[...], NT)
        d_expand = (d_active * slope_ref[here, :].astype(F32)).astype(BF16)
        turned[:, here] = d_expand.T
        bias += jnp.sum(d_expand.astype(F32), 0, keepdims=True)
        total[here, :] += dot(d_expand, expand_ref[...], NT)
    row = lax.broadcasted_iota(jnp.int32, bias_ref.shape, 0)
    bias_ref[...] = jnp.where(row == step, bias, bias_ref[...])
    grads_ref[0] = dot(active_t_ref[...], d_down_ref[...]).astype(BF16)
    grads_ref[1] = dot(turned[...], normed_ref[...]).astype(BF16)

    if not last:

        @pl.when(step == steps - 1)
        def _():
            total_ref[...] = total[...].astype(BF16)

    else:

        @pl.when(step == steps - 1)
        def _():
            for copy in late:
                copy.wait()
            gain = gain_ref[...].astype(F32)
            d_gain = jnp.zeros((1, total.shape[1]), F32)
            d_shift = d_gain
            d_bias = d_gain
            for here in pieces:
                d_normed = total[here, :] + (
                    d_down_ref[here, :].astype(F32) + d_attn_ref[here, :].astype(F32)
                )
                hat = hat_ref[here, :].astype(F32)
                d_gain += jnp.sum(d_normed * hat, 0, keepdims=True)
                d_shift += jnp.sum(d_normed, 0, keepdims=True)
                d_attn = norm_back(d_normed, hat, scale_ref[here, :][:, 0:1], gain).astype(BF16)
                d_attn_ref[here, :] = d_attn
                d_bias += jnp.sum(d_attn.astype(F32), 0, keepdims=True)
                d_mixed_ref[here, :] = dot(d_attn, output_proj_ref[...], NT).astype(BF16)
            sums_ref[...] = stack_rows([d_gain, d_shift, d_bias])


def feed_back(which, d_down, slope, active_t, shrink, expand, normed, norm, block=512):
    tokens, width = d_down.shape
    half = slope.shape[1] // 2
    steps = half // block
    last = norm is not None
    at = lambda i, which: which[0] * steps + i
    whole = lambda *shape: pl.BlockSpec(
        shape, lambda i, which: (0,) * len(shape), pipeline_mode=pl.Buffered(1)
    )
    in_specs = [
        whole(tokens, width),
        pl.BlockSpec((tokens, block), lambda i, which: (0, at(i, which))),
        pl.BlockSpec((block, tokens), lambda i, which: (at(i, which), 0)),
        pl.BlockSpec((block, width), lambda i, which: (at(i, which), 0)),
        pl.BlockSpec((width, block), lambda i, which: (0, at(i, which))),
        whole(tokens, width),
    ]
    out_specs = [
        pl.BlockSpec((2, block, width), lambda i, which: (0, i, 0)),
        whole(8, block),
    ]
    out_shape = hbm_shapes(((2, half, width), BF16), ((8, block), F32))
    scratch = [pltpu.VMEM((block, tokens), BF16), pltpu.VMEM((tokens, width), F32)]
    extra = ()
    if last:
        gain, *late = norm
        extra = (gain, *map(in_hbm, late))
        in_specs += [whole(1, width)] + [pl.BlockSpec(memory_space=pl.ANY)] * len(late)
        out_specs += [whole(tokens, width)] * 2 + [whole(8, width)]
        out_shape += hbm_shapes(
            ((tokens, width), BF16), ((tokens, width), BF16), ((8, width), F32)
        )
        scratch += [
            pltpu.VMEM((tokens, width), BF16),
            pltpu.VMEM((tokens, PAIR), F32),
            pltpu.VMEM((width, width), BF16),
            pltpu.SemaphoreType.DMA((4,)),
        ]
    else:
        out_specs.append(whole(tokens, width))
        out_shape += hbm_shapes(((tokens, width), BF16))
    return pl.pallas_call(
        functools.partial(feed_back_kernel, steps=steps, block=min(512, tokens), last=last),
        grid_spec=pltpu.PrefetchScalarGridSpec(
            num_scalar_prefetch=1,
            grid=(steps,),
            in_specs=in_specs,
            out_specs=out_specs,
            scratch_shapes=scratch,
        ),
        out_shape=out_shape,
        compiler_params=pltpu.CompilerParams(vmem_limit_bytes=44 * 2**20),
        cost_estimate=BRIEF,
        name="feed_back_last" if last else "feed_back",
    )(which, *map(in_hbm, (d_down, slope, active_t, shrink, expand, normed)), *extra)


def pack_kernel(at_ref, flat_ref, marks_ref, *refs, order):
    outs, sems = refs[:-1], refs[-1]
    piece = flat_ref.shape[1]
    for part, out_ref in zip(order, outs):
        marks = marks_ref[pl.ds(at_ref[0] ^ part, 1), :].astype(F32)
        out_ref[piece:, :] = jnp.zeros((MARK_ROWS, out_ref.shape[1]), BF16)
        out_ref[piece:, 0:piece] = jnp.broadcast_to(marks, (MARK_ROWS, piece)).astype(BF16)
    copies = [
        pltpu.make_async_copy(
            flat_ref.at[at_ref[0] ^ part], out_ref.at[pl.ds(0, piece)], sems.at[index]
        )
        for index, (part, out_ref) in enumerate(zip(order, outs))
    ]
    for copy in copies:
        copy.start()
    for copy in copies:
        copy.wait()


MARK_ROWS = 16


def pack(at, flat, marks, order):
    held, piece, width = flat.shape
    vmem = pl.BlockSpec(memory_space=pltpu.VMEM)
    return pl.pallas_call(
        functools.partial(pack_kernel, order=order),
        in_specs=[
            pl.BlockSpec(memory_space=pltpu.SMEM),
            pl.BlockSpec(memory_space=pl.ANY),
            vmem,
        ],
        out_specs=[vmem] * held,
        out_shape=shapes(*[((piece + MARK_ROWS, width), BF16)] * held),
        scratch_shapes=[pltpu.SemaphoreType.DMA((held,))],
        compiler_params=pltpu.CompilerParams(vmem_limit_bytes=16 * 2**20),
        cost_estimate=BRIEF,
        name="pack",
    )(at, in_hbm(flat), marks)


def unpack_kernel(*refs):
    parts, (rows_ref, marks_ref) = refs[:-2], refs[-2:]
    piece = rows_ref.shape[0] // len(parts)
    for index, ref in enumerate(parts):
        here = slice(index * piece, (index + 1) * piece)
        rows_ref[here, :] = ref[0:piece, :]
        marks = ref[piece:, 0:piece].astype(F32)[0:1, :]
        marks_ref[here, :] = jnp.broadcast_to(marks, (PAIR, piece)).T.astype(BF16)


def unpack(parts):
    width = parts[0].shape[1]
    tokens = len(parts) * (parts[0].shape[0] - MARK_ROWS)
    return pl.pallas_call(
        unpack_kernel,
        grid=(1,),
        in_specs=[fixed(*part.shape) for part in parts],
        out_specs=[fixed(tokens, width), fixed(tokens, PAIR)],
        out_shape=hbm_shapes(((tokens, width), BF16), ((tokens, PAIR), BF16)),
        compiler_params=pltpu.CompilerParams(vmem_limit_bytes=16 * 2**20),
        cost_estimate=BRIEF,
        name="unpack",
    )(*parts)


def weight_kernel(
    core_ref,
    first_sums_ref,
    second_sums_ref,
    own_bias_ref,
    other_bias_ref,
    *refs,
    steps,
):
    sources, (other_ref, own_ref, small_ref) = refs[:6], refs[6:9]
    targets, (inputs_t, mixed_t, sems) = refs[9:15], refs[15:]
    inputs_ref, dq_ref, dk_ref, dv_ref, mixed_ref, d_attn_ref = targets
    copies = [
        pltpu.make_async_copy(source, target, sems.at[index])
        for index, (source, target) in enumerate(zip(sources, targets))
    ]
    for copy in copies:
        copy.start()
    count = inputs_ref.shape[1] // 2
    core = core_ref[0]
    for ref in (other_ref, own_ref):
        if ref.shape[0] > 4 * count:
            ref[4 * count :, :] = jnp.zeros((ref.shape[0] - 4 * count, ref.shape[1]), BF16)
    copies[0].wait()
    inputs_t[...] = inputs_ref[...].T
    for at, right_ref in enumerate((dq_ref, dk_ref, dv_ref, d_attn_ref)):
        copies[at + 1].wait()
        left_ref = inputs_t
        if at == 3:
            copies[5].wait()
            mixed_t[...] = mixed_ref[...].T
            left_ref = mixed_t
        for half, out_ref in ((1 - core, other_ref), (core, own_ref)):
            rows = pl.ds(pl.multiple_of(half * count, PAIR), count)
            out_ref[at * count : (at + 1) * count, :] = dot(left_ref[rows, :], right_ref[...]).astype(
                BF16
            )
    small_ref[...] = jnp.zeros_like(small_ref)
    small_ref[0:1, :] = jnp.sum(dq_ref[...].astype(F32), 0, keepdims=True)
    small_ref[1:2, :] = jnp.sum(dv_ref[...].astype(F32), 0, keepdims=True)
    small_ref[2:5, :] = first_sums_ref[0:3, :]
    small_ref[5:8, :] = second_sums_ref[0:3, :]
    block = own_bias_ref.shape[1]
    own, other = own_bias_ref[0:steps, :], other_bias_ref[0:steps, :]
    small_ref[8 : 8 + steps, 0:block] = jnp.where(core == 0, own, other)
    small_ref[8 + steps : 8 + 2 * steps, 0:block] = jnp.where(core == 0, other, own)


def weight_halves(core, values, unit, sums, steps):
    tokens, width = values[0].shape
    rows = -(-2 * width // unit) * unit
    vmem = pl.BlockSpec(memory_space=pltpu.VMEM)
    anywhere = pl.BlockSpec(memory_space=pl.ANY)
    return pl.pallas_call(
        functools.partial(weight_kernel, steps=steps),
        in_specs=[pl.BlockSpec(memory_space=pltpu.SMEM)] + [vmem] * 4 + [anywhere] * 6,
        out_specs=[vmem] * 3,
        out_shape=shapes(
            ((rows, width), BF16), ((rows, width), BF16), ((SMALL, width), F32)
        ),
        scratch_shapes=[pltpu.VMEM((tokens, width), BF16)] * 6
        + [pltpu.VMEM((width, tokens), BF16)] * 2
        + [pltpu.SemaphoreType.DMA((6,))],
        compiler_params=pltpu.CompilerParams(vmem_limit_bytes=32 * 2**20),
        cost_estimate=BRIEF,
        name="weight_halves",
    )(core, *sums, *map(in_hbm, values))


def input_grad_kernel(*refs, held):
    sources, outs = refs[:7], refs[7 : 7 + held]
    (d_attn, *factors), total, sems = refs[7 + held : 14 + held], refs[-2], refs[-1]
    copies = [
        pltpu.make_async_copy(source, target, sems.at[index])
        for index, (source, target) in enumerate(zip(sources, (d_attn, *factors)))
    ]
    for copy in copies:
        copy.start()
    piece = outs[0].shape[0]
    copies[0].wait()
    for index in range(3):
        for copy in copies[2 * index + 1 : 2 * index + 3]:
            copy.wait()
        left, right = factors[2 * index : 2 * index + 2]
        for number, out_ref in enumerate(outs):
            here = slice(number * piece, (number + 1) * piece)
            before = d_attn[here, :].astype(F32) if index == 0 else total[here, :]
            value = before + dot(left[here, :], right[...], NT)
            if index < 2:
                total[here, :] = value
            else:
                out_ref[...] = value.astype(BF16)


def input_grad(d_attn, factors, held):
    tokens, width = d_attn.shape
    anywhere = pl.BlockSpec(memory_space=pl.ANY)
    values = [d_attn] + [value for pair in factors for value in pair]
    return pl.pallas_call(
        functools.partial(input_grad_kernel, held=held),
        in_specs=[anywhere] * 7,
        out_specs=[pl.BlockSpec(memory_space=pltpu.VMEM)] * held,
        out_shape=shapes(*[((tokens // held, width), BF16)] * held),
        scratch_shapes=[pltpu.VMEM(value.shape, BF16) for value in values]
        + [pltpu.VMEM((tokens, width), F32), pltpu.SemaphoreType.DMA((7,))],
        compiler_params=pltpu.CompilerParams(vmem_limit_bytes=24 * 2**20),
        cost_estimate=BRIEF,
        name="input_grad",
    )(*map(in_hbm, values))


def feed_out_kernel(which_ref, half_ref, *refs, steps):
    del which_ref
    shrink_ref, expand_ref = refs[-2:]

    @pl.when(pl.program_id(0) < steps)
    def _():
        shrink_ref[...] = half_ref[...].astype(F32)

    @pl.when(pl.program_id(0) >= steps)
    def _():
        expand_ref[...] = half_ref[...].T.astype(F32)


def feed_out(which, values, before=(), block=512):
    width = values.shape[1]
    half = values.shape[0] // 2
    steps = half // block
    return pl.pallas_call(
        functools.partial(feed_out_kernel, steps=steps),
        grid_spec=pltpu.PrefetchScalarGridSpec(
            num_scalar_prefetch=1,
            grid=(2 * steps,),
            in_specs=[pl.BlockSpec((block, width), lambda i, which: (i, 0))]
            + [pl.BlockSpec(memory_space=pl.ANY)] * len(before),
            out_specs=[
                pl.BlockSpec(
                    (block, width),
                    lambda i, which: (which[0] * steps + jnp.minimum(i, steps - 1), 0),
                ),
                pl.BlockSpec(
                    (width, block),
                    lambda i, which: (0, which[0] * steps + jnp.maximum(i - steps, 0)),
                ),
            ],
        ),
        out_shape=shapes(((2 * half, width), F32), ((width, 2 * half), F32)),
        input_output_aliases={2 + i: i for i in range(len(before))},
        compiler_params=pltpu.CompilerParams(vmem_limit_bytes=16 * 2**20),
        cost_estimate=BRIEF,
        name="feed_out",
    )(which, values, *before)


def attn_out_kernel(which_ref, half_ref, *refs):
    del which_ref
    for index, out_ref in enumerate(refs[-4:]):

        @pl.when(pl.program_id(0) == index)
        def _(out_ref=out_ref):
            out_ref[...] = half_ref[...].astype(F32)


def attn_out(which, values, before=()):
    width = values.shape[1]
    half = width // 2
    return pl.pallas_call(
        attn_out_kernel,
        grid_spec=pltpu.PrefetchScalarGridSpec(
            num_scalar_prefetch=1,
            grid=(4,),
            in_specs=[pl.BlockSpec((half, width), lambda i, which: (i, 0))]
            + [pl.BlockSpec(memory_space=pl.ANY)] * len(before),
            out_specs=[pl.BlockSpec((half, width), lambda i, which: (which[0], 0))] * 4,
        ),
        out_shape=shapes(*[((width, width), F32)] * 4),
        input_output_aliases={2 + i: i for i in range(len(before))},
        compiler_params=pltpu.CompilerParams(vmem_limit_bytes=24 * 2**20),
        cost_estimate=BRIEF,
        name="attn_out",
    )(which, values, *before)


def place_kernel(at_ref, *refs):
    del at_ref
    out_ref = refs[-1]
    for index, ref in enumerate(refs[:-1]):

        @pl.when(pl.program_id(0) == index)
        def _(ref=ref):
            out_ref[0] = ref[...]


def place(at, parts):
    piece, width = parts[0].shape
    held = len(parts)
    return pl.pallas_call(
        place_kernel,
        grid_spec=pltpu.PrefetchScalarGridSpec(
            num_scalar_prefetch=1,
            grid=(held,),
            in_specs=[pl.BlockSpec((piece, width), lambda i, at: (0, 0))] * held,
            out_specs=pl.BlockSpec((1, piece, width), lambda i, at: (at[0] ^ i, 0, 0)),
        ),
        out_shape=jax.ShapeDtypeStruct((held, piece, width), BF16),
        compiler_params=pltpu.CompilerParams(vmem_limit_bytes=16 * 2**20),
        cost_estimate=BRIEF,
        name="place",
    )(at, *parts)


def rows_of(ref, which, count, base=0):
    return ref[pl.ds(pl.multiple_of(base + which * count, 16), count), :]


def sum_of(terms):
    return functools.reduce(lambda a, b: a + b, [t.astype(F32) for t in terms]).astype(BF16)


def scatter_kernel(bits_ref, *refs, groups):
    outs = refs[-2 * groups :]
    ins = refs[: -2 * groups]
    together = len(ins) == 2
    base = 0
    for group in range(groups):
        terms = ins if together else ins[2 * group : 2 * group + 2]
        sent_ref, kept_ref = outs[2 * group : 2 * group + 2]
        count = kept_ref.shape[0]
        here = bits_ref[group]
        sent_ref[...] = sum_of([rows_of(term, 1 - here, count, base) for term in terms])
        kept_ref[...] = sum_of([rows_of(term, here, count, base) for term in terms])
        if together:
            base += 2 * count


def local_call(kernel, bits, values, out_shape, name):
    vmem = pl.BlockSpec(memory_space=pltpu.VMEM)
    return pl.pallas_call(
        kernel,
        in_specs=[pl.BlockSpec(memory_space=pltpu.SMEM)] + [vmem] * len(values),
        out_specs=[vmem] * len(out_shape),
        out_shape=out_shape,
        compiler_params=pltpu.CompilerParams(vmem_limit_bytes=24 * 2**20),
        cost_estimate=BRIEF,
        name=name,
    )(bits, *values)


def scatter_local(bits, pairs, counts=None):
    if counts is None:
        counts = [kept.shape[0] for kept, _ in pairs]
    groups = len(counts)
    counts = [count // 2 for count in counts]
    width = pairs[0][0].shape[1]
    outs = local_call(
        functools.partial(scatter_kernel, groups=groups),
        bits,
        [value for pair in pairs for value in pair],
        shapes(*[((count, width), BF16) for count in counts for _ in range(2)]),
        "scatter_local",
    )
    return [outs[2 * i : 2 * i + 2] for i in range(groups)]


def scatter_first_kernel(bits_ref, own_at, got_at, *refs, counts):
    outs, (own, got, sems) = refs[:-3], refs[-3:]
    spans = []
    base = 0
    for group, count in enumerate(counts):
        for kept in range(2):
            half = bits_ref[group] if kept else 1 - bits_ref[group]
            start = pl.multiple_of(base + half * (count // 2), 16)
            spans.append((start, count // 2, outs[2 * group + kept]))
        base += count
    spans = spans[0::2] + spans[1::2]
    copies = []
    for index, (start, count, _) in enumerate(spans):
        rows = pl.ds(start, count)
        for which, (source, target) in enumerate(((own_at, own), (got_at, got))):
            copies.append(
                pltpu.make_async_copy(source.at[rows], target.at[rows], sems.at[2 * index + which])
            )
            copies[-1].start()
    for index, (start, count, out_ref) in enumerate(spans):
        for copy in copies[2 * index : 2 * index + 2]:
            copy.wait()
        rows = pl.ds(start, count)
        out_ref[...] = sum_of([own[rows, :], got[rows, :]])


def scatter_first(bits, own, got, counts):
    rows, width = own.shape
    anywhere = pl.BlockSpec(memory_space=pl.ANY)
    vmem = pl.BlockSpec(memory_space=pltpu.VMEM)
    outs = pl.pallas_call(
        functools.partial(scatter_first_kernel, counts=counts),
        in_specs=[pl.BlockSpec(memory_space=pltpu.SMEM), anywhere, anywhere],
        out_specs=[vmem] * (2 * len(counts)),
        out_shape=shapes(*[((count // 2, width), BF16) for count in counts for _ in range(2)]),
        scratch_shapes=[pltpu.VMEM((rows, width), BF16)] * 2
        + [pltpu.SemaphoreType.DMA((4 * len(counts),))],
        compiler_params=pltpu.CompilerParams(vmem_limit_bytes=24 * 2**20),
        cost_estimate=BRIEF,
        name="scatter_first",
    )(bits, in_hbm(own), in_hbm(got))
    return [outs[2 * group : 2 * group + 2] for group in range(len(counts))]


SMALL = 16


def put_small(ref, at, values):
    ref[at : at + SMALL, :] = values.astype(BF16)


def get_small(ref, at):
    return ref[at : at + SMALL, :].astype(F32)


def settle_kernel(bits_ref, *refs, groups, small):
    del bits_ref
    ins, outs = refs[: 2 * groups], refs[2 * groups + small :]
    for group in range(groups):
        count = ins[2 * group].shape[0]
        outs[group][0:count, :] = sum_of([ins[2 * group][...], ins[2 * group + 1][...]])
        if small and group == 0:
            put_small(outs[group], count, refs[2 * groups][...])


def settle_local(bits, pairs, small):
    width = pairs[0][0].shape[1]
    counts = [kept.shape[0] for kept, _ in pairs]
    if small is not None:
        counts[0] += SMALL
    return local_call(
        functools.partial(settle_kernel, groups=len(pairs), small=int(small is not None)),
        bits,
        [value for pair in pairs for value in pair] + ([] if small is None else [small]),
        shapes(*[((count, width), BF16) for count in counts]),
        "settle_local",
    )


def add_kernel(bits_ref, *refs, groups, small):
    del bits_ref
    ins, outs = refs[: 2 * groups], refs[2 * groups :]
    for group in range(groups):
        own_ref, got_ref = ins[2 * group : 2 * group + 2]
        extra = SMALL if small and group == 0 else 0
        count = own_ref.shape[0] - extra
        outs[group][0:count, :] = sum_of([own_ref[0:count, :], got_ref[0:count, :]])
        if extra:
            put_small(outs[group], count, get_small(own_ref, count) + get_small(got_ref, count))


def add_local(bits, pairs, small):
    return local_call(
        functools.partial(add_kernel, groups=len(pairs), small=small),
        bits,
        [value for pair in pairs for value in pair],
        shapes(*[(own.shape, BF16) for own, _ in pairs]),
        "add_local",
    )


def join_kernel(bits_ref, *refs, groups, small, merged, pieces):
    ins, outs = refs[: 2 * pieces * groups], list(refs[2 * pieces * groups :])
    parts = len(outs) // groups
    base = 0
    for group in range(groups):
        owns = ins[2 * pieces * group : 2 * pieces * group + 2 * pieces : 2]
        gots = ins[2 * pieces * group + 1 : 2 * pieces * group + 2 * pieces : 2]
        extra = SMALL if small and group == 0 else 0
        count = owns[0].shape[0] - extra
        here = bits_ref[group]
        if parts > 1:
            for half, out_ref in enumerate(outs[2 * group : 2 * group + 2]):

                @pl.when(here == half)
                def _(out_ref=out_ref):
                    out_ref[...] = owns[0][...]

                @pl.when(here != half)
                def _(out_ref=out_ref):
                    out_ref[...] = gots[0][...]

            continue
        out_ref = outs[0 if merged else group]
        whole = count * pieces
        for half, refs_of in ((here, owns), (1 - here, gots)):
            for index, ref in enumerate(refs_of):
                start = pl.multiple_of(base + half * whole + index * count, 16)
                out_ref[pl.ds(start, count), :] = ref[0:count, :]
        if extra:
            at = out_ref.shape[0] - SMALL if merged else base + 2 * whole
            put_small(out_ref, at, get_small(owns[0], count) + get_small(gots[0], count))
        if merged:
            base += 2 * whole


def join_local(bits, arrived, small, merged, parts=1):
    width = arrived[0][0].shape[1]
    pieces = len(arrived[0]) // 2
    counts = [2 * pieces * group[0].shape[0] for group in arrived]
    if small:
        counts[0] -= SMALL
    if merged:
        counts = [sum(counts)]
    counts = [count // parts for count in counts for _ in range(parts)]
    return local_call(
        functools.partial(
            join_kernel, groups=len(arrived), small=small, merged=merged, pieces=pieces
        ),
        bits,
        [value for group in arrived for value in group],
        shapes(*[((count, width), BF16) for count in counts]),
        "join_local",
    )


def tie(*values):
    return lax.optimization_barrier(values)


def pick(which, parts):
    if len(parts) == 1:
        return parts[0]
    half = len(parts) // 2
    return jnp.where(which < half, pick(which, parts[:half]), pick(which - half, parts[half:]))


def column_sum(values):
    return jnp.sum(values.astype(F32), 0)


class Stage:
    def __init__(self, sizes, bits):
        self.bits = bits
        rows, seq = sizes
        self.pairs = []
        for index in range(rows * seq):
            axis, bit = bits[index & 1]
            self.pairs.append((index, index ^ ((1 << bit) * (seq if axis == "rows" else 1))))

    def here(self):
        first, second = [(lax.axis_index(axis) >> bit) & 1 for axis, bit in self.bits]
        if self.bits[0] == self.bits[1]:
            return first
        return jnp.where(lax.axis_index("seq") & 1 == 0, first, second)

    def swap(self, values):
        return lax.ppermute(values, ("rows", "seq"), self.pairs)


def total_over_chips(own, got, core_stage, orders, small=None, near=False):
    depth = len(orders[0][1])
    groups = range(len(orders))

    def bits_at(step):
        return jnp.stack([stages[step].here() for _, stages in orders]).astype(jnp.int32)

    def pairs_of(flat):
        return [flat[i : i + 2] for i in range(0, len(flat), 2)]

    def send(step, values, keep):
        flat = []
        for group in groups:
            flat += [keep[group], orders[group][1][step].swap(values[group])]
        return flat

    counts = [count for count, _ in orders]
    if near:
        parts = scatter_local(bits_at(0), [[own, got]], counts)
    else:
        parts = scatter_first(bits_at(0), own, got, counts)
    last = depth - 1 if near else depth
    for step in range(1, last + 1):
        flat = yield send(step - 1, [p[0] for p in parts], [p[1] for p in parts])
        if step < last:
            parts = scatter_local(bits_at(step), pairs_of(flat))
    values = settle_local(bits_at(0), pairs_of(flat), small)
    if near:
        flat = yield send(last, values, values)
        values = add_local(bits_at(0), pairs_of(flat), small is not None)
    carried = small is not None
    for step in reversed(range(last)):
        flat = yield send(step, values, values)
        parts = 2 if step == 1 and not carried else 1
        values = join_local(bits_at(step), pairs_of(flat), carried, step == 0, parts)
        if parts > 1:
            lower = yield send(0, values[0::2], values[0::2])
            upper = yield send(0, values[1::2], values[1::2])
            arrived = [list(low) + list(high) for low, high in zip(pairs_of(lower), pairs_of(upper))]
            values = join_local(bits_at(0), arrived, carried, True)
            break
    both = yield [values[0], core_stage.swap(values[0])]
    return both


def arriving(values):
    values = yield values
    return values[1::2]


class Flow:
    def __init__(self, steps, left):
        self.steps = steps
        self.left = left
        self.pending = next(steps)
        self.result = None


class Timetable:
    def __init__(self):
        self.flows = []

    def open(self, steps, left=1):
        self.flows.append(Flow(steps, left))
        return self.flows[-1]

    def advance(self, moving, *values):
        flows = [flow for flow in self.flows if flow.result is None]
        held = [flow.pending if flow in moving else flow.pending[0::2] for flow in flows]
        tied = list(tie(*values, *[value for part in held for value in part]))
        values, tied = tied[: len(values)], tied[len(values) :]
        for flow, part in zip(flows, held):
            back, tied = tied[: len(part)], tied[len(part) :]
            if flow not in moving:
                flow.pending[0::2] = back
                continue
            flow.left -= 1
            try:
                flow.pending = flow.steps.send(back)
            except StopIteration as end:
                flow.result = end.value
        return self.settle(*values) if moving and values else values

    def settle(self, *values):
        return self.advance([], *values)


def solution(mesh):
    seq_size = mesh.shape["seq"]
    rows_size = mesh.shape["rows"]
    seq_bits = seq_size.bit_length() - 1
    rows_bits = rows_size.bit_length() - 1
    off_chip = [("seq", bit) for bit in range(1, seq_bits)]
    off_chip += [("rows", bit) for bit in range(rows_bits)]
    first, *middle, ahead, final = off_chip
    sizes = (rows_size, seq_size)
    core_stage = Stage(sizes, [("seq", 0)] * 2)
    straight = [first] + middle + [ahead, final]
    turned = middle + [ahead, first, final]
    spun = [ahead, first] + middle + [final]
    wide = [Stage(sizes, bits) for bits in zip(straight, turned)]
    slim = [Stage(sizes, bits) for bits in zip(spun, spun)]

    def body(
        hidden_in,
        segments,
        grad_mask,
        grad_out,
        query_proj,
        query_bias,
        key_proj,
        value_proj,
        value_bias,
        output_proj,
        output_bias,
        first_gain,
        first_shift,
        expand_proj,
        expand_bias,
        shrink_proj,
        shrink_bias,
        second_gain,
        second_shift,
    ):
        micro, rows_here, piece, width = hidden_in.shape
        held = micro * rows_here
        sharers = seq_size // held
        tokens = held * piece
        source_at = lax.axis_index("seq") % held
        core = core_stage.here()
        core_at = core.reshape(1).astype(jnp.int32)

        def trade(to_rows, part):
            there = [(s, (s % held ^ part) * sharers + s // held) for s in range(seq_size)]
            return there if to_rows else [(b, a) for a, b in there]

        def to_rows(values):
            return [
                lax.ppermute(
                    lax.dynamic_index_in_dim(values, source_at ^ part, 0, False),
                    "seq",
                    trade(True, part),
                )
                for part in range(held)
            ]

        def send_pieces(values, chosen=range(held)):
            return [
                value
                for part in chosen
                for value in (values[part], lax.ppermute(values[part], "seq", trade(False, part)))
            ]

        def place_pieces(parts):
            at = source_at.reshape(1).astype(jnp.int32)
            return place(at, parts).reshape((micro, rows_here) + parts[0].shape)

        same_row = [[r * sharers + g for g in range(sharers)] for r in range(held)]

        def all_keys(values):
            if sharers == 1:
                return values
            return lax.all_gather(values, "seq", axis=0, tiled=True, axis_index_groups=same_row)

        def own_keys(values):
            if sharers == 1:
                return values
            return lax.psum_scatter(
                values, "seq", scatter_dimension=0, tiled=True, axis_index_groups=same_row
            ).astype(BF16)

        order = tuple(reversed(range(held)))
        packed = pack(
            source_at.reshape(1).astype(jnp.int32),
            hidden_in.reshape(held, piece, width),
            segments.reshape(held, piece),
            order,
        )
        arrived = [
            lax.ppermute(value, "seq", trade(True, part)) for part, value in zip(order, packed)
        ]
        inputs, seg_q = unpack(arrived[::-1])
        masked = (grad_out * grad_mask[..., None].astype(BF16)).reshape(held, piece, width)
        masked, inputs, seg_q = tie(masked, inputs, seg_q)
        upstream = to_rows(masked)

        queries = (
            (dot(inputs, query_proj) + query_bias.astype(F32)) * 0.125
        ).astype(BF16)
        keys = all_keys(dot(inputs, key_proj).astype(BF16))
        values = all_keys((dot(inputs, value_proj) + value_bias.astype(F32)).astype(BF16))
        seg_k = all_keys(seg_q)
        mixed, query_side = attention_forward(queries, keys, values, seg_q, seg_k)
        row = lambda vector: vector.reshape(1, -1)
        hat, scale, normed, active_t, slope, d_down, second_sums, *result = feed_forward(
            inputs,
            mixed,
            upstream,
            (
                output_proj,
                row(output_bias),
                row(first_gain),
                row(first_shift),
                expand_proj,
                row(expand_bias),
                shrink_proj,
                row(shrink_bias),
                row(second_gain),
                row(second_shift),
            ),
        )
        table = Timetable()
        advance = table.advance
        layer_flow = table.open(arriving(send_pieces(result)))

        def chips(own, got, orders, small=None):
            near = small is not None
            steps = total_over_chips(own, got, core_stage, orders, small, near)
            return table.open(steps, 2 * len(wide) + (0 if near else 2))

        back = functools.partial(
            feed_back,
            slope=slope,
            active_t=active_t,
            shrink=shrink_proj,
            expand=expand_proj,
            normed=normed,
        )
        other, other_bias, d_normed = back(1 - core_at, d_down, norm=None)
        half = other.shape[1]
        got = core_stage.swap(other.reshape(2 * half, width))
        own, own_bias, d_attn, d_mixed, first_sums = back(
            core_at, d_down, norm=(row(first_gain), d_normed, hat, scale, output_proj)
        )
        own, got, d_mixed = advance([layer_flow], own.reshape(2 * half, width), got, d_mixed)
        unit = 16 << len(off_chip)

        def thirds(count):
            less = count // unit // 3 * unit
            return [(count - less, wide)] + ([(less, slim)] if less else [])

        feed_flow = chips(own, got, thirds(2 * half))

        pairs = width // PAIR
        kept = BF16 if sharers == 1 else F32
        grads = None
        for first, last in ((0, pairs),):
            grads = attention_backward(
                query_side, keys, values, seg_k, mixed, d_mixed, kept, first, last - first, grads
            )
            *grads, d_mixed = advance([feed_flow], *grads, d_mixed)

        d_query, d_keys, d_values = grads
        d_key = own_keys(d_keys)
        d_value = own_keys(d_values)
        steps = half // other_bias.shape[1]
        other, own, small = weight_halves(
            core_at,
            (inputs, d_query, d_key, d_value, mixed, d_attn),
            unit,
            (first_sums, second_sums, own_bias, other_bias),
            steps,
        )
        other, own, small, d_query, d_key, d_value = advance(
            [feed_flow], other, own, small, d_query, d_key, d_value
        )
        got = core_stage.swap(other)
        d_input = input_grad(
            d_attn, ((d_query, query_proj), (d_key, key_proj), (d_value, value_proj)), held
        )
        own, got, small, *d_input = advance([feed_flow], own, got, small, *d_input)
        attn_flow = chips(own, got, [(own.shape[0], wide)], small)
        held_back = held // 2
        soon = [part for part in range(held) if part != held_back]
        piece_flow = table.open(arriving(send_pieces(d_input, soon)))
        last_flow = table.open(arriving(send_pieces(d_input, [held_back])))

        both = [feed_flow, attn_flow]
        layer_out = place_pieces(list(map(in_hbm, layer_flow.result)))
        (layer_out,) = advance(both, layer_out)
        advance(both + [piece_flow])
        advance(both)
        advance(both + [last_flow])
        arrived = list(piece_flow.result)
        arrived.insert(held_back, last_flow.result[0])
        grad_in = place_pieces(arrived)
        (grad_in,) = advance(both, grad_in)
        while feed_flow.left > 1:
            advance(both)
        feed_grads = feed_out(core_at, feed_flow.pending[0])
        feed_grads = advance(both, *feed_grads)
        feed_grads = feed_out(1 - core_at, feed_flow.result[1], feed_grads)
        while attn_flow.left > 1:
            feed_grads = advance([attn_flow], *feed_grads)
        attn_grads = attn_out(core_at, attn_flow.pending[0])
        attn_grads = advance([attn_flow], *attn_grads)
        own, got = attn_flow.result
        attn_grads = attn_out(1 - core_at, got, attn_grads)
        totals = own[-SMALL:].astype(F32) + got[-SMALL:].astype(F32)
        shrink_grad, expand_grad = feed_grads
        expand_bias_grad = totals[8 : 8 + 2 * steps, : other_bias.shape[1]].reshape(-1)
        return (
            layer_out,
            grad_in,
            attn_grads[0],
            totals[0],
            attn_grads[1],
            attn_grads[2],
            totals[1],
            attn_grads[3],
            totals[4],
            totals[2],
            totals[3],
            expand_grad,
            expand_bias_grad,
            shrink_grad,
            totals[7],
            totals[5],
            totals[6],
        )

    split = P(None, "rows", "seq", None)
    whole = P()
    return jax.shard_map(
        body,
        mesh=mesh,
        in_specs=(split, P(None, "rows", "seq"), P(None, "rows", "seq"), split) + (whole,) * 15,
        out_specs=(split, split) + (whole,) * 15,
        check_vma=False,
    )
```

```python
import functools

import jax
import jax.numpy as jnp
from jax import lax
from jax.experimental import pallas as pl
from jax.experimental.pallas import tpu as pltpu
from jax.sharding import PartitionSpec as P

DH = 64
PAIR = 128
MASKED = 1e30
F32 = jnp.float32
BF16 = jnp.bfloat16
NT = (((1,), (1,)), ((), ()))
NN = (((1,), (0,)), ((), ()))
BRIEF = pl.CostEstimate(flops=1, bytes_accessed=1, transcendentals=0)


def left_dot(first, second):
    return lax.dot_general(first, second, (((0,), (0,)), ((), ())), preferred_element_type=F32)


def right_dot(first, second):
    return lax.dot_general(first, second, NT, preferred_element_type=F32)


def split_three(values):
    high = values.astype(BF16)
    rest = values - high.astype(F32)
    middle = rest.astype(BF16)
    low = (rest - middle.astype(F32)).astype(BF16)
    return high.astype(F32), middle.astype(F32), low.astype(F32)


def own_lanes(shape, head):
    lane = lax.broadcasted_iota(jnp.int32, shape, 1)
    own = lane < DH if head == 0 else lane >= DH
    return own, lane % DH


def key_features(lane, seg):
    return jnp.where(
        lane < 3,
        1.0,
        jnp.where(lane == 3, -MASKED * (1.0 - seg), jnp.where(lane == 4, -MASKED * seg, 0.0)),
    ).astype(BF16)


def forward_kernel(q_ref, k_ref, v_ref, seg_q_ref, seg_k_ref, mixed_ref, query_ref, *, block):
    queries = q_ref.shape[0]
    keys = k_ref.shape[0]
    for head in range(2):
        own_k, lane_k = own_lanes((keys, PAIR), head)
        key_side = jnp.where(own_k, k_ref[...], key_features(lane_k, seg_k_ref[...].astype(F32)))
        value_side = jnp.where(own_k, v_ref[...], jnp.ones((), BF16))
        own_q, lane_q = own_lanes((block, PAIR), head)
        for start in range(0, queries, block):
            here = slice(start, start + block)
            q = q_ref[here, :]
            seg = seg_q_ref[here, :].astype(F32)
            seg_side = jnp.where(lane_q == 3, seg, jnp.where(lane_q == 4, 1.0 - seg, 0.0))
            query_side = jnp.where(own_q, q, seg_side.astype(BF16))
            scores = lax.dot_general(query_side, key_side, NT, preferred_element_type=F32)
            peak = jnp.max(scores, -1, keepdims=True)
            raised = jnp.exp(scores - peak).astype(BF16)
            summed = lax.dot_general(raised, value_side, NN, preferred_element_type=F32)
            total = summed[:, DH : DH + 1] if head == 0 else summed[:, 0:1]
            mixed = (summed / total).astype(BF16)
            shift = jnp.broadcast_to(-(peak + jnp.log(total)), (block, PAIR))
            high, middle, low = split_three(shift)
            extra = jnp.where(
                lane_q == 0,
                high,
                jnp.where(lane_q == 1, middle, jnp.where(lane_q == 2, low, seg_side)),
            )
            query_ref[head, here, :] = jnp.where(own_q, q, extra.astype(BF16))
            if head == 0:
                mixed_ref[here, :] = mixed
            else:
                mixed_ref[here, :] = jnp.where(own_q, mixed, mixed_ref[here, :])


def attention_forward(q, k, v, seg_q, seg_k):
    queries, width = q.shape
    keys = k.shape[0]
    pairs = width // PAIR
    column = lambda i: (0, i)
    whole = lambda i: (0, 0)
    return pl.pallas_call(
        functools.partial(forward_kernel, block=min(512, queries)),
        grid=(pairs,),
        in_specs=[
            pl.BlockSpec((queries, PAIR), column),
            pl.BlockSpec((keys, PAIR), column),
            pl.BlockSpec((keys, PAIR), column),
            pl.BlockSpec((queries, PAIR), whole),
            pl.BlockSpec((keys, PAIR), whole),
        ],
        out_specs=[
            pl.BlockSpec((queries, PAIR), column),
            pl.BlockSpec((2, queries, PAIR), lambda i: (i, 0, 0)),
        ],
        out_shape=[
            pltpu.HBM((queries, width), BF16),
            pltpu.HBM((2 * pairs, queries, PAIR), BF16),
        ],
        compiler_params=pltpu.CompilerParams(vmem_limit_bytes=24 * 2**20),
        cost_estimate=BRIEF,
        name="attention_forward",
    )(q, k, v, seg_q, seg_k)


def backward_kernel(
    query_ref, k_ref, v_ref, seg_k_ref, mixed_ref, d_mixed_ref, *refs, block
):
    dq_ref, dk_ref, dv_ref, dqt = refs[-4:]
    queries = mixed_ref.shape[0]
    keys = k_ref.shape[0]
    d_mixed = d_mixed_ref[...]
    product = d_mixed.astype(F32) * mixed_ref[...].astype(F32)
    for head in range(2):
        own_q, lane_q = own_lanes((queries, PAIR), head)
        own_k, lane_k = own_lanes((block, PAIR), head)
        delta = -jnp.sum(jnp.where(own_q, product, 0.0), -1, keepdims=True)
        high, middle, low = split_three(jnp.broadcast_to(delta, (queries, PAIR)))
        extra = jnp.where(
            lane_q == 0, high, jnp.where(lane_q == 1, middle, jnp.where(lane_q == 2, low, 0.0))
        )
        d_side = jnp.where(own_q, d_mixed, extra.astype(BF16))
        query_side = query_ref[head]
        ones = jnp.where(lane_k < 3, 1.0, 0.0).astype(BF16)
        for start in range(0, keys, block):
            here = slice(start, start + block)
            k = k_ref[here, :]
            seg = seg_k_ref[here, :].astype(F32)
            key_side = jnp.where(own_k, k, key_features(lane_k, seg))
            value_side = jnp.where(own_k, v_ref[here, :], ones)
            shifted = lax.dot_general(key_side, query_side, NT, preferred_element_type=F32)
            probs = jnp.exp(shifted)
            d_probs = lax.dot_general(value_side, d_side, NT, preferred_element_type=F32)
            d_scores = (probs * d_probs).astype(BF16)
            dv = lax.dot_general(probs.astype(BF16), d_mixed, NN, preferred_element_type=F32)
            dk = lax.dot_general(d_scores, query_side, NN, preferred_element_type=F32)
            turned = k.T[head * DH : (head + 1) * DH, :]
            dq = lax.dot_general(turned, d_scores, NN, preferred_element_type=F32)
            mine = slice(head * DH, (head + 1) * DH)
            if start == 0:
                dqt[mine, :] = dq
            else:
                dqt[mine, :] += dq
            dv = dv.astype(dv_ref.dtype)
            dk = dk.astype(dk_ref.dtype)
            if head == 0:
                dk_ref[here, :] = dk
                dv_ref[here, :] = dv
            else:
                dk_ref[here, :] = jnp.where(own_k, dk, dk_ref[here, :])
                dv_ref[here, :] = jnp.where(own_k, dv, dv_ref[here, :])
    dq_ref[...] = (dqt[...] * 0.125).astype(BF16).T


def attention_backward(query_side, k, v, seg_k, mixed, d_mixed, kept, first, count, before):
    queries, width = mixed.shape
    keys = k.shape[0]
    column = lambda i: (0, i + first)
    held = [] if before is None else list(before)
    return pl.pallas_call(
        functools.partial(backward_kernel, block=min(512, keys)),
        grid=(count,),
        in_specs=[
            pl.BlockSpec((2, queries, PAIR), lambda i: (i + first, 0, 0)),
            pl.BlockSpec((keys, PAIR), column),
            pl.BlockSpec((keys, PAIR), column),
            pl.BlockSpec((keys, PAIR), lambda i: (0, 0)),
            pl.BlockSpec((queries, PAIR), column),
            pl.BlockSpec((queries, PAIR), column),
        ]
        + [pl.BlockSpec(memory_space=pl.ANY)] * len(held),
        out_specs=[
            pl.BlockSpec((queries, PAIR), column),
            pl.BlockSpec((keys, PAIR), column),
            pl.BlockSpec((keys, PAIR), column),
        ],
        input_output_aliases={6 + i: i for i in range(len(held))},
        out_shape=[
            pltpu.HBM((queries, width), BF16),
            pltpu.HBM((keys, width), kept),
            pltpu.HBM((keys, width), kept),
        ],
        scratch_shapes=[pltpu.VMEM((PAIR, queries), F32)],
        compiler_params=pltpu.CompilerParams(vmem_limit_bytes=24 * 2**20),
        cost_estimate=BRIEF,
        name="attention_backward",
    )(in_hbm(query_side), k, v, seg_k, in_hbm(mixed), in_hbm(d_mixed), *map(in_hbm, held))


def dot(first, second, dims=NN):
    return lax.dot_general(first, second, dims, preferred_element_type=F32)


def gelu_pair(values):
    below = 0.5 + 0.5 * lax.erf(values * 0.7071067811865476)
    density = jnp.exp(-0.5 * values * values) * 0.3989422804014327
    return values * below, below + values * density


def normalise(values):
    centred = values - jnp.mean(values, -1, keepdims=True)
    scale = lax.rsqrt(jnp.mean(centred * centred, -1, keepdims=True) + 1e-06)
    return centred * scale, scale


def norm_back(upstream, hat, scale, gain):
    d_hat = upstream * gain
    return scale * (
        d_hat
        - jnp.mean(d_hat, -1, keepdims=True)
        - hat * jnp.mean(d_hat * hat, -1, keepdims=True)
    )


def stack_rows(rows):
    filler = jnp.zeros((8 - len(rows), rows[0].shape[1]), F32)
    return jnp.concatenate(rows + [filler], 0)


def feed_forward_kernel(
    inputs_ref,
    mixed_ref,
    output_proj_ref,
    output_bias_ref,
    gain_one_ref,
    shift_one_ref,
    expand_ref,
    expand_bias_ref,
    shrink_ref,
    shrink_bias_ref,
    gain_two_ref,
    shift_two_ref,
    *refs,
    steps,
    held,
):
    upstream_refs = refs[:held]
    hat_out, scale_ref, normed_out, active_t_ref, slope_ref = refs[held : held + 5]
    d_down_out, sums_ref = refs[held + 5 : held + 7]
    outs = refs[held + 7 : 2 * held + 7]
    total, hat_ref, normed_ref, d_down_ref, out_ref, sems = refs[2 * held + 7 :]
    block = total.shape[0] // held
    early = [
        pltpu.make_async_copy(hat_ref, hat_out, sems.at[0]),
        pltpu.make_async_copy(normed_ref, normed_out, sems.at[1]),
    ]
    late = []
    for index, out in enumerate(outs):
        rows = pl.ds(index * block, block)
        late.append(pltpu.make_async_copy(out_ref.at[rows], out, sems.at[2 + 2 * index]))
        late.append(
            pltpu.make_async_copy(d_down_ref.at[rows], d_down_out.at[rows], sems.at[3 + 2 * index])
        )
    step = pl.program_id(0)
    tokens = total.shape[0]
    pieces = [slice(start, start + block) for start in range(0, tokens, block)]

    @pl.when(step == 0)
    def _():
        for here in pieces:
            first_sum = (
                inputs_ref[here, :].astype(F32)
                + dot(mixed_ref[here, :], output_proj_ref[...])
                + output_bias_ref[...].astype(F32)
            )
            hat, scale = normalise(first_sum)
            hat_ref[here, :] = hat.astype(BF16)
            scale_ref[here, :] = jnp.broadcast_to(scale, (block, PAIR))
            normed = gain_one_ref[...].astype(F32) * hat + shift_one_ref[...].astype(F32)
            normed_ref[here, :] = normed.astype(BF16)
            total[here, :] = normed + shrink_bias_ref[...].astype(F32)
        for copy in early:
            copy.start()

    for here in pieces:
        expanded = dot(normed_ref[here, :], expand_ref[...]) + expand_bias_ref[...].astype(F32)
        active, slope = gelu_pair(expanded)
        active = active.astype(BF16)
        slope_ref[here, :] = slope.astype(BF16)
        active_t_ref[:, here] = active.T
        total[here, :] += dot(active, shrink_ref[...])

    @pl.when(step == steps - 1)
    def _():
        gain = gain_two_ref[...].astype(F32)
        d_gain = jnp.zeros((1, total.shape[1]), F32)
        d_shift = d_gain
        d_bias = d_gain
        for index, (here, upstream_ref) in enumerate(zip(pieces, upstream_refs)):
            hat, scale = normalise(total[here, :])
            out_ref[here, :] = (gain * hat + shift_two_ref[...].astype(F32)).astype(BF16)
            late[2 * index].start()
            upstream = upstream_ref[...].astype(F32)
            d_gain += jnp.sum(upstream * hat, 0, keepdims=True)
            d_shift += jnp.sum(upstream, 0, keepdims=True)
            d_down = norm_back(upstream, hat, scale, gain).astype(BF16)
            d_down_ref[here, :] = d_down
            late[2 * index + 1].start()
            d_bias += jnp.sum(d_down.astype(F32), 0, keepdims=True)
        sums_ref[...] = stack_rows([d_gain, d_shift, d_bias])
        for copy in early + late:
            copy.wait()


def in_hbm(values):
    return pltpu.with_memory_space_constraint(values, pltpu.HBM)


def hbm_shapes(*pairs):
    return [pltpu.HBM(shape, dtype) for shape, dtype in pairs]


def fixed(*shape):
    return pl.BlockSpec(shape, lambda i: (0,) * len(shape), pipeline_mode=pl.Buffered(1))


def shapes(*pairs):
    return [jax.ShapeDtypeStruct(shape, dtype) for shape, dtype in pairs]


def feed_forward(inputs, mixed, upstream, weights, block=768):
    tokens, width = inputs.shape
    units = weights[4].shape[1]
    steps = units // block
    held = len(upstream)
    piece = tokens // held
    row = fixed(1, width)
    return pl.pallas_call(
        functools.partial(feed_forward_kernel, steps=steps, held=held),
        grid=(steps,),
        in_specs=[fixed(tokens, width)] * 2
        + [fixed(width, width), row, row, row]
        + [
            pl.BlockSpec((width, block), lambda i: (0, i)),
            pl.BlockSpec((1, block), lambda i: (0, i)),
            pl.BlockSpec((block, width), lambda i: (i, 0)),
            row,
            row,
            row,
        ]
        + [fixed(piece, width)] * held,
        out_specs=[
            pl.BlockSpec(memory_space=pl.ANY),
            fixed(tokens, PAIR),
            pl.BlockSpec(memory_space=pl.ANY),
            pl.BlockSpec((block, tokens), lambda i: (i, 0)),
            pl.BlockSpec((tokens, block), lambda i: (0, i)),
            pl.BlockSpec(memory_space=pl.ANY),
            fixed(8, width),
        ]
        + [pl.BlockSpec(memory_space=pl.ANY)] * held,
        out_shape=hbm_shapes(
            ((tokens, width), BF16),
            ((tokens, PAIR), F32),
            ((tokens, width), BF16),
            ((units, tokens), BF16),
            ((tokens, units), BF16),
            ((tokens, width), BF16),
            ((8, width), F32),
            *[((piece, width), BF16)] * held,
        ),
        scratch_shapes=[
            pltpu.VMEM((tokens, width), F32),
            pltpu.VMEM((tokens, width), BF16),
            pltpu.VMEM((tokens, width), BF16),
            pltpu.VMEM((tokens, width), BF16),
            pltpu.VMEM((tokens, width), BF16),
            pltpu.SemaphoreType.DMA((2 + 2 * held,)),
        ],
        compiler_params=pltpu.CompilerParams(vmem_limit_bytes=36 * 2**20),
        cost_estimate=BRIEF,
        name="feed_forward",
    )(inputs, in_hbm(mixed), *map(in_hbm, weights), *upstream)


def feed_back_kernel(
    which_ref,
    d_down_ref,
    slope_ref,
    active_t_ref,
    shrink_ref,
    expand_ref,
    normed_ref,
    *refs,
    steps,
    block,
    last,
):
    step = pl.program_id(0)
    if last:
        gain_ref, *late_refs = refs[:5]
        grads_ref, bias_ref, d_attn_ref, d_mixed_ref, sums_ref = refs[5:10]
        turned, total, hat_ref, scale_ref, output_proj_ref, sems = refs[10:]
        late = [
            pltpu.make_async_copy(source, target, sems.at[index])
            for index, (source, target) in enumerate(
                zip(late_refs, (d_attn_ref, hat_ref, scale_ref, output_proj_ref))
            )
        ]

        @pl.when(step == 0)
        def _():
            for copy in late:
                copy.start()

    else:
        grads_ref, bias_ref, total_ref, turned, total = refs
    tokens = total.shape[0]
    pieces = [slice(start, start + block) for start in range(0, tokens, block)]

    @pl.when(step == 0)
    def _():
        total[...] = jnp.zeros_like(total)
        bias_ref[...] = jnp.zeros_like(bias_ref)

    bias = jnp.zeros((1, slope_ref.shape[1]), F32)
    for here in pieces:
        d_active = dot(d_down_ref[here, :], shrink_ref[...], NT)
        d_expand = (d_active * slope_ref[here, :].astype(F32)).astype(BF16)
        turned[:, here] = d_expand.T
        bias += jnp.sum(d_expand.astype(F32), 0, keepdims=True)
        total[here, :] += dot(d_expand, expand_ref[...], NT)
    row = lax.broadcasted_iota(jnp.int32, bias_ref.shape, 0)
    bias_ref[...] = jnp.where(row == step, bias, bias_ref[...])
    grads_ref[0] = dot(active_t_ref[...], d_down_ref[...]).astype(BF16)
    grads_ref[1] = dot(turned[...], normed_ref[...]).astype(BF16)

    if not last:

        @pl.when(step == steps - 1)
        def _():
            total_ref[...] = total[...].astype(BF16)

    else:

        @pl.when(step == steps - 1)
        def _():
            for copy in late:
                copy.wait()
            gain = gain_ref[...].astype(F32)
            d_gain = jnp.zeros((1, total.shape[1]), F32)
            d_shift = d_gain
            d_bias = d_gain
            for here in pieces:
                d_normed = total[here, :] + (
                    d_down_ref[here, :].astype(F32) + d_attn_ref[here, :].astype(F32)
                )
                hat = hat_ref[here, :].astype(F32)
                d_gain += jnp.sum(d_normed * hat, 0, keepdims=True)
                d_shift += jnp.sum(d_normed, 0, keepdims=True)
                d_attn = norm_back(d_normed, hat, scale_ref[here, :][:, 0:1], gain).astype(BF16)
                d_attn_ref[here, :] = d_attn
                d_bias += jnp.sum(d_attn.astype(F32), 0, keepdims=True)
                d_mixed_ref[here, :] = dot(d_attn, output_proj_ref[...], NT).astype(BF16)
            sums_ref[...] = stack_rows([d_gain, d_shift, d_bias])


def feed_back(which, d_down, slope, active_t, shrink, expand, normed, norm, block=512):
    tokens, width = d_down.shape
    half = slope.shape[1] // 2
    steps = half // block
    last = norm is not None
    at = lambda i, which: which[0] * steps + i
    whole = lambda *shape: pl.BlockSpec(
        shape, lambda i, which: (0,) * len(shape), pipeline_mode=pl.Buffered(1)
    )
    in_specs = [
        whole(tokens, width),
        pl.BlockSpec((tokens, block), lambda i, which: (0, at(i, which))),
        pl.BlockSpec((block, tokens), lambda i, which: (at(i, which), 0)),
        pl.BlockSpec((block, width), lambda i, which: (at(i, which), 0)),
        pl.BlockSpec((width, block), lambda i, which: (0, at(i, which))),
        whole(tokens, width),
    ]
    out_specs = [
        pl.BlockSpec((2, block, width), lambda i, which: (0, i, 0)),
        whole(8, block),
    ]
    out_shape = hbm_shapes(((2, half, width), BF16), ((8, block), F32))
    scratch = [pltpu.VMEM((block, tokens), BF16), pltpu.VMEM((tokens, width), F32)]
    extra = ()
    if last:
        gain, *late = norm
        extra = (gain, *map(in_hbm, late))
        in_specs += [whole(1, width)] + [pl.BlockSpec(memory_space=pl.ANY)] * len(late)
        out_specs += [whole(tokens, width)] * 2 + [whole(8, width)]
        out_shape += hbm_shapes(
            ((tokens, width), BF16), ((tokens, width), BF16), ((8, width), F32)
        )
        scratch += [
            pltpu.VMEM((tokens, width), BF16),
            pltpu.VMEM((tokens, PAIR), F32),
            pltpu.VMEM((width, width), BF16),
            pltpu.SemaphoreType.DMA((4,)),
        ]
    else:
        out_specs.append(whole(tokens, width))
        out_shape += hbm_shapes(((tokens, width), BF16))
    return pl.pallas_call(
        functools.partial(feed_back_kernel, steps=steps, block=min(512, tokens), last=last),
        grid_spec=pltpu.PrefetchScalarGridSpec(
            num_scalar_prefetch=1,
            grid=(steps,),
            in_specs=in_specs,
            out_specs=out_specs,
            scratch_shapes=scratch,
        ),
        out_shape=out_shape,
        compiler_params=pltpu.CompilerParams(vmem_limit_bytes=44 * 2**20),
        cost_estimate=BRIEF,
        name="feed_back_last" if last else "feed_back",
    )(which, *map(in_hbm, (d_down, slope, active_t, shrink, expand, normed)), *extra)


def pack_kernel(at_ref, flat_ref, marks_ref, *refs, order):
    outs, sems = refs[:-1], refs[-1]
    piece = flat_ref.shape[1]
    for part, out_ref in zip(order, outs):
        marks = marks_ref[pl.ds(at_ref[0] ^ part, 1), :].astype(F32)
        out_ref[piece:, :] = jnp.zeros((MARK_ROWS, out_ref.shape[1]), BF16)
        out_ref[piece:, 0:piece] = jnp.broadcast_to(marks, (MARK_ROWS, piece)).astype(BF16)
    copies = [
        pltpu.make_async_copy(
            flat_ref.at[at_ref[0] ^ part], out_ref.at[pl.ds(0, piece)], sems.at[index]
        )
        for index, (part, out_ref) in enumerate(zip(order, outs))
    ]
    for copy in copies:
        copy.start()
    for copy in copies:
        copy.wait()


MARK_ROWS = 16


def pack(at, flat, marks, order):
    held, piece, width = flat.shape
    vmem = pl.BlockSpec(memory_space=pltpu.VMEM)
    return pl.pallas_call(
        functools.partial(pack_kernel, order=order),
        in_specs=[
            pl.BlockSpec(memory_space=pltpu.SMEM),
            pl.BlockSpec(memory_space=pl.ANY),
            vmem,
        ],
        out_specs=[vmem] * held,
        out_shape=shapes(*[((piece + MARK_ROWS, width), BF16)] * held),
        scratch_shapes=[pltpu.SemaphoreType.DMA((held,))],
        compiler_params=pltpu.CompilerParams(vmem_limit_bytes=16 * 2**20),
        cost_estimate=BRIEF,
        name="pack",
    )(at, in_hbm(flat), marks)


def unpack_kernel(*refs):
    parts, (rows_ref, marks_ref) = refs[:-2], refs[-2:]
    piece = rows_ref.shape[0] // len(parts)
    for index, ref in enumerate(parts):
        here = slice(index * piece, (index + 1) * piece)
        rows_ref[here, :] = ref[0:piece, :]
        marks = ref[piece:, 0:piece].astype(F32)[0:1, :]
        marks_ref[here, :] = jnp.broadcast_to(marks, (PAIR, piece)).T.astype(BF16)


def unpack(parts):
    width = parts[0].shape[1]
    tokens = len(parts) * (parts[0].shape[0] - MARK_ROWS)
    return pl.pallas_call(
        unpack_kernel,
        grid=(1,),
        in_specs=[fixed(*part.shape) for part in parts],
        out_specs=[fixed(tokens, width), fixed(tokens, PAIR)],
        out_shape=hbm_shapes(((tokens, width), BF16), ((tokens, PAIR), BF16)),
        compiler_params=pltpu.CompilerParams(vmem_limit_bytes=16 * 2**20),
        cost_estimate=BRIEF,
        name="unpack",
    )(*parts)


def weight_kernel(
    core_ref,
    first_sums_ref,
    second_sums_ref,
    own_bias_ref,
    other_bias_ref,
    *refs,
    steps,
):
    sources, (other_ref, own_ref, small_ref) = refs[:6], refs[6:9]
    targets, (inputs_t, mixed_t, sems) = refs[9:15], refs[15:]
    inputs_ref, dq_ref, dk_ref, dv_ref, mixed_ref, d_attn_ref = targets
    copies = [
        pltpu.make_async_copy(source, target, sems.at[index])
        for index, (source, target) in enumerate(zip(sources, targets))
    ]
    for copy in copies:
        copy.start()
    count = inputs_ref.shape[1] // 2
    core = core_ref[0]
    for ref in (other_ref, own_ref):
        if ref.shape[0] > 4 * count:
            ref[4 * count :, :] = jnp.zeros((ref.shape[0] - 4 * count, ref.shape[1]), BF16)
    copies[0].wait()
    inputs_t[...] = inputs_ref[...].T
    for at, right_ref in enumerate((dq_ref, dk_ref, dv_ref, d_attn_ref)):
        copies[at + 1].wait()
        left_ref = inputs_t
        if at == 3:
            copies[5].wait()
            mixed_t[...] = mixed_ref[...].T
            left_ref = mixed_t
        for half, out_ref in ((1 - core, other_ref), (core, own_ref)):
            rows = pl.ds(pl.multiple_of(half * count, PAIR), count)
            out_ref[at * count : (at + 1) * count, :] = dot(left_ref[rows, :], right_ref[...]).astype(
                BF16
            )
    small_ref[...] = jnp.zeros_like(small_ref)
    small_ref[0:1, :] = jnp.sum(dq_ref[...].astype(F32), 0, keepdims=True)
    small_ref[1:2, :] = jnp.sum(dv_ref[...].astype(F32), 0, keepdims=True)
    small_ref[2:5, :] = first_sums_ref[0:3, :]
    small_ref[5:8, :] = second_sums_ref[0:3, :]
    block = own_bias_ref.shape[1]
    own, other = own_bias_ref[0:steps, :], other_bias_ref[0:steps, :]
    small_ref[8 : 8 + steps, 0:block] = jnp.where(core == 0, own, other)
    small_ref[8 + steps : 8 + 2 * steps, 0:block] = jnp.where(core == 0, other, own)


def weight_halves(core, values, unit, sums, steps):
    tokens, width = values[0].shape
    rows = -(-2 * width // unit) * unit
    vmem = pl.BlockSpec(memory_space=pltpu.VMEM)
    anywhere = pl.BlockSpec(memory_space=pl.ANY)
    return pl.pallas_call(
        functools.partial(weight_kernel, steps=steps),
        in_specs=[pl.BlockSpec(memory_space=pltpu.SMEM)] + [vmem] * 4 + [anywhere] * 6,
        out_specs=[vmem] * 3,
        out_shape=shapes(
            ((rows, width), BF16), ((rows, width), BF16), ((SMALL, width), F32)
        ),
        scratch_shapes=[pltpu.VMEM((tokens, width), BF16)] * 6
        + [pltpu.VMEM((width, tokens), BF16)] * 2
        + [pltpu.SemaphoreType.DMA((6,))],
        compiler_params=pltpu.CompilerParams(vmem_limit_bytes=32 * 2**20),
        cost_estimate=BRIEF,
        name="weight_halves",
    )(core, *sums, *map(in_hbm, values))


def input_grad_kernel(*refs, held):
    sources, outs = refs[:7], refs[7 : 7 + held]
    (d_attn, *factors), total, sems = refs[7 + held : 14 + held], refs[-2], refs[-1]
    copies = [
        pltpu.make_async_copy(source, target, sems.at[index])
        for index, (source, target) in enumerate(zip(sources, (d_attn, *factors)))
    ]
    for copy in copies:
        copy.start()
    piece = outs[0].shape[0]
    copies[0].wait()
    for index in range(3):
        for copy in copies[2 * index + 1 : 2 * index + 3]:
            copy.wait()
        left, right = factors[2 * index : 2 * index + 2]
        for number, out_ref in enumerate(outs):
            here = slice(number * piece, (number + 1) * piece)
            before = d_attn[here, :].astype(F32) if index == 0 else total[here, :]
            value = before + dot(left[here, :], right[...], NT)
            if index < 2:
                total[here, :] = value
            else:
                out_ref[...] = value.astype(BF16)


def input_grad(d_attn, factors, held):
    tokens, width = d_attn.shape
    anywhere = pl.BlockSpec(memory_space=pl.ANY)
    values = [d_attn] + [value for pair in factors for value in pair]
    return pl.pallas_call(
        functools.partial(input_grad_kernel, held=held),
        in_specs=[anywhere] * 7,
        out_specs=[pl.BlockSpec(memory_space=pltpu.VMEM)] * held,
        out_shape=shapes(*[((tokens // held, width), BF16)] * held),
        scratch_shapes=[pltpu.VMEM(value.shape, BF16) for value in values]
        + [pltpu.VMEM((tokens, width), F32), pltpu.SemaphoreType.DMA((7,))],
        compiler_params=pltpu.CompilerParams(vmem_limit_bytes=24 * 2**20),
        cost_estimate=BRIEF,
        name="input_grad",
    )(*map(in_hbm, values))


def feed_out_kernel(which_ref, half_ref, *refs, steps):
    del which_ref
    shrink_ref, expand_ref = refs[-2:]

    @pl.when(pl.program_id(0) < steps)
    def _():
        shrink_ref[...] = half_ref[...].astype(F32)

    @pl.when(pl.program_id(0) >= steps)
    def _():
        expand_ref[...] = half_ref[...].T.astype(F32)


def feed_out(which, values, before=(), block=512):
    width = values.shape[1]
    half = values.shape[0] // 2
    steps = half // block
    return pl.pallas_call(
        functools.partial(feed_out_kernel, steps=steps),
        grid_spec=pltpu.PrefetchScalarGridSpec(
            num_scalar_prefetch=1,
            grid=(2 * steps,),
            in_specs=[pl.BlockSpec((block, width), lambda i, which: (i, 0))]
            + [pl.BlockSpec(memory_space=pl.ANY)] * len(before),
            out_specs=[
                pl.BlockSpec(
                    (block, width),
                    lambda i, which: (which[0] * steps + jnp.minimum(i, steps - 1), 0),
                ),
                pl.BlockSpec(
                    (width, block),
                    lambda i, which: (0, which[0] * steps + jnp.maximum(i - steps, 0)),
                ),
            ],
        ),
        out_shape=shapes(((2 * half, width), F32), ((width, 2 * half), F32)),
        input_output_aliases={2 + i: i for i in range(len(before))},
        compiler_params=pltpu.CompilerParams(vmem_limit_bytes=16 * 2**20),
        cost_estimate=BRIEF,
        name="feed_out",
    )(which, values, *before)


def attn_out_kernel(which_ref, half_ref, *refs):
    del which_ref
    for index, out_ref in enumerate(refs[-4:]):

        @pl.when(pl.program_id(0) == index)
        def _(out_ref=out_ref):
            out_ref[...] = half_ref[...].astype(F32)


def attn_out(which, values, before=()):
    width = values.shape[1]
    half = width // 2
    return pl.pallas_call(
        attn_out_kernel,
        grid_spec=pltpu.PrefetchScalarGridSpec(
            num_scalar_prefetch=1,
            grid=(4,),
            in_specs=[pl.BlockSpec((half, width), lambda i, which: (i, 0))]
            + [pl.BlockSpec(memory_space=pl.ANY)] * len(before),
            out_specs=[pl.BlockSpec((half, width), lambda i, which: (which[0], 0))] * 4,
        ),
        out_shape=shapes(*[((width, width), F32)] * 4),
        input_output_aliases={2 + i: i for i in range(len(before))},
        compiler_params=pltpu.CompilerParams(vmem_limit_bytes=24 * 2**20),
        cost_estimate=BRIEF,
        name="attn_out",
    )(which, values, *before)


def place_kernel(at_ref, *refs):
    del at_ref
    out_ref = refs[-1]
    for index, ref in enumerate(refs[:-1]):

        @pl.when(pl.program_id(0) == index)
        def _(ref=ref):
            out_ref[0] = ref[...]


def place(at, parts):
    piece, width = parts[0].shape
    held = len(parts)
    return pl.pallas_call(
        place_kernel,
        grid_spec=pltpu.PrefetchScalarGridSpec(
            num_scalar_prefetch=1,
            grid=(held,),
            in_specs=[pl.BlockSpec((piece, width), lambda i, at: (0, 0))] * held,
            out_specs=pl.BlockSpec((1, piece, width), lambda i, at: (at[0] ^ i, 0, 0)),
        ),
        out_shape=jax.ShapeDtypeStruct((held, piece, width), BF16),
        compiler_params=pltpu.CompilerParams(vmem_limit_bytes=16 * 2**20),
        cost_estimate=BRIEF,
        name="place",
    )(at, *parts)


def rows_of(ref, which, count, base=0):
    return ref[pl.ds(pl.multiple_of(base + which * count, 16), count), :]


def sum_of(terms):
    return functools.reduce(lambda a, b: a + b, [t.astype(F32) for t in terms]).astype(BF16)


def scatter_kernel(bits_ref, *refs, groups):
    outs = refs[-2 * groups :]
    ins = refs[: -2 * groups]
    together = len(ins) == 2
    base = 0
    for group in range(groups):
        terms = ins if together else ins[2 * group : 2 * group + 2]
        sent_ref, kept_ref = outs[2 * group : 2 * group + 2]
        count = kept_ref.shape[0]
        here = bits_ref[group]
        sent_ref[...] = sum_of([rows_of(term, 1 - here, count, base) for term in terms])
        kept_ref[...] = sum_of([rows_of(term, here, count, base) for term in terms])
        if together:
            base += 2 * count


def local_call(kernel, bits, values, out_shape, name):
    vmem = pl.BlockSpec(memory_space=pltpu.VMEM)
    return pl.pallas_call(
        kernel,
        in_specs=[pl.BlockSpec(memory_space=pltpu.SMEM)] + [vmem] * len(values),
        out_specs=[vmem] * len(out_shape),
        out_shape=out_shape,
        compiler_params=pltpu.CompilerParams(vmem_limit_bytes=24 * 2**20),
        cost_estimate=BRIEF,
        name=name,
    )(bits, *values)


def scatter_local(bits, pairs, counts=None):
    if counts is None:
        counts = [kept.shape[0] for kept, _ in pairs]
    groups = len(counts)
    counts = [count // 2 for count in counts]
    width = pairs[0][0].shape[1]
    outs = local_call(
        functools.partial(scatter_kernel, groups=groups),
        bits,
        [value for pair in pairs for value in pair],
        shapes(*[((count, width), BF16) for count in counts for _ in range(2)]),
        "scatter_local",
    )
    return [outs[2 * i : 2 * i + 2] for i in range(groups)]


def scatter_first_kernel(bits_ref, own_at, got_at, *refs, counts):
    outs, (own, got, sems) = refs[:-3], refs[-3:]
    spans = []
    base = 0
    for group, count in enumerate(counts):
        for kept in range(2):
            half = bits_ref[group] if kept else 1 - bits_ref[group]
            start = pl.multiple_of(base + half * (count // 2), 16)
            spans.append((start, count // 2, outs[2 * group + kept]))
        base += count
    spans = spans[0::2] + spans[1::2]
    copies = []
    for index, (start, count, _) in enumerate(spans):
        rows = pl.ds(start, count)
        for which, (source, target) in enumerate(((own_at, own), (got_at, got))):
            copies.append(
                pltpu.make_async_copy(source.at[rows], target.at[rows], sems.at[2 * index + which])
            )
            copies[-1].start()
    for index, (start, count, out_ref) in enumerate(spans):
        for copy in copies[2 * index : 2 * index + 2]:
            copy.wait()
        rows = pl.ds(start, count)
        out_ref[...] = sum_of([own[rows, :], got[rows, :]])


def scatter_first(bits, own, got, counts):
    rows, width = own.shape
    anywhere = pl.BlockSpec(memory_space=pl.ANY)
    vmem = pl.BlockSpec(memory_space=pltpu.VMEM)
    outs = pl.pallas_call(
        functools.partial(scatter_first_kernel, counts=counts),
        in_specs=[pl.BlockSpec(memory_space=pltpu.SMEM), anywhere, anywhere],
        out_specs=[vmem] * (2 * len(counts)),
        out_shape=shapes(*[((count // 2, width), BF16) for count in counts for _ in range(2)]),
        scratch_shapes=[pltpu.VMEM((rows, width), BF16)] * 2
        + [pltpu.SemaphoreType.DMA((4 * len(counts),))],
        compiler_params=pltpu.CompilerParams(vmem_limit_bytes=24 * 2**20),
        cost_estimate=BRIEF,
        name="scatter_first",
    )(bits, in_hbm(own), in_hbm(got))
    return [outs[2 * group : 2 * group + 2] for group in range(len(counts))]


SMALL = 16


def put_small(ref, at, values):
    ref[at : at + SMALL, :] = values.astype(BF16)


def get_small(ref, at):
    return ref[at : at + SMALL, :].astype(F32)


def settle_kernel(bits_ref, *refs, groups, small):
    del bits_ref
    ins, outs = refs[: 2 * groups], refs[2 * groups + small :]
    for group in range(groups):
        count = ins[2 * group].shape[0]
        outs[group][0:count, :] = sum_of([ins[2 * group][...], ins[2 * group + 1][...]])
        if small and group == 0:
            put_small(outs[group], count, refs[2 * groups][...])


def settle_local(bits, pairs, small):
    width = pairs[0][0].shape[1]
    counts = [kept.shape[0] for kept, _ in pairs]
    if small is not None:
        counts[0] += SMALL
    return local_call(
        functools.partial(settle_kernel, groups=len(pairs), small=int(small is not None)),
        bits,
        [value for pair in pairs for value in pair] + ([] if small is None else [small]),
        shapes(*[((count, width), BF16) for count in counts]),
        "settle_local",
    )


def add_kernel(bits_ref, *refs, groups, small):
    del bits_ref
    ins, outs = refs[: 2 * groups], refs[2 * groups :]
    for group in range(groups):
        own_ref, got_ref = ins[2 * group : 2 * group + 2]
        extra = SMALL if small and group == 0 else 0
        count = own_ref.shape[0] - extra
        outs[group][0:count, :] = sum_of([own_ref[0:count, :], got_ref[0:count, :]])
        if extra:
            put_small(outs[group], count, get_small(own_ref, count) + get_small(got_ref, count))


def add_local(bits, pairs, small):
    return local_call(
        functools.partial(add_kernel, groups=len(pairs), small=small),
        bits,
        [value for pair in pairs for value in pair],
        shapes(*[(own.shape, BF16) for own, _ in pairs]),
        "add_local",
    )


def join_kernel(bits_ref, *refs, groups, small, merged, pieces):
    ins, outs = refs[: 2 * pieces * groups], list(refs[2 * pieces * groups :])
    parts = len(outs) // groups
    base = 0
    for group in range(groups):
        owns = ins[2 * pieces * group : 2 * pieces * group + 2 * pieces : 2]
        gots = ins[2 * pieces * group + 1 : 2 * pieces * group + 2 * pieces : 2]
        extra = SMALL if small and group == 0 else 0
        count = owns[0].shape[0] - extra
        here = bits_ref[group]
        if parts > 1:
            for half, out_ref in enumerate(outs[2 * group : 2 * group + 2]):

                @pl.when(here == half)
                def _(out_ref=out_ref):
                    out_ref[...] = owns[0][...]

                @pl.when(here != half)
                def _(out_ref=out_ref):
                    out_ref[...] = gots[0][...]

            continue
        out_ref = outs[0 if merged else group]
        whole = count * pieces
        for half, refs_of in ((here, owns), (1 - here, gots)):
            for index, ref in enumerate(refs_of):
                start = pl.multiple_of(base + half * whole + index * count, 16)
                out_ref[pl.ds(start, count), :] = ref[0:count, :]
        if extra:
            at = out_ref.shape[0] - SMALL if merged else base + 2 * whole
            put_small(out_ref, at, get_small(owns[0], count) + get_small(gots[0], count))
        if merged:
            base += 2 * whole


def join_local(bits, arrived, small, merged, parts=1):
    width = arrived[0][0].shape[1]
    pieces = len(arrived[0]) // 2
    counts = [2 * pieces * group[0].shape[0] for group in arrived]
    if small:
        counts[0] -= SMALL
    if merged:
        counts = [sum(counts)]
    counts = [count // parts for count in counts for _ in range(parts)]
    return local_call(
        functools.partial(
            join_kernel, groups=len(arrived), small=small, merged=merged, pieces=pieces
        ),
        bits,
        [value for group in arrived for value in group],
        shapes(*[((count, width), BF16) for count in counts]),
        "join_local",
    )


def tie(*values):
    return lax.optimization_barrier(values)


def pick(which, parts):
    if len(parts) == 1:
        return parts[0]
    half = len(parts) // 2
    return jnp.where(which < half, pick(which, parts[:half]), pick(which - half, parts[half:]))


def column_sum(values):
    return jnp.sum(values.astype(F32), 0)


class Stage:
    def __init__(self, sizes, bits):
        self.bits = bits
        rows, seq = sizes
        self.pairs = []
        for index in range(rows * seq):
            axis, bit = bits[index & 1]
            self.pairs.append((index, index ^ ((1 << bit) * (seq if axis == "rows" else 1))))

    def here(self):
        first, second = [(lax.axis_index(axis) >> bit) & 1 for axis, bit in self.bits]
        if self.bits[0] == self.bits[1]:
            return first
        return jnp.where(lax.axis_index("seq") & 1 == 0, first, second)

    def swap(self, values):
        return lax.ppermute(values, ("rows", "seq"), self.pairs)


def total_over_chips(own, got, core_stage, orders, small=None, near=False):
    depth = len(orders[0][1])
    groups = range(len(orders))

    def bits_at(step):
        return jnp.stack([stages[step].here() for _, stages in orders]).astype(jnp.int32)

    def pairs_of(flat):
        return [flat[i : i + 2] for i in range(0, len(flat), 2)]

    def send(step, values, keep):
        flat = []
        for group in groups:
            flat += [keep[group], orders[group][1][step].swap(values[group])]
        return flat

    counts = [count for count, _ in orders]
    if near:
        parts = scatter_local(bits_at(0), [[own, got]], counts)
    else:
        parts = scatter_first(bits_at(0), own, got, counts)
    last = depth - 1 if near else depth
    for step in range(1, last + 1):
        flat = yield send(step - 1, [p[0] for p in parts], [p[1] for p in parts])
        if step < last:
            parts = scatter_local(bits_at(step), pairs_of(flat))
    values = settle_local(bits_at(0), pairs_of(flat), small)
    if near:
        flat = yield send(last, values, values)
        values = add_local(bits_at(0), pairs_of(flat), small is not None)
    carried = small is not None
    for step in reversed(range(last)):
        flat = yield send(step, values, values)
        parts = 2 if step == 1 and not carried else 1
        values = join_local(bits_at(step), pairs_of(flat), carried, step == 0, parts)
        if parts > 1:
            lower = yield send(0, values[0::2], values[0::2])
            upper = yield send(0, values[1::2], values[1::2])
            arrived = [list(low) + list(high) for low, high in zip(pairs_of(lower), pairs_of(upper))]
            values = join_local(bits_at(0), arrived, carried, True)
            break
    both = yield [values[0], core_stage.swap(values[0])]
    return both


def arriving(values):
    values = yield values
    return values[1::2]


class Flow:
    def __init__(self, steps, left):
        self.steps = steps
        self.left = left
        self.pending = next(steps)
        self.result = None


class Timetable:
    def __init__(self):
        self.flows = []

    def open(self, steps, left=1):
        self.flows.append(Flow(steps, left))
        return self.flows[-1]

    def advance(self, moving, *values):
        flows = [flow for flow in self.flows if flow.result is None]
        held = [flow.pending if flow in moving else flow.pending[0::2] for flow in flows]
        tied = list(tie(*values, *[value for part in held for value in part]))
        values, tied = tied[: len(values)], tied[len(values) :]
        for flow, part in zip(flows, held):
            back, tied = tied[: len(part)], tied[len(part) :]
            if flow not in moving:
                flow.pending[0::2] = back
                continue
            flow.left -= 1
            try:
                flow.pending = flow.steps.send(back)
            except StopIteration as end:
                flow.result = end.value
        return self.settle(*values) if moving and values else values

    def settle(self, *values):
        return self.advance([], *values)


def solution(mesh):
    seq_size = mesh.shape["seq"]
    rows_size = mesh.shape["rows"]
    seq_bits = seq_size.bit_length() - 1
    rows_bits = rows_size.bit_length() - 1
    off_chip = [("seq", bit) for bit in range(1, seq_bits)]
    off_chip += [("rows", bit) for bit in range(rows_bits)]
    first, *middle, ahead, final = off_chip
    sizes = (rows_size, seq_size)
    core_stage = Stage(sizes, [("seq", 0)] * 2)
    straight = [first] + middle + [ahead, final]
    turned = middle + [ahead, first, final]
    spun = [ahead, first] + middle + [final]
    wide = [Stage(sizes, bits) for bits in zip(straight, turned)]
    slim = [Stage(sizes, bits) for bits in zip(spun, spun)]

    def body(
        hidden_in,
        segments,
        grad_mask,
        grad_out,
        query_proj,
        query_bias,
        key_proj,
        value_proj,
        value_bias,
        output_proj,
        output_bias,
        first_gain,
        first_shift,
        expand_proj,
        expand_bias,
        shrink_proj,
        shrink_bias,
        second_gain,
        second_shift,
    ):
        micro, rows_here, piece, width = hidden_in.shape
        held = micro * rows_here
        sharers = seq_size // held
        tokens = held * piece
        source_at = lax.axis_index("seq") % held
        core = core_stage.here()
        core_at = core.reshape(1).astype(jnp.int32)

        def trade(to_rows, part):
            there = [(s, (s % held ^ part) * sharers + s // held) for s in range(seq_size)]
            return there if to_rows else [(b, a) for a, b in there]

        def to_rows(values):
            return [
                lax.ppermute(
                    lax.dynamic_index_in_dim(values, source_at ^ part, 0, False),
                    "seq",
                    trade(True, part),
                )
                for part in range(held)
            ]

        def send_pieces(values, chosen=range(held)):
            return [
                value
                for part in chosen
                for value in (values[part], lax.ppermute(values[part], "seq", trade(False, part)))
            ]

        def place_pieces(parts):
            at = source_at.reshape(1).astype(jnp.int32)
            return place(at, parts).reshape((micro, rows_here) + parts[0].shape)

        same_row = [[r * sharers + g for g in range(sharers)] for r in range(held)]

        def all_keys(values):
            if sharers == 1:
                return values
            return lax.all_gather(values, "seq", axis=0, tiled=True, axis_index_groups=same_row)

        def own_keys(values):
            if sharers == 1:
                return values
            return lax.psum_scatter(
                values, "seq", scatter_dimension=0, tiled=True, axis_index_groups=same_row
            ).astype(BF16)

        order = tuple(reversed(range(held)))
        packed = pack(
            source_at.reshape(1).astype(jnp.int32),
            hidden_in.reshape(held, piece, width),
            segments.reshape(held, piece),
            order,
        )
        arrived = [
            lax.ppermute(value, "seq", trade(True, part)) for part, value in zip(order, packed)
        ]
        inputs, seg_q = unpack(arrived[::-1])
        masked = (grad_out * grad_mask[..., None].astype(BF16)).reshape(held, piece, width)
        masked, inputs, seg_q = tie(masked, inputs, seg_q)
        upstream = to_rows(masked)

        queries = (
            (dot(inputs, query_proj) + query_bias.astype(F32)) * 0.125
        ).astype(BF16)
        keys = all_keys(dot(inputs, key_proj).astype(BF16))
        values = all_keys((dot(inputs, value_proj) + value_bias.astype(F32)).astype(BF16))
        seg_k = all_keys(seg_q)
        mixed, query_side = attention_forward(queries, keys, values, seg_q, seg_k)
        row = lambda vector: vector.reshape(1, -1)
        hat, scale, normed, active_t, slope, d_down, second_sums, *result = feed_forward(
            inputs,
            mixed,
            upstream,
            (
                output_proj,
                row(output_bias),
                row(first_gain),
                row(first_shift),
                expand_proj,
                row(expand_bias),
                shrink_proj,
                row(shrink_bias),
                row(second_gain),
                row(second_shift),
            ),
        )
        table = Timetable()
        advance = table.advance
        layer_flow = table.open(arriving(send_pieces(result)))

        def chips(own, got, orders, small=None):
            near = small is not None
            steps = total_over_chips(own, got, core_stage, orders, small, near)
            return table.open(steps, 2 * len(wide) + (0 if near else 2))

        back = functools.partial(
            feed_back,
            slope=slope,
            active_t=active_t,
            shrink=shrink_proj,
            expand=expand_proj,
            normed=normed,
        )
        other, other_bias, d_normed = back(1 - core_at, d_down, norm=None)
        half = other.shape[1]
        got = core_stage.swap(other.reshape(2 * half, width))
        own, own_bias, d_attn, d_mixed, first_sums = back(
            core_at, d_down, norm=(row(first_gain), d_normed, hat, scale, output_proj)
        )
        own, got, d_mixed = advance([layer_flow], own.reshape(2 * half, width), got, d_mixed)
        unit = 16 << len(off_chip)

        def thirds(count):
            less = count // unit // 3 * unit
            return [(count - less, wide)] + ([(less, slim)] if less else [])

        feed_flow = chips(own, got, thirds(2 * half))

        pairs = width // PAIR
        kept = BF16 if sharers == 1 else F32
        grads = None
        for first, last in ((0, pairs),):
            grads = attention_backward(
                query_side, keys, values, seg_k, mixed, d_mixed, kept, first, last - first, grads
            )
            *grads, d_mixed = advance([feed_flow], *grads, d_mixed)

        d_query, d_keys, d_values = grads
        d_key = own_keys(d_keys)
        d_value = own_keys(d_values)
        steps = half // other_bias.shape[1]
        other, own, small = weight_halves(
            core_at,
            (inputs, d_query, d_key, d_value, mixed, d_attn),
            unit,
            (first_sums, second_sums, own_bias, other_bias),
            steps,
        )
        other, own, small, d_query, d_key, d_value = advance(
            [feed_flow], other, own, small, d_query, d_key, d_value
        )
        got = core_stage.swap(other)
        d_input = input_grad(
            d_attn, ((d_query, query_proj), (d_key, key_proj), (d_value, value_proj)), held
        )
        own, got, small, *d_input = advance([feed_flow], own, got, small, *d_input)
        attn_flow = chips(own, got, [(own.shape[0], wide)], small)
        held_back = held // 2
        soon = [part for part in range(held) if part != held_back]
        piece_flow = table.open(arriving(send_pieces(d_input, soon)))
        last_flow = table.open(arriving(send_pieces(d_input, [held_back])))

        both = [feed_flow, attn_flow]
        layer_out = place_pieces(list(map(in_hbm, layer_flow.result)))
        (layer_out,) = advance(both, layer_out)
        advance(both + [piece_flow])
        advance(both)
        advance(both + [last_flow])
        arrived = list(piece_flow.result)
        arrived.insert(held_back, last_flow.result[0])
        grad_in = place_pieces(arrived)
        (grad_in,) = advance(both, grad_in)
        while feed_flow.left > 1:
            advance(both)
        feed_grads = feed_out(core_at, feed_flow.pending[0])
        feed_grads = advance(both, *feed_grads)
        feed_grads = feed_out(1 - core_at, feed_flow.result[1], feed_grads)
        while attn_flow.left > 1:
            feed_grads = advance([attn_flow], *feed_grads)
        attn_grads = attn_out(core_at, attn_flow.pending[0])
        attn_grads = advance([attn_flow], *attn_grads)
        own, got = attn_flow.result
        attn_grads = attn_out(1 - core_at, got, attn_grads)
        totals = own[-SMALL:].astype(F32) + got[-SMALL:].astype(F32)
        shrink_grad, expand_grad = feed_grads
        expand_bias_grad = totals[8 : 8 + 2 * steps, : other_bias.shape[1]].reshape(-1)
        return (
            layer_out,
            grad_in,
            attn_grads[0],
            totals[0],
            attn_grads[1],
            attn_grads[2],
            totals[1],
            attn_grads[3],
            totals[4],
            totals[2],
            totals[3],
            expand_grad,
            expand_bias_grad,
            shrink_grad,
            totals[7],
            totals[5],
            totals[6],
        )

    split = P(None, "rows", "seq", None)
    whole = P()
    return jax.shard_map(
        body,
        mesh=mesh,
        in_specs=(split, P(None, "rows", "seq"), P(None, "rows", "seq"), split) + (whole,) * 15,
        out_specs=(split, split) + (whole,) * 15,
        check_vma=False,
    )
```

```python
import functools

import jax
import jax.numpy as jnp
from jax import lax
from jax.experimental import pallas as pl
from jax.experimental.pallas import tpu as pltpu
from jax.sharding import PartitionSpec as P

DH = 64
PAIR = 128
MASKED = 1e30
F32 = jnp.float32
BF16 = jnp.bfloat16
NT = (((1,), (1,)), ((), ()))
NN = (((1,), (0,)), ((), ()))
BRIEF = pl.CostEstimate(flops=1, bytes_accessed=1, transcendentals=0)


def left_dot(first, second):
    return lax.dot_general(first, second, (((0,), (0,)), ((), ())), preferred_element_type=F32)


def right_dot(first, second):
    return lax.dot_general(first, second, NT, preferred_element_type=F32)


def split_three(values):
    high = values.astype(BF16)
    rest = values - high.astype(F32)
    middle = rest.astype(BF16)
    low = (rest - middle.astype(F32)).astype(BF16)
    return high.astype(F32), middle.astype(F32), low.astype(F32)


def own_lanes(shape, head):
    lane = lax.broadcasted_iota(jnp.int32, shape, 1)
    own = lane < DH if head == 0 else lane >= DH
    return own, lane % DH


def key_features(lane, seg):
    return jnp.where(
        lane < 3,
        1.0,
        jnp.where(lane == 3, -MASKED * (1.0 - seg), jnp.where(lane == 4, -MASKED * seg, 0.0)),
    ).astype(BF16)


def forward_kernel(q_ref, k_ref, v_ref, seg_q_ref, seg_k_ref, mixed_ref, query_ref, *, block):
    queries = q_ref.shape[0]
    keys = k_ref.shape[0]
    for head in range(2):
        own_k, lane_k = own_lanes((keys, PAIR), head)
        key_side = jnp.where(own_k, k_ref[...], key_features(lane_k, seg_k_ref[...].astype(F32)))
        value_side = jnp.where(own_k, v_ref[...], jnp.ones((), BF16))
        own_q, lane_q = own_lanes((block, PAIR), head)
        for start in range(0, queries, block):
            here = slice(start, start + block)
            q = q_ref[here, :]
            seg = seg_q_ref[here, :].astype(F32)
            seg_side = jnp.where(lane_q == 3, seg, jnp.where(lane_q == 4, 1.0 - seg, 0.0))
            query_side = jnp.where(own_q, q, seg_side.astype(BF16))
            scores = lax.dot_general(query_side, key_side, NT, preferred_element_type=F32)
            peak = jnp.max(scores, -1, keepdims=True)
            raised = jnp.exp(scores - peak).astype(BF16)
            summed = lax.dot_general(raised, value_side, NN, preferred_element_type=F32)
            total = summed[:, DH : DH + 1] if head == 0 else summed[:, 0:1]
            mixed = (summed / total).astype(BF16)
            shift = jnp.broadcast_to(-(peak + jnp.log(total)), (block, PAIR))
            high, middle, low = split_three(shift)
            extra = jnp.where(
                lane_q == 0,
                high,
                jnp.where(lane_q == 1, middle, jnp.where(lane_q == 2, low, seg_side)),
            )
            query_ref[head, here, :] = jnp.where(own_q, q, extra.astype(BF16))
            if head == 0:
                mixed_ref[here, :] = mixed
            else:
                mixed_ref[here, :] = jnp.where(own_q, mixed, mixed_ref[here, :])


def attention_forward(q, k, v, seg_q, seg_k):
    queries, width = q.shape
    keys = k.shape[0]
    pairs = width // PAIR
    column = lambda i: (0, i)
    whole = lambda i: (0, 0)
    return pl.pallas_call(
        functools.partial(forward_kernel, block=min(512, queries)),
        grid=(pairs,),
        in_specs=[
            pl.BlockSpec((queries, PAIR), column),
            pl.BlockSpec((keys, PAIR), column),
            pl.BlockSpec((keys, PAIR), column),
            pl.BlockSpec((queries, PAIR), whole),
            pl.BlockSpec((keys, PAIR), whole),
        ],
        out_specs=[
            pl.BlockSpec((queries, PAIR), column),
            pl.BlockSpec((2, queries, PAIR), lambda i: (i, 0, 0)),
        ],
        out_shape=[
            pltpu.HBM((queries, width), BF16),
            pltpu.HBM((2 * pairs, queries, PAIR), BF16),
        ],
        compiler_params=pltpu.CompilerParams(vmem_limit_bytes=24 * 2**20),
        cost_estimate=BRIEF,
        name="attention_forward",
    )(q, k, v, seg_q, seg_k)


def backward_kernel(
    query_ref, k_ref, v_ref, seg_k_ref, mixed_ref, d_mixed_ref, *refs, block
):
    dq_ref, dk_ref, dv_ref, dqt = refs[-4:]
    queries = mixed_ref.shape[0]
    keys = k_ref.shape[0]
    d_mixed = d_mixed_ref[...]
    product = d_mixed.astype(F32) * mixed_ref[...].astype(F32)
    for head in range(2):
        own_q, lane_q = own_lanes((queries, PAIR), head)
        own_k, lane_k = own_lanes((block, PAIR), head)
        delta = -jnp.sum(jnp.where(own_q, product, 0.0), -1, keepdims=True)
        high, middle, low = split_three(jnp.broadcast_to(delta, (queries, PAIR)))
        extra = jnp.where(
            lane_q == 0, high, jnp.where(lane_q == 1, middle, jnp.where(lane_q == 2, low, 0.0))
        )
        d_side = jnp.where(own_q, d_mixed, extra.astype(BF16))
        query_side = query_ref[head]
        ones = jnp.where(lane_k < 3, 1.0, 0.0).astype(BF16)
        for start in range(0, keys, block):
            here = slice(start, start + block)
            k = k_ref[here, :]
            seg = seg_k_ref[here, :].astype(F32)
            key_side = jnp.where(own_k, k, key_features(lane_k, seg))
            value_side = jnp.where(own_k, v_ref[here, :], ones)
            shifted = lax.dot_general(key_side, query_side, NT, preferred_element_type=F32)
            probs = jnp.exp(shifted)
            d_probs = lax.dot_general(value_side, d_side, NT, preferred_element_type=F32)
            d_scores = (probs * d_probs).astype(BF16)
            dv = lax.dot_general(probs.astype(BF16), d_mixed, NN, preferred_element_type=F32)
            dk = lax.dot_general(d_scores, query_side, NN, preferred_element_type=F32)
            turned = k.T[head * DH : (head + 1) * DH, :]
            dq = lax.dot_general(turned, d_scores, NN, preferred_element_type=F32)
            mine = slice(head * DH, (head + 1) * DH)
            if start == 0:
                dqt[mine, :] = dq
            else:
                dqt[mine, :] += dq
            dv = dv.astype(dv_ref.dtype)
            dk = dk.astype(dk_ref.dtype)
            if head == 0:
                dk_ref[here, :] = dk
                dv_ref[here, :] = dv
            else:
                dk_ref[here, :] = jnp.where(own_k, dk, dk_ref[here, :])
                dv_ref[here, :] = jnp.where(own_k, dv, dv_ref[here, :])
    dq_ref[...] = (dqt[...] * 0.125).astype(BF16).T


def attention_backward(query_side, k, v, seg_k, mixed, d_mixed, kept, first, count, before):
    queries, width = mixed.shape
    keys = k.shape[0]
    column = lambda i: (0, i + first)
    held = [] if before is None else list(before)
    return pl.pallas_call(
        functools.partial(backward_kernel, block=min(512, keys)),
        grid=(count,),
        in_specs=[
            pl.BlockSpec((2, queries, PAIR), lambda i: (i + first, 0, 0)),
            pl.BlockSpec((keys, PAIR), column),
            pl.BlockSpec((keys, PAIR), column),
            pl.BlockSpec((keys, PAIR), lambda i: (0, 0)),
            pl.BlockSpec((queries, PAIR), column),
            pl.BlockSpec((queries, PAIR), column),
        ]
        + [pl.BlockSpec(memory_space=pl.ANY)] * len(held),
        out_specs=[
            pl.BlockSpec((queries, PAIR), column),
            pl.BlockSpec((keys, PAIR), column),
            pl.BlockSpec((keys, PAIR), column),
        ],
        input_output_aliases={6 + i: i for i in range(len(held))},
        out_shape=[
            pltpu.HBM((queries, width), BF16),
            pltpu.HBM((keys, width), kept),
            pltpu.HBM((keys, width), kept),
        ],
        scratch_shapes=[pltpu.VMEM((PAIR, queries), F32)],
        compiler_params=pltpu.CompilerParams(vmem_limit_bytes=24 * 2**20),
        cost_estimate=BRIEF,
        name="attention_backward",
    )(in_hbm(query_side), k, v, seg_k, in_hbm(mixed), in_hbm(d_mixed), *map(in_hbm, held))


def dot(first, second, dims=NN):
    return lax.dot_general(first, second, dims, preferred_element_type=F32)


def gelu_pair(values):
    below = 0.5 + 0.5 * lax.erf(values * 0.7071067811865476)
    density = jnp.exp(-0.5 * values * values) * 0.3989422804014327
    return values * below, below + values * density


def normalise(values):
    centred = values - jnp.mean(values, -1, keepdims=True)
    scale = lax.rsqrt(jnp.mean(centred * centred, -1, keepdims=True) + 1e-06)
    return centred * scale, scale


def norm_back(upstream, hat, scale, gain):
    d_hat = upstream * gain
    return scale * (
        d_hat
        - jnp.mean(d_hat, -1, keepdims=True)
        - hat * jnp.mean(d_hat * hat, -1, keepdims=True)
    )


def stack_rows(rows):
    filler = jnp.zeros((8 - len(rows), rows[0].shape[1]), F32)
    return jnp.concatenate(rows + [filler], 0)


def feed_forward_kernel(
    inputs_ref,
    mixed_ref,
    output_proj_ref,
    output_bias_ref,
    gain_one_ref,
    shift_one_ref,
    expand_ref,
    expand_bias_ref,
    shrink_ref,
    shrink_bias_ref,
    gain_two_ref,
    shift_two_ref,
    *refs,
    steps,
    held,
):
    upstream_refs = refs[:held]
    hat_out, scale_ref, normed_out, active_t_ref, slope_ref = refs[held : held + 5]
    d_down_ref, sums_ref = refs[held + 5 : held + 7]
    out_refs = refs[held + 7 : 2 * held + 7]
    total, hat_ref, normed_ref, sems = refs[2 * held + 7 :]
    block = total.shape[0] // held
    early = [
        pltpu.make_async_copy(hat_ref, hat_out, sems.at[0]),
        pltpu.make_async_copy(normed_ref, normed_out, sems.at[1]),
    ]
    step = pl.program_id(0)
    tokens = total.shape[0]
    pieces = [slice(start, start + block) for start in range(0, tokens, block)]

    @pl.when(step == 0)
    def _():
        for here in pieces:
            first_sum = (
                inputs_ref[here, :].astype(F32)
                + dot(mixed_ref[here, :], output_proj_ref[...])
                + output_bias_ref[...].astype(F32)
            )
            hat, scale = normalise(first_sum)
            hat_ref[here, :] = hat.astype(BF16)
            scale_ref[here, :] = jnp.broadcast_to(scale, (block, PAIR))
            normed = gain_one_ref[...].astype(F32) * hat + shift_one_ref[...].astype(F32)
            normed_ref[here, :] = normed.astype(BF16)
            total[here, :] = normed + shrink_bias_ref[...].astype(F32)
        for copy in early:
            copy.start()

    for here in pieces:
        expanded = dot(normed_ref[here, :], expand_ref[...]) + expand_bias_ref[...].astype(F32)
        active, slope = gelu_pair(expanded)
        active = active.astype(BF16)
        slope_ref[here, :] = slope.astype(BF16)
        active_t_ref[:, here] = active.T
        total[here, :] += dot(active, shrink_ref[...])

    @pl.when(step == steps - 1)
    def _():
        gain = gain_two_ref[...].astype(F32)
        d_gain = jnp.zeros((1, total.shape[1]), F32)
        d_shift = d_gain
        d_bias = d_gain
        for here, upstream_ref, out_ref in zip(pieces, upstream_refs, out_refs):
            hat, scale = normalise(total[here, :])
            out_ref[...] = (gain * hat + shift_two_ref[...].astype(F32)).astype(BF16)
            upstream = upstream_ref[...].astype(F32)
            d_gain += jnp.sum(upstream * hat, 0, keepdims=True)
            d_shift += jnp.sum(upstream, 0, keepdims=True)
            d_down = norm_back(upstream, hat, scale, gain).astype(BF16)
            d_down_ref[here, :] = d_down
            d_bias += jnp.sum(d_down.astype(F32), 0, keepdims=True)
        sums_ref[...] = stack_rows([d_gain, d_shift, d_bias])
        for copy in early:
            copy.wait()


def in_hbm(values):
    return pltpu.with_memory_space_constraint(values, pltpu.HBM)


def hbm_shapes(*pairs):
    return [pltpu.HBM(shape, dtype) for shape, dtype in pairs]


def fixed(*shape):
    return pl.BlockSpec(shape, lambda i: (0,) * len(shape), pipeline_mode=pl.Buffered(1))


def shapes(*pairs):
    return [jax.ShapeDtypeStruct(shape, dtype) for shape, dtype in pairs]


def feed_forward(inputs, mixed, upstream, weights, block=768):
    tokens, width = inputs.shape
    units = weights[4].shape[1]
    steps = units // block
    held = len(upstream)
    piece = tokens // held
    row = fixed(1, width)
    return pl.pallas_call(
        functools.partial(feed_forward_kernel, steps=steps, held=held),
        grid=(steps,),
        in_specs=[fixed(tokens, width)] * 2
        + [fixed(width, width), row, row, row]
        + [
            pl.BlockSpec((width, block), lambda i: (0, i)),
            pl.BlockSpec((1, block), lambda i: (0, i)),
            pl.BlockSpec((block, width), lambda i: (i, 0)),
            row,
            row,
            row,
        ]
        + [fixed(piece, width)] * held,
        out_specs=[
            pl.BlockSpec(memory_space=pl.ANY),
            fixed(tokens, PAIR),
            pl.BlockSpec(memory_space=pl.ANY),
            pl.BlockSpec((block, tokens), lambda i: (i, 0)),
            pl.BlockSpec((tokens, block), lambda i: (0, i)),
            fixed(tokens, width),
            fixed(8, width),
        ]
        + [fixed(piece, width)] * held,
        out_shape=hbm_shapes(
            ((tokens, width), BF16),
            ((tokens, PAIR), F32),
            ((tokens, width), BF16),
            ((units, tokens), BF16),
            ((tokens, units), BF16),
            ((tokens, width), BF16),
            ((8, width), F32),
        )
        + shapes(*[((piece, width), BF16)] * held),
        scratch_shapes=[
            pltpu.VMEM((tokens, width), F32),
            pltpu.VMEM((tokens, width), BF16),
            pltpu.VMEM((tokens, width), BF16),
            pltpu.SemaphoreType.DMA((2,)),
        ],
        compiler_params=pltpu.CompilerParams(vmem_limit_bytes=36 * 2**20),
        cost_estimate=BRIEF,
        name="feed_forward",
    )(inputs, in_hbm(mixed), *map(in_hbm, weights), *upstream)


def feed_back_kernel(
    which_ref,
    d_down_ref,
    slope_ref,
    active_t_ref,
    shrink_ref,
    expand_ref,
    normed_ref,
    *refs,
    steps,
    block,
    last,
):
    step = pl.program_id(0)
    if last:
        gain_ref, *late_refs = refs[:5]
        grads_ref, bias_ref, d_attn_ref, d_mixed_ref, sums_ref = refs[5:10]
        turned, total, hat_ref, scale_ref, output_proj_ref, sems = refs[10:]
        late = [
            pltpu.make_async_copy(source, target, sems.at[index])
            for index, (source, target) in enumerate(
                zip(late_refs, (d_attn_ref, hat_ref, scale_ref, output_proj_ref))
            )
        ]

        @pl.when(step == 0)
        def _():
            for copy in late:
                copy.start()

    else:
        grads_ref, bias_ref, total_ref, turned, total = refs
    tokens = total.shape[0]
    pieces = [slice(start, start + block) for start in range(0, tokens, block)]

    @pl.when(step == 0)
    def _():
        total[...] = jnp.zeros_like(total)
        bias_ref[...] = jnp.zeros_like(bias_ref)

    bias = jnp.zeros((1, slope_ref.shape[1]), F32)
    for here in pieces:
        d_active = dot(d_down_ref[here, :], shrink_ref[...], NT)
        d_expand = (d_active * slope_ref[here, :].astype(F32)).astype(BF16)
        turned[:, here] = d_expand.T
        bias += jnp.sum(d_expand.astype(F32), 0, keepdims=True)
        total[here, :] += dot(d_expand, expand_ref[...], NT)
    row = lax.broadcasted_iota(jnp.int32, bias_ref.shape, 0)
    bias_ref[...] = jnp.where(row == step, bias, bias_ref[...])
    grads_ref[0] = dot(active_t_ref[...], d_down_ref[...]).astype(BF16)
    grads_ref[1] = dot(turned[...], normed_ref[...]).astype(BF16)

    if not last:

        @pl.when(step == steps - 1)
        def _():
            total_ref[...] = total[...].astype(BF16)

    else:

        @pl.when(step == steps - 1)
        def _():
            for copy in late:
                copy.wait()
            gain = gain_ref[...].astype(F32)
            d_gain = jnp.zeros((1, total.shape[1]), F32)
            d_shift = d_gain
            d_bias = d_gain
            for here in pieces:
                d_normed = total[here, :] + (
                    d_down_ref[here, :].astype(F32) + d_attn_ref[here, :].astype(F32)
                )
                hat = hat_ref[here, :].astype(F32)
                d_gain += jnp.sum(d_normed * hat, 0, keepdims=True)
                d_shift += jnp.sum(d_normed, 0, keepdims=True)
                d_attn = norm_back(d_normed, hat, scale_ref[here, :][:, 0:1], gain).astype(BF16)
                d_attn_ref[here, :] = d_attn
                d_bias += jnp.sum(d_attn.astype(F32), 0, keepdims=True)
                d_mixed_ref[here, :] = dot(d_attn, output_proj_ref[...], NT).astype(BF16)
            sums_ref[...] = stack_rows([d_gain, d_shift, d_bias])


def feed_back(which, d_down, slope, active_t, shrink, expand, normed, norm, block=512):
    tokens, width = d_down.shape
    half = slope.shape[1] // 2
    steps = half // block
    last = norm is not None
    at = lambda i, which: which[0] * steps + i
    whole = lambda *shape: pl.BlockSpec(
        shape, lambda i, which: (0,) * len(shape), pipeline_mode=pl.Buffered(1)
    )
    in_specs = [
        whole(tokens, width),
        pl.BlockSpec((tokens, block), lambda i, which: (0, at(i, which))),
        pl.BlockSpec((block, tokens), lambda i, which: (at(i, which), 0)),
        pl.BlockSpec((block, width), lambda i, which: (at(i, which), 0)),
        pl.BlockSpec((width, block), lambda i, which: (0, at(i, which))),
        whole(tokens, width),
    ]
    out_specs = [
        pl.BlockSpec((2, block, width), lambda i, which: (0, i, 0)),
        whole(8, block),
    ]
    out_shape = hbm_shapes(((2, half, width), BF16), ((8, block), F32))
    scratch = [pltpu.VMEM((block, tokens), BF16), pltpu.VMEM((tokens, width), F32)]
    extra = ()
    if last:
        gain, *late = norm
        extra = (gain, *map(in_hbm, late))
        in_specs += [whole(1, width)] + [pl.BlockSpec(memory_space=pl.ANY)] * len(late)
        out_specs += [whole(tokens, width)] * 2 + [whole(8, width)]
        out_shape += hbm_shapes(
            ((tokens, width), BF16), ((tokens, width), BF16), ((8, width), F32)
        )
        scratch += [
            pltpu.VMEM((tokens, width), BF16),
            pltpu.VMEM((tokens, PAIR), F32),
            pltpu.VMEM((width, width), BF16),
            pltpu.SemaphoreType.DMA((4,)),
        ]
    else:
        out_specs.append(whole(tokens, width))
        out_shape += hbm_shapes(((tokens, width), BF16))
    return pl.pallas_call(
        functools.partial(feed_back_kernel, steps=steps, block=min(512, tokens), last=last),
        grid_spec=pltpu.PrefetchScalarGridSpec(
            num_scalar_prefetch=1,
            grid=(steps,),
            in_specs=in_specs,
            out_specs=out_specs,
            scratch_shapes=scratch,
        ),
        out_shape=out_shape,
        compiler_params=pltpu.CompilerParams(vmem_limit_bytes=44 * 2**20),
        cost_estimate=BRIEF,
        name="feed_back_last" if last else "feed_back",
    )(which, *map(in_hbm, (d_down, slope, active_t, shrink, expand, normed)), *extra)


def pack_kernel(at_ref, flat_ref, marks_ref, *refs, order):
    outs, sems = refs[:-1], refs[-1]
    piece = flat_ref.shape[1]
    for part, out_ref in zip(order, outs):
        marks = marks_ref[pl.ds(at_ref[0] ^ part, 1), :].astype(F32)
        out_ref[piece:, :] = jnp.zeros((MARK_ROWS, out_ref.shape[1]), BF16)
        out_ref[piece:, 0:piece] = jnp.broadcast_to(marks, (MARK_ROWS, piece)).astype(BF16)
    copies = [
        pltpu.make_async_copy(
            flat_ref.at[at_ref[0] ^ part], out_ref.at[pl.ds(0, piece)], sems.at[index]
        )
        for index, (part, out_ref) in enumerate(zip(order, outs))
    ]
    for copy in copies:
        copy.start()
    for copy in copies:
        copy.wait()


MARK_ROWS = 16


def pack(at, flat, marks, order):
    held, piece, width = flat.shape
    vmem = pl.BlockSpec(memory_space=pltpu.VMEM)
    return pl.pallas_call(
        functools.partial(pack_kernel, order=order),
        in_specs=[
            pl.BlockSpec(memory_space=pltpu.SMEM),
            pl.BlockSpec(memory_space=pl.ANY),
            vmem,
        ],
        out_specs=[vmem] * held,
        out_shape=shapes(*[((piece + MARK_ROWS, width), BF16)] * held),
        scratch_shapes=[pltpu.SemaphoreType.DMA((held,))],
        compiler_params=pltpu.CompilerParams(vmem_limit_bytes=16 * 2**20),
        cost_estimate=BRIEF,
        name="pack",
    )(at, in_hbm(flat), marks)


def unpack_kernel(*refs):
    parts, (rows_ref, marks_ref) = refs[:-2], refs[-2:]
    piece = rows_ref.shape[0] // len(parts)
    for index, ref in enumerate(parts):
        here = slice(index * piece, (index + 1) * piece)
        rows_ref[here, :] = ref[0:piece, :]
        marks = ref[piece:, 0:piece].astype(F32)[0:1, :]
        marks_ref[here, :] = jnp.broadcast_to(marks, (PAIR, piece)).T.astype(BF16)


def unpack(parts):
    width = parts[0].shape[1]
    tokens = len(parts) * (parts[0].shape[0] - MARK_ROWS)
    return pl.pallas_call(
        unpack_kernel,
        grid=(1,),
        in_specs=[fixed(*part.shape) for part in parts],
        out_specs=[fixed(tokens, width), fixed(tokens, PAIR)],
        out_shape=hbm_shapes(((tokens, width), BF16), ((tokens, PAIR), BF16)),
        compiler_params=pltpu.CompilerParams(vmem_limit_bytes=16 * 2**20),
        cost_estimate=BRIEF,
        name="unpack",
    )(*parts)


def weight_kernel(
    core_ref,
    first_sums_ref,
    second_sums_ref,
    own_bias_ref,
    other_bias_ref,
    *refs,
    steps,
):
    sources, (other_ref, own_ref, small_ref) = refs[:6], refs[6:9]
    targets, (inputs_t, mixed_t, sems) = refs[9:15], refs[15:]
    inputs_ref, dq_ref, dk_ref, dv_ref, mixed_ref, d_attn_ref = targets
    copies = [
        pltpu.make_async_copy(source, target, sems.at[index])
        for index, (source, target) in enumerate(zip(sources, targets))
    ]
    for copy in copies:
        copy.start()
    count = inputs_ref.shape[1] // 2
    core = core_ref[0]
    for ref in (other_ref, own_ref):
        if ref.shape[0] > 4 * count:
            ref[4 * count :, :] = jnp.zeros((ref.shape[0] - 4 * count, ref.shape[1]), BF16)
    copies[0].wait()
    inputs_t[...] = inputs_ref[...].T
    for at, right_ref in enumerate((dq_ref, dk_ref, dv_ref, d_attn_ref)):
        copies[at + 1].wait()
        left_ref = inputs_t
        if at == 3:
            copies[5].wait()
            mixed_t[...] = mixed_ref[...].T
            left_ref = mixed_t
        for half, out_ref in ((1 - core, other_ref), (core, own_ref)):
            rows = pl.ds(pl.multiple_of(half * count, PAIR), count)
            out_ref[at * count : (at + 1) * count, :] = dot(left_ref[rows, :], right_ref[...]).astype(
                BF16
            )
    small_ref[...] = jnp.zeros_like(small_ref)
    small_ref[0:1, :] = jnp.sum(dq_ref[...].astype(F32), 0, keepdims=True)
    small_ref[1:2, :] = jnp.sum(dv_ref[...].astype(F32), 0, keepdims=True)
    small_ref[2:5, :] = first_sums_ref[0:3, :]
    small_ref[5:8, :] = second_sums_ref[0:3, :]
    block = own_bias_ref.shape[1]
    own, other = own_bias_ref[0:steps, :], other_bias_ref[0:steps, :]
    small_ref[8 : 8 + steps, 0:block] = jnp.where(core == 0, own, other)
    small_ref[8 + steps : 8 + 2 * steps, 0:block] = jnp.where(core == 0, other, own)


def weight_halves(core, values, unit, sums, steps):
    tokens, width = values[0].shape
    rows = -(-2 * width // unit) * unit
    vmem = pl.BlockSpec(memory_space=pltpu.VMEM)
    anywhere = pl.BlockSpec(memory_space=pl.ANY)
    return pl.pallas_call(
        functools.partial(weight_kernel, steps=steps),
        in_specs=[pl.BlockSpec(memory_space=pltpu.SMEM)] + [vmem] * 4 + [anywhere] * 6,
        out_specs=[vmem] * 3,
        out_shape=shapes(
            ((rows, width), BF16), ((rows, width), BF16), ((SMALL, width), F32)
        ),
        scratch_shapes=[pltpu.VMEM((tokens, width), BF16)] * 6
        + [pltpu.VMEM((width, tokens), BF16)] * 2
        + [pltpu.SemaphoreType.DMA((6,))],
        compiler_params=pltpu.CompilerParams(vmem_limit_bytes=32 * 2**20),
        cost_estimate=BRIEF,
        name="weight_halves",
    )(core, *sums, *map(in_hbm, values))


def input_grad_kernel(*refs, held):
    sources, outs = refs[:7], refs[7 : 7 + held]
    (d_attn, *factors), total, sems = refs[7 + held : 14 + held], refs[-2], refs[-1]
    copies = [
        pltpu.make_async_copy(source, target, sems.at[index])
        for index, (source, target) in enumerate(zip(sources, (d_attn, *factors)))
    ]
    for copy in copies:
        copy.start()
    piece = outs[0].shape[0]
    copies[0].wait()
    for index in range(3):
        for copy in copies[2 * index + 1 : 2 * index + 3]:
            copy.wait()
        left, right = factors[2 * index : 2 * index + 2]
        for number, out_ref in enumerate(outs):
            here = slice(number * piece, (number + 1) * piece)
            before = d_attn[here, :].astype(F32) if index == 0 else total[here, :]
            value = before + dot(left[here, :], right[...], NT)
            if index < 2:
                total[here, :] = value
            else:
                out_ref[...] = value.astype(BF16)


def input_grad(d_attn, factors, held):
    tokens, width = d_attn.shape
    anywhere = pl.BlockSpec(memory_space=pl.ANY)
    values = [d_attn] + [value for pair in factors for value in pair]
    return pl.pallas_call(
        functools.partial(input_grad_kernel, held=held),
        in_specs=[anywhere] * 7,
        out_specs=[pl.BlockSpec(memory_space=pltpu.VMEM)] * held,
        out_shape=shapes(*[((tokens // held, width), BF16)] * held),
        scratch_shapes=[pltpu.VMEM(value.shape, BF16) for value in values]
        + [pltpu.VMEM((tokens, width), F32), pltpu.SemaphoreType.DMA((7,))],
        compiler_params=pltpu.CompilerParams(vmem_limit_bytes=24 * 2**20),
        cost_estimate=BRIEF,
        name="input_grad",
    )(*map(in_hbm, values))


def feed_out_kernel(which_ref, half_ref, *refs, steps):
    del which_ref
    shrink_ref, expand_ref = refs[-2:]

    @pl.when(pl.program_id(0) < steps)
    def _():
        shrink_ref[...] = half_ref[...].astype(F32)

    @pl.when(pl.program_id(0) >= steps)
    def _():
        expand_ref[...] = half_ref[...].T.astype(F32)


def feed_out(which, values, before=(), block=768):
    width = values.shape[1]
    half = values.shape[0] // 2
    steps = half // block
    return pl.pallas_call(
        functools.partial(feed_out_kernel, steps=steps),
        grid_spec=pltpu.PrefetchScalarGridSpec(
            num_scalar_prefetch=1,
            grid=(2 * steps,),
            in_specs=[pl.BlockSpec((block, width), lambda i, which: (i, 0))]
            + [pl.BlockSpec(memory_space=pl.ANY)] * len(before),
            out_specs=[
                pl.BlockSpec(
                    (block, width),
                    lambda i, which: (which[0] * steps + jnp.minimum(i, steps - 1), 0),
                ),
                pl.BlockSpec(
                    (width, block),
                    lambda i, which: (0, which[0] * steps + jnp.maximum(i - steps, 0)),
                ),
            ],
        ),
        out_shape=shapes(((2 * half, width), F32), ((width, 2 * half), F32)),
        input_output_aliases={2 + i: i for i in range(len(before))},
        compiler_params=pltpu.CompilerParams(vmem_limit_bytes=28 * 2**20),
        cost_estimate=BRIEF,
        name="feed_out",
    )(which, values, *before)


def attn_out_kernel(which_ref, half_ref, *refs):
    del which_ref
    for index, out_ref in enumerate(refs[-4:]):

        @pl.when(pl.program_id(0) == index)
        def _(out_ref=out_ref):
            out_ref[...] = half_ref[...].astype(F32)


def attn_out(which, values, before=()):
    width = values.shape[1]
    half = width // 2
    return pl.pallas_call(
        attn_out_kernel,
        grid_spec=pltpu.PrefetchScalarGridSpec(
            num_scalar_prefetch=1,
            grid=(4,),
            in_specs=[pl.BlockSpec((half, width), lambda i, which: (i, 0))]
            + [pl.BlockSpec(memory_space=pl.ANY)] * len(before),
            out_specs=[pl.BlockSpec((half, width), lambda i, which: (which[0], 0))] * 4,
        ),
        out_shape=shapes(*[((width, width), F32)] * 4),
        input_output_aliases={2 + i: i for i in range(len(before))},
        compiler_params=pltpu.CompilerParams(vmem_limit_bytes=24 * 2**20),
        cost_estimate=BRIEF,
        name="attn_out",
    )(which, values, *before)


def place_kernel(at_ref, *refs):
    del at_ref
    out_ref = refs[-1]
    for index, ref in enumerate(refs[:-1]):

        @pl.when(pl.program_id(0) == index)
        def _(ref=ref):
            out_ref[0] = ref[...]


def place(at, parts):
    piece, width = parts[0].shape
    held = len(parts)
    return pl.pallas_call(
        place_kernel,
        grid_spec=pltpu.PrefetchScalarGridSpec(
            num_scalar_prefetch=1,
            grid=(held,),
            in_specs=[pl.BlockSpec((piece, width), lambda i, at: (0, 0))] * held,
            out_specs=pl.BlockSpec((1, piece, width), lambda i, at: (at[0] ^ i, 0, 0)),
        ),
        out_shape=jax.ShapeDtypeStruct((held, piece, width), BF16),
        compiler_params=pltpu.CompilerParams(vmem_limit_bytes=16 * 2**20),
        cost_estimate=BRIEF,
        name="place",
    )(at, *parts)


def rows_of(ref, which, count, base=0):
    return ref[pl.ds(pl.multiple_of(base + which * count, 16), count), :]


def sum_of(terms):
    return functools.reduce(lambda a, b: a + b, [t.astype(F32) for t in terms]).astype(BF16)


def scatter_kernel(bits_ref, *refs, groups):
    outs = refs[-2 * groups :]
    ins = refs[: -2 * groups]
    together = len(ins) == 2
    base = 0
    for group in range(groups):
        terms = ins if together else ins[2 * group : 2 * group + 2]
        sent_ref, kept_ref = outs[2 * group : 2 * group + 2]
        count = kept_ref.shape[0]
        here = bits_ref[group]
        sent_ref[...] = sum_of([rows_of(term, 1 - here, count, base) for term in terms])
        kept_ref[...] = sum_of([rows_of(term, here, count, base) for term in terms])
        if together:
            base += 2 * count


def local_call(kernel, bits, values, out_shape, name):
    vmem = pl.BlockSpec(memory_space=pltpu.VMEM)
    return pl.pallas_call(
        kernel,
        in_specs=[pl.BlockSpec(memory_space=pltpu.SMEM)] + [vmem] * len(values),
        out_specs=[vmem] * len(out_shape),
        out_shape=out_shape,
        compiler_params=pltpu.CompilerParams(vmem_limit_bytes=24 * 2**20),
        cost_estimate=BRIEF,
        name=name,
    )(bits, *values)


def scatter_local(bits, pairs, counts=None):
    if counts is None:
        counts = [kept.shape[0] for kept, _ in pairs]
    groups = len(counts)
    counts = [count // 2 for count in counts]
    width = pairs[0][0].shape[1]
    outs = local_call(
        functools.partial(scatter_kernel, groups=groups),
        bits,
        [value for pair in pairs for value in pair],
        shapes(*[((count, width), BF16) for count in counts for _ in range(2)]),
        "scatter_local",
    )
    return [outs[2 * i : 2 * i + 2] for i in range(groups)]


def scatter_first_kernel(bits_ref, own_at, got_at, *refs, counts):
    outs, (own, got, sems) = refs[:-3], refs[-3:]
    spans = []
    base = 0
    for group, count in enumerate(counts):
        for kept in range(2):
            half = bits_ref[group] if kept else 1 - bits_ref[group]
            start = pl.multiple_of(base + half * (count // 2), 16)
            spans.append((start, count // 2, outs[2 * group + kept]))
        base += count
    spans = spans[0::2] + spans[1::2]
    copies = []
    for index, (start, count, _) in enumerate(spans):
        rows = pl.ds(start, count)
        for which, (source, target) in enumerate(((own_at, own), (got_at, got))):
            copies.append(
                pltpu.make_async_copy(source.at[rows], target.at[rows], sems.at[2 * index + which])
            )
            copies[-1].start()
    for index, (start, count, out_ref) in enumerate(spans):
        for copy in copies[2 * index : 2 * index + 2]:
            copy.wait()
        rows = pl.ds(start, count)
        out_ref[...] = sum_of([own[rows, :], got[rows, :]])


def scatter_first(bits, own, got, counts):
    rows, width = own.shape
    anywhere = pl.BlockSpec(memory_space=pl.ANY)
    vmem = pl.BlockSpec(memory_space=pltpu.VMEM)
    outs = pl.pallas_call(
        functools.partial(scatter_first_kernel, counts=counts),
        in_specs=[pl.BlockSpec(memory_space=pltpu.SMEM), anywhere, anywhere],
        out_specs=[vmem] * (2 * len(counts)),
        out_shape=shapes(*[((count // 2, width), BF16) for count in counts for _ in range(2)]),
        scratch_shapes=[pltpu.VMEM((rows, width), BF16)] * 2
        + [pltpu.SemaphoreType.DMA((4 * len(counts),))],
        compiler_params=pltpu.CompilerParams(vmem_limit_bytes=24 * 2**20),
        cost_estimate=BRIEF,
        name="scatter_first",
    )(bits, in_hbm(own), in_hbm(got))
    return [outs[2 * group : 2 * group + 2] for group in range(len(counts))]


SMALL = 16


def put_small(ref, at, values):
    ref[at : at + SMALL, :] = values.astype(BF16)


def get_small(ref, at):
    return ref[at : at + SMALL, :].astype(F32)


def settle_kernel(bits_ref, *refs, groups, small):
    del bits_ref
    ins, outs = refs[: 2 * groups], refs[2 * groups + small :]
    for group in range(groups):
        count = ins[2 * group].shape[0]
        outs[group][0:count, :] = sum_of([ins[2 * group][...], ins[2 * group + 1][...]])
        if small and group == 0:
            put_small(outs[group], count, refs[2 * groups][...])


def settle_local(bits, pairs, small):
    width = pairs[0][0].shape[1]
    counts = [kept.shape[0] for kept, _ in pairs]
    if small is not None:
        counts[0] += SMALL
    return local_call(
        functools.partial(settle_kernel, groups=len(pairs), small=int(small is not None)),
        bits,
        [value for pair in pairs for value in pair] + ([] if small is None else [small]),
        shapes(*[((count, width), BF16) for count in counts]),
        "settle_local",
    )


def add_kernel(bits_ref, *refs, groups, small):
    del bits_ref
    ins, outs = refs[: 2 * groups], refs[2 * groups :]
    for group in range(groups):
        own_ref, got_ref = ins[2 * group : 2 * group + 2]
        extra = SMALL if small and group == 0 else 0
        count = own_ref.shape[0] - extra
        outs[group][0:count, :] = sum_of([own_ref[0:count, :], got_ref[0:count, :]])
        if extra:
            put_small(outs[group], count, get_small(own_ref, count) + get_small(got_ref, count))


def add_local(bits, pairs, small):
    return local_call(
        functools.partial(add_kernel, groups=len(pairs), small=small),
        bits,
        [value for pair in pairs for value in pair],
        shapes(*[(own.shape, BF16) for own, _ in pairs]),
        "add_local",
    )


def join_kernel(bits_ref, *refs, groups, small, merged, pieces):
    ins, outs = refs[: 2 * pieces * groups], list(refs[2 * pieces * groups :])
    parts = len(outs) // groups
    base = 0
    for group in range(groups):
        owns = ins[2 * pieces * group : 2 * pieces * group + 2 * pieces : 2]
        gots = ins[2 * pieces * group + 1 : 2 * pieces * group + 2 * pieces : 2]
        extra = SMALL if small and group == 0 else 0
        count = owns[0].shape[0] - extra
        here = bits_ref[group]
        if parts > 1:
            for half, out_ref in enumerate(outs[2 * group : 2 * group + 2]):

                @pl.when(here == half)
                def _(out_ref=out_ref):
                    out_ref[...] = owns[0][...]

                @pl.when(here != half)
                def _(out_ref=out_ref):
                    out_ref[...] = gots[0][...]

            continue
        out_ref = outs[0 if merged else group]
        whole = count * pieces
        for half, refs_of in ((here, owns), (1 - here, gots)):
            for index, ref in enumerate(refs_of):
                start = pl.multiple_of(base + half * whole + index * count, 16)
                out_ref[pl.ds(start, count), :] = ref[0:count, :]
        if extra:
            at = out_ref.shape[0] - SMALL if merged else base + 2 * whole
            put_small(out_ref, at, get_small(owns[0], count) + get_small(gots[0], count))
        if merged:
            base += 2 * whole


def join_local(bits, arrived, small, merged, parts=1):
    width = arrived[0][0].shape[1]
    pieces = len(arrived[0]) // 2
    counts = [2 * pieces * group[0].shape[0] for group in arrived]
    if small:
        counts[0] -= SMALL
    if merged:
        counts = [sum(counts)]
    counts = [count // parts for count in counts for _ in range(parts)]
    return local_call(
        functools.partial(
            join_kernel, groups=len(arrived), small=small, merged=merged, pieces=pieces
        ),
        bits,
        [value for group in arrived for value in group],
        shapes(*[((count, width), BF16) for count in counts]),
        "join_local",
    )


def tie(*values):
    return lax.optimization_barrier(values)


def pick(which, parts):
    if len(parts) == 1:
        return parts[0]
    half = len(parts) // 2
    return jnp.where(which < half, pick(which, parts[:half]), pick(which - half, parts[half:]))


def column_sum(values):
    return jnp.sum(values.astype(F32), 0)


class Stage:
    def __init__(self, sizes, bits):
        self.bits = bits
        rows, seq = sizes
        self.pairs = []
        for index in range(rows * seq):
            axis, bit = bits[index & 1]
            self.pairs.append((index, index ^ ((1 << bit) * (seq if axis == "rows" else 1))))

    def here(self):
        first, second = [(lax.axis_index(axis) >> bit) & 1 for axis, bit in self.bits]
        if self.bits[0] == self.bits[1]:
            return first
        return jnp.where(lax.axis_index("seq") & 1 == 0, first, second)

    def swap(self, values):
        return lax.ppermute(values, ("rows", "seq"), self.pairs)


def total_over_chips(own, got, core_stage, orders, small=None, near=False):
    depth = len(orders[0][1])
    groups = range(len(orders))

    def bits_at(step):
        return jnp.stack([stages[step].here() for _, stages in orders]).astype(jnp.int32)

    def pairs_of(flat):
        return [flat[i : i + 2] for i in range(0, len(flat), 2)]

    def send(step, values, keep):
        flat = []
        for group in groups:
            flat += [keep[group], orders[group][1][step].swap(values[group])]
        return flat

    counts = [count for count, _ in orders]
    if near:
        parts = scatter_local(bits_at(0), [[own, got]], counts)
    else:
        parts = scatter_first(bits_at(0), own, got, counts)
    last = depth - 1 if near else depth
    for step in range(1, last + 1):
        flat = yield send(step - 1, [p[0] for p in parts], [p[1] for p in parts])
        if step < last:
            parts = scatter_local(bits_at(step), pairs_of(flat))
    values = settle_local(bits_at(0), pairs_of(flat), small)
    if near:
        flat = yield send(last, values, values)
        values = add_local(bits_at(0), pairs_of(flat), small is not None)
    carried = small is not None
    for step in reversed(range(last)):
        flat = yield send(step, values, values)
        parts = 2 if step == 1 and not carried else 1
        values = join_local(bits_at(step), pairs_of(flat), carried, step == 0, parts)
        if parts > 1:
            lower = yield send(0, values[0::2], values[0::2])
            upper = yield send(0, values[1::2], values[1::2])
            arrived = [list(low) + list(high) for low, high in zip(pairs_of(lower), pairs_of(upper))]
            values = join_local(bits_at(0), arrived, carried, True)
            break
    both = yield [values[0], core_stage.swap(values[0])]
    return both


def arriving(values):
    values = yield values
    return values[1::2]


class Flow:
    def __init__(self, steps, left):
        self.steps = steps
        self.left = left
        self.pending = next(steps)
        self.result = None


class Timetable:
    def __init__(self):
        self.flows = []

    def open(self, steps, left=1):
        self.flows.append(Flow(steps, left))
        return self.flows[-1]

    def advance(self, moving, *values):
        flows = [flow for flow in self.flows if flow.result is None]
        held = [flow.pending if flow in moving else flow.pending[0::2] for flow in flows]
        tied = list(tie(*values, *[value for part in held for value in part]))
        values, tied = tied[: len(values)], tied[len(values) :]
        for flow, part in zip(flows, held):
            back, tied = tied[: len(part)], tied[len(part) :]
            if flow not in moving:
                flow.pending[0::2] = back
                continue
            flow.left -= 1
            try:
                flow.pending = flow.steps.send(back)
            except StopIteration as end:
                flow.result = end.value
        return self.settle(*values) if moving and values else values

    def settle(self, *values):
        return self.advance([], *values)


def solution(mesh):
    seq_size = mesh.shape["seq"]
    rows_size = mesh.shape["rows"]
    seq_bits = seq_size.bit_length() - 1
    rows_bits = rows_size.bit_length() - 1
    off_chip = [("seq", bit) for bit in range(1, seq_bits)]
    off_chip += [("rows", bit) for bit in range(rows_bits)]
    first, *middle, ahead, final = off_chip
    sizes = (rows_size, seq_size)
    core_stage = Stage(sizes, [("seq", 0)] * 2)
    straight = [first] + middle + [ahead, final]
    turned = middle + [ahead, first, final]
    spun = [ahead, first] + middle + [final]
    wide = [Stage(sizes, bits) for bits in zip(straight, turned)]
    slim = [Stage(sizes, bits) for bits in zip(spun, spun)]

    def body(
        hidden_in,
        segments,
        grad_mask,
        grad_out,
        query_proj,
        query_bias,
        key_proj,
        value_proj,
        value_bias,
        output_proj,
        output_bias,
        first_gain,
        first_shift,
        expand_proj,
        expand_bias,
        shrink_proj,
        shrink_bias,
        second_gain,
        second_shift,
    ):
        micro, rows_here, piece, width = hidden_in.shape
        held = micro * rows_here
        sharers = seq_size // held
        tokens = held * piece
        source_at = lax.axis_index("seq") % held
        core = core_stage.here()
        core_at = core.reshape(1).astype(jnp.int32)

        def trade(to_rows, part):
            there = [(s, (s % held ^ part) * sharers + s // held) for s in range(seq_size)]
            return there if to_rows else [(b, a) for a, b in there]

        def to_rows(values):
            return [
                lax.ppermute(
                    lax.dynamic_index_in_dim(values, source_at ^ part, 0, False),
                    "seq",
                    trade(True, part),
                )
                for part in range(held)
            ]

        def send_pieces(values, chosen=range(held)):
            return [
                value
                for part in chosen
                for value in (values[part], lax.ppermute(values[part], "seq", trade(False, part)))
            ]

        def place_pieces(parts):
            at = source_at.reshape(1).astype(jnp.int32)
            return place(at, parts).reshape((micro, rows_here) + parts[0].shape)

        same_row = [[r * sharers + g for g in range(sharers)] for r in range(held)]

        def all_keys(values):
            if sharers == 1:
                return values
            return lax.all_gather(values, "seq", axis=0, tiled=True, axis_index_groups=same_row)

        def own_keys(values):
            if sharers == 1:
                return values
            return lax.psum_scatter(
                values, "seq", scatter_dimension=0, tiled=True, axis_index_groups=same_row
            ).astype(BF16)

        order = tuple(reversed(range(held)))
        packed = pack(
            source_at.reshape(1).astype(jnp.int32),
            hidden_in.reshape(held, piece, width),
            segments.reshape(held, piece),
            order,
        )
        arrived = [
            lax.ppermute(value, "seq", trade(True, part)) for part, value in zip(order, packed)
        ]
        inputs, seg_q = unpack(arrived[::-1])
        masked = (grad_out * grad_mask[..., None].astype(BF16)).reshape(held, piece, width)
        masked, inputs, seg_q = tie(masked, inputs, seg_q)
        upstream = to_rows(masked)

        queries = (
            (dot(inputs, query_proj) + query_bias.astype(F32)) * 0.125
        ).astype(BF16)
        keys = all_keys(dot(inputs, key_proj).astype(BF16))
        values = all_keys((dot(inputs, value_proj) + value_bias.astype(F32)).astype(BF16))
        seg_k = all_keys(seg_q)
        mixed, query_side = attention_forward(queries, keys, values, seg_q, seg_k)
        row = lambda vector: vector.reshape(1, -1)
        hat, scale, normed, active_t, slope, d_down, second_sums, *result = feed_forward(
            inputs,
            mixed,
            upstream,
            (
                output_proj,
                row(output_bias),
                row(first_gain),
                row(first_shift),
                expand_proj,
                row(expand_bias),
                shrink_proj,
                row(shrink_bias),
                row(second_gain),
                row(second_shift),
            ),
        )
        table = Timetable()
        advance = table.advance
        layer_flow = table.open(arriving(send_pieces(result)))

        def chips(own, got, orders, small=None):
            near = small is not None
            steps = total_over_chips(own, got, core_stage, orders, small, near)
            return table.open(steps, 2 * len(wide) + (0 if near else 2))

        back = functools.partial(
            feed_back,
            slope=slope,
            active_t=active_t,
            shrink=shrink_proj,
            expand=expand_proj,
            normed=normed,
        )
        other, other_bias, d_normed = back(1 - core_at, d_down, norm=None)
        half = other.shape[1]
        got = core_stage.swap(other.reshape(2 * half, width))
        own, own_bias, d_attn, d_mixed, first_sums = back(
            core_at, d_down, norm=(row(first_gain), d_normed, hat, scale, output_proj)
        )
        own, got, d_mixed = advance([layer_flow], own.reshape(2 * half, width), got, d_mixed)
        unit = 16 << len(off_chip)

        def thirds(count):
            less = count // unit // 3 * unit
            return [(count - less, wide)] + ([(less, slim)] if less else [])

        feed_flow = chips(own, got, thirds(2 * half))

        pairs = width // PAIR
        kept = BF16 if sharers == 1 else F32
        grads = None
        for first, last in ((0, pairs),):
            grads = attention_backward(
                query_side, keys, values, seg_k, mixed, d_mixed, kept, first, last - first, grads
            )
            *grads, d_mixed = advance([feed_flow], *grads, d_mixed)

        d_query, d_keys, d_values = grads
        d_key = own_keys(d_keys)
        d_value = own_keys(d_values)
        steps = half // other_bias.shape[1]
        other, own, small = weight_halves(
            core_at,
            (inputs, d_query, d_key, d_value, mixed, d_attn),
            unit,
            (first_sums, second_sums, own_bias, other_bias),
            steps,
        )
        other, own, small, d_query, d_key, d_value = advance(
            [feed_flow], other, own, small, d_query, d_key, d_value
        )
        got = core_stage.swap(other)
        d_input = input_grad(
            d_attn, ((d_query, query_proj), (d_key, key_proj), (d_value, value_proj)), held
        )
        own, got, small, *d_input = advance([feed_flow], own, got, small, *d_input)
        attn_flow = chips(own, got, [(own.shape[0], wide)], small)
        held_back = held // 2
        soon = [part for part in range(held) if part != held_back]
        piece_flow = table.open(arriving(send_pieces(d_input, soon)))
        last_flow = table.open(arriving(send_pieces(d_input, [held_back])))

        both = [feed_flow, attn_flow]
        layer_out = place_pieces(list(map(in_hbm, layer_flow.result)))
        (layer_out,) = advance(both, layer_out)
        advance(both + [piece_flow])
        advance(both)
        advance(both + [last_flow])
        arrived = list(piece_flow.result)
        arrived.insert(held_back, last_flow.result[0])
        grad_in = place_pieces(arrived)
        (grad_in,) = advance(both, grad_in)
        while feed_flow.left > 1:
            advance(both)
        feed_grads = feed_out(core_at, feed_flow.pending[0])
        feed_grads = advance(both, *feed_grads)
        feed_grads = feed_out(1 - core_at, feed_flow.result[1], feed_grads)
        while attn_flow.left > 1:
            feed_grads = advance([attn_flow], *feed_grads)
        attn_grads = attn_out(core_at, attn_flow.pending[0])
        attn_grads = advance([attn_flow], *attn_grads)
        own, got = attn_flow.result
        attn_grads = attn_out(1 - core_at, got, attn_grads)
        totals = own[-SMALL:].astype(F32) + got[-SMALL:].astype(F32)
        shrink_grad, expand_grad = feed_grads
        expand_bias_grad = totals[8 : 8 + 2 * steps, : other_bias.shape[1]].reshape(-1)
        return (
            layer_out,
            grad_in,
            attn_grads[0],
            totals[0],
            attn_grads[1],
            attn_grads[2],
            totals[1],
            attn_grads[3],
            totals[4],
            totals[2],
            totals[3],
            expand_grad,
            expand_bias_grad,
            shrink_grad,
            totals[7],
            totals[5],
            totals[6],
        )

    split = P(None, "rows", "seq", None)
    whole = P()
    return jax.shard_map(
        body,
        mesh=mesh,
        in_specs=(split, P(None, "rows", "seq"), P(None, "rows", "seq"), split) + (whole,) * 15,
        out_specs=(split, split) + (whole,) * 15,
        check_vma=False,
    )
```
